32 devices in a mesh: rows: 16 (over z, y, x), hid: 2 (over core).
Axes of the slice: x: 2, y: 2, z: 4, core: 2. Of those that a mesh axis runs over, the one named last changes fastest.
Arguments:
- hidden_in: bfloat16 [4096, 768], P('rows', 'hid'), may hold values from -6 to 6
- d_out: bfloat16 [4096, 768], P('rows', 'hid'), may hold values from -6 to 6
- gains: float32 [2, 2, 768], P(None, None, 'hid'), may hold values from 0.25 to 1.75
- mixer: bfloat16 [2, 3, 4, 192, 192], P(None, None, 'hid'), may hold values from -0.4375 to 0.4375
- skip: float32 [2, 768], P(None, 'hid'), may hold values from -3 to 3
- filters: float32 [2, 2, 128, 768], P(None, None, None, 'hid'), may hold values from -0.5 to 0.5
- gate_up: bfloat16 [2, 2, 768, 3072], P(None, None, None, 'hid'), may hold values from -0.21875 to 0.21875
- down: bfloat16 [2, 768, 3072], P(None, None, 'hid'), may hold values from -0.109375 to 0.109375
Outputs:
- hidden_out: bfloat16 [4096, 768], P('rows', 'hid')
- grad_in: float32 [4096, 768], P('rows', 'hid')
- grad_gains: float32 [2, 2, 768], P(None, None, 'hid')
- grad_mixer: float32 [2, 3, 4, 192, 192], P(None, None, 'hid')
- grad_skip: float32 [2, 768], P(None, 'hid')
- grad_filters: float32 [2, 2, 128, 768], P(None, None, None, 'hid')
- grad_gate_up: float32 [2, 2, 768, 3072], P(None, None, 'rows', 'hid')
- grad_down: float32 [2, 768, 3072], P(None, 'rows', 'hid')
The draws below stay inside these ranges and needn't reach their ends.
All inputs are finite; a program needn't handle non-finite values.
Results may differ from the reference program's by a relative error of at most 0.019.
Values may be sent and summed in bfloat16 or wider, within the bound.
A program may use at most 192 MiB of HBM per device.

```python
import math
import jax
import jax.numpy as jnp
from jax import lax

D = 768
FF = 3072
BLOCKS = 4
ORDER = 128
BSIZE = 192
LAYERS = 2
TOKENS = 4096
LENGTH = 4096
SEQS = 1


def levels(own_key, extent, split, low, largest):
    level = 1.0
    for position, shards_of in split:
        heights = jax.random.uniform(jax.random.fold_in(jax.random.fold_in(own_key, 6), position), (shards_of,), jnp.float32, low / len(split), largest / len(split))
        level = level * jnp.repeat(jnp.exp(heights), extent[position] // shards_of).reshape((-1,) + (1,) * (len(extent) - 1 - position))
    return level


def bell_draw(stream_key, dims, scale, bound, cuts=(), held_as=jnp.bfloat16):
    entries = scale * jax.random.normal(stream_key, dims, jnp.float32)
    if cuts:
        entries = entries * levels(stream_key, dims, cuts, -0.22, 0.18)
    return jnp.clip(entries, -bound, bound).astype(held_as)


def setup_inputs(seed: int = 0) -> dict:
    splits = jax.random.split(jax.random.key(seed), 9)
    return {
        "hidden_in": bell_draw(splits[0], (TOKENS, D), 1.0, 6.0, ((0, 16), (1, 2))),
        "d_out": bell_draw(splits[1], (TOKENS, D), 1.0, 6.0, ((0, 16), (1, 2))),
        "gains": jnp.clip(1.0 + 0.15 * jax.random.normal(splits[2], (LAYERS, 2, D), jnp.float32), 0.25, 1.75),
        "mixer": bell_draw(splits[3], (LAYERS, 3, BLOCKS, BSIZE, BSIZE), BSIZE ** -0.5, 0.4375, ((2, 2),)),
        "skip": bell_draw(splits[4], (LAYERS, D), 0.5, 3.0, ((1, 2),), jnp.float32),
        "filters": bell_draw(splits[5], (LAYERS, 2, ORDER, D), ORDER ** -0.5, 0.5, ((3, 2),), jnp.float32),
        "gate_up": bell_draw(splits[6], (LAYERS, 2, D, FF), D ** -0.5, 0.21875, ((3, 2),)),
        "down": bell_draw(splits[7], (LAYERS, D, FF), FF ** -0.5, 0.109375, ((2, 2),)),
    }


norm_eps = 1e-05
filter_decay = 0.02
exact = lax.Precision.HIGHEST

@jax.custom_vjp
def low(v):
    return lax.optimization_barrier(v.astype(jnp.bfloat16)).astype(jnp.float32)

@jax.custom_vjp
def low_back(v):
    return v

def low_keep(v):
    return (low(v), None)

def low_pass(kept, grad):
    return (grad,)

def back_keep(v):
    return (v, None)

def back_low(kept, grad):
    return (low(grad),)
low.defvjp(low_keep, low_pass)
low_back.defvjp(back_keep, back_low)

def positions(length):
    half_order = ORDER // 2
    steps = jnp.arange(length, dtype=jnp.int32)
    index_list = jnp.arange(half_order, dtype=jnp.int32)
    multiple = 1 + index_list * index_list * (length // 4) // (half_order * half_order)
    phase = (steps[:, None] * multiple[None, :] % length).astype(jnp.float32) * (2.0 * math.pi / length)
    return jnp.concatenate([jnp.sin(phase), jnp.cos(phase)], axis=1)

def envelope(length, channels, width):
    fraction = (channels * 37 % width).astype(jnp.float32) / (width - 1)
    start_log = math.log(1.0 / 40.0)
    rate_list = jnp.exp(start_log + (math.log(1.5 / length) - start_log) * fraction)
    steps = jnp.arange(length, dtype=jnp.int32).astype(jnp.float32)
    decay = jnp.exp(-steps[:, None] * rate_list[None, :])
    return decay * lax.rsqrt(2.0 * lax.optimization_barrier(jnp.sum(decay * decay, axis=0)))

def layer_norm(stream, gain):
    mean_row = lax.optimization_barrier(jnp.mean(stream, axis=-1, keepdims=True))
    square_mean = lax.optimization_barrier(jnp.mean(stream * stream, axis=-1, keepdims=True))
    return (stream - mean_row) * lax.rsqrt(square_mean - mean_row * mean_row + norm_eps) * gain

def block_mix(values, weight):
    blocks = values.reshape(values.shape[0], weight.shape[0], weight.shape[1])
    mixed_blocks = jnp.einsum('tbi,bio->tbo', blocks, weight, precision=exact)
    return mixed_blocks.reshape(values.shape[0], -1)

def long_conv(signal, forward_taps, backward_taps):
    length = signal.shape[0]
    size_all = 2 * length
    kernel = jnp.concatenate([forward_taps, jnp.zeros((1, signal.shape[1]), forward_taps.dtype), backward_taps[1:][::-1]], axis=0)
    product = jnp.fft.rfft(signal, n=size_all, axis=0) * jnp.fft.rfft(kernel, axis=0)
    return jnp.fft.irfft(product, n=size_all, axis=0)[:length]

def mixer_layer(stream, gains, mixer, skip, kernels, gate_up, down):
    normed = low(layer_norm(stream, gains[0]))
    inner = low(low_back(block_mix(normed, mixer[0])))
    gate_v = low_back(block_mix(normed, mixer[1]))
    conv = low(low_back(long_conv(low_back(inner), kernels[0], kernels[1])))
    mixed = low(gate_v * (conv + skip * inner))
    middle = stream + low_back(block_mix(mixed, mixer[2]))
    normed_two = low(layer_norm(middle, gains[1]))
    gate_act = low_back(jnp.dot(normed_two, gate_up[0], precision=exact))
    up_act = low_back(jnp.dot(normed_two, gate_up[1], precision=exact))
    hidden = low(jax.nn.gelu(gate_act, approximate=True) * up_act)
    return middle + low_back(jnp.dot(hidden, down.T, precision=exact))

def reference(hidden_in, d_out, gains, mixer, skip, filters, gate_up, down):
    gains = gains.astype(jnp.float32)
    mixer = mixer.astype(jnp.float32)
    skip = skip.astype(jnp.float32)
    filters = filters.astype(jnp.float32)
    gate_up = gate_up.astype(jnp.float32)
    down = down.astype(jnp.float32)
    pos_table = positions(LENGTH)
    shape_env = envelope(LENGTH, jnp.arange(D, dtype=jnp.int32), D)

    def build(weights):
        raw_filter = jnp.einsum('tf,lefd->letd', pos_table, weights, precision=exact)
        return (raw_filter * shape_env, filter_decay * jnp.sum(raw_filter * raw_filter))
    (kernels, penalty), build_back = jax.vjp(build, filters)

    def run(stream, gains_in, mixer_in, skip_in, kernels_in, gate_up_in, down_in):
        for layer_index in range(LAYERS):
            stream = mixer_layer(stream, gains_in[layer_index], mixer_in[layer_index], skip_in[layer_index], kernels_in[layer_index], gate_up_in[layer_index], down_in[layer_index])
        return stream
    params = (gains, mixer, skip, kernels, gate_up, down)

    def one_sequence(totals, inputs_pair):
        seq_rows, cotangent = inputs_pair
        result, pull_back = jax.vjp(run, seq_rows, *params)
        grads = pull_back(cotangent)
        totals = jax.tree.map(lambda first_arg, second_arg: first_arg + second_arg, totals, grads[1:])
        return (totals, (result.astype(jnp.bfloat16), grads[0]))
    initial = jax.tree.map(jnp.zeros_like, params)
    inputs_all = hidden_in.astype(jnp.float32).reshape(SEQS, LENGTH, D)
    cotangents = d_out.astype(jnp.float32).reshape(SEQS, LENGTH, D)
    totals, (outputs, grad_rows) = lax.scan(one_sequence, initial, (inputs_all, cotangents))
    grad_filters, = build_back((totals[3], jnp.ones_like(penalty)))
    return (outputs.reshape(TOKENS, D), grad_rows.reshape(TOKENS, D), totals[0], totals[1], totals[2], grad_filters, totals[4], totals[5])
```

```python
import functools
import math

import jax
import jax.numpy as jnp
import numpy as np
from jax import lax
from jax.experimental import pallas as pl
from jax.experimental.pallas import tpu as pltpu
from jax.sharding import PartitionSpec as P

ORDER = 128
SEQ_LEN = 8192
LANES = 128
NORM_EPS = 1e-05
DECAY = 0.02
MESH = pl.DeviceIdType.MESH
BF16 = jnp.bfloat16
F32 = jnp.float32
MIB = 2**20
GELU_C = math.sqrt(2.0 / math.pi)


def round_up(value, step):
    return -(-value // step) * step


def whole():
    return pl.BlockSpec(memory_space=pltpu.VMEM)


def nn(a, b):
    return lax.dot_general(a, b, (((1,), (0,)), ((), ())), preferred_element_type=F32)


def nt(a, b):
    return lax.dot_general(a, b, (((1,), (1,)), ((), ())), preferred_element_type=F32)


def tn(a, b):
    return lax.dot_general(a, b, (((0,), (0,)), ((), ())), preferred_element_type=F32)


def position_table(length):
    half_order = ORDER // 2
    index_list = np.arange(half_order)
    multiple = 1 + index_list * index_list * (length // 4) // (half_order * half_order)
    phase = (np.arange(length)[:, None] * multiple[None, :] % length) * (2.0 * math.pi / length)
    return np.concatenate([np.sin(phase), np.cos(phase)], axis=1)


def dft_tables(length):
    blocks = length // LANES
    size = 2 * length
    outer = 2 * blocks
    k = np.arange(outer)
    n = np.arange(blocks)
    m = np.arange(LANES)
    angle = 2.0 * math.pi * (np.outer(k, n) % outer) / outer
    outer_fwd = np.concatenate([np.cos(angle), -np.sin(angle)], axis=0)
    outer_inv = np.concatenate([np.cos(angle), -np.sin(angle)], axis=0).T / size
    angle = 2.0 * math.pi * (np.outer(m, m) % LANES) / LANES
    cos, sin = np.cos(angle), np.sin(angle)
    inner_fwd = np.block([[cos, -sin], [sin, cos]])
    inner_inv = np.block([[cos, sin], [-sin, cos]])
    angle = 2.0 * math.pi * np.outer(k, m) / size
    twist = np.concatenate([np.cos(angle), np.sin(angle)], axis=1)
    half = lambda table: jnp.asarray(table, F32).astype(BF16)
    return (half(outer_fwd), half(outer_inv), half(inner_fwd), half(inner_inv), jnp.asarray(twist, F32))


def normalize(values):
    mean = jnp.mean(values, axis=1, keepdims=True)
    square = jnp.mean(values * values, axis=1, keepdims=True)
    inv = lax.rsqrt(square - mean * mean + NORM_EPS)
    return (values - mean) * inv, inv


def norm_back(grad, normal, inv, gain):
    scaled = grad * gain
    mean = jnp.mean(scaled, axis=1, keepdims=True)
    cross = jnp.mean(scaled * normal, axis=1, keepdims=True)
    return inv * (scaled - mean - normal * cross), jnp.sum(grad * normal, axis=0, keepdims=True)


def gelu_parts(gate):
    square = gate * gate
    tanh = jnp.tanh(GELU_C * gate * (1.0 + 0.044715 * square))
    half = 0.5 * (1.0 + tanh)
    value = gate * half
    slope = half + 0.5 * gate * (1.0 - tanh * tanh) * (GELU_C * (1.0 + 3.0 * 0.044715 * square))
    return value, slope


def enter(count, hid):
    me = lax.axis_index("rows") * hid + lax.axis_index("hid")
    barrier = pltpu.get_barrier_semaphore()

    def greet(step, carry):
        peer = lax.rem(me + step, count)
        pl.semaphore_signal(
            barrier, inc=1, device_id=(peer // hid, lax.rem(peer, hid)), device_id_type=MESH
        )
        return carry

    lax.fori_loop(1, count, greet, 0)
    return barrier


def exchange_start(source, target, sems, count, rows, hid, piece, by_owner):
    send, recv, local = sems
    row = lax.axis_index("rows")
    col = lax.axis_index("hid")
    token_id = row * hid + col
    owner_id = col * rows + row
    mine_there = token_id if by_owner else owner_id
    mine_here = owner_id if by_owner else token_id
    at = lambda index: pl.ds(pl.multiple_of(index * piece, piece), piece)
    pltpu.make_async_copy(source.at[at(mine_here)], target.at[at(mine_there)], local).start()

    def post(step, carry):
        peer = lax.rem(token_id + step, count)
        peer_row = peer // hid
        peer_col = lax.rem(peer, hid)
        there = (peer_col * rows + peer_row) if by_owner else peer
        pltpu.make_async_remote_copy(
            src_ref=source.at[at(there)],
            dst_ref=target.at[at(mine_there)],
            send_sem=send,
            recv_sem=recv,
            device_id=(peer_row, peer_col),
            device_id_type=MESH,
        ).start()
        return carry

    lax.fori_loop(1, count, post, 0)


def exchange_wait(source, target, sems, count, rows, hid, piece):
    send, recv, local = sems
    row = lax.axis_index("rows")
    col = lax.axis_index("hid")
    pltpu.make_async_copy(
        source.at[pl.ds(0, piece)], target.at[pl.ds(0, piece)], local
    ).wait()
    span = pl.ds(0, (count - 1) * piece)
    pltpu.make_async_remote_copy(
        src_ref=source.at[span],
        dst_ref=target.at[span],
        send_sem=send,
        recv_sem=recv,
        device_id=(row, hid - 1 - col),
        device_id_type=MESH,
    ).wait()


class Sizes:
    def __init__(self, rows, hid, width, hidden, tokens):
        self.rows, self.hid, self.width, self.hidden = rows, hid, width, hidden
        self.count = rows * hid
        self.chans = width // self.count
        self.piece = round_up(self.chans, 16)
        self.length = min(SEQ_LEN, tokens)
        self.seqs = tokens // self.length
        self.blocks = self.length // LANES
        self.outer = 2 * self.blocks
        self.pairs = self.seqs * self.chans
        self.half = width // hid
        self.padded = rows * self.piece
        self.channels = self.count * self.piece


def spread_in(source, wide, lines, stride, blocks):
    for place, line in enumerate(lines):
        wide[:, place * LANES : (place + 1) * LANES] = source[
            pl.ds(line, blocks, stride=stride), :
        ].astype(wide.dtype)


def dft(wide, spectrum, tables, mid, flat, lines, outer, offset=0):
    outer_fwd, inner_fwd, twist = tables
    mid[:, : lines * LANES] = nn(outer_fwd[...], wide[:, : lines * LANES])
    cos = twist[:, :LANES]
    sin = twist[:, LANES:]
    for line in range(lines):
        lanes = pl.ds(line * LANES, LANES)
        real = mid[0:outer, lanes]
        imag = mid[outer : 2 * outer, lanes]
        rows = pl.ds(line * outer, outer)
        flat[rows, 0:LANES] = (real * cos + imag * sin).astype(BF16)
        flat[rows, LANES:] = (imag * cos - real * sin).astype(BF16)
    spectrum[0 : lines * outer, :] = nn(flat[0 : lines * outer, :], inner_fwd[...])


def inverse_dft(flat, tables, mid_half, lines, outer):
    outer_inv, inner_inv, twist = tables
    cos = twist[:, :LANES]
    sin = twist[:, LANES:]
    for line in range(lines):
        rows = pl.ds(line * outer, outer)
        lanes = pl.ds(line * LANES, LANES)
        part = nn(flat[rows, :], inner_inv[...])
        real = part[:, :LANES]
        imag = part[:, LANES:]
        mid_half[0:outer, lanes] = (real * cos - imag * sin).astype(BF16)
        mid_half[outer : 2 * outer, lanes] = (imag * cos + real * sin).astype(BF16)
    return nn(outer_inv[...], mid_half[:, : lines * LANES])


def spread_out(value, target, lines, stride, blocks):
    for place, line in enumerate(lines):
        target[pl.ds(line, blocks, stride=stride), :] = value[
            :, place * LANES : (place + 1) * LANES
        ]


def signal_lines(sz):
    return [seq * sz.blocks * sz.piece + chan for seq in range(sz.seqs) for chan in range(sz.chans)]


def conv_forward_kernel(
    sz,
    inner_ref,
    taps_ref,
    pos_ref,
    env_ref,
    outer_fwd,
    outer_inv,
    inner_fwd,
    inner_inv,
    twist,
    conv_ref,
    filt_spec,
    sig_spec,
    landed,
    staged,
    tall,
    wide,
    mid,
    flat,
    mid_half,
    sems_in,
    sems_out,
):
    barrier = enter(sz.count, sz.hid)
    pl.semaphore_wait(barrier, sz.count - 1)
    into = tuple(sems_in.at[i] for i in range(3))
    back = tuple(sems_out.at[i] for i in range(3))
    exchange_start(inner_ref, landed, into, sz.count, sz.rows, sz.hid, sz.piece, True)

    piece, blocks, outer = sz.piece, sz.blocks, sz.outer
    step = 4
    for start in range(0, blocks, step):
        span = slice(start * LANES, (start + step) * LANES)
        raw = nn(taps_ref[...], pos_ref[:, span])
        kernels = raw * env_ref[:, span]
        for block in range(step):
            tall[pl.ds((start + block) * 2 * piece, 2 * piece), :] = kernels[
                :, block * LANES : (block + 1) * LANES
            ]
    lines = [way * piece + chan for way in range(2) for chan in range(sz.chans)]
    spread_in(tall, wide, lines, 2 * piece, blocks)
    dft(wide, sig_spec, (outer_fwd, inner_fwd, twist), mid, flat, len(lines), outer)
    span = sz.chans * outer
    filt_spec[:, :LANES] = sig_spec[0:span, :LANES] + sig_spec[span : 2 * span, :LANES]
    filt_spec[:, LANES:] = sig_spec[0:span, LANES:] - sig_spec[span : 2 * span, LANES:]

    exchange_wait(inner_ref, landed, into, sz.count, sz.rows, sz.hid, piece)
    tall[0 : sz.channels, :] = landed[...].astype(F32)
    lines = signal_lines(sz)
    spread_in(tall, wide, lines, piece, blocks)
    dft(wide, sig_spec, (outer_fwd, inner_fwd, twist), mid, flat, sz.pairs, outer)
    for seq in range(sz.seqs):
        rows = pl.ds(seq * span, span)
        sig_re, sig_im = sig_spec[rows, :LANES], sig_spec[rows, LANES:]
        fil_re, fil_im = filt_spec[:, :LANES], filt_spec[:, LANES:]
        flat[rows, :LANES] = (sig_re * fil_re - sig_im * fil_im).astype(BF16)
        flat[rows, LANES:] = (sig_re * fil_im + sig_im * fil_re).astype(BF16)
    result = inverse_dft(flat, (outer_inv, inner_inv, twist), mid_half, sz.pairs, outer)
    spread_out(result, tall, lines, piece, blocks)
    staged[...] = tall[0 : sz.channels, :].astype(BF16)
    exchange_start(staged, conv_ref, back, sz.count, sz.rows, sz.hid, piece, False)
    exchange_wait(staged, conv_ref, back, sz.count, sz.rows, sz.hid, piece)


def conv_forward(sz, inner, taps, pos, env, tables, cid):
    outer_fwd, outer_inv, inner_fwd, inner_inv, twist = tables
    wide_lines = max(2 * sz.chans, sz.pairs)
    return pl.pallas_call(
        functools.partial(conv_forward_kernel, sz),
        out_shape=(
            jax.ShapeDtypeStruct((sz.channels, LANES), BF16),
            jax.ShapeDtypeStruct((sz.chans * sz.outer, 2 * LANES), F32),
            jax.ShapeDtypeStruct((wide_lines * sz.outer, 2 * LANES), F32),
        ),
        in_specs=[whole()] * 9,
        out_specs=(whole(),) * 3,
        scratch_shapes=[
            pltpu.VMEM((sz.channels, LANES), BF16),
            pltpu.VMEM((sz.channels, LANES), BF16),
            pltpu.VMEM((max(2 * sz.piece * sz.blocks, sz.channels), LANES), F32),
            pltpu.VMEM((sz.blocks, wide_lines * LANES), BF16),
            pltpu.VMEM((2 * sz.outer, wide_lines * LANES), F32),
            pltpu.VMEM((wide_lines * sz.outer, 2 * LANES), BF16),
            pltpu.VMEM((2 * sz.outer, sz.pairs * LANES), BF16),
            pltpu.SemaphoreType.DMA((3,)),
            pltpu.SemaphoreType.DMA((3,)),
        ],
        compiler_params=pltpu.CompilerParams(
            collective_id=cid, has_side_effects=True, vmem_limit_bytes=48 * MIB
        ),
        name="conv_forward",
    )(inner, taps, pos, env, outer_fwd, outer_inv, inner_fwd, inner_inv, twist)


def conv_backward_kernel(
    sz,
    grad_ref,
    filt_spec,
    sig_spec,
    taps_ref,
    pos_ref,
    env_ref,
    outer_fwd,
    outer_inv,
    inner_fwd,
    inner_inv,
    twist,
    back_ref,
    taps_grad,
    landed,
    staged,
    tall,
    wide,
    mid,
    flat,
    mid_half,
    grad_spec,
    sems_in,
    sems_out,
):
    barrier = enter(sz.count, sz.hid)
    pl.semaphore_wait(barrier, sz.count - 1)
    into = tuple(sems_in.at[i] for i in range(3))
    back = tuple(sems_out.at[i] for i in range(3))
    piece, blocks, outer = sz.piece, sz.blocks, sz.outer
    exchange_start(grad_ref, landed, into, sz.count, sz.rows, sz.hid, piece, True)
    exchange_wait(grad_ref, landed, into, sz.count, sz.rows, sz.hid, piece)
    tall[0 : sz.channels, :] = landed[...].astype(F32)
    lines = signal_lines(sz)
    spread_in(tall, wide, lines, piece, blocks)
    dft(wide, grad_spec, (outer_fwd, inner_fwd, twist), mid, flat, sz.pairs, outer)
    span = sz.chans * outer
    for seq in range(sz.seqs):
        rows = pl.ds(seq * span, span)
        re, im = grad_spec[rows, :LANES], grad_spec[rows, LANES:]
        fil_re, fil_im = filt_spec[:, :LANES], filt_spec[:, LANES:]
        flat[rows, :LANES] = (re * fil_re + im * fil_im).astype(BF16)
        flat[rows, LANES:] = (im * fil_re - re * fil_im).astype(BF16)
    inv_tables = (outer_inv, inner_inv, twist)
    result = inverse_dft(flat, inv_tables, mid_half, sz.pairs, outer)
    spread_out(result, tall, lines, piece, blocks)
    staged[...] = tall[0 : sz.channels, :].astype(BF16)
    exchange_start(staged, back_ref, back, sz.count, sz.rows, sz.hid, piece, False)

    total_re = jnp.zeros((span, LANES), F32)
    total_im = jnp.zeros((span, LANES), F32)
    for seq in range(sz.seqs):
        rows = pl.ds(seq * span, span)
        re, im = grad_spec[rows, :LANES], grad_spec[rows, LANES:]
        sig_re, sig_im = sig_spec[rows, :LANES], sig_spec[rows, LANES:]
        total_re += re * sig_re + im * sig_im
        total_im += im * sig_re - re * sig_im
    flat[0:span, :LANES] = total_re.astype(BF16)
    flat[span : 2 * span, :LANES] = total_re.astype(BF16)
    flat[0:span, LANES:] = total_im.astype(BF16)
    flat[span : 2 * span, LANES:] = (-total_im).astype(BF16)
    result = inverse_dft(flat, inv_tables, mid_half, 2 * sz.chans, outer)
    lines = [way * piece + chan for way in range(2) for chan in range(sz.chans)]
    if sz.chans < piece:
        tall[...] = jnp.zeros_like(tall)
    spread_out(result, tall, lines, 2 * piece, blocks)
    total = jnp.zeros((2 * piece, ORDER), F32)
    step = 4
    for start in range(0, blocks, step):
        span = slice(start * LANES, (start + step) * LANES)
        raw = nn(taps_ref[...], pos_ref[:, span])
        grads = jnp.concatenate(
            [
                tall[pl.ds((start + block) * 2 * piece, 2 * piece), :]
                for block in range(step)
            ],
            axis=1,
        )
        grads = grads * env_ref[:, span] + (2.0 * DECAY) * raw
        total += nt(grads.astype(BF16), pos_ref[:, span])
    taps_grad[...] = total

    exchange_wait(staged, back_ref, back, sz.count, sz.rows, sz.hid, piece)


def conv_backward(sz, grad, filt_spec, sig_spec, taps, pos, env, tables, cid):
    outer_fwd, outer_inv, inner_fwd, inner_inv, twist = tables
    wide_lines = max(2 * sz.chans, sz.pairs)
    return pl.pallas_call(
        functools.partial(conv_backward_kernel, sz),
        out_shape=(
            jax.ShapeDtypeStruct((sz.channels, LANES), BF16),
            jax.ShapeDtypeStruct((2 * sz.piece, ORDER), F32),
        ),
        in_specs=[whole()] * 11,
        out_specs=(whole(),) * 2,
        scratch_shapes=[
            pltpu.VMEM((sz.channels, LANES), BF16),
            pltpu.VMEM((sz.channels, LANES), BF16),
            pltpu.VMEM((max(2 * sz.piece * sz.blocks, sz.channels), LANES), F32),
            pltpu.VMEM((sz.blocks, wide_lines * LANES), BF16),
            pltpu.VMEM((2 * sz.outer, wide_lines * LANES), F32),
            pltpu.VMEM((wide_lines * sz.outer, 2 * LANES), BF16),
            pltpu.VMEM((2 * sz.outer, wide_lines * LANES), BF16),
            pltpu.VMEM((sz.pairs * sz.outer, 2 * LANES), F32),
            pltpu.SemaphoreType.DMA((3,)),
            pltpu.SemaphoreType.DMA((3,)),
        ],
        compiler_params=pltpu.CompilerParams(
            collective_id=cid, has_side_effects=True, vmem_limit_bytes=48 * MIB
        ),
        name="conv_backward",
    )(grad, filt_spec, sig_spec, taps, pos, env, outer_fwd, outer_inv, inner_fwd, inner_inv, twist)


def project(sz, normed, w_in, w_gate, inner_ref, gate_ref):
    for side in range(sz.hid):
        rows = slice(side * sz.padded, (side + 1) * sz.padded)
        part = normed[:, side * sz.half : (side + 1) * sz.half]
        inner_ref[rows, :] = nt(w_in[side], part).astype(BF16)
        gate_ref[rows, :] = nt(w_gate[side], part)


def first_kernel(sz, x_ref, gain_ref, w_in, w_gate, normed_ref, inner_ref, gate_ref):
    normal, _ = normalize(x_ref[...].astype(F32))
    normed = (normal * gain_ref[0:1, :]).astype(BF16)
    normed_ref[...] = normed
    project(sz, normed, w_in, w_gate, inner_ref, gate_ref)


def first(sz, x, gains, w_in, w_gate):
    tokens = x.shape[0]
    return pl.pallas_call(
        functools.partial(first_kernel, sz),
        out_shape=(
            jax.ShapeDtypeStruct((tokens, sz.width), BF16),
            jax.ShapeDtypeStruct((sz.channels, tokens), BF16),
            jax.ShapeDtypeStruct((sz.channels, tokens), F32),
        ),
        in_specs=[whole()] * 4,
        out_specs=(whole(),) * 3,
        compiler_params=pltpu.CompilerParams(vmem_limit_bytes=32 * MIB),
        name="first_projection",
    )(x, gains, w_in, w_gate)


def mix_out(sz, mixed, w_out):
    parts = []
    for side in range(sz.hid):
        rows = slice(side * sz.padded, (side + 1) * sz.padded)
        parts.append(tn(mixed[rows, :], w_out[side]))
    return jnp.concatenate(parts, axis=1)


def ff_specs(sz, layer, tile):
    steps = sz.hidden // sz.hid // tile
    first_half = lambda i: jnp.minimum(i, steps - 1)
    second = lambda i: jnp.maximum(i - steps, 0)
    specs = []
    for place in (first_half, second):
        specs.append(
            pl.BlockSpec((1, 2, sz.width, tile), lambda i, place=place: (layer, 0, 0, place(i)))
        )
        specs.append(pl.BlockSpec((1, sz.width, tile), lambda i, place=place: (layer, 0, place(i))))
    return specs, steps


def forward_kernel(
    sz,
    steps,
    conv_ref,
    inner_ref,
    gate_ref,
    skip_ref,
    x_ref,
    gain_ref,
    next_gain,
    w_out,
    w_in,
    w_gate,
    up_a,
    down_a,
    up_b,
    down_b,
    summed_ref,
    mixed_ref,
    middle_ref,
    normed_two,
    next_x,
    next_normed,
    next_inner,
    next_gate,
):
    index = pl.program_id(0)

    @pl.when(index == 0)
    def _():
        summed = conv_ref[...].astype(F32) + skip_ref[...] * inner_ref[...].astype(F32)
        summed_ref[...] = summed
        mixed_ref[...] = (gate_ref[...] * summed).astype(BF16)
        middle = x_ref[...].astype(F32) + mix_out(sz, mixed_ref, w_out)
        middle_ref[...] = middle
        normal, _ = normalize(middle)
        normed_two[...] = (normal * gain_ref[1:2, :]).astype(BF16)
        next_x[...] = middle

    def accumulate(up_ref, down_ref):
        gate = nn(normed_two[...], up_ref[0, 0])
        up = nn(normed_two[...], up_ref[0, 1])
        value, _ = gelu_parts(gate)
        next_x[...] += nt((value * up).astype(BF16), down_ref[0])

    pl.when(index < steps)(lambda: accumulate(up_a, down_a))
    pl.when(index >= steps)(lambda: accumulate(up_b, down_b))

    @pl.when(index == 2 * steps - 1)
    def _():
        normal, _ = normalize(next_x[...])
        normed = (normal * next_gain[0:1, :]).astype(BF16)
        next_normed[...] = normed
        project(sz, normed, w_in, w_gate, next_inner, next_gate)


def full(shape):
    return pl.BlockSpec(shape, lambda i: (0,) * len(shape))


def forward(sz, layer, conv, inner, gate, skip, x, gains, next_gains, w_out, w_in, w_gate, ff):
    tokens = x.shape[0]
    tile = 512
    specs, steps = ff_specs(sz, layer, tile)
    small = (conv, inner, gate, skip, x, gains, next_gains, w_out, w_in, w_gate)
    outs = (
        ((sz.channels, tokens), F32),
        ((sz.channels, tokens), BF16),
        ((tokens, sz.width), F32),
        ((tokens, sz.width), BF16),
        ((tokens, sz.width), F32),
        ((tokens, sz.width), BF16),
        ((sz.channels, tokens), BF16),
        ((sz.channels, tokens), F32),
    )
    return pl.pallas_call(
        functools.partial(forward_kernel, sz, steps),
        grid=(2 * steps,),
        out_shape=tuple(jax.ShapeDtypeStruct(shape, kind) for shape, kind in outs),
        in_specs=[full(entry.shape) for entry in small] + specs,
        out_specs=tuple(full(shape) for shape, kind in outs),
        compiler_params=pltpu.CompilerParams(
            dimension_semantics=("arbitrary",), vmem_limit_bytes=48 * MIB
        ),
        name="token_forward",
    )(*small, *ff)


def block_grads(sz, tall, flat, target, slot):
    blocks_side = target.shape[1] // sz.hid
    size = sz.half // blocks_side
    rows = sz.padded // blocks_side
    for side in range(sz.hid):
        for block in range(blocks_side):
            begin = side * sz.padded + block * rows
            place = side * sz.half + block * size
            target[slot, side * blocks_side + block] = nn(
                tall[begin : begin + rows, :], flat[:, place : place + size]
            ).astype(target.dtype)


def ff_backward_tile(normed, grad, up_ref, down_ref, total, out_total):
    gate = nn(normed, up_ref[0, 0])
    up = nn(normed, up_ref[0, 1])
    grad_hidden = nn(grad, down_ref[0])
    value, slope = gelu_parts(gate)
    if out_total is not None:
        out_total[...] += nt((value * up).astype(BF16), down_ref[0])
    grad_gate = (slope * up * grad_hidden).astype(BF16)
    grad_up = (value * grad_hidden).astype(BF16)
    total[...] += nt(grad_gate, up_ref[0, 0]) + nt(grad_up, up_ref[0, 1])


def mixer_backward(
    sz, grad_next, middle, total, gain, mixed, summed, gate, w_out, outs
):
    grad_middle, mixer_grad, grad_gate, grad_summed, grad_conv, gain_grad = outs
    normal, inv = normalize(middle)
    back, gain_grad[...] = norm_back(total, normal, inv, gain)
    result = grad_next + back
    grad_middle[...] = result
    grad_o = result.astype(BF16)
    block_grads(sz, mixed, grad_o, mixer_grad, 0)
    for side in range(sz.hid):
        rows = slice(side * sz.padded, (side + 1) * sz.padded)
        grad_mixed = nt(w_out[side], grad_o[:, side * sz.half : (side + 1) * sz.half])
        grad_gate[rows, :] = (grad_mixed * summed[rows, :]).astype(BF16)
        through = grad_mixed * gate[rows, :]
        grad_summed[rows, :] = through
        grad_conv[rows, :] = through.astype(BF16)


def mixer_outs(sz, tokens, blocks):
    size = sz.width // blocks
    return (
        ((tokens, sz.width), F32),
        ((1, blocks, sz.channels // blocks, size), BF16),
        ((sz.channels, tokens), BF16),
        ((sz.channels, tokens), F32),
        ((sz.channels, tokens), BF16),
        ((1, sz.width), F32),
    )


def turn_kernel(
    sz,
    steps,
    conv_ref,
    inner_ref,
    gate_ref,
    skip_ref,
    x_ref,
    gain_ref,
    grad_ref,
    w_out,
    up_a,
    down_a,
    up_b,
    down_b,
    hidden_out,
    normed_two,
    grad_middle,
    mixer_grad,
    grad_gate,
    grad_summed,
    grad_conv,
    gain_grad,
    summed,
    mixed,
    middle,
    out_total,
    total,
):
    index = pl.program_id(0)

    @pl.when(index == 0)
    def _():
        summed[...] = conv_ref[...].astype(F32) + skip_ref[...] * inner_ref[...].astype(F32)
        mixed[...] = (gate_ref[...] * summed[...]).astype(BF16)
        middle[...] = x_ref[...].astype(F32) + mix_out(sz, mixed, w_out)
        normal, _ = normalize(middle[...])
        normed_two[...] = (normal * gain_ref[1:2, :]).astype(BF16)
        out_total[...] = middle[...]
        total[...] = jnp.zeros_like(total)

    def accumulate(up_ref, down_ref):
        ff_backward_tile(normed_two[...], grad_ref[...], up_ref, down_ref, total, out_total)

    pl.when(index < steps)(lambda: accumulate(up_a, down_a))
    pl.when(index >= steps)(lambda: accumulate(up_b, down_b))

    @pl.when(index == 2 * steps - 1)
    def _():
        hidden_out[...] = out_total[...].astype(BF16)
        outs = (grad_middle, mixer_grad, grad_gate, grad_summed, grad_conv, gain_grad)
        mixer_backward(
            sz,
            grad_ref[...].astype(F32),
            middle[...],
            total[...],
            gain_ref[1:2, :],
            mixed,
            summed,
            gate_ref,
            w_out,
            outs,
        )


def turn(sz, layer, blocks, conv, inner, gate, skip, x, gains, grad, w_out, ff):
    tokens = x.shape[0]
    specs, steps = ff_specs(sz, layer, 512)
    small = (conv, inner, gate, skip, x, gains, grad, w_out)
    outs = (((tokens, sz.width), BF16), ((tokens, sz.width), BF16)) + mixer_outs(sz, tokens, blocks)
    return pl.pallas_call(
        functools.partial(turn_kernel, sz, steps),
        grid=(2 * steps,),
        out_shape=tuple(jax.ShapeDtypeStruct(shape, kind) for shape, kind in outs),
        in_specs=[full(entry.shape) for entry in small] + specs,
        out_specs=tuple(full(shape) for shape, kind in outs),
        scratch_shapes=[
            pltpu.VMEM((sz.channels, tokens), F32),
            pltpu.VMEM((sz.channels, tokens), BF16),
            pltpu.VMEM((tokens, sz.width), F32),
            pltpu.VMEM((tokens, sz.width), F32),
            pltpu.VMEM((tokens, sz.width), F32),
        ],
        compiler_params=pltpu.CompilerParams(
            dimension_semantics=("arbitrary",), vmem_limit_bytes=48 * MIB
        ),
        name="token_turn",
    )(*small, *ff)


def input_backward(
    sz, back, through, grad_gate, skip, normed, x, gain, w_in, w_gate, grad_middle, mixer_grad
):
    inner_grad = (skip * through + back.astype(F32)).astype(BF16)
    block_grads(sz, inner_grad, normed, mixer_grad, 0)
    block_grads(sz, grad_gate, normed, mixer_grad, 1)
    parts = []
    for side in range(sz.hid):
        rows = slice(side * sz.padded, (side + 1) * sz.padded)
        parts.append(tn(inner_grad[rows, :], w_in[side]) + tn(grad_gate[rows, :], w_gate[side]))
    normal, inv = normalize(x)
    result, gain_grad = norm_back(jnp.concatenate(parts, axis=1), normal, inv, gain)
    return grad_middle + result, gain_grad


def backward_kernel(
    sz,
    steps,
    back_ref,
    through_ref,
    gate_grad_ref,
    skip_ref,
    normed_ref,
    x_ref,
    gain_ref,
    w_in,
    w_gate,
    grad_middle_ref,
    normed_two,
    middle_ref,
    summed_ref,
    gate_ref,
    mixed_ref,
    low_gain,
    w_out,
    up_a,
    down_a,
    up_b,
    down_b,
    input_grad,
    input_gain,
    grad_ff,
    grad_middle,
    mixer_grad,
    grad_gate,
    grad_summed,
    grad_conv,
    gain_grad,
    grad_next,
    total,
):
    index = pl.program_id(0)

    @pl.when(index == 0)
    def _():
        result, input_gain[...] = input_backward(
            sz,
            back_ref[...],
            through_ref[...],
            gate_grad_ref[...],
            skip_ref[...],
            normed_ref[...],
            x_ref[...],
            gain_ref[0:1, :],
            w_in,
            w_gate,
            grad_middle_ref[...],
            input_grad,
        )
        grad_next[...] = result
        grad_ff[...] = result.astype(BF16)
        total[...] = jnp.zeros_like(total)

    def accumulate(up_ref, down_ref):
        ff_backward_tile(normed_two[...], grad_ff[...], up_ref, down_ref, total, None)

    pl.when(index < steps)(lambda: accumulate(up_a, down_a))
    pl.when(index >= steps)(lambda: accumulate(up_b, down_b))

    @pl.when(index == 2 * steps - 1)
    def _():
        outs = (grad_middle, mixer_grad, grad_gate, grad_summed, grad_conv, gain_grad)
        mixer_backward(
            sz,
            grad_next[...],
            middle_ref[...],
            total[...],
            low_gain[1:2, :],
            mixed_ref,
            summed_ref,
            gate_ref,
            w_out,
            outs,
        )


def input_outs(sz, blocks):
    size = sz.width // blocks
    return (((2, blocks, sz.channels // blocks, size), BF16), ((1, sz.width), F32))


def backward(
    sz,
    layer,
    blocks,
    back,
    through,
    gate_grad,
    skip,
    normed,
    x,
    gains,
    w_in,
    w_gate,
    grad_middle,
    normed_two,
    middle,
    summed,
    gate,
    mixed,
    low_gains,
    w_out,
    ff,
):
    tokens = x.shape[0]
    specs, steps = ff_specs(sz, layer, 512)
    small = (
        back,
        through,
        gate_grad,
        skip,
        normed,
        x,
        gains,
        w_in,
        w_gate,
        grad_middle,
        normed_two,
        middle,
        summed,
        gate,
        mixed,
        low_gains,
        w_out,
    )
    outs = (
        input_outs(sz, blocks) + (((tokens, sz.width), BF16),) + mixer_outs(sz, tokens, blocks)
    )
    return pl.pallas_call(
        functools.partial(backward_kernel, sz, steps),
        grid=(2 * steps,),
        out_shape=tuple(jax.ShapeDtypeStruct(shape, kind) for shape, kind in outs),
        in_specs=[full(entry.shape) for entry in small] + specs,
        out_specs=tuple(full(shape) for shape, kind in outs),
        scratch_shapes=[
            pltpu.VMEM((tokens, sz.width), F32),
            pltpu.VMEM((tokens, sz.width), F32),
        ],
        compiler_params=pltpu.CompilerParams(
            dimension_semantics=("arbitrary",), vmem_limit_bytes=48 * MIB
        ),
        name="token_backward",
    )(*small, *ff)


def last_kernel(
    sz,
    back_ref,
    through_ref,
    gate_grad_ref,
    skip_ref,
    normed_ref,
    x_ref,
    gain_ref,
    w_in,
    w_gate,
    grad_middle_ref,
    input_grad,
    input_gain,
    grad_in,
):
    grad_in[...], input_gain[...] = input_backward(
        sz,
        back_ref[...],
        through_ref[...],
        gate_grad_ref[...],
        skip_ref[...],
        normed_ref[...],
        x_ref[...].astype(F32),
        gain_ref[0:1, :],
        w_in,
        w_gate,
        grad_middle_ref[...],
        input_grad,
    )


def last(sz, blocks, *args):
    tokens = args[5].shape[0]
    outs = input_outs(sz, blocks) + (((tokens, sz.width), F32),)
    return pl.pallas_call(
        functools.partial(last_kernel, sz),
        out_shape=tuple(jax.ShapeDtypeStruct(shape, kind) for shape, kind in outs),
        in_specs=[whole()] * len(args),
        out_specs=(whole(),) * len(outs),
        compiler_params=pltpu.CompilerParams(vmem_limit_bytes=32 * MIB),
        name="last_projection",
    )(*args)


def ff_grads_kernel(normed_ref, grad_ref, up_ref, down_ref, out_ref, hidden, grad_gate, grad_up):
    tokens = normed_ref.shape[0]
    chunk = 256
    for start in range(0, tokens, chunk):
        rows = pl.ds(start, chunk)
        normed = normed_ref[rows, :]
        gate = nn(normed, up_ref[0])
        up = nn(normed, up_ref[1])
        through = nn(grad_ref[rows, :], down_ref[...])
        value, slope = gelu_parts(gate)
        hidden[rows, :] = (value * up).astype(BF16)
        grad_gate[rows, :] = (slope * up * through).astype(BF16)
        grad_up[rows, :] = (value * through).astype(BF16)
    out_ref[0] = tn(normed_ref[...], grad_gate[...]).astype(BF16)
    out_ref[1] = tn(normed_ref[...], grad_up[...]).astype(BF16)
    out_ref[2] = tn(grad_ref[...], hidden[...]).astype(BF16)


def ff_grads(normed, grad, up, down):
    tokens, width = normed.shape
    units = down.shape[1]
    return pl.pallas_call(
        ff_grads_kernel,
        out_shape=jax.ShapeDtypeStruct((3, width, units), BF16),
        in_specs=[whole()] * 4,
        out_specs=whole(),
        scratch_shapes=[pltpu.VMEM((tokens, units), BF16)] * 3,
        compiler_params=pltpu.CompilerParams(vmem_limit_bytes=48 * MIB),
        name="ff_weight_grads",
    )(normed, grad, up, down)


def row_exchange_kernel(rows, parts, *refs):
    sources, targets, sems = refs[:parts], refs[parts : 2 * parts], refs[2 * parts]
    row = lax.axis_index("rows")
    col = lax.axis_index("hid")
    barrier = pltpu.get_barrier_semaphore()

    def greet(step, carry):
        peer = lax.rem(row + step, rows)
        pl.semaphore_signal(barrier, inc=1, device_id=(peer, col), device_id_type=MESH)
        return carry

    lax.fori_loop(1, rows, greet, 0)
    for part in range(parts):
        pltpu.make_async_copy(
            sources[part].at[row], targets[part].at[row], sems.at[part, 2]
        ).start()
    pl.semaphore_wait(barrier, rows - 1)

    def post(step, carry):
        peer = lax.rem(row + step, rows)
        for part in range(parts):
            pltpu.make_async_remote_copy(
                src_ref=sources[part].at[peer],
                dst_ref=targets[part].at[row],
                send_sem=sems.at[part, 0],
                recv_sem=sems.at[part, 1],
                device_id=(peer, col),
                device_id_type=MESH,
            ).start()
        return carry

    lax.fori_loop(1, rows, post, 0)
    for part in range(parts):
        pltpu.make_async_copy(
            sources[part].at[0], targets[part].at[0], sems.at[part, 2]
        ).wait()
        span = pl.ds(0, rows - 1)
        pltpu.make_async_remote_copy(
            src_ref=sources[part].at[span],
            dst_ref=targets[part].at[span],
            send_sem=sems.at[part, 0],
            recv_sem=sems.at[part, 1],
            device_id=(lax.rem(row + 1, rows), col),
            device_id_type=MESH,
        ).wait()


def row_exchange(arrays, rows, cid):
    parts = len(arrays)
    return pl.pallas_call(
        functools.partial(row_exchange_kernel, rows, parts),
        out_shape=tuple(jax.ShapeDtypeStruct(entry.shape, entry.dtype) for entry in arrays),
        in_specs=[pl.BlockSpec(memory_space=pl.ANY)] * parts,
        out_specs=(pl.BlockSpec(memory_space=pl.ANY),) * parts,
        scratch_shapes=[pltpu.SemaphoreType.DMA((parts, 3))],
        compiler_params=pltpu.CompilerParams(collective_id=cid, has_side_effects=True),
        name="row_exchange",
    )(*arrays)


def swap(value):
    return lax.ppermute(value, "hid", [(0, 1), (1, 0)])


def both_halves(own, axis):
    other = swap(own)
    low = lax.axis_index("hid") == 0
    return jnp.concatenate([jnp.where(low, own, other), jnp.where(low, other, own)], axis=axis)


def own_tokens(part):
    tokens = part.shape[0] // 2
    side = lax.axis_index("hid")
    keep = lax.dynamic_slice_in_dim(part, side * tokens, tokens, 0)
    other = swap(lax.dynamic_slice_in_dim(part, (1 - side) * tokens, tokens, 0))
    low = side == 0
    return jnp.concatenate([jnp.where(low, keep, other), jnp.where(low, other, keep)], axis=1)


def own_features(part):
    half = part.shape[1] // 2
    side = lax.axis_index("hid")
    keep = lax.dynamic_slice_in_dim(part, side * half, half, 1)
    other = swap(lax.dynamic_slice_in_dim(part, (1 - side) * half, half, 1))
    low = side == 0
    return jnp.concatenate([jnp.where(low, keep, other), jnp.where(low, other, keep)], axis=0)


def padded_mixer(sz, mixer):
    layers, kinds, blocks, size, _ = mixer.shape
    chan_first = jnp.concatenate([jnp.swapaxes(mixer[:, :2], 3, 4), mixer[:, 2:]], axis=1)
    grouped = chan_first.reshape(layers, kinds, blocks, size // sz.chans, sz.chans, size)
    grouped = jnp.pad(grouped, ((0, 0),) * 4 + ((0, sz.piece - sz.chans), (0, 0)))
    grouped = grouped.reshape(layers, kinds, blocks, -1, size)
    parts = [
        jnp.pad(grouped[:, :, block], ((0, 0),) * 3 + ((block * size, (blocks - 1 - block) * size),))
        for block in range(blocks)
    ]
    return jnp.concatenate(parts, axis=2)


def padded_channels(sz, values):
    lead = values.shape[:-1]
    grouped = values.reshape(lead + (sz.rows, sz.chans))
    grouped = jnp.pad(grouped, ((0, 0),) * (len(lead) + 1) + ((0, sz.piece - sz.chans),))
    return grouped.reshape(lead + (sz.padded,))


def envelopes(sz):
    row = lax.axis_index("rows")
    first_chan = lax.axis_index("hid") * sz.half + row * sz.chans
    channels = first_chan + jnp.arange(sz.piece, dtype=jnp.int32)
    fraction = (channels * 37 % sz.width).astype(F32) / (sz.width - 1)
    start_log = math.log(1.0 / 40.0)
    rate = jnp.exp(start_log + (math.log(1.5 / sz.length) - start_log) * fraction)
    steps = jnp.arange(sz.length, dtype=jnp.int32).astype(F32)
    decay = jnp.exp(-steps[None, :] * rate[:, None])
    shape = decay * lax.rsqrt(2.0 * jnp.sum(decay * decay, axis=1, keepdims=True))
    return jnp.concatenate([shape, shape * (steps > 0)[None, :]], axis=0)


def plane_gather(value):
    size = lax.axis_size("rows")
    for bit in (1, 2):
        other = lax.ppermute(value, "rows", [(r, r ^ bit) for r in range(size)])
        value = jnp.concatenate([value, other], axis=0)
    return jnp.concatenate([value, swap(value)], axis=0)


def on_device(hidden_in, d_out, gains, mixer, skip, filters, gate_up, down):
    layers = gate_up.shape[0]
    rows = lax.axis_size("rows")
    hid = lax.axis_size("hid")
    width = gate_up.shape[2]
    hidden = gate_up.shape[3] * hid
    blocks = mixer.shape[2] * hid
    block_size = mixer.shape[3]
    sz = Sizes(rows, hid, width, hidden, hidden_in.shape[0] * rows)
    row = lax.axis_index("rows")

    x = own_tokens(hidden_in)
    gains_all = both_halves(gains, 2)
    skip_all = both_halves(padded_channels(sz, skip), 1)[:, :, None]
    weights = both_halves(padded_mixer(sz, mixer)[:, :, None], 2)
    gate_up_b = swap(gate_up)
    down_b = swap(down)
    ff = (gate_up, down, gate_up_b, down_b)
    grad_out = own_tokens(d_out)

    tables = dft_tables(sz.length)
    pos = jnp.asarray(position_table(sz.length).T, F32).astype(BF16)
    env = envelopes(sz)
    taps = lax.dynamic_slice_in_dim(filters, row * sz.chans, sz.chans, 3)
    taps = jnp.pad(taps, ((0, 0),) * 3 + ((0, sz.piece - sz.chans),))
    taps = jnp.swapaxes(taps, 2, 3).reshape(layers, 2 * sz.piece, ORDER).astype(BF16)

    normed, inner, gate = first(sz, x, gains_all[0], weights[0, 0], weights[0, 1])
    stored = []
    for layer in range(layers):
        conv, filt_spec, sig_spec = conv_forward(sz, inner, taps[layer], pos, env, tables, 0)
        stored.append(dict(x=x, normed=normed, inner=inner, gate=gate, f=filt_spec, s=sig_spec))
        if layer < layers - 1:
            summed, mixed, middle, normed_two, x, normed, next_inner, next_gate = forward(
                sz,
                layer,
                conv,
                inner,
                gate,
                skip_all[layer],
                x,
                gains_all[layer],
                gains_all[layer + 1],
                weights[layer, 2],
                weights[layer + 1, 0],
                weights[layer + 1, 1],
                ff,
            )
            stored[-1].update(summed=summed, mixed=mixed, middle=middle, normed_two=normed_two)
            inner, gate = next_inner, next_gate

    top = layers - 1
    hidden_out, normed_two, *rest = turn(
        sz,
        top,
        blocks,
        conv,
        inner,
        gate,
        skip_all[top],
        x,
        gains_all[top],
        grad_out,
        weights[top, 2],
        ff,
    )
    stored[top].update(normed_two=normed_two)
    grad_ff = grad_out
    units = sz.hidden // hid // 4
    unit_start = lax.rem(row, 4) * units
    ff_parts, mixer_parts, gain_parts, skip_parts, taps_parts = [], [], [], [], []
    for layer in reversed(range(layers)):
        kept = stored[layer]
        grad_middle, out_grad, grad_gate, grad_summed, grad_conv, gain_two = rest
        ff_parts.insert(
            0,
            ff_grads(
                plane_gather(kept["normed_two"]),
                plane_gather(grad_ff),
                lax.dynamic_slice_in_dim(gate_up[layer], unit_start, units, 2),
                lax.dynamic_slice_in_dim(down[layer], unit_start, units, 1),
            ),
        )
        back, taps_grad = conv_backward(
            sz, grad_conv, kept["f"], kept["s"], taps[layer], pos, env, tables, 1
        )
        skip_parts.insert(0, jnp.sum(grad_summed * kept["inner"].astype(F32), axis=1))
        taps_parts.insert(0, taps_grad)
        common = (
            back,
            grad_summed,
            grad_gate,
            skip_all[layer],
            kept["normed"],
            kept["x"],
            gains_all[layer],
            weights[layer, 0],
            weights[layer, 1],
            grad_middle,
        )
        if layer > 0:
            low = stored[layer - 1]
            in_grad, gain_one, grad_ff, *rest = backward(
                sz,
                layer - 1,
                blocks,
                *common,
                low["normed_two"],
                low["middle"],
                low["summed"],
                low["gate"],
                low["mixed"],
                gains_all[layer - 1],
                weights[layer - 1, 2],
                ff,
            )
        else:
            in_grad, gain_one, grad_in = last(sz, blocks, *common)
        mixer_parts.insert(0, jnp.concatenate([in_grad, out_grad], axis=0))
        gain_parts.insert(0, jnp.concatenate([gain_one, gain_two], axis=0))

    piece_rows = width // rows
    padded_rows = round_up(piece_rows, 16)
    pieces = jnp.stack(ff_parts).reshape(layers, 3, rows, piece_rows, units)
    pieces = jnp.pad(pieces, ((0, 0),) * 3 + ((0, padded_rows - piece_rows), (0, 0)))
    pieces = jnp.moveaxis(pieces, 2, 0)
    (arrived,) = row_exchange((pieces,), rows, 2)
    arrived = arrived.reshape(rows // 4, 4, layers, 3, padded_rows, units)[:, :, :, :, :piece_rows]
    summed_ff = jnp.sum(arrived.astype(F32), axis=0)
    summed_ff = jnp.moveaxis(summed_ff, 0, 3).reshape(layers, 3, piece_rows, 4 * units)

    mixers = jnp.stack(mixer_parts).reshape(layers, 3, blocks, -1, sz.piece, block_size)
    mixers = mixers[:, :, :, :, : sz.chans].reshape(layers, 3, blocks, block_size, block_size)
    small = jnp.concatenate(
        [jnp.stack(gain_parts).reshape(-1), jnp.stack(skip_parts).reshape(-1)]
    )
    mixers, small = lax.psum((mixers.astype(F32), small), ("rows", "hid"))
    side = lax.axis_index("hid")
    mixers = lax.dynamic_slice_in_dim(mixers, side * (blocks // hid), blocks // hid, 2)
    mixers = jnp.concatenate([jnp.swapaxes(mixers[:, :2], 3, 4), mixers[:, 2:]], axis=1)
    gain_size = layers * 2 * width
    gain_out = lax.dynamic_slice_in_dim(
        small[:gain_size].reshape(layers, 2, width), side * sz.half, sz.half, 2
    )
    skip_out = small[gain_size:].reshape(layers, hid, rows, sz.piece)[..., : sz.chans]
    skip_out = lax.dynamic_index_in_dim(skip_out, side, 1, False).reshape(layers, sz.half)
    taps_out = jnp.stack(taps_parts).reshape(layers, 2, sz.piece, ORDER)[:, :, : sz.chans]
    taps_out = lax.all_gather(taps_out, "rows", axis=2, tiled=True)
    return (
        own_features(hidden_out),
        own_features(grad_in),
        gain_out,
        mixers,
        skip_out,
        jnp.swapaxes(taps_out, 2, 3),
        summed_ff[:, :2],
        summed_ff[:, 2],
    )


def solution(mesh):
    placed = (
        P("rows", "hid"),
        P("rows", "hid"),
        P(None, None, "hid"),
        P(None, None, "hid", None, None),
        P(None, "hid"),
        P(None, None, None, "hid"),
        P(None, None, None, "hid"),
        P(None, None, "hid"),
    )
    return jax.shard_map(
        on_device,
        mesh=mesh,
        in_specs=placed,
        out_specs=(
            P("rows", "hid"),
            P("rows", "hid"),
            P(None, None, "hid"),
            P(None, None, "hid", None, None),
            P(None, "hid"),
            P(None, None, None, "hid"),
            P(None, None, "rows", "hid"),
            P(None, "rows", "hid"),
        ),
        check_vma=False,
    )
```

```python
import functools
import math

import jax
import jax.numpy as jnp
import numpy as np
from jax import lax
from jax.experimental import pallas as pl
from jax.experimental.pallas import tpu as pltpu
from jax.sharding import PartitionSpec as P

ORDER = 128
SEQ_LEN = 8192
LANES = 128
NORM_EPS = 1e-05
DECAY = 0.02
MESH = pl.DeviceIdType.MESH
BF16 = jnp.bfloat16
F32 = jnp.float32
MIB = 2**20
GELU_C = math.sqrt(2.0 / math.pi)


def round_up(value, step):
    return -(-value // step) * step


def whole():
    return pl.BlockSpec(memory_space=pltpu.VMEM)


def nn(a, b):
    return lax.dot_general(a, b, (((1,), (0,)), ((), ())), preferred_element_type=F32)


def nt(a, b):
    return lax.dot_general(a, b, (((1,), (1,)), ((), ())), preferred_element_type=F32)


def tn(a, b):
    return lax.dot_general(a, b, (((0,), (0,)), ((), ())), preferred_element_type=F32)


def position_table(length):
    half_order = ORDER // 2
    index_list = np.arange(half_order)
    multiple = 1 + index_list * index_list * (length // 4) // (half_order * half_order)
    phase = (np.arange(length)[:, None] * multiple[None, :] % length) * (2.0 * math.pi / length)
    return np.concatenate([np.sin(phase), np.cos(phase)], axis=1)


def dft_tables(length):
    blocks = length // LANES
    size = 2 * length
    outer = 2 * blocks
    k = np.arange(outer)
    n = np.arange(blocks)
    m = np.arange(LANES)
    angle = 2.0 * math.pi * (np.outer(k, n) % outer) / outer
    outer_fwd = np.concatenate([np.cos(angle), -np.sin(angle)], axis=0)
    outer_inv = np.concatenate([np.cos(angle), -np.sin(angle)], axis=0).T / size
    angle = 2.0 * math.pi * (np.outer(m, m) % LANES) / LANES
    cos, sin = np.cos(angle), np.sin(angle)
    inner_fwd = np.block([[cos, -sin], [sin, cos]])
    inner_inv = np.block([[cos, sin], [-sin, cos]])
    angle = 2.0 * math.pi * np.outer(k, m) / size
    twist = np.concatenate([np.cos(angle), np.sin(angle)], axis=1)
    half = lambda table: jnp.asarray(table, F32).astype(BF16)
    return (half(outer_fwd), half(outer_inv), half(inner_fwd), half(inner_inv), jnp.asarray(twist, F32))


def normalize(values):
    mean = jnp.mean(values, axis=1, keepdims=True)
    square = jnp.mean(values * values, axis=1, keepdims=True)
    inv = lax.rsqrt(square - mean * mean + NORM_EPS)
    return (values - mean) * inv, inv


def norm_back(grad, normal, inv, gain):
    scaled = grad * gain
    mean = jnp.mean(scaled, axis=1, keepdims=True)
    cross = jnp.mean(scaled * normal, axis=1, keepdims=True)
    return inv * (scaled - mean - normal * cross), jnp.sum(grad * normal, axis=0, keepdims=True)


def gelu_parts(gate):
    square = gate * gate
    tanh = jnp.tanh(GELU_C * gate * (1.0 + 0.044715 * square))
    half = 0.5 * (1.0 + tanh)
    value = gate * half
    slope = half + 0.5 * gate * (1.0 - tanh * tanh) * (GELU_C * (1.0 + 3.0 * 0.044715 * square))
    return value, slope


class Sizes:
    def __init__(self, rows, hid, tokens, width, hidden, layers, blocks):
        self.rows, self.hid, self.width, self.layers = rows, hid, width, layers
        self.count = rows * hid
        self.own = tokens // self.count
        self.half = width // hid
        self.units = hidden // hid
        self.blocks = blocks
        self.size = width // blocks
        self.side_blocks = blocks // hid
        self.chans = width // self.count
        self.piece = round_up(self.chans, 16)
        self.channels = self.count * self.piece
        self.length = min(SEQ_LEN, tokens)
        self.seqs = tokens // self.length
        self.steps = self.length // LANES
        self.outer = 2 * self.steps
        self.pairs = self.seqs * self.chans
        self.lines = max(self.chans, self.pairs)
        self.group = 4
        self.peers = rows // self.group
        self.part = self.units // self.group
        self.depth = width // rows
        self.deep = round_up(self.depth, 16)
        self.early = 3 * layers - 1
        self.early_rows = round_up(-(-(self.early * self.size + 16) // rows), 16)
        self.late_rows = round_up(-(-(self.size + 16) // rows), 16)
        self.taps_rows = round_up(2 * self.chans + 1, 16)


    @classmethod
    def of(cls, hidden_in, d_out, gains, mixer, skip, filters, gate_up, down):
        rows, hid = lax.axis_size("rows"), lax.axis_size("hid")
        layers, _, width, units = gate_up.shape
        tokens = hidden_in.shape[0] * rows
        return cls(rows, hid, tokens, width, units * hid, layers, mixer.shape[2] * hid)


class Links:
    def __init__(self, sz, sems, local_sems):
        self.sz, self.sems, self.local_sems = sz, sems, local_sems
        self.used = 0
        self.used_local = 0
        self.row = lax.axis_index("rows")
        self.col = lax.axis_index("hid")
        self.plane = lax.rem(self.row, sz.peers)
        self.line = self.row // sz.peers

    def pair(self):
        first = self.used
        self.used += 2
        return self.sems.at[first], self.sems.at[first + 1]

    def copy(self, source, target, pair, row, col):
        return pltpu.make_async_remote_copy(
            src_ref=source,
            dst_ref=target,
            send_sem=pair[0],
            recv_sem=pair[1],
            device_id=(row, col),
            device_id_type=MESH,
        )

    def sibling(self, source, target):
        copy = self.copy(source, target, self.pair(), self.row, self.sz.hid - 1 - self.col)
        copy.start()
        return copy

    def load(self, source, target):
        copy = pltpu.make_async_copy(source, target, self.local_sems.at[self.used_local])
        self.used_local += 1
        copy.start()
        return copy

    def groups(self, count, me, row_of, source_of, target):
        pair = self.pair()

        def post(step, carry):
            member = lax.rem(me + step, count)
            self.copy(source_of(member), target, pair, row_of(member), self.col).start()
            return carry

        lax.fori_loop(1, count, post, 0)
        return pair

    def in_plane(self, source_of, target):
        row_of = lambda member: self.line * self.sz.peers + member
        return self.groups(self.sz.peers, self.plane, row_of, source_of, target)

    def in_line(self, source_of, target):
        row_of = lambda member: member * self.sz.peers + self.plane
        return self.groups(self.sz.group, self.line, row_of, source_of, target)

    def in_rows(self, source_of, target):
        return self.groups(self.sz.rows, self.row, lambda member: member, source_of, target)

    def wait(self, pair, span):
        self.copy(span, span, pair, self.row, self.sz.hid - 1 - self.col).wait()


def greet_all(sz):
    me = lax.axis_index("rows") * sz.hid + lax.axis_index("hid")
    barrier = pltpu.get_barrier_semaphore()

    def greet(step, carry):
        peer = lax.rem(me + step, sz.count)
        pl.semaphore_signal(
            barrier,
            inc=1,
            device_id=(peer // sz.hid, lax.rem(peer, sz.hid)),
            device_id_type=MESH,
        )
        return carry

    lax.fori_loop(1, sz.count, greet, 0)
    return barrier


def pieces_start(sz, links, source, target, by_owner):
    pair = links.pair()
    local = links.local_sems.at[links.used_local]
    links.used_local += 1
    token_id = links.row * sz.hid + links.col
    owner_id = links.col * sz.rows + links.row
    there, here = (token_id, owner_id) if by_owner else (owner_id, token_id)
    at = lambda index: pl.ds(pl.multiple_of(index * sz.piece, sz.piece), sz.piece)
    pltpu.make_async_copy(source.at[at(here)], target.at[at(there)], local).start()

    def post(step, carry):
        peer = lax.rem(token_id + step, sz.count)
        row, col = peer // sz.hid, lax.rem(peer, sz.hid)
        index = (col * sz.rows + row) if by_owner else peer
        links.copy(source.at[at(index)], target.at[at(there)], pair, row, col).start()
        return carry

    lax.fori_loop(1, sz.count, post, 0)
    return pair, local


def pieces_wait(sz, links, target, tokens):
    pair, local = tokens
    first = target.at[pl.ds(0, sz.piece)]
    pltpu.make_async_copy(first, first, local).wait()
    links.wait(pair, target.at[pl.ds(0, (sz.count - 1) * sz.piece)])


def spread_in(source, wide, lines, stride, steps):
    for place, line in enumerate(lines):
        wide[:, place * LANES : (place + 1) * LANES] = source[
            pl.ds(line, steps, stride=stride), :
        ].astype(wide.dtype)


CHUNK = 8


def dft(b, lines, outer, target):
    cos = b.twist[:, :LANES]
    sin = b.twist[:, LANES:]
    for start in range(0, lines, CHUNK):
        here = min(CHUNK, lines - start)
        lanes = slice(start * LANES, (start + here) * LANES)
        b.mid[:, : here * LANES] = nn(b.outer_fwd[...], b.wide[:, lanes])
        for line in range(here):
            lanes = slice(line * LANES, (line + 1) * LANES)
            real = b.mid[0:outer, lanes]
            imag = b.mid[outer : 2 * outer, lanes]
            rows = slice((start + line) * outer, (start + line + 1) * outer)
            b.flat[rows, 0:LANES] = (real * cos + imag * sin).astype(BF16)
            b.flat[rows, LANES:] = (imag * cos - real * sin).astype(BF16)
        rows = slice(start * outer, (start + here) * outer)
        target[rows, :] = nn(b.flat[rows, :], b.inner_fwd[...])


def inverse_dft(b, lines, outer, put):
    cos = b.twist[:, :LANES]
    sin = b.twist[:, LANES:]
    for start in range(0, lines, CHUNK):
        here = min(CHUNK, lines - start)
        for line in range(here):
            rows = slice((start + line) * outer, (start + line + 1) * outer)
            lanes = slice(line * LANES, (line + 1) * LANES)
            part = nn(b.flat[rows, :], b.inner_inv[...])
            real = part[:, :LANES]
            imag = part[:, LANES:]
            b.mid_half[0:outer, lanes] = (real * cos - imag * sin).astype(BF16)
            b.mid_half[outer : 2 * outer, lanes] = (imag * cos + real * sin).astype(BF16)
        value = nn(b.outer_inv[...], b.mid_half[:, : here * LANES])
        for line in range(here):
            put(start + line, value[:, line * LANES : (line + 1) * LANES])


def put_lines(target, lines, stride, steps):
    def put(place, value):
        target[pl.ds(lines[place], steps, stride=stride), :] = value

    return put


def signal_lines(sz):
    return [seq * sz.steps * sz.piece + chan for seq in range(sz.seqs) for chan in range(sz.chans)]


def own_taps(sz, filters):
    start = lax.axis_index("rows") * sz.chans
    chan = lax.broadcasted_iota(jnp.int32, (sz.piece, sz.half), 0)
    lane = lax.broadcasted_iota(jnp.int32, (sz.piece, sz.half), 1)
    pick = jnp.where((lane == start + chan) & (chan < sz.chans), 1.0, 0.0).astype(BF16)
    parts = [nt(pick, filters[way].astype(BF16)) for way in range(2)]
    return jnp.concatenate(parts, axis=0).astype(BF16)


def own_envelope(sz, env):
    first_chan = lax.axis_index("hid") * sz.half + lax.axis_index("rows") * sz.chans
    channel = first_chan + lax.broadcasted_iota(jnp.int32, (sz.piece, LANES), 0)
    fraction = lax.rem(channel * 37, sz.width).astype(F32) / (sz.width - 1)
    start_log = math.log(1.0 / 40.0)
    rate = jnp.exp(start_log + (math.log(1.5 / sz.length) - start_log) * fraction)
    lane = lax.broadcasted_iota(jnp.int32, (sz.piece, LANES), 1)
    power = jnp.zeros((sz.piece, LANES), F32)
    for step in range(sz.steps):
        decay = jnp.exp(-(lane + step * LANES).astype(F32) * rate)
        env[0 : sz.piece, step * LANES : (step + 1) * LANES] = decay
        power += decay * decay
    scale = lax.rsqrt(2.0 * jnp.sum(power, axis=1, keepdims=True))
    for step in range(sz.steps):
        lanes = slice(step * LANES, (step + 1) * LANES)
        value = env[0 : sz.piece, lanes] * scale
        env[0 : sz.piece, lanes] = value
        env[sz.piece :, lanes] = jnp.where(lane + step * LANES > 0, value, 0.0)


def filter_spectrum(sz, b, layer):
    piece, steps, outer = sz.piece, sz.steps, sz.outer
    taps = own_taps(sz, b.filters[layer])
    chunk = 4
    for start in range(0, steps, chunk):
        span = slice(start * LANES, (start + chunk) * LANES)
        kernels = nn(taps, b.pos[:, span]) * b.env[:, span]
        for step in range(chunk):
            b.tall[pl.ds((start + step) * 2 * piece, 2 * piece), :] = kernels[
                :, step * LANES : (step + 1) * LANES
            ]
    spec = b.filt_spec[layer]
    span = sz.chans * outer
    for way in range(2):
        lines = [way * piece + chan for chan in range(sz.chans)]
        spread_in(b.tall, b.wide, lines, 2 * piece, steps)
        dft(b, sz.chans, outer, b.spec)
        if way == 0:
            spec[...] = b.spec[0:span, :].astype(BF16)
        else:
            spec[:, :LANES] = (spec[:, :LANES].astype(F32) + b.spec[0:span, :LANES]).astype(BF16)
            spec[:, LANES:] = (spec[:, LANES:].astype(F32) - b.spec[0:span, LANES:]).astype(BF16)


def conv_forward(sz, b, layer, landed):
    b.tall[0 : sz.channels, :] = landed[...].astype(F32)
    lines = signal_lines(sz)
    spread_in(b.tall, b.wide, lines, sz.piece, sz.steps)
    dft(b, sz.pairs, sz.outer, b.spec)
    span = sz.chans * sz.outer
    filt = b.filt_spec[layer]
    for seq in range(sz.seqs):
        rows = slice(seq * span, (seq + 1) * span)
        re, im = b.spec[rows, :LANES], b.spec[rows, LANES:]
        b.sig_spec[layer][rows, :LANES] = re.astype(BF16)
        b.sig_spec[layer][rows, LANES:] = im.astype(BF16)
        fil_re, fil_im = filt[:, :LANES].astype(F32), filt[:, LANES:].astype(F32)
        b.flat[rows, :LANES] = (re * fil_re - im * fil_im).astype(BF16)
        b.flat[rows, LANES:] = (re * fil_im + im * fil_re).astype(BF16)
    inverse_dft(b, sz.pairs, sz.outer, put_lines(b.tall, lines, sz.piece, sz.steps))
    b.staged[...] = b.tall[0 : sz.channels, :].astype(BF16)


def conv_backward(sz, b, layer, landed):
    b.tall[0 : sz.channels, :] = landed[...].astype(F32)
    lines = signal_lines(sz)
    spread_in(b.tall, b.wide, lines, sz.piece, sz.steps)
    dft(b, sz.pairs, sz.outer, b.spec)
    span = sz.chans * sz.outer
    filt = b.filt_spec[layer]
    for seq in range(sz.seqs):
        rows = slice(seq * span, (seq + 1) * span)
        re, im = b.spec[rows, :LANES], b.spec[rows, LANES:]
        fil_re, fil_im = filt[:, :LANES].astype(F32), filt[:, LANES:].astype(F32)
        b.flat[rows, :LANES] = (re * fil_re + im * fil_im).astype(BF16)
        b.flat[rows, LANES:] = (im * fil_re - re * fil_im).astype(BF16)
    inverse_dft(b, sz.pairs, sz.outer, put_lines(b.tall, lines, sz.piece, sz.steps))
    b.staged[...] = b.tall[0 : sz.channels, :].astype(BF16)


def taps_gradient(sz, b, layer, landed, signal):
    span = sz.chans * sz.outer
    total_re = jnp.zeros((span, LANES), F32)
    total_im = jnp.zeros((span, LANES), F32)
    for seq in range(sz.seqs):
        rows = slice(seq * span, (seq + 1) * span)
        re, im = b.spec[rows, :LANES], b.spec[rows, LANES:]
        sig = b.sig_spec[layer]
        sig_re, sig_im = sig[rows, :LANES].astype(F32), sig[rows, LANES:].astype(F32)
        total_re += re * sig_re + im * sig_im
        total_im += im * sig_re - re * sig_im
    piece = sz.piece
    b.tall[...] = jnp.zeros_like(b.tall)
    for way in range(2):
        b.flat[0:span, :LANES] = total_re.astype(BF16)
        b.flat[0:span, LANES:] = (total_im if way == 0 else -total_im).astype(BF16)
        lines = [way * piece + chan for chan in range(sz.chans)]
        inverse_dft(b, sz.chans, sz.outer, put_lines(b.tall, lines, 2 * piece, sz.steps))
    taps = own_taps(sz, b.filters[layer])
    total = jnp.zeros((2 * piece, ORDER), F32)
    chunk = 4
    for start in range(0, sz.steps, chunk):
        lanes = slice(start * LANES, (start + chunk) * LANES)
        raw = nn(taps, b.pos[:, lanes])
        grads = jnp.concatenate(
            [b.tall[pl.ds((start + step) * 2 * piece, 2 * piece), :] for step in range(chunk)],
            axis=1,
        )
        grads = grads * b.env[:, lanes] + (2.0 * DECAY) * raw
        total += nt(grads.astype(BF16), b.pos[:, lanes])
    products = jnp.zeros((piece, LANES), F32)
    for block in range(sz.count):
        rows = slice(block * piece, (block + 1) * piece)
        products += landed[rows, :].astype(F32) * signal[rows, :].astype(F32)
    column = jnp.sum(products, axis=1, keepdims=True)
    row = jnp.transpose(jnp.broadcast_to(column, (piece, LANES)))[0:8, :]
    b.taps_work[...] = jnp.zeros_like(b.taps_work)
    b.taps_work[0 : sz.chans, :] = total[0 : sz.chans, :]
    b.taps_work[sz.chans : 2 * sz.chans, :] = total[piece : piece + sz.chans, :]
    b.taps_work[2 * sz.chans : 2 * sz.chans + 1, 0:piece] = row[0:1, :]


def block_of(sz, block):
    return slice(block * sz.size, (block + 1) * sz.size)


def pad_pieces(sz, b, source, target):
    for owner in range(sz.count):
        b.tall[owner * sz.piece : owner * sz.piece + sz.chans, :] = source[
            owner * sz.chans : (owner + 1) * sz.chans, :
        ]
    target[...] = b.tall[0 : sz.channels, :].astype(BF16)


def unpad_pieces(sz, b, source, target):
    b.tall[0 : sz.channels, :] = source[...].astype(F32)
    for owner in range(sz.count):
        target[owner * sz.chans : (owner + 1) * sz.chans, :] = b.tall[
            owner * sz.piece : owner * sz.piece + sz.chans, :
        ]


def project(sz, b, layer):
    for block in range(sz.blocks):
        rows = block_of(sz, block)
        part = b.normed[layer][:, rows]
        b.wide_own[rows, :] = nt(b.mixer[layer, 0, block], part)
        b.gate[layer][rows, :] = nt(b.mixer[layer, 1, block], part)
    b.inner[layer][...] = b.wide_own[...].astype(BF16)
    pad_pieces(sz, b, b.wide_own, b.message)


def mix(sz, b, layer, conv):
    summed, mixed, middle = b.summed[layer], b.mixed[layer], b.middle[layer]
    unpad_pieces(sz, b, conv, b.wide_own)
    summed[...] = b.wide_own[...] + b.skip[layer][...] * b.inner[layer][...].astype(F32)
    mixed[...] = (b.gate[layer][...] * summed[...]).astype(BF16)
    for block in range(sz.blocks):
        rows = block_of(sz, block)
        middle[:, rows] = tn(mixed[rows, :], b.mixer[layer, 2, block])
    middle[...] = middle[...] + b.stream[layer][...]


def mixer_gradient(sz, b, kind_row, values, mine, give):
    low = lax.axis_index("hid") == 0
    left = jnp.concatenate(values[: sz.side_blocks], axis=1)
    right = jnp.concatenate(values[sz.side_blocks :], axis=1)
    rows = slice(kind_row * sz.size, (kind_row + 1) * sz.size)
    mine[rows, :] = jnp.where(low, left, right).astype(BF16)
    give[rows, :] = jnp.where(low, right, left).astype(BF16)


def gain_gradient(sz, b, row, value, mine, give):
    low = lax.axis_index("hid") == 0
    left, right = value[:, : sz.half], value[:, sz.half :]
    mine[row : row + 1, :] = jnp.where(low, left, right)
    give[row : row + 1, :] = jnp.where(low, right, left)


def mixer_backward(sz, b, layer, grad_next, total):
    normal, inv = normalize(b.middle[layer][...])
    gain = b.gain[layer, 1:2, :]
    back, gain_grad = norm_back(total, normal, inv, gain)
    result = grad_next + back
    b.grad_middle[...] = result
    b.grad_o[...] = result.astype(BF16)
    for block in range(sz.blocks):
        rows = block_of(sz, block)
        grad_mixed = nt(b.mixer[layer, 2, block], b.grad_o[:, rows])
        b.gate_grad[rows, :] = (grad_mixed * b.summed[layer][rows, :]).astype(BF16)
        b.summed_grad[rows, :] = grad_mixed * b.gate[layer][rows, :]
    pad_pieces(sz, b, b.summed_grad, b.message)
    return gain_grad


def out_gradient(sz, b, layer):
    return [
        nn(b.mixed[layer][block_of(sz, block), :], b.grad_o[:, block_of(sz, block)])
        for block in range(sz.blocks)
    ]


def in_gradient(sz, b, layer, grads):
    return [
        jnp.transpose(
            nn(grads[block_of(sz, block), :], b.normed[layer][:, block_of(sz, block)])
        )
        for block in range(sz.blocks)
    ]


def input_backward(sz, b, layer, back):
    unpad_pieces(sz, b, back, b.wide_own)
    b.inner_grad[...] = (b.skip[layer][...] * b.summed_grad[...] + b.wide_own[...]).astype(BF16)
    for block in range(sz.blocks):
        rows = block_of(sz, block)
        b.work[:, rows] = tn(b.inner_grad[rows, :], b.mixer[layer, 0, block]) + tn(
            b.gate_grad[rows, :], b.mixer[layer, 1, block]
        )
    normal, inv = normalize(b.stream[layer][...])
    result, gain_grad = norm_back(
        b.work[...], normal, inv, b.gain[layer, 0:1, :]
    )
    return b.grad_middle[...] + result, gain_grad


def ff_forward(sz, b, layer):
    tile = 512
    rows = slice(0, 2 * sz.own)
    b.out_sum[...] = jnp.zeros_like(b.out_sum)

    def body(step, carry):
        lanes = pl.ds(pl.multiple_of(step * tile, tile), tile)
        normed = b.nbuf[layer][rows, :]
        gate = nn(normed, b.up[layer, 0, :, lanes])
        up = nn(normed, b.up[layer, 1, :, lanes])
        value, _ = gelu_parts(gate)
        b.out_sum[...] += nt((value * up).astype(BF16), b.down[layer, :, lanes])
        return carry

    lax.fori_loop(0, sz.units // tile, body, 0)


def ff_backward(sz, b, layer, with_out):
    tile = 512
    rows = slice(0, 2 * sz.own)
    b.grad_sum[...] = jnp.zeros_like(b.grad_sum)
    if with_out:
        b.out_sum[...] = jnp.zeros_like(b.out_sum)

    def body(step, carry):
        lanes = pl.ds(pl.multiple_of(step * tile, tile), tile)
        normed = b.nbuf[layer][rows, :]
        gate = nn(normed, b.up[layer, 0, :, lanes])
        up = nn(normed, b.up[layer, 1, :, lanes])
        through = nn(b.gbuf[layer][rows, :], b.down[layer, :, lanes])
        value, slope = gelu_parts(gate)
        if with_out:
            b.out_sum[...] += nt((value * up).astype(BF16), b.down[layer, :, lanes])
        gate_grad = (slope * up * through).astype(BF16)
        up_grad = (value * through).astype(BF16)
        b.grad_sum[...] += nt(gate_grad, b.up[layer, 0, :, lanes]) + nt(
            up_grad, b.up[layer, 1, :, lanes]
        )
        return carry

    lax.fori_loop(0, sz.units // tile, body, 0)


def ff_gradients(sz, b, layer, links):
    start = pl.multiple_of(links.line * sz.part, LANES)
    units = pl.ds(start, sz.part)
    chunk = 2 * sz.own

    def body(step, carry):
        rows = pl.ds(pl.multiple_of(step * chunk, chunk), chunk)
        normed = b.nbuf[layer][rows, :]
        gate = nn(normed, b.up[layer, 0, :, units])
        up = nn(normed, b.up[layer, 1, :, units])
        through = nn(b.gbuf[layer][rows, :], b.down[layer, :, units])
        value, slope = gelu_parts(gate)
        b.unit_grad[0, rows, :] = (slope * up * through).astype(BF16)
        b.unit_grad[1, rows, :] = (value * through).astype(BF16)
        b.unit_grad[2, rows, :] = (value * up).astype(BF16)
        return carry

    lax.fori_loop(0, sz.group, body, 0)
    split = sz.width // 2
    for begin in (0, split):
        lanes = slice(begin, begin + split)
        for kind in range(3):
            left = b.gbuf[layer] if kind == 2 else b.nbuf[layer]
            b.product[...] = tn(left[:, lanes], b.unit_grad[kind])
            for first in range(0, split, sz.depth):
                owner = (begin + first) // sz.depth
                line, peer = owner // sz.peers, owner % sz.peers
                b.pieces[peer, line, kind, 0 : sz.depth, :] = b.product[
                    first : first + sz.depth, :
                ].astype(BF16)
    b.summing[layer][links.plane] = b.pieces[links.plane]


def sum_pieces(sz, b, layer, links):
    for line in range(sz.group):
        for kind in range(3):
            total = b.summing[layer][0, line, kind].astype(F32)
            for peer in range(1, sz.peers):
                total += b.summing[layer][peer, line, kind].astype(F32)
            b.part_sum[layer][line, kind] = total.astype(BF16)


class Named:
    pass


def layout(sz):
    layers, own, width = sz.layers, sz.own, sz.width
    wide = 2 * sz.piece * sz.steps
    span = sz.early_rows * sz.rows
    late = sz.late_rows * sz.rows
    per_layer = dict(
        stream=((own, width), F32),
        normed=((own, width), BF16),
        inner=((width, own), BF16),
        gate=((width, own), F32),
        summed=((width, own), F32),
        mixed=((width, own), BF16),
        middle=((own, width), F32),
        nbuf=((2 * sz.group * own, width), BF16),
        gbuf=((2 * sz.group * own, width), BF16),
        skip=((width, LANES), F32),
        filt_spec=((sz.chans * sz.outer, 2 * LANES), BF16),
        sig_spec=((sz.pairs * sz.outer, 2 * LANES), BF16),
        fore_in=((sz.channels, LANES), BF16),
        fore_out=((sz.channels, LANES), BF16),
        back_in=((sz.channels, LANES), BF16),
        back_out=((sz.channels, LANES), BF16),
        summing=((sz.peers, sz.group, 3, sz.deep, sz.part), BF16),
        part_sum=((sz.group, 3, sz.deep, sz.part), BF16),
        grad_got=((own, width), BF16),
        out_got=((own, width), BF16),
    )
    single = dict(
        x=((own, width), BF16),
        gain=((layers, 2, width), F32),
        skip_rows=((layers, width), F32),
        mixer=((layers, 3, sz.blocks, sz.size, sz.size), BF16),
        filters=((layers, 2, ORDER, sz.half), F32),
        pos=((ORDER, sz.length), BF16),
        outer_fwd=((2 * sz.outer, sz.steps), BF16),
        outer_inv=((sz.steps, 2 * sz.outer), BF16),
        inner_fwd=((2 * LANES, 2 * LANES), BF16),
        inner_inv=((2 * LANES, 2 * LANES), BF16),
        twist=((sz.outer, 2 * LANES), F32),
        up=((layers, 2, width, sz.units), BF16),
        down=((layers, width, sz.units), BF16),
        env=((2 * sz.piece, sz.length), F32),
        tall=((max(wide, sz.channels), LANES), F32),
        wide=((sz.steps, sz.lines * LANES), BF16),
        mid=((2 * sz.outer, CHUNK * LANES), F32),
        flat=((sz.lines * sz.outer, 2 * LANES), BF16),
        mid_half=((2 * sz.outer, CHUNK * LANES), BF16),
        spec=((sz.lines * sz.outer, 2 * LANES), F32),
        message=((sz.channels, LANES), BF16),
        staged=((sz.channels, LANES), BF16),
        wide_own=((width, own), F32),
        work=((own, width), F32),
        grad_next=((own, width), F32),
        grad_middle=((own, width), F32),
        grad_o=((own, width), BF16),
        gate_grad=((width, own), BF16),
        summed_grad=((width, own), F32),
        inner_grad=((width, own), BF16),
        out_sum=((2 * own, width), F32),
        grad_sum=((2 * own, width), F32),
        out_give=((own, width), BF16),
        sum_give=((own, width), BF16),
        unit_grad=((3, 2 * sz.group * own, sz.part), BF16),
        product=((width // 2, sz.part), F32),
        pieces=((sz.peers, sz.group, 3, sz.deep, sz.part), BF16),
        taps_work=((sz.taps_rows, ORDER), F32),
        gain_mine=((16, sz.half), F32),
        gain_give=((16, sz.half), F32),
        early_mine=((span, sz.half), BF16),
        early_give=((span, sz.half), BF16),
        early_got=((span, sz.half), BF16),
        early_plane=((sz.peers, sz.group * sz.early_rows, sz.half), BF16),
        early_sum=((sz.group * sz.early_rows, sz.half), BF16),
        early_line=((sz.group, sz.early_rows, sz.half), BF16),
        late_gain_mine=((16, sz.half), F32),
        late_gain_give=((16, sz.half), F32),
        late_mine=((late, sz.half), BF16),
        late_give=((late, sz.half), BF16),
        late_got=((late, sz.half), BF16),
        late_in=((sz.rows, sz.late_rows, sz.half), BF16),
        late_sum=((sz.late_rows, sz.half), BF16),
        out_keep=((2, own, sz.half), BF16),
        in_keep=((2, own, sz.half), F32),
        taps_send=((layers, sz.taps_rows, ORDER), BF16),
        late_out=((sz.late_rows, sz.half), BF16),
        early_out=((sz.early_rows, sz.half), BF16),
    )
    names, specs = [], []
    for name, (shape, kind) in per_layer.items():
        for layer in range(layers):
            names.append((name, layer))
            specs.append(pltpu.VMEM(shape, kind))
    for name, (shape, kind) in single.items():
        names.append((name, None))
        specs.append(pltpu.VMEM(shape, kind))
    return names, specs


TABLES = ("pos", "outer_fwd", "outer_inv", "inner_fwd", "inner_inv", "twist")
INPUTS = ("hidden_in", "d_out", "gains", "mixer", "skip", "filters", "gate_up", "down") + TABLES
OUTPUTS = ("hidden_out", "grad_in", "early", "late", "taps", "units")


def program_kernel(sz, *refs):
    names, _ = layout(sz)
    inputs = dict(zip(INPUTS, refs))
    outputs = dict(zip(OUTPUTS, refs[len(INPUTS) :]))
    scratch = refs[len(INPUTS) + len(OUTPUTS) :]
    b = Named()
    for (name, layer), ref in zip(names, scratch):
        if layer is None:
            setattr(b, name, ref)
        else:
            setattr(b, name, getattr(b, name, ()) + (ref,))
    links = Links(sz, scratch[len(names)], scratch[len(names) + 1])
    own = sz.own
    top = sz.layers - 1
    col = links.col
    low = col == 0
    mine_rows = pl.ds(pl.multiple_of(col * own, own), own)
    other_rows = pl.ds(pl.multiple_of((1 - col) * own, own), own)

    barrier = greet_all(sz)
    lanes = pl.ds(pl.multiple_of(col * sz.half, sz.half), sz.half)
    sides = pl.ds(col * sz.side_blocks, sz.side_blocks)
    halves = (
        ("x", inputs["hidden_in"], b.x.at[:, lanes]),
        ("mixer", inputs["mixer"], b.mixer.at[:, :, sides]),
        ("gains", inputs["gains"], b.gain.at[:, :, lanes]),
        ("skip", inputs["skip"], b.skip_rows.at[:, lanes]),
        ("g", inputs["d_out"], b.gbuf[top].at[pl.ds(0, own), lanes]),
    )
    loads = {}
    for name, source, target in halves:
        if name in ("x", "g"):
            source = source.at[mine_rows]
        loads[name] = links.load(source, target)
    loads["filters"] = links.load(inputs["filters"], b.filters)
    for name in TABLES:
        loads[name] = links.load(inputs[name], getattr(b, name))
    for layer in range(sz.layers):
        loads["up", layer] = links.load(inputs["gate_up"].at[layer], b.up.at[layer])
        loads["down", layer] = links.load(inputs["down"].at[layer], b.down.at[layer])
    b.gain_mine[...] = jnp.zeros_like(b.gain_mine)
    b.gain_give[...] = jnp.zeros_like(b.gain_give)
    b.late_gain_mine[...] = jnp.zeros_like(b.late_gain_mine)
    b.late_gain_give[...] = jnp.zeros_like(b.late_gain_give)
    pl.semaphore_wait(barrier, sz.count - 1)
    got = {}
    for name, source, target in halves:
        if name in ("x", "g"):
            source = source.at[other_rows]
        got[name] = links.sibling(source, target)

    def both(*wanted):
        for name in wanted:
            loads[name].wait()
            got[name].wait()

    def turn_mixer(layer, kind):
        for block in range(sz.blocks):
            b.mixer[layer, kind, block] = jnp.transpose(b.mixer[layer, kind, block])

    def norm_to(source, target, layer, which):
        normal, _ = normalize(source)
        target[...] = (normal * b.gain[layer, which : which + 1, :]).astype(BF16)

    both("x", "gains")
    b.stream[0][...] = b.x[...].astype(F32)
    norm_to(b.stream[0][...], b.normed[0], 0, 0)
    both("mixer")
    turn_mixer(0, 0)
    turn_mixer(0, 1)

    def gather_own(buffer):
        return links.sibling(buffer.at[pl.ds(0, own)], buffer.at[pl.ds(own, own)])

    def gather_line(buffer):
        pair = links.pair()
        for step in range(1, sz.group):
            member = lax.rem(links.line + step, sz.group)
            slot = pl.ds((1 + step) * own, own)
            links.copy(
                buffer.at[pl.ds(0, own)],
                buffer.at[slot],
                pair,
                member * sz.peers + links.plane,
                col,
            ).start()
        return pair

    def gather_rest(buffer, pair):
        arrived = buffer.at[pl.ds(2 * own, (sz.group - 1) * own)]
        links.wait(pair, arrived)
        return links.sibling(
            arrived, buffer.at[pl.ds((1 + sz.group) * own, (sz.group - 1) * own)]
        )

    project(sz, b, 0)
    for layer in range(sz.layers):
        moving = pieces_start(sz, links, b.message, b.fore_in[layer], True)
        if layer == 0:
            for name in ("filters", "pos", "outer_fwd", "inner_fwd", "twist"):
                loads[name].wait()
            own_envelope(sz, b.env)
        filter_spectrum(sz, b, layer)
        if layer == 0:
            for name in ("outer_inv", "inner_inv"):
                loads[name].wait()
            both("skip", "g")
            for each in range(sz.layers):
                row = b.skip_rows[each : each + 1, :]
                b.skip[each][...] = jnp.transpose(jnp.broadcast_to(row, (LANES, sz.width)))
        pieces_wait(sz, links, b.fore_in[layer], moving)
        conv_forward(sz, b, layer, b.fore_in[layer])
        moving = pieces_start(sz, links, b.staged, b.fore_out[layer], False)
        if layer == 0:
            for each in range(1, sz.layers):
                turn_mixer(each, 0)
                turn_mixer(each, 1)
            top_own = gather_own(b.gbuf[top])
            top_line = gather_line(b.gbuf[top])
        loads["up", layer].wait()
        loads["down", layer].wait()
        pieces_wait(sz, links, b.fore_out[layer], moving)
        mix(sz, b, layer, b.fore_out[layer])
        norm_to(b.middle[layer][...], b.nbuf[layer].at[pl.ds(0, own)], layer, 1)
        near = gather_own(b.nbuf[layer])
        far = gather_line(b.nbuf[layer])
        near.wait()
        if layer < top:
            ff_forward(sz, b, layer)
            b.out_give[...] = b.out_sum[own:, :].astype(BF16)
            moving = links.sibling(b.out_give, b.out_got[layer])
            if layer == 0:
                top_own.wait()
                top_rest = gather_rest(b.gbuf[top], top_line)
            moving.wait()
            value = b.middle[layer][...] + b.out_sum[0:own, :] + b.out_got[layer][...].astype(F32)
            b.stream[layer + 1][...] = value
            norm_to(value, b.normed[layer + 1], layer + 1, 0)
            project(sz, b, layer + 1)
            low_rest = gather_rest(b.nbuf[layer], far)

    ff_backward(sz, b, top, True)
    b.sum_give[...] = b.grad_sum[own:, :].astype(BF16)
    moving = links.sibling(b.sum_give, b.grad_got[top])
    b.out_give[...] = b.out_sum[own:, :].astype(BF16)
    out_moving = links.sibling(b.out_give, b.out_got[top])
    moving.wait()
    total = b.grad_sum[0:own, :] + b.grad_got[top][...].astype(F32)
    grad_next = b.gbuf[top][0:own, :].astype(F32)
    gain_grad = mixer_backward(sz, b, top, grad_next, total)
    moving = pieces_start(sz, links, b.message, b.back_in[top], True)
    gain_gradient(sz, b, 2 * top, gain_grad, b.gain_mine, b.gain_give)
    early_row = 0
    mixer_gradient(sz, b, early_row, out_gradient(sz, b, top), b.early_mine, b.early_give)
    early_row += 1

    out_moving.wait()
    value = b.middle[top][...] + b.out_sum[0:own, :] + b.out_got[top][...].astype(F32)
    value = value.astype(BF16)
    left, right = value[:, : sz.half], value[:, sz.half :]
    b.out_keep[0] = jnp.where(low, left, right)
    b.out_keep[1] = jnp.where(low, right, left)
    place = outputs["hidden_out"].at[mine_rows]
    ending = [links.load(b.out_keep.at[0], place), links.sibling(b.out_keep.at[1], place)]
    if sz.layers > 1:
        low_rest.wait()
        top_rest.wait()

    waiting = {}
    taps_moving = []
    units_moving = []

    def send_units(layer):
        target = outputs["units"].at[layer, links.line]
        ending.append(links.load(b.part_sum[layer].at[links.line], target))
        return links.in_line(lambda member: b.part_sum[layer].at[member], target)

    for layer in reversed(range(sz.layers)):
        if layer == top:
            rest = gather_rest(b.nbuf[top], far)
        else:
            rest = gather_rest(b.gbuf[layer], far)
            links.wait(waiting["plane"], b.summing[layer + 1].at[pl.ds(0, sz.peers - 1)])
            sum_pieces(sz, b, layer + 1, links)
            units_moving.append(send_units(layer + 1))
            if layer == 0:
                early_pair.wait()
                b.early_mine[...] = (
                    b.early_mine[...].astype(F32) + b.early_got[...].astype(F32)
                ).astype(BF16)
                slab = sz.group * sz.early_rows
                at = lambda index: pl.ds(pl.multiple_of(index * slab, slab), slab)
                plane_pair = links.in_plane(
                    lambda member: b.early_mine.at[at(member)], b.early_plane.at[links.plane]
                )
        pieces_wait(sz, links, b.back_in[layer], moving)
        conv_backward(sz, b, layer, b.back_in[layer])
        moving = pieces_start(sz, links, b.staged, b.back_out[layer], False)
        taps_gradient(sz, b, layer, b.back_in[layer], b.fore_in[layer])
        b.taps_send[layer] = b.taps_work[...].astype(BF16)
        place = outputs["taps"].at[links.row, layer]
        ending.append(links.load(b.taps_send.at[layer], place))
        taps_moving.append(links.in_rows(lambda member: b.taps_send.at[layer], place))
        rest.wait()
        ff_gradients(sz, b, layer, links)
        waiting["plane"] = links.in_plane(
            lambda member: b.pieces.at[member], b.summing[layer].at[links.plane]
        )
        pieces_wait(sz, links, b.back_out[layer], moving)
        value, gain_grad = input_backward(sz, b, layer, b.back_out[layer])
        if layer > 0:
            b.grad_next[...] = value
            b.gbuf[layer - 1][0:own, :] = value.astype(BF16)
            near = gather_own(b.gbuf[layer - 1])
            far = gather_line(b.gbuf[layer - 1])
            gain_gradient(sz, b, 2 * layer - 1, gain_grad, b.gain_mine, b.gain_give)
            for grads in (b.inner_grad, b.gate_grad):
                mixer_gradient(
                    sz, b, early_row, in_gradient(sz, b, layer, grads), b.early_mine, b.early_give
                )
                early_row += 1
            near.wait()
            ff_backward(sz, b, layer - 1, False)
            b.sum_give[...] = b.grad_sum[own:, :].astype(BF16)
            moving = links.sibling(b.sum_give, b.grad_got[layer - 1])
            moving.wait()
            total = b.grad_sum[0:own, :] + b.grad_got[layer - 1][...].astype(F32)
            gain_grad = mixer_backward(sz, b, layer - 1, b.grad_next[...], total)
            moving = pieces_start(sz, links, b.message, b.back_in[layer - 1], True)
            gain_gradient(sz, b, 2 * layer - 2, gain_grad, b.gain_mine, b.gain_give)
            mixer_gradient(
                sz, b, early_row, out_gradient(sz, b, layer - 1), b.early_mine, b.early_give
            )
            early_row += 1
            if layer == 1:
                mixer_gradient(
                    sz,
                    b,
                    early_row,
                    in_gradient(sz, b, 0, b.gate_grad),
                    b.early_mine,
                    b.early_give,
                )
                early_row += 1
                rows = slice(early_row * sz.size, early_row * sz.size + 16)
                b.early_mine[rows, :] = b.gain_mine[...].astype(BF16)
                b.early_give[rows, :] = b.gain_give[...].astype(BF16)
                last = slice(early_row * sz.size + 16, sz.rows * sz.early_rows)
                b.early_mine[last, :] = jnp.zeros_like(b.early_mine[last, :])
                b.early_give[last, :] = jnp.zeros_like(b.early_give[last, :])
                early_pair = links.sibling(b.early_give, b.early_got)

    left, right = value[:, : sz.half], value[:, sz.half :]
    b.in_keep[0] = jnp.where(low, left, right)
    b.in_keep[1] = jnp.where(low, right, left)
    place = outputs["grad_in"].at[mine_rows]
    ending += [links.load(b.in_keep.at[0], place), links.sibling(b.in_keep.at[1], place)]
    mixer_gradient(
        sz, b, 0, in_gradient(sz, b, 0, b.inner_grad), b.late_mine, b.late_give
    )
    gain_gradient(sz, b, 0, gain_grad, b.late_gain_mine, b.late_gain_give)
    rows = slice(sz.size, sz.size + 16)
    b.late_mine[rows, :] = b.late_gain_mine[...].astype(BF16)
    b.late_give[rows, :] = b.late_gain_give[...].astype(BF16)
    last = slice(sz.size + 16, sz.rows * sz.late_rows)
    b.late_mine[last, :] = jnp.zeros_like(b.late_mine[last, :])
    b.late_give[last, :] = jnp.zeros_like(b.late_give[last, :])
    late_pair = links.sibling(b.late_give, b.late_got)

    links.wait(plane_pair, b.early_plane.at[pl.ds(0, sz.peers - 1)])
    b.early_plane[links.plane] = b.early_mine[at(links.plane), :]
    total = b.early_plane[0].astype(F32)
    for peer in range(1, sz.peers):
        total += b.early_plane[peer].astype(F32)
    b.early_sum[...] = total.astype(BF16)
    deep = sz.early_rows
    one = lambda index: pl.ds(pl.multiple_of(index * deep, deep), deep)
    line_pair = links.in_line(
        lambda member: b.early_sum.at[one(member)], b.early_line.at[links.line]
    )

    late_pair.wait()
    b.late_mine[...] = (b.late_mine[...].astype(F32) + b.late_got[...].astype(F32)).astype(BF16)
    few = lambda index: pl.ds(pl.multiple_of(index * sz.late_rows, sz.late_rows), sz.late_rows)
    rows_pair = links.in_rows(
        lambda member: b.late_mine.at[few(member)], b.late_in.at[links.row]
    )

    links.wait(line_pair, b.early_line.at[pl.ds(0, sz.group - 1)])
    b.early_line[links.line] = b.early_sum[one(links.line), :]
    total = b.early_line[0].astype(F32)
    for member in range(1, sz.group):
        total += b.early_line[member].astype(F32)
    early = outputs["early"]
    b.early_out[...] = total.astype(BF16)
    place = early.at[links.plane * sz.group + links.line]
    early_own = links.load(b.early_out, place)
    spread_line = links.in_line(lambda member: b.early_out, place)

    links.wait(rows_pair, b.late_in.at[pl.ds(0, sz.rows - 1)])
    b.late_in[links.row] = b.late_mine[few(links.row), :]
    late = outputs["late"]
    b.late_out[...] = jnp.sum(b.late_in[...].astype(F32), axis=0).astype(BF16)
    ending.append(links.load(b.late_out, late.at[links.row]))
    spread_rows = links.in_rows(lambda member: b.late_out, late.at[links.row])

    links.wait(waiting["plane"], b.summing[0].at[pl.ds(0, sz.peers - 1)])
    sum_pieces(sz, b, 0, links)
    units_moving.append(send_units(0))
    early_own.wait()
    links.wait(spread_line, early.at[pl.ds(0, sz.group - 1)])
    mine = pl.ds(pl.multiple_of(links.plane * sz.group, sz.group), sz.group)
    spread_plane = links.in_plane(lambda member: early.at[mine], early.at[mine])

    for layer, pair in zip(reversed(range(sz.layers)), units_moving):
        links.wait(pair, outputs["units"].at[layer, pl.ds(0, sz.group - 1)])
    links.wait(spread_plane, early.at[pl.ds(0, (sz.peers - 1) * sz.group)])
    links.wait(spread_rows, late.at[pl.ds(0, sz.rows - 1)])
    for layer, pair in zip(reversed(range(sz.layers)), taps_moving):
        links.wait(pair, outputs["taps"].at[pl.ds(0, sz.rows - 1), layer])
    for copy in ending:
        copy.wait()


def program(sz, arrays):
    names, scratch = layout(sz)
    outs = (
        ((2 * sz.own, sz.half), BF16),
        ((2 * sz.own, sz.half), F32),
        ((sz.rows, sz.early_rows, sz.half), BF16),
        ((sz.rows, sz.late_rows, sz.half), BF16),
        ((sz.rows, sz.layers, sz.taps_rows, ORDER), BF16),
        ((sz.layers, sz.group, 3, sz.deep, sz.part), BF16),
    )
    return pl.pallas_call(
        functools.partial(program_kernel, sz),
        out_shape=tuple(jax.ShapeDtypeStruct(shape, kind) for shape, kind in outs),
        in_specs=[pl.BlockSpec(memory_space=pl.ANY)] * len(arrays),
        out_specs=(pl.BlockSpec(memory_space=pl.ANY),) * len(outs),
        scratch_shapes=scratch
        + [pltpu.SemaphoreType.DMA((120,)), pltpu.SemaphoreType.DMA((40,))],
        compiler_params=pltpu.CompilerParams(
            collective_id=0, has_side_effects=True, vmem_limit_bytes=63 * MIB
        ),
        name="program",
    )(*arrays)


def together(sz, hidden_in, d_out, gains, mixer, skip, filters, gate_up, down):
    rows, layers = sz.rows, sz.layers
    pos = jnp.asarray(position_table(sz.length).T, F32).astype(BF16)
    arrays = (hidden_in, d_out, gains, mixer, skip, filters, gate_up, down, pos)
    hidden_out, grad_in, early, late, taps, units = program(sz, arrays + dft_tables(sz.length))

    def matrix(payload, place):
        value = payload[place * sz.size : (place + 1) * sz.size].astype(F32)
        blocks = [value[:, block_of(sz, block)] for block in range(sz.side_blocks)]
        return jnp.stack(blocks)

    early = early.reshape(-1, sz.half)
    late = late.reshape(-1, sz.half)
    places = []
    for layer in reversed(range(layers)):
        places += [(layer, 2)]
        places += [(layer, 0), (layer, 1)] if layer > 0 else [(layer, 1)]
    found = {place: matrix(early, index) for index, place in enumerate(places)}
    found[0, 0] = matrix(late, 0)
    mixers = jnp.stack(
        [jnp.stack([found[layer, kind] for kind in range(3)]) for layer in range(layers)]
    )
    gain_rows = early[sz.early * sz.size : sz.early * sz.size + 2 * layers - 1]
    gain_rows = jnp.concatenate([late[sz.size : sz.size + 1], gain_rows[: 2 * layers - 1]], axis=0)
    gain_out = gain_rows.astype(F32).reshape(layers, 2, sz.half)
    skip_out = jnp.transpose(taps[:, :, 2 * sz.chans, : sz.chans], (1, 0, 2))
    taps_out = taps[:, :, : 2 * sz.chans].reshape(rows, layers, 2, sz.chans, ORDER)
    taps_out = jnp.transpose(taps_out, (1, 2, 4, 0, 3)).reshape(layers, 2, ORDER, sz.half)
    units = jnp.moveaxis(units[:, :, :, : sz.depth].astype(F32), 1, 3)
    units = units.reshape(layers, 3, sz.depth, sz.units)
    return (
        hidden_out,
        grad_in,
        gain_out,
        mixers,
        skip_out.astype(F32).reshape(layers, sz.half),
        taps_out.astype(F32),
        units[:, :2],
        units[:, 2],
    )


def apart_enter(count, hid):
    me = lax.axis_index("rows") * hid + lax.axis_index("hid")
    barrier = pltpu.get_barrier_semaphore()

    def greet(step, carry):
        peer = lax.rem(me + step, count)
        pl.semaphore_signal(
            barrier, inc=1, device_id=(peer // hid, lax.rem(peer, hid)), device_id_type=MESH
        )
        return carry

    lax.fori_loop(1, count, greet, 0)
    return barrier


def apart_exchange_start(source, target, sems, count, rows, hid, piece, by_owner):
    send, recv, local = sems
    row = lax.axis_index("rows")
    col = lax.axis_index("hid")
    token_id = row * hid + col
    owner_id = col * rows + row
    mine_there = token_id if by_owner else owner_id
    mine_here = owner_id if by_owner else token_id
    at = lambda index: pl.ds(pl.multiple_of(index * piece, piece), piece)
    pltpu.make_async_copy(source.at[at(mine_here)], target.at[at(mine_there)], local).start()

    def post(step, carry):
        peer = lax.rem(token_id + step, count)
        peer_row = peer // hid
        peer_col = lax.rem(peer, hid)
        there = (peer_col * rows + peer_row) if by_owner else peer
        pltpu.make_async_remote_copy(
            src_ref=source.at[at(there)],
            dst_ref=target.at[at(mine_there)],
            send_sem=send,
            recv_sem=recv,
            device_id=(peer_row, peer_col),
            device_id_type=MESH,
        ).start()
        return carry

    lax.fori_loop(1, count, post, 0)


def apart_exchange_wait(source, target, sems, count, rows, hid, piece):
    send, recv, local = sems
    row = lax.axis_index("rows")
    col = lax.axis_index("hid")
    pltpu.make_async_copy(
        source.at[pl.ds(0, piece)], target.at[pl.ds(0, piece)], local
    ).wait()
    span = pl.ds(0, (count - 1) * piece)
    pltpu.make_async_remote_copy(
        src_ref=source.at[span],
        dst_ref=target.at[span],
        send_sem=send,
        recv_sem=recv,
        device_id=(row, hid - 1 - col),
        device_id_type=MESH,
    ).wait()


class apart_Sizes:
    def __init__(self, rows, hid, width, hidden, tokens):
        self.rows, self.hid, self.width, self.hidden = rows, hid, width, hidden
        self.count = rows * hid
        self.chans = width // self.count
        self.piece = round_up(self.chans, 16)
        self.length = min(SEQ_LEN, tokens)
        self.seqs = tokens // self.length
        self.blocks = self.length // LANES
        self.outer = 2 * self.blocks
        self.pairs = self.seqs * self.chans
        self.half = width // hid
        self.padded = rows * self.piece
        self.channels = self.count * self.piece


def apart_spread_in(source, wide, lines, stride, blocks):
    for place, line in enumerate(lines):
        wide[:, place * LANES : (place + 1) * LANES] = source[
            pl.ds(line, blocks, stride=stride), :
        ].astype(wide.dtype)


def apart_dft(wide, spectrum, tables, mid, flat, lines, outer, offset=0):
    outer_fwd, inner_fwd, twist = tables
    mid[:, : lines * LANES] = nn(outer_fwd[...], wide[:, : lines * LANES])
    cos = twist[:, :LANES]
    sin = twist[:, LANES:]
    for line in range(lines):
        lanes = pl.ds(line * LANES, LANES)
        real = mid[0:outer, lanes]
        imag = mid[outer : 2 * outer, lanes]
        rows = pl.ds(line * outer, outer)
        flat[rows, 0:LANES] = (real * cos + imag * sin).astype(BF16)
        flat[rows, LANES:] = (imag * cos - real * sin).astype(BF16)
    spectrum[0 : lines * outer, :] = nn(flat[0 : lines * outer, :], inner_fwd[...])


def apart_inverse_dft(flat, tables, mid_half, lines, outer):
    outer_inv, inner_inv, twist = tables
    cos = twist[:, :LANES]
    sin = twist[:, LANES:]
    for line in range(lines):
        rows = pl.ds(line * outer, outer)
        lanes = pl.ds(line * LANES, LANES)
        part = nn(flat[rows, :], inner_inv[...])
        real = part[:, :LANES]
        imag = part[:, LANES:]
        mid_half[0:outer, lanes] = (real * cos - imag * sin).astype(BF16)
        mid_half[outer : 2 * outer, lanes] = (imag * cos + real * sin).astype(BF16)
    return nn(outer_inv[...], mid_half[:, : lines * LANES])


def apart_spread_out(value, target, lines, stride, blocks):
    for place, line in enumerate(lines):
        target[pl.ds(line, blocks, stride=stride), :] = value[
            :, place * LANES : (place + 1) * LANES
        ]


def apart_signal_lines(sz):
    return [seq * sz.blocks * sz.piece + chan for seq in range(sz.seqs) for chan in range(sz.chans)]


def apart_conv_forward_kernel(
    sz,
    inner_ref,
    taps_ref,
    pos_ref,
    env_ref,
    outer_fwd,
    outer_inv,
    inner_fwd,
    inner_inv,
    twist,
    conv_ref,
    filt_spec,
    sig_spec,
    landed,
    staged,
    tall,
    wide,
    mid,
    flat,
    mid_half,
    sems_in,
    sems_out,
):
    barrier = apart_enter(sz.count, sz.hid)
    pl.semaphore_wait(barrier, sz.count - 1)
    into = tuple(sems_in.at[i] for i in range(3))
    back = tuple(sems_out.at[i] for i in range(3))
    apart_exchange_start(inner_ref, landed, into, sz.count, sz.rows, sz.hid, sz.piece, True)

    piece, blocks, outer = sz.piece, sz.blocks, sz.outer
    step = 4
    for start in range(0, blocks, step):
        span = slice(start * LANES, (start + step) * LANES)
        raw = nn(taps_ref[...], pos_ref[:, span])
        kernels = raw * env_ref[:, span]
        for block in range(step):
            tall[pl.ds((start + block) * 2 * piece, 2 * piece), :] = kernels[
                :, block * LANES : (block + 1) * LANES
            ]
    lines = [way * piece + chan for way in range(2) for chan in range(sz.chans)]
    apart_spread_in(tall, wide, lines, 2 * piece, blocks)
    apart_dft(wide, sig_spec, (outer_fwd, inner_fwd, twist), mid, flat, len(lines), outer)
    span = sz.chans * outer
    filt_spec[:, :LANES] = sig_spec[0:span, :LANES] + sig_spec[span : 2 * span, :LANES]
    filt_spec[:, LANES:] = sig_spec[0:span, LANES:] - sig_spec[span : 2 * span, LANES:]

    apart_exchange_wait(inner_ref, landed, into, sz.count, sz.rows, sz.hid, piece)
    tall[0 : sz.channels, :] = landed[...].astype(F32)
    lines = apart_signal_lines(sz)
    apart_spread_in(tall, wide, lines, piece, blocks)
    apart_dft(wide, sig_spec, (outer_fwd, inner_fwd, twist), mid, flat, sz.pairs, outer)
    for seq in range(sz.seqs):
        rows = pl.ds(seq * span, span)
        sig_re, sig_im = sig_spec[rows, :LANES], sig_spec[rows, LANES:]
        fil_re, fil_im = filt_spec[:, :LANES], filt_spec[:, LANES:]
        flat[rows, :LANES] = (sig_re * fil_re - sig_im * fil_im).astype(BF16)
        flat[rows, LANES:] = (sig_re * fil_im + sig_im * fil_re).astype(BF16)
    result = apart_inverse_dft(flat, (outer_inv, inner_inv, twist), mid_half, sz.pairs, outer)
    apart_spread_out(result, tall, lines, piece, blocks)
    staged[...] = tall[0 : sz.channels, :].astype(BF16)
    apart_exchange_start(staged, conv_ref, back, sz.count, sz.rows, sz.hid, piece, False)
    apart_exchange_wait(staged, conv_ref, back, sz.count, sz.rows, sz.hid, piece)


def apart_conv_forward(sz, inner, taps, pos, env, tables, cid):
    outer_fwd, outer_inv, inner_fwd, inner_inv, twist = tables
    wide_lines = max(2 * sz.chans, sz.pairs)
    return pl.pallas_call(
        functools.partial(apart_conv_forward_kernel, sz),
        out_shape=(
            jax.ShapeDtypeStruct((sz.channels, LANES), BF16),
            jax.ShapeDtypeStruct((sz.chans * sz.outer, 2 * LANES), F32),
            jax.ShapeDtypeStruct((wide_lines * sz.outer, 2 * LANES), F32),
        ),
        in_specs=[whole()] * 9,
        out_specs=(whole(),) * 3,
        scratch_shapes=[
            pltpu.VMEM((sz.channels, LANES), BF16),
            pltpu.VMEM((sz.channels, LANES), BF16),
            pltpu.VMEM((max(2 * sz.piece * sz.blocks, sz.channels), LANES), F32),
            pltpu.VMEM((sz.blocks, wide_lines * LANES), BF16),
            pltpu.VMEM((2 * sz.outer, wide_lines * LANES), F32),
            pltpu.VMEM((wide_lines * sz.outer, 2 * LANES), BF16),
            pltpu.VMEM((2 * sz.outer, sz.pairs * LANES), BF16),
            pltpu.SemaphoreType.DMA((3,)),
            pltpu.SemaphoreType.DMA((3,)),
        ],
        compiler_params=pltpu.CompilerParams(
            collective_id=cid, has_side_effects=True, vmem_limit_bytes=48 * MIB
        ),
        name="conv_forward",
    )(inner, taps, pos, env, outer_fwd, outer_inv, inner_fwd, inner_inv, twist)


def apart_conv_backward_kernel(
    sz,
    grad_ref,
    filt_spec,
    sig_spec,
    taps_ref,
    pos_ref,
    env_ref,
    outer_fwd,
    outer_inv,
    inner_fwd,
    inner_inv,
    twist,
    back_ref,
    taps_grad,
    landed,
    staged,
    tall,
    wide,
    mid,
    flat,
    mid_half,
    grad_spec,
    sems_in,
    sems_out,
):
    barrier = apart_enter(sz.count, sz.hid)
    pl.semaphore_wait(barrier, sz.count - 1)
    into = tuple(sems_in.at[i] for i in range(3))
    back = tuple(sems_out.at[i] for i in range(3))
    piece, blocks, outer = sz.piece, sz.blocks, sz.outer
    apart_exchange_start(grad_ref, landed, into, sz.count, sz.rows, sz.hid, piece, True)
    apart_exchange_wait(grad_ref, landed, into, sz.count, sz.rows, sz.hid, piece)
    tall[0 : sz.channels, :] = landed[...].astype(F32)
    lines = apart_signal_lines(sz)
    apart_spread_in(tall, wide, lines, piece, blocks)
    apart_dft(wide, grad_spec, (outer_fwd, inner_fwd, twist), mid, flat, sz.pairs, outer)
    span = sz.chans * outer
    for seq in range(sz.seqs):
        rows = pl.ds(seq * span, span)
        re, im = grad_spec[rows, :LANES], grad_spec[rows, LANES:]
        fil_re, fil_im = filt_spec[:, :LANES], filt_spec[:, LANES:]
        flat[rows, :LANES] = (re * fil_re + im * fil_im).astype(BF16)
        flat[rows, LANES:] = (im * fil_re - re * fil_im).astype(BF16)
    inv_tables = (outer_inv, inner_inv, twist)
    result = apart_inverse_dft(flat, inv_tables, mid_half, sz.pairs, outer)
    apart_spread_out(result, tall, lines, piece, blocks)
    staged[...] = tall[0 : sz.channels, :].astype(BF16)
    apart_exchange_start(staged, back_ref, back, sz.count, sz.rows, sz.hid, piece, False)

    total_re = jnp.zeros((span, LANES), F32)
    total_im = jnp.zeros((span, LANES), F32)
    for seq in range(sz.seqs):
        rows = pl.ds(seq * span, span)
        re, im = grad_spec[rows, :LANES], grad_spec[rows, LANES:]
        sig_re, sig_im = sig_spec[rows, :LANES], sig_spec[rows, LANES:]
        total_re += re * sig_re + im * sig_im
        total_im += im * sig_re - re * sig_im
    flat[0:span, :LANES] = total_re.astype(BF16)
    flat[span : 2 * span, :LANES] = total_re.astype(BF16)
    flat[0:span, LANES:] = total_im.astype(BF16)
    flat[span : 2 * span, LANES:] = (-total_im).astype(BF16)
    result = apart_inverse_dft(flat, inv_tables, mid_half, 2 * sz.chans, outer)
    lines = [way * piece + chan for way in range(2) for chan in range(sz.chans)]
    if sz.chans < piece:
        tall[...] = jnp.zeros_like(tall)
    apart_spread_out(result, tall, lines, 2 * piece, blocks)
    total = jnp.zeros((2 * piece, ORDER), F32)
    step = 4
    for start in range(0, blocks, step):
        span = slice(start * LANES, (start + step) * LANES)
        raw = nn(taps_ref[...], pos_ref[:, span])
        grads = jnp.concatenate(
            [
                tall[pl.ds((start + block) * 2 * piece, 2 * piece), :]
                for block in range(step)
            ],
            axis=1,
        )
        grads = grads * env_ref[:, span] + (2.0 * DECAY) * raw
        total += nt(grads.astype(BF16), pos_ref[:, span])
    taps_grad[...] = total

    apart_exchange_wait(staged, back_ref, back, sz.count, sz.rows, sz.hid, piece)


def apart_conv_backward(sz, grad, filt_spec, sig_spec, taps, pos, env, tables, cid):
    outer_fwd, outer_inv, inner_fwd, inner_inv, twist = tables
    wide_lines = max(2 * sz.chans, sz.pairs)
    return pl.pallas_call(
        functools.partial(apart_conv_backward_kernel, sz),
        out_shape=(
            jax.ShapeDtypeStruct((sz.channels, LANES), BF16),
            jax.ShapeDtypeStruct((2 * sz.piece, ORDER), F32),
        ),
        in_specs=[whole()] * 11,
        out_specs=(whole(),) * 2,
        scratch_shapes=[
            pltpu.VMEM((sz.channels, LANES), BF16),
            pltpu.VMEM((sz.channels, LANES), BF16),
            pltpu.VMEM((max(2 * sz.piece * sz.blocks, sz.channels), LANES), F32),
            pltpu.VMEM((sz.blocks, wide_lines * LANES), BF16),
            pltpu.VMEM((2 * sz.outer, wide_lines * LANES), F32),
            pltpu.VMEM((wide_lines * sz.outer, 2 * LANES), BF16),
            pltpu.VMEM((2 * sz.outer, wide_lines * LANES), BF16),
            pltpu.VMEM((sz.pairs * sz.outer, 2 * LANES), F32),
            pltpu.SemaphoreType.DMA((3,)),
            pltpu.SemaphoreType.DMA((3,)),
        ],
        compiler_params=pltpu.CompilerParams(
            collective_id=cid, has_side_effects=True, vmem_limit_bytes=48 * MIB
        ),
        name="conv_backward",
    )(grad, filt_spec, sig_spec, taps, pos, env, outer_fwd, outer_inv, inner_fwd, inner_inv, twist)


def apart_project(sz, normed, w_in, w_gate, inner_ref, gate_ref):
    for side in range(sz.hid):
        rows = slice(side * sz.padded, (side + 1) * sz.padded)
        part = normed[:, side * sz.half : (side + 1) * sz.half]
        inner_ref[rows, :] = nt(w_in[side], part).astype(BF16)
        gate_ref[rows, :] = nt(w_gate[side], part)


def apart_first_kernel(sz, x_ref, gain_ref, w_in, w_gate, normed_ref, inner_ref, gate_ref):
    normal, _ = normalize(x_ref[...].astype(F32))
    normed = (normal * gain_ref[0:1, :]).astype(BF16)
    normed_ref[...] = normed
    apart_project(sz, normed, w_in, w_gate, inner_ref, gate_ref)


def apart_first(sz, x, gains, w_in, w_gate):
    tokens = x.shape[0]
    return pl.pallas_call(
        functools.partial(apart_first_kernel, sz),
        out_shape=(
            jax.ShapeDtypeStruct((tokens, sz.width), BF16),
            jax.ShapeDtypeStruct((sz.channels, tokens), BF16),
            jax.ShapeDtypeStruct((sz.channels, tokens), F32),
        ),
        in_specs=[whole()] * 4,
        out_specs=(whole(),) * 3,
        compiler_params=pltpu.CompilerParams(vmem_limit_bytes=32 * MIB),
        name="first_projection",
    )(x, gains, w_in, w_gate)


def apart_mix_out(sz, mixed, w_out):
    parts = []
    for side in range(sz.hid):
        rows = slice(side * sz.padded, (side + 1) * sz.padded)
        parts.append(tn(mixed[rows, :], w_out[side]))
    return jnp.concatenate(parts, axis=1)


def apart_ff_specs(sz, layer, tile):
    steps = sz.hidden // sz.hid // tile
    first_half = lambda i: jnp.minimum(i, steps - 1)
    second = lambda i: jnp.maximum(i - steps, 0)
    specs = []
    for place in (first_half, second):
        specs.append(
            pl.BlockSpec((1, 2, sz.width, tile), lambda i, place=place: (layer, 0, 0, place(i)))
        )
        specs.append(pl.BlockSpec((1, sz.width, tile), lambda i, place=place: (layer, 0, place(i))))
    return specs, steps


def apart_forward_kernel(
    sz,
    steps,
    conv_ref,
    inner_ref,
    gate_ref,
    skip_ref,
    x_ref,
    gain_ref,
    next_gain,
    w_out,
    w_in,
    w_gate,
    up_a,
    down_a,
    up_b,
    down_b,
    summed_ref,
    mixed_ref,
    middle_ref,
    normed_two,
    next_x,
    next_normed,
    next_inner,
    next_gate,
):
    index = pl.program_id(0)

    @pl.when(index == 0)
    def _():
        summed = conv_ref[...].astype(F32) + skip_ref[...] * inner_ref[...].astype(F32)
        summed_ref[...] = summed
        mixed_ref[...] = (gate_ref[...] * summed).astype(BF16)
        middle = x_ref[...].astype(F32) + apart_mix_out(sz, mixed_ref, w_out)
        middle_ref[...] = middle
        normal, _ = normalize(middle)
        normed_two[...] = (normal * gain_ref[1:2, :]).astype(BF16)
        next_x[...] = middle

    def accumulate(up_ref, down_ref):
        gate = nn(normed_two[...], up_ref[0, 0])
        up = nn(normed_two[...], up_ref[0, 1])
        value, _ = gelu_parts(gate)
        next_x[...] += nt((value * up).astype(BF16), down_ref[0])

    pl.when(index < steps)(lambda: accumulate(up_a, down_a))
    pl.when(index >= steps)(lambda: accumulate(up_b, down_b))

    @pl.when(index == 2 * steps - 1)
    def _():
        normal, _ = normalize(next_x[...])
        normed = (normal * next_gain[0:1, :]).astype(BF16)
        next_normed[...] = normed
        apart_project(sz, normed, w_in, w_gate, next_inner, next_gate)


def apart_full(shape):
    return pl.BlockSpec(shape, lambda i: (0,) * len(shape))


def apart_forward(sz, layer, conv, inner, gate, skip, x, gains, next_gains, w_out, w_in, w_gate, ff):
    tokens = x.shape[0]
    tile = 512
    specs, steps = apart_ff_specs(sz, layer, tile)
    small = (conv, inner, gate, skip, x, gains, next_gains, w_out, w_in, w_gate)
    outs = (
        ((sz.channels, tokens), F32),
        ((sz.channels, tokens), BF16),
        ((tokens, sz.width), F32),
        ((tokens, sz.width), BF16),
        ((tokens, sz.width), F32),
        ((tokens, sz.width), BF16),
        ((sz.channels, tokens), BF16),
        ((sz.channels, tokens), F32),
    )
    return pl.pallas_call(
        functools.partial(apart_forward_kernel, sz, steps),
        grid=(2 * steps,),
        out_shape=tuple(jax.ShapeDtypeStruct(shape, kind) for shape, kind in outs),
        in_specs=[apart_full(entry.shape) for entry in small] + specs,
        out_specs=tuple(apart_full(shape) for shape, kind in outs),
        compiler_params=pltpu.CompilerParams(
            dimension_semantics=("arbitrary",), vmem_limit_bytes=48 * MIB
        ),
        name="token_forward",
    )(*small, *ff)


def apart_block_grads(sz, tall, flat, target, slot):
    blocks_side = target.shape[1] // sz.hid
    size = sz.half // blocks_side
    rows = sz.padded // blocks_side
    for side in range(sz.hid):
        for block in range(blocks_side):
            begin = side * sz.padded + block * rows
            place = side * sz.half + block * size
            target[slot, side * blocks_side + block] = nn(
                tall[begin : begin + rows, :], flat[:, place : place + size]
            ).astype(target.dtype)


def apart_ff_backward_tile(normed, grad, up_ref, down_ref, total, out_total):
    gate = nn(normed, up_ref[0, 0])
    up = nn(normed, up_ref[0, 1])
    grad_hidden = nn(grad, down_ref[0])
    value, slope = gelu_parts(gate)
    if out_total is not None:
        out_total[...] += nt((value * up).astype(BF16), down_ref[0])
    grad_gate = (slope * up * grad_hidden).astype(BF16)
    grad_up = (value * grad_hidden).astype(BF16)
    total[...] += nt(grad_gate, up_ref[0, 0]) + nt(grad_up, up_ref[0, 1])


def apart_mixer_backward(
    sz, grad_next, middle, total, gain, mixed, summed, gate, w_out, outs
):
    grad_middle, mixer_grad, grad_gate, grad_summed, grad_conv, gain_grad = outs
    normal, inv = normalize(middle)
    back, gain_grad[...] = norm_back(total, normal, inv, gain)
    result = grad_next + back
    grad_middle[...] = result
    grad_o = result.astype(BF16)
    apart_block_grads(sz, mixed, grad_o, mixer_grad, 0)
    for side in range(sz.hid):
        rows = slice(side * sz.padded, (side + 1) * sz.padded)
        grad_mixed = nt(w_out[side], grad_o[:, side * sz.half : (side + 1) * sz.half])
        grad_gate[rows, :] = (grad_mixed * summed[rows, :]).astype(BF16)
        through = grad_mixed * gate[rows, :]
        grad_summed[rows, :] = through
        grad_conv[rows, :] = through.astype(BF16)


def apart_mixer_outs(sz, tokens, blocks):
    size = sz.width // blocks
    return (
        ((tokens, sz.width), F32),
        ((1, blocks, sz.channels // blocks, size), BF16),
        ((sz.channels, tokens), BF16),
        ((sz.channels, tokens), F32),
        ((sz.channels, tokens), BF16),
        ((1, sz.width), F32),
    )


def apart_turn_kernel(
    sz,
    steps,
    conv_ref,
    inner_ref,
    gate_ref,
    skip_ref,
    x_ref,
    gain_ref,
    grad_ref,
    w_out,
    up_a,
    down_a,
    up_b,
    down_b,
    hidden_out,
    normed_two,
    grad_middle,
    mixer_grad,
    grad_gate,
    grad_summed,
    grad_conv,
    gain_grad,
    summed,
    mixed,
    middle,
    out_total,
    total,
):
    index = pl.program_id(0)

    @pl.when(index == 0)
    def _():
        summed[...] = conv_ref[...].astype(F32) + skip_ref[...] * inner_ref[...].astype(F32)
        mixed[...] = (gate_ref[...] * summed[...]).astype(BF16)
        middle[...] = x_ref[...].astype(F32) + apart_mix_out(sz, mixed, w_out)
        normal, _ = normalize(middle[...])
        normed_two[...] = (normal * gain_ref[1:2, :]).astype(BF16)
        out_total[...] = middle[...]
        total[...] = jnp.zeros_like(total)

    def accumulate(up_ref, down_ref):
        apart_ff_backward_tile(normed_two[...], grad_ref[...], up_ref, down_ref, total, out_total)

    pl.when(index < steps)(lambda: accumulate(up_a, down_a))
    pl.when(index >= steps)(lambda: accumulate(up_b, down_b))

    @pl.when(index == 2 * steps - 1)
    def _():
        hidden_out[...] = out_total[...].astype(BF16)
        outs = (grad_middle, mixer_grad, grad_gate, grad_summed, grad_conv, gain_grad)
        apart_mixer_backward(
            sz,
            grad_ref[...].astype(F32),
            middle[...],
            total[...],
            gain_ref[1:2, :],
            mixed,
            summed,
            gate_ref,
            w_out,
            outs,
        )


def apart_turn(sz, layer, blocks, conv, inner, gate, skip, x, gains, grad, w_out, ff):
    tokens = x.shape[0]
    specs, steps = apart_ff_specs(sz, layer, 512)
    small = (conv, inner, gate, skip, x, gains, grad, w_out)
    outs = (((tokens, sz.width), BF16), ((tokens, sz.width), BF16)) + apart_mixer_outs(sz, tokens, blocks)
    return pl.pallas_call(
        functools.partial(apart_turn_kernel, sz, steps),
        grid=(2 * steps,),
        out_shape=tuple(jax.ShapeDtypeStruct(shape, kind) for shape, kind in outs),
        in_specs=[apart_full(entry.shape) for entry in small] + specs,
        out_specs=tuple(apart_full(shape) for shape, kind in outs),
        scratch_shapes=[
            pltpu.VMEM((sz.channels, tokens), F32),
            pltpu.VMEM((sz.channels, tokens), BF16),
            pltpu.VMEM((tokens, sz.width), F32),
            pltpu.VMEM((tokens, sz.width), F32),
            pltpu.VMEM((tokens, sz.width), F32),
        ],
        compiler_params=pltpu.CompilerParams(
            dimension_semantics=("arbitrary",), vmem_limit_bytes=48 * MIB
        ),
        name="token_turn",
    )(*small, *ff)


def apart_input_backward(
    sz, back, through, grad_gate, skip, normed, x, gain, w_in, w_gate, grad_middle, mixer_grad
):
    inner_grad = (skip * through + back.astype(F32)).astype(BF16)
    apart_block_grads(sz, inner_grad, normed, mixer_grad, 0)
    apart_block_grads(sz, grad_gate, normed, mixer_grad, 1)
    parts = []
    for side in range(sz.hid):
        rows = slice(side * sz.padded, (side + 1) * sz.padded)
        parts.append(tn(inner_grad[rows, :], w_in[side]) + tn(grad_gate[rows, :], w_gate[side]))
    normal, inv = normalize(x)
    result, gain_grad = norm_back(jnp.concatenate(parts, axis=1), normal, inv, gain)
    return grad_middle + result, gain_grad


def apart_backward_kernel(
    sz,
    steps,
    back_ref,
    through_ref,
    gate_grad_ref,
    skip_ref,
    normed_ref,
    x_ref,
    gain_ref,
    w_in,
    w_gate,
    grad_middle_ref,
    normed_two,
    middle_ref,
    summed_ref,
    gate_ref,
    mixed_ref,
    low_gain,
    w_out,
    up_a,
    down_a,
    up_b,
    down_b,
    input_grad,
    input_gain,
    grad_ff,
    grad_middle,
    mixer_grad,
    grad_gate,
    grad_summed,
    grad_conv,
    gain_grad,
    grad_next,
    total,
):
    index = pl.program_id(0)

    @pl.when(index == 0)
    def _():
        result, input_gain[...] = apart_input_backward(
            sz,
            back_ref[...],
            through_ref[...],
            gate_grad_ref[...],
            skip_ref[...],
            normed_ref[...],
            x_ref[...],
            gain_ref[0:1, :],
            w_in,
            w_gate,
            grad_middle_ref[...],
            input_grad,
        )
        grad_next[...] = result
        grad_ff[...] = result.astype(BF16)
        total[...] = jnp.zeros_like(total)

    def accumulate(up_ref, down_ref):
        apart_ff_backward_tile(normed_two[...], grad_ff[...], up_ref, down_ref, total, None)

    pl.when(index < steps)(lambda: accumulate(up_a, down_a))
    pl.when(index >= steps)(lambda: accumulate(up_b, down_b))

    @pl.when(index == 2 * steps - 1)
    def _():
        outs = (grad_middle, mixer_grad, grad_gate, grad_summed, grad_conv, gain_grad)
        apart_mixer_backward(
            sz,
            grad_next[...],
            middle_ref[...],
            total[...],
            low_gain[1:2, :],
            mixed_ref,
            summed_ref,
            gate_ref,
            w_out,
            outs,
        )


def apart_input_outs(sz, blocks):
    size = sz.width // blocks
    return (((2, blocks, sz.channels // blocks, size), BF16), ((1, sz.width), F32))


def apart_backward(
    sz,
    layer,
    blocks,
    back,
    through,
    gate_grad,
    skip,
    normed,
    x,
    gains,
    w_in,
    w_gate,
    grad_middle,
    normed_two,
    middle,
    summed,
    gate,
    mixed,
    low_gains,
    w_out,
    ff,
):
    tokens = x.shape[0]
    specs, steps = apart_ff_specs(sz, layer, 512)
    small = (
        back,
        through,
        gate_grad,
        skip,
        normed,
        x,
        gains,
        w_in,
        w_gate,
        grad_middle,
        normed_two,
        middle,
        summed,
        gate,
        mixed,
        low_gains,
        w_out,
    )
    outs = (
        apart_input_outs(sz, blocks) + (((tokens, sz.width), BF16),) + apart_mixer_outs(sz, tokens, blocks)
    )
    return pl.pallas_call(
        functools.partial(apart_backward_kernel, sz, steps),
        grid=(2 * steps,),
        out_shape=tuple(jax.ShapeDtypeStruct(shape, kind) for shape, kind in outs),
        in_specs=[apart_full(entry.shape) for entry in small] + specs,
        out_specs=tuple(apart_full(shape) for shape, kind in outs),
        scratch_shapes=[
            pltpu.VMEM((tokens, sz.width), F32),
            pltpu.VMEM((tokens, sz.width), F32),
        ],
        compiler_params=pltpu.CompilerParams(
            dimension_semantics=("arbitrary",), vmem_limit_bytes=48 * MIB
        ),
        name="token_backward",
    )(*small, *ff)


def apart_last_kernel(
    sz,
    back_ref,
    through_ref,
    gate_grad_ref,
    skip_ref,
    normed_ref,
    x_ref,
    gain_ref,
    w_in,
    w_gate,
    grad_middle_ref,
    input_grad,
    input_gain,
    grad_in,
):
    grad_in[...], input_gain[...] = apart_input_backward(
        sz,
        back_ref[...],
        through_ref[...],
        gate_grad_ref[...],
        skip_ref[...],
        normed_ref[...],
        x_ref[...].astype(F32),
        gain_ref[0:1, :],
        w_in,
        w_gate,
        grad_middle_ref[...],
        input_grad,
    )


def apart_last(sz, blocks, *args):
    tokens = args[5].shape[0]
    outs = apart_input_outs(sz, blocks) + (((tokens, sz.width), F32),)
    return pl.pallas_call(
        functools.partial(apart_last_kernel, sz),
        out_shape=tuple(jax.ShapeDtypeStruct(shape, kind) for shape, kind in outs),
        in_specs=[whole()] * len(args),
        out_specs=(whole(),) * len(outs),
        compiler_params=pltpu.CompilerParams(vmem_limit_bytes=32 * MIB),
        name="last_projection",
    )(*args)


def apart_ff_grads_kernel(normed_ref, grad_ref, up_ref, down_ref, out_ref, hidden, grad_gate, grad_up):
    tokens = normed_ref.shape[0]
    chunk = 256
    for start in range(0, tokens, chunk):
        rows = pl.ds(start, chunk)
        normed = normed_ref[rows, :]
        gate = nn(normed, up_ref[0])
        up = nn(normed, up_ref[1])
        through = nn(grad_ref[rows, :], down_ref[...])
        value, slope = gelu_parts(gate)
        hidden[rows, :] = (value * up).astype(BF16)
        grad_gate[rows, :] = (slope * up * through).astype(BF16)
        grad_up[rows, :] = (value * through).astype(BF16)
    out_ref[0] = tn(normed_ref[...], grad_gate[...]).astype(BF16)
    out_ref[1] = tn(normed_ref[...], grad_up[...]).astype(BF16)
    out_ref[2] = tn(grad_ref[...], hidden[...]).astype(BF16)


def apart_ff_grads(normed, grad, up, down):
    tokens, width = normed.shape
    units = down.shape[1]
    return pl.pallas_call(
        apart_ff_grads_kernel,
        out_shape=jax.ShapeDtypeStruct((3, width, units), BF16),
        in_specs=[whole()] * 4,
        out_specs=whole(),
        scratch_shapes=[pltpu.VMEM((tokens, units), BF16)] * 3,
        compiler_params=pltpu.CompilerParams(vmem_limit_bytes=48 * MIB),
        name="ff_weight_grads",
    )(normed, grad, up, down)


def apart_row_exchange_kernel(rows, parts, *refs):
    sources, targets, sems = refs[:parts], refs[parts : 2 * parts], refs[2 * parts]
    row = lax.axis_index("rows")
    col = lax.axis_index("hid")
    barrier = pltpu.get_barrier_semaphore()

    def greet(step, carry):
        peer = lax.rem(row + step, rows)
        pl.semaphore_signal(barrier, inc=1, device_id=(peer, col), device_id_type=MESH)
        return carry

    lax.fori_loop(1, rows, greet, 0)
    for part in range(parts):
        pltpu.make_async_copy(
            sources[part].at[row], targets[part].at[row], sems.at[part, 2]
        ).start()
    pl.semaphore_wait(barrier, rows - 1)

    def post(step, carry):
        peer = lax.rem(row + step, rows)
        for part in range(parts):
            pltpu.make_async_remote_copy(
                src_ref=sources[part].at[peer],
                dst_ref=targets[part].at[row],
                send_sem=sems.at[part, 0],
                recv_sem=sems.at[part, 1],
                device_id=(peer, col),
                device_id_type=MESH,
            ).start()
        return carry

    lax.fori_loop(1, rows, post, 0)
    for part in range(parts):
        pltpu.make_async_copy(
            sources[part].at[0], targets[part].at[0], sems.at[part, 2]
        ).wait()
        span = pl.ds(0, rows - 1)
        pltpu.make_async_remote_copy(
            src_ref=sources[part].at[span],
            dst_ref=targets[part].at[span],
            send_sem=sems.at[part, 0],
            recv_sem=sems.at[part, 1],
            device_id=(lax.rem(row + 1, rows), col),
            device_id_type=MESH,
        ).wait()


def apart_row_exchange(arrays, rows, cid):
    parts = len(arrays)
    return pl.pallas_call(
        functools.partial(apart_row_exchange_kernel, rows, parts),
        out_shape=tuple(jax.ShapeDtypeStruct(entry.shape, entry.dtype) for entry in arrays),
        in_specs=[pl.BlockSpec(memory_space=pl.ANY)] * parts,
        out_specs=(pl.BlockSpec(memory_space=pl.ANY),) * parts,
        scratch_shapes=[pltpu.SemaphoreType.DMA((parts, 3))],
        compiler_params=pltpu.CompilerParams(collective_id=cid, has_side_effects=True),
        name="row_exchange",
    )(*arrays)


def apart_swap(value):
    return lax.ppermute(value, "hid", [(0, 1), (1, 0)])


def apart_both_halves(own, axis):
    other = apart_swap(own)
    low = lax.axis_index("hid") == 0
    return jnp.concatenate([jnp.where(low, own, other), jnp.where(low, other, own)], axis=axis)


def apart_own_tokens(part):
    tokens = part.shape[0] // 2
    side = lax.axis_index("hid")
    keep = lax.dynamic_slice_in_dim(part, side * tokens, tokens, 0)
    other = apart_swap(lax.dynamic_slice_in_dim(part, (1 - side) * tokens, tokens, 0))
    low = side == 0
    return jnp.concatenate([jnp.where(low, keep, other), jnp.where(low, other, keep)], axis=1)


def apart_own_features(part):
    half = part.shape[1] // 2
    side = lax.axis_index("hid")
    keep = lax.dynamic_slice_in_dim(part, side * half, half, 1)
    other = apart_swap(lax.dynamic_slice_in_dim(part, (1 - side) * half, half, 1))
    low = side == 0
    return jnp.concatenate([jnp.where(low, keep, other), jnp.where(low, other, keep)], axis=0)


def apart_padded_mixer(sz, mixer):
    layers, kinds, blocks, size, _ = mixer.shape
    chan_first = jnp.concatenate([jnp.swapaxes(mixer[:, :2], 3, 4), mixer[:, 2:]], axis=1)
    grouped = chan_first.reshape(layers, kinds, blocks, size // sz.chans, sz.chans, size)
    grouped = jnp.pad(grouped, ((0, 0),) * 4 + ((0, sz.piece - sz.chans), (0, 0)))
    grouped = grouped.reshape(layers, kinds, blocks, -1, size)
    parts = [
        jnp.pad(grouped[:, :, block], ((0, 0),) * 3 + ((block * size, (blocks - 1 - block) * size),))
        for block in range(blocks)
    ]
    return jnp.concatenate(parts, axis=2)


def apart_padded_channels(sz, values):
    lead = values.shape[:-1]
    grouped = values.reshape(lead + (sz.rows, sz.chans))
    grouped = jnp.pad(grouped, ((0, 0),) * (len(lead) + 1) + ((0, sz.piece - sz.chans),))
    return grouped.reshape(lead + (sz.padded,))


def apart_envelopes(sz):
    row = lax.axis_index("rows")
    first_chan = lax.axis_index("hid") * sz.half + row * sz.chans
    channels = first_chan + jnp.arange(sz.piece, dtype=jnp.int32)
    fraction = (channels * 37 % sz.width).astype(F32) / (sz.width - 1)
    start_log = math.log(1.0 / 40.0)
    rate = jnp.exp(start_log + (math.log(1.5 / sz.length) - start_log) * fraction)
    steps = jnp.arange(sz.length, dtype=jnp.int32).astype(F32)
    decay = jnp.exp(-steps[None, :] * rate[:, None])
    shape = decay * lax.rsqrt(2.0 * jnp.sum(decay * decay, axis=1, keepdims=True))
    return jnp.concatenate([shape, shape * (steps > 0)[None, :]], axis=0)


def apart_plane_gather(value):
    size = lax.axis_size("rows")
    for bit in (1, 2):
        other = lax.ppermute(value, "rows", [(r, r ^ bit) for r in range(size)])
        value = jnp.concatenate([value, other], axis=0)
    return jnp.concatenate([value, apart_swap(value)], axis=0)


def apart_on_device(hidden_in, d_out, gains, mixer, skip, filters, gate_up, down):
    layers = gate_up.shape[0]
    rows = lax.axis_size("rows")
    hid = lax.axis_size("hid")
    width = gate_up.shape[2]
    hidden = gate_up.shape[3] * hid
    blocks = mixer.shape[2] * hid
    block_size = mixer.shape[3]
    sz = apart_Sizes(rows, hid, width, hidden, hidden_in.shape[0] * rows)
    row = lax.axis_index("rows")

    x = apart_own_tokens(hidden_in)
    gains_all = apart_both_halves(gains, 2)
    skip_all = apart_both_halves(apart_padded_channels(sz, skip), 1)[:, :, None]
    weights = apart_both_halves(apart_padded_mixer(sz, mixer)[:, :, None], 2)
    gate_up_b = apart_swap(gate_up)
    down_b = apart_swap(down)
    ff = (gate_up, down, gate_up_b, down_b)
    grad_out = apart_own_tokens(d_out)

    tables = dft_tables(sz.length)
    pos = jnp.asarray(position_table(sz.length).T, F32).astype(BF16)
    env = apart_envelopes(sz)
    taps = lax.dynamic_slice_in_dim(filters, row * sz.chans, sz.chans, 3)
    taps = jnp.pad(taps, ((0, 0),) * 3 + ((0, sz.piece - sz.chans),))
    taps = jnp.swapaxes(taps, 2, 3).reshape(layers, 2 * sz.piece, ORDER).astype(BF16)

    normed, inner, gate = apart_first(sz, x, gains_all[0], weights[0, 0], weights[0, 1])
    stored = []
    for layer in range(layers):
        conv, filt_spec, sig_spec = apart_conv_forward(sz, inner, taps[layer], pos, env, tables, 0)
        stored.append(dict(x=x, normed=normed, inner=inner, gate=gate, f=filt_spec, s=sig_spec))
        if layer < layers - 1:
            summed, mixed, middle, normed_two, x, normed, next_inner, next_gate = apart_forward(
                sz,
                layer,
                conv,
                inner,
                gate,
                skip_all[layer],
                x,
                gains_all[layer],
                gains_all[layer + 1],
                weights[layer, 2],
                weights[layer + 1, 0],
                weights[layer + 1, 1],
                ff,
            )
            stored[-1].update(summed=summed, mixed=mixed, middle=middle, normed_two=normed_two)
            inner, gate = next_inner, next_gate

    top = layers - 1
    hidden_out, normed_two, *rest = apart_turn(
        sz,
        top,
        blocks,
        conv,
        inner,
        gate,
        skip_all[top],
        x,
        gains_all[top],
        grad_out,
        weights[top, 2],
        ff,
    )
    stored[top].update(normed_two=normed_two)
    grad_ff = grad_out
    units = sz.hidden // hid // 4
    unit_start = lax.rem(row, 4) * units
    ff_parts, mixer_parts, gain_parts, skip_parts, taps_parts = [], [], [], [], []
    for layer in reversed(range(layers)):
        kept = stored[layer]
        grad_middle, out_grad, grad_gate, grad_summed, grad_conv, gain_two = rest
        ff_parts.insert(
            0,
            apart_ff_grads(
                apart_plane_gather(kept["normed_two"]),
                apart_plane_gather(grad_ff),
                lax.dynamic_slice_in_dim(gate_up[layer], unit_start, units, 2),
                lax.dynamic_slice_in_dim(down[layer], unit_start, units, 1),
            ),
        )
        back, taps_grad = apart_conv_backward(
            sz, grad_conv, kept["f"], kept["s"], taps[layer], pos, env, tables, 1
        )
        skip_parts.insert(0, jnp.sum(grad_summed * kept["inner"].astype(F32), axis=1))
        taps_parts.insert(0, taps_grad)
        common = (
            back,
            grad_summed,
            grad_gate,
            skip_all[layer],
            kept["normed"],
            kept["x"],
            gains_all[layer],
            weights[layer, 0],
            weights[layer, 1],
            grad_middle,
        )
        if layer > 0:
            low = stored[layer - 1]
            in_grad, gain_one, grad_ff, *rest = apart_backward(
                sz,
                layer - 1,
                blocks,
                *common,
                low["normed_two"],
                low["middle"],
                low["summed"],
                low["gate"],
                low["mixed"],
                gains_all[layer - 1],
                weights[layer - 1, 2],
                ff,
            )
        else:
            in_grad, gain_one, grad_in = apart_last(sz, blocks, *common)
        mixer_parts.insert(0, jnp.concatenate([in_grad, out_grad], axis=0))
        gain_parts.insert(0, jnp.concatenate([gain_one, gain_two], axis=0))

    piece_rows = width // rows
    padded_rows = round_up(piece_rows, 16)
    pieces = jnp.stack(ff_parts).reshape(layers, 3, rows, piece_rows, units)
    pieces = jnp.pad(pieces, ((0, 0),) * 3 + ((0, padded_rows - piece_rows), (0, 0)))
    pieces = jnp.moveaxis(pieces, 2, 0)
    (arrived,) = apart_row_exchange((pieces,), rows, 2)
    arrived = arrived.reshape(rows // 4, 4, layers, 3, padded_rows, units)[:, :, :, :, :piece_rows]
    summed_ff = jnp.sum(arrived.astype(F32), axis=0)
    summed_ff = jnp.moveaxis(summed_ff, 0, 3).reshape(layers, 3, piece_rows, 4 * units)

    mixers = jnp.stack(mixer_parts).reshape(layers, 3, blocks, -1, sz.piece, block_size)
    mixers = mixers[:, :, :, :, : sz.chans].reshape(layers, 3, blocks, block_size, block_size)
    small = jnp.concatenate(
        [jnp.stack(gain_parts).reshape(-1), jnp.stack(skip_parts).reshape(-1)]
    )
    mixers, small = lax.psum((mixers.astype(F32), small), ("rows", "hid"))
    side = lax.axis_index("hid")
    mixers = lax.dynamic_slice_in_dim(mixers, side * (blocks // hid), blocks // hid, 2)
    mixers = jnp.concatenate([jnp.swapaxes(mixers[:, :2], 3, 4), mixers[:, 2:]], axis=1)
    gain_size = layers * 2 * width
    gain_out = lax.dynamic_slice_in_dim(
        small[:gain_size].reshape(layers, 2, width), side * sz.half, sz.half, 2
    )
    skip_out = small[gain_size:].reshape(layers, hid, rows, sz.piece)[..., : sz.chans]
    skip_out = lax.dynamic_index_in_dim(skip_out, side, 1, False).reshape(layers, sz.half)
    taps_out = jnp.stack(taps_parts).reshape(layers, 2, sz.piece, ORDER)[:, :, : sz.chans]
    taps_out = lax.all_gather(taps_out, "rows", axis=2, tiled=True)
    return (
        apart_own_features(hidden_out),
        apart_own_features(grad_in),
        gain_out,
        mixers,
        skip_out,
        jnp.swapaxes(taps_out, 2, 3),
        summed_ff[:, :2],
        summed_ff[:, 2],
    )


def vmem_bytes(sz):
    total = 0
    for spec in layout(sz)[1]:
        size = jnp.dtype(spec.dtype).itemsize
        *lead, rows, lanes = spec.shape
        total += math.prod(lead) * round_up(rows, 32 // size) * round_up(lanes, LANES) * size
    return total


def on_device(*arrays):
    sz = Sizes.of(*arrays)
    if vmem_bytes(sz) <= 60 * MIB:
        return together(sz, *arrays)
    return apart_on_device(*arrays)


def solution(mesh):
    placed = (
        P("rows", "hid"),
        P("rows", "hid"),
        P(None, None, "hid"),
        P(None, None, "hid", None, None),
        P(None, "hid"),
        P(None, None, None, "hid"),
        P(None, None, None, "hid"),
        P(None, None, "hid"),
    )
    return jax.shard_map(
        on_device,
        mesh=mesh,
        in_specs=placed,
        out_specs=(
            P("rows", "hid"),
            P("rows", "hid"),
            P(None, None, "hid"),
            P(None, None, "hid", None, None),
            P(None, "hid"),
            P(None, None, None, "hid"),
            P(None, None, "rows", "hid"),
            P(None, "rows", "hid"),
        ),
        check_vma=False,
    )
```

```python
import functools
import math

import jax
import jax.numpy as jnp
import numpy as np
from jax import lax
from jax.experimental import pallas as pl
from jax.experimental.pallas import tpu as pltpu
from jax.sharding import PartitionSpec as P

ORDER = 128
SEQ_LEN = 8192
LANES = 128
NORM_EPS = 1e-05
DECAY = 0.02
MESH = pl.DeviceIdType.MESH
BF16 = jnp.bfloat16
F32 = jnp.float32
MIB = 2**20
GELU_C = math.sqrt(2.0 / math.pi)


def round_up(value, step):
    return -(-value // step) * step


def whole():
    return pl.BlockSpec(memory_space=pltpu.VMEM)


def nn(a, b):
    return lax.dot_general(a, b, (((1,), (0,)), ((), ())), preferred_element_type=F32)


def nt(a, b):
    return lax.dot_general(a, b, (((1,), (1,)), ((), ())), preferred_element_type=F32)


def tn(a, b):
    return lax.dot_general(a, b, (((0,), (0,)), ((), ())), preferred_element_type=F32)


def position_table(length):
    half_order = ORDER // 2
    index_list = np.arange(half_order)
    multiple = 1 + index_list * index_list * (length // 4) // (half_order * half_order)
    phase = (np.arange(length)[:, None] * multiple[None, :] % length) * (2.0 * math.pi / length)
    return np.concatenate([np.sin(phase), np.cos(phase)], axis=1)


def dft_tables(length):
    blocks = length // LANES
    size = 2 * length
    outer = 2 * blocks
    k = np.arange(outer)
    n = np.arange(blocks)
    m = np.arange(LANES)
    angle = 2.0 * math.pi * (np.outer(k, n) % outer) / outer
    outer_fwd = np.concatenate([np.cos(angle), -np.sin(angle)], axis=0)
    outer_inv = np.concatenate([np.cos(angle), -np.sin(angle)], axis=0).T / size
    angle = 2.0 * math.pi * (np.outer(m, m) % LANES) / LANES
    cos, sin = np.cos(angle), np.sin(angle)
    inner_fwd = np.block([[cos, -sin], [sin, cos]])
    inner_inv = np.block([[cos, sin], [-sin, cos]])
    angle = 2.0 * math.pi * np.outer(k, m) / size
    twist = np.concatenate([np.cos(angle), np.sin(angle)], axis=1)
    half = lambda table: jnp.asarray(table, F32).astype(BF16)
    return (half(outer_fwd), half(outer_inv), half(inner_fwd), half(inner_inv), jnp.asarray(twist, F32))


def normalize(values):
    mean = jnp.mean(values, axis=1, keepdims=True)
    square = jnp.mean(values * values, axis=1, keepdims=True)
    inv = lax.rsqrt(square - mean * mean + NORM_EPS)
    return (values - mean) * inv, inv


def norm_back(grad, normal, inv, gain):
    scaled = grad * gain
    mean = jnp.mean(scaled, axis=1, keepdims=True)
    cross = jnp.mean(scaled * normal, axis=1, keepdims=True)
    return inv * (scaled - mean - normal * cross), jnp.sum(grad * normal, axis=0, keepdims=True)


def gelu_parts(gate):
    square = gate * gate
    tanh = jnp.tanh(GELU_C * gate * (1.0 + 0.044715 * square))
    half = 0.5 * (1.0 + tanh)
    value = gate * half
    slope = half + 0.5 * gate * (1.0 - tanh * tanh) * (GELU_C * (1.0 + 3.0 * 0.044715 * square))
    return value, slope


class Sizes:
    def __init__(self, rows, hid, tokens, width, hidden, layers, blocks):
        self.rows, self.hid, self.width, self.layers = rows, hid, width, layers
        self.count = rows * hid
        self.own = tokens // self.count
        self.half = width // hid
        self.units = hidden // hid
        self.blocks = blocks
        self.size = width // blocks
        self.side_blocks = blocks // hid
        self.couple = 2 * width // self.count
        self.big = round_up(self.couple // 2, 16)
        self.small = self.couple - self.big
        self.length = min(SEQ_LEN, tokens)
        self.seqs = tokens // self.length
        self.steps = self.length // LANES
        self.outer = 2 * self.steps
        self.pairs = self.seqs * self.big
        self.group = 4
        self.peers = rows // self.group
        self.part = self.units // self.group
        self.depth = width // rows
        self.deep = round_up(self.depth, 16)
        self.deeps = tuple(
            round_up(-(-rows_needed // rows), 16)
            for rows_needed in (3 * (layers - 1) * self.size, 2 * self.size + 16)
        )
        self.late_rows = round_up(-(-(self.size + 16) // rows), 16)
        self.taps_rows = round_up(2 * self.big + 1, 16)


    @classmethod
    def of(cls, hidden_in, d_out, gains, mixer, skip, filters, gate_up, down):
        rows, hid = lax.axis_size("rows"), lax.axis_size("hid")
        layers, _, width, units = gate_up.shape
        tokens = hidden_in.shape[0] * rows
        return cls(rows, hid, tokens, width, units * hid, layers, mixer.shape[2] * hid)


    def fits(self):
        whole_tiles = self.small > 0 and self.small % 16 == 0 and self.rows % 8 == 0
        whole_tiles = whole_tiles and self.own == LANES and self.depth % 16 == 0
        whole_tiles = whole_tiles and self.peers == 4 and self.layers == 2
        whole_tiles = whole_tiles and all(self.size % deep == 0 for deep in self.deeps)
        total = 0
        for spec in layout(self)[1]:
            size = jnp.dtype(spec.dtype).itemsize
            *lead, rows, lanes = spec.shape
            total += math.prod(lead) * round_up(rows, 32 // size) * round_up(lanes, LANES) * size
        return whole_tiles and total <= 60 * MIB


class Links:
    def __init__(self, sz, sems, local_sems):
        self.sz, self.sems, self.local_sems = sz, sems, local_sems
        self.used = 0
        self.used_local = 0
        self.row = lax.axis_index("rows")
        self.col = lax.axis_index("hid")
        self.plane = lax.rem(self.row, sz.peers)
        self.line = self.row // sz.peers

    def pair(self):
        first = self.used
        self.used += 2
        return self.sems.at[first], self.sems.at[first + 1]

    def copy(self, source, target, pair, row, col):
        return pltpu.make_async_remote_copy(
            src_ref=source,
            dst_ref=target,
            send_sem=pair[0],
            recv_sem=pair[1],
            device_id=(row, col),
            device_id_type=MESH,
        )

    def sibling(self, source, target):
        copy = self.copy(source, target, self.pair(), self.row, self.sz.hid - 1 - self.col)
        copy.start()
        return copy

    def load(self, source, target):
        copy = pltpu.make_async_copy(source, target, self.local_sems.at[self.used_local])
        self.used_local += 1
        copy.start()
        return copy

    def groups(self, count, me, row_of, source_of, target):
        pair = self.pair()

        def post(step, carry):
            member = lax.rem(me + step, count)
            self.copy(source_of(member), target, pair, row_of(member), self.col).start()
            return carry

        lax.fori_loop(1, count, post, 0)
        return pair

    def in_plane(self, source_of, target):
        row_of = lambda member: self.line * self.sz.peers + member
        return self.groups(self.sz.peers, self.plane, row_of, source_of, target)

    def in_line(self, source_of, target):
        row_of = lambda member: member * self.sz.peers + self.plane
        return self.groups(self.sz.group, self.line, row_of, source_of, target)

    def in_rows(self, source_of, target):
        return self.groups(self.sz.rows, self.row, lambda member: member, source_of, target)

    def wait(self, pair, span):
        self.copy(span, span, pair, self.row, self.sz.hid - 1 - self.col).wait()


class Plane:
    def __init__(self, links):
        self.links = links
        self.me = links.plane
        along_x = self.me + 1 - 2 * lax.rem(self.me, 2)
        along_y = self.me + 2 - 4 * (self.me // 2)
        self.near = (along_x, along_y)
        self.far = (along_y, along_x)
        self.across = 3 - self.me

    def send(self, copies):
        links = self.links
        pair = links.pair()
        for source, target, member in copies:
            row = links.line * links.sz.peers + member
            links.copy(source, target, pair, row, links.col).start()
        return pair


class PlaneSum(Plane):
    def __init__(self, links, source, first, give, second):
        super().__init__(links)
        self.source, self.first, self.give, self.second = source, first, give, second

    def start(self):
        copies = []
        for half in range(2):
            for which, member in enumerate((self.near[half], self.across)):
                target = self.first.at[half, which]
                copies.append((self.source(member, half), target, self.near[half]))
        self.pair = self.send(copies)

    def middle(self):
        self.links.wait(self.pair, self.first)
        copies = []
        for half in range(2):
            theirs = self.source(self.far[half], half)[...].astype(F32)
            self.give[half] = (theirs + self.first[half, 1].astype(F32)).astype(BF16)
            mine = self.source(self.me, half)[...].astype(F32)
            self.first[half, 0] = (mine + self.first[half, 0].astype(F32)).astype(BF16)
            copies.append((self.give.at[half], self.second.at[half], self.far[half]))
        self.pair = self.send(copies)

    def end(self):
        self.links.wait(self.pair, self.second)

    def sums(self):
        for half in range(2):
            total = self.first[half, 0].astype(F32) + self.second[half].astype(F32)
            self.second[half] = total.astype(BF16)
        count = self.links.sz.group // 2
        return lambda member: self.second.at[member // count, lax.rem(member, count)]


class PlaneSpread(Plane):
    def __init__(self, links, place, span):
        super().__init__(links)
        self.place, self.span = place, span

    def start(self):
        copies = []
        for half in range(2):
            here = self.place(self.me, half)
            copies.append((here, here, self.near[half]))
        self.pair = self.send(copies)

    def middle(self):
        self.links.wait(self.pair, self.span(1))
        copies = []
        for half in range(2):
            for member in (self.me, self.near[half]):
                here = self.place(member, half)
                copies.append((here, here, self.far[half]))
        self.pair = self.send(copies)

    def end(self):
        self.links.wait(self.pair, self.span(2))


LOAD_BUFFERS = ("mine", "give", "got", "first", "second_give", "second", "line_in", "out")


class Payload:
    def __init__(self, sz, b, links, index, output):
        self.sz, self.links, self.output = sz, links, output
        self.deep = sz.deeps[index]
        for name in LOAD_BUFFERS:
            setattr(self, name, getattr(b, "load_" + name)[index])
        half = lambda which: pl.ds(which * (sz.group // 2), sz.group // 2)
        self.plane = PlaneSum(
            links,
            lambda member, which: self.mine.at[member, half(which)],
            self.first,
            self.second_give,
            self.second,
        )
        self.spread = PlaneSpread(
            links,
            lambda member, which: self.got.at[member, half(which)],
            lambda count: self.got.at[pl.ds(0, count)],
        )
        self.half = half

    def matrix(self, place, values):
        sz = self.sz
        low = lax.axis_index("hid") == 0
        left = jnp.concatenate(values[: sz.side_blocks], axis=1)
        right = jnp.concatenate(values[sz.side_blocks :], axis=1)
        mine = jnp.where(low, left, right).astype(BF16)
        give = jnp.where(low, right, left).astype(BF16)
        count = sz.size // self.deep
        for part in range(count):
            index = place * count + part
            rows = slice(part * self.deep, (part + 1) * self.deep)
            self.mine[index // sz.group, index % sz.group] = mine[rows, :]
            self.give[index // sz.group, index % sz.group] = give[rows, :]

    def rows16(self, place, mine, give):
        index = place * (self.sz.size // self.deep)
        self.mine[index // self.sz.group, index % self.sz.group, 0:16] = mine.astype(BF16)
        self.give[index // self.sz.group, index % self.sz.group, 0:16] = give.astype(BF16)

    def to_partner(self):
        self.copy = self.links.sibling(self.give, self.got)

    def to_plane(self):
        done(self.copy)
        self.mine[...] = (self.mine[...].astype(F32) + self.got[...].astype(F32)).astype(BF16)
        self.plane.start()

    def middle(self):
        self.plane.middle()

    def to_line(self):
        self.plane.end()
        self.sums = self.plane.sums()
        links = self.links
        self.pair = links.in_line(self.sums, self.line_in.at[links.line])

    def back_line(self):
        links, sz = self.links, self.sz
        links.wait(self.pair, self.line_in.at[pl.ds(0, sz.group - 1)])
        self.line_in[links.line] = self.sums(links.line)[...]
        total = self.line_in[0].astype(F32)
        for member in range(1, sz.group):
            total += self.line_in[member].astype(F32)
        self.out[...] = total.astype(BF16)
        self.got[links.plane, links.line] = self.out[...]
        self.pair = links.in_line(lambda member: self.out, self.got.at[links.plane, links.line])

    def back_plane(self):
        self.links.wait(self.pair, self.got.at[0, pl.ds(0, self.sz.group - 1)])
        self.spread.start()

    def finish(self):
        self.spread.end()
        return self.links.load(self.got, self.output)


def greet_all(sz):
    me = lax.axis_index("rows") * sz.hid + lax.axis_index("hid")
    barrier = pltpu.get_barrier_semaphore()

    def greet(step, carry):
        peer = lax.rem(me + step, sz.count)
        pl.semaphore_signal(
            barrier,
            inc=1,
            device_id=(peer // sz.hid, lax.rem(peer, sz.hid)),
            device_id_type=MESH,
        )
        return carry

    lax.fori_loop(1, sz.count, greet, 0)
    return barrier


class Exchange:
    def __init__(self, sz, links):
        self.sz, self.links = sz, links
        self.odd = lax.rem(links.row, 2)
        self.token = links.row * sz.hid + links.col

    def channels(self, row, col, size):
        sz = self.sz
        start = col * sz.half + (row // 2) * sz.couple + lax.rem(row, 2) * sz.big
        return pl.ds(pl.multiple_of(start, 16), size)

    def block(self, token, size):
        return pl.ds(pl.multiple_of(token * self.sz.big, 16), size)

    def far_first(self):
        line = self.links.line
        odd = lax.rem(line, 2)
        across = 2 * (1 - line // 2)
        return across + odd, across + 1 - odd, line + 1 - 2 * odd, line

    def by_size(self, body):
        pl.when(self.odd == 0)(lambda: body(self.sz.big))
        pl.when(self.odd == 1)(lambda: body(self.sz.small))

    def local(self):
        local = self.links.local_sems.at[self.links.used_local]
        self.links.used_local += 1
        return local

    def to_owners(self, source, target):
        sz, links = self.sz, self.links
        pair, local = links.pair(), self.local()

        def own(size):
            pltpu.make_async_copy(
                source.at[self.channels(links.row, links.col, size)],
                target.at[self.block(self.token, size)],
                local,
            ).start()

        self.by_size(own)
        half = sz.peers * sz.hid // 2
        first = (links.plane // 2) * sz.hid + links.col

        for turn, line in enumerate(self.far_first()):

            def post(step, carry):
                index = lax.rem(first + step, half)
                col = lax.rem(index, sz.hid)
                for odd, size in ((0, sz.big), (1, sz.small)):
                    row = line * sz.peers + 2 * (index // sz.hid) + odd

                    def send():
                        links.copy(
                            source.at[self.channels(row, col, size)],
                            target.at[self.block(self.token, size)],
                            pair,
                            row,
                            col,
                        ).start()

                    if turn < sz.group - 1:
                        send()
                    else:
                        pl.when((step > 0) | (self.odd != odd))(send)
                return carry

            lax.fori_loop(0, half, post, 0)
        return pair, local

    def to_tokens(self, source, target):
        sz, links = self.sz, self.links
        pair, local = links.pair(), self.local()

        def send(size):
            mine = target.at[self.channels(links.row, links.col, size)]
            pltpu.make_async_copy(source.at[self.block(self.token, size)], mine, local).start()

            devices = sz.peers * sz.hid
            first = links.plane * sz.hid + links.col

            for turn, line in enumerate(self.far_first()):

                def post(step, carry):
                    index = lax.rem(first + step, devices)
                    row, col = line * sz.peers + index // sz.hid, lax.rem(index, sz.hid)
                    peer = row * sz.hid + col
                    links.copy(source.at[self.block(peer, size)], mine, pair, row, col).start()
                    return carry

                lax.fori_loop(0 if turn < sz.group - 1 else 1, devices, post, 0)

        self.by_size(send)
        return pair, local

    def wait(self, tokens, by_tokens, by_owners, sent_by_tokens):
        sz, links = self.sz, self.links
        pair, local = tokens

        def wait(size):
            first = by_owners.at[pl.ds(0, size)]
            pltpu.make_async_copy(first, first, local).wait()
            all_tokens = by_owners.at[pl.ds(0, (sz.count - 1) * size)]
            all_channels = by_tokens.at[pl.ds(0, sz.width - size)]
            sent, came = all_tokens, all_channels
            if sent_by_tokens:
                sent, came = came, sent
            links.copy(came, came, pair, links.row, 1 - links.col).wait_recv()
            links.copy(sent, sent, pair, links.row, 1 - links.col).wait_send()

        self.by_size(wait)

    def owners_wait(self, tokens, source, target):
        self.wait(tokens, source, target, True)

    def tokens_wait(self, tokens, source, target):
        self.wait(tokens, target, source, False)


def spread_in(source, wide, lines, stride, steps):
    for place, line in enumerate(lines):
        wide[:, place * LANES : (place + 1) * LANES] = source[
            pl.ds(line, steps, stride=stride), :
        ].astype(wide.dtype)


CHUNK = 8


def dft(b, lines, outer, target):
    cos = b.twist[:, :LANES]
    sin = b.twist[:, LANES:]
    for start in range(0, lines, CHUNK):
        here = min(CHUNK, lines - start)
        lanes = slice(start * LANES, (start + here) * LANES)
        b.mid[:, : here * LANES] = nn(b.outer_fwd[...], b.wide[:, lanes])
        for line in range(here):
            lanes = slice(line * LANES, (line + 1) * LANES)
            real = b.mid[0:outer, lanes]
            imag = b.mid[outer : 2 * outer, lanes]
            rows = slice((start + line) * outer, (start + line + 1) * outer)
            b.flat[rows, 0:LANES] = (real * cos + imag * sin).astype(BF16)
            b.flat[rows, LANES:] = (imag * cos - real * sin).astype(BF16)
        rows = slice(start * outer, (start + here) * outer)
        target[rows, :] = nn(b.flat[rows, :], b.inner_fwd[...])


def inverse_dft(b, lines, outer, put):
    cos = b.twist[:, :LANES]
    sin = b.twist[:, LANES:]
    for start in range(0, lines, CHUNK):
        here = min(CHUNK, lines - start)
        for line in range(here):
            rows = slice((start + line) * outer, (start + line + 1) * outer)
            lanes = slice(line * LANES, (line + 1) * LANES)
            part = nn(b.flat[rows, :], b.inner_inv[...])
            real = part[:, :LANES]
            imag = part[:, LANES:]
            b.mid_half[0:outer, lanes] = (real * cos - imag * sin).astype(BF16)
            b.mid_half[outer : 2 * outer, lanes] = (imag * cos + real * sin).astype(BF16)
        value = nn(b.outer_inv[...], b.mid_half[:, : here * LANES])
        for line in range(here):
            put(start + line, value[:, line * LANES : (line + 1) * LANES])


def put_lines(target, lines, stride, steps):
    def put(place, value):
        target[pl.ds(lines[place], steps, stride=stride), :] = value

    return put


def signal_lines(sz):
    return [seq * sz.steps * sz.big + chan for seq in range(sz.seqs) for chan in range(sz.big)]


def first_channel(sz):
    row = lax.axis_index("rows")
    return (row // 2) * sz.couple + lax.rem(row, 2) * sz.big


def own_taps(sz, filters):
    start = first_channel(sz)
    chan = lax.broadcasted_iota(jnp.int32, (sz.big, sz.half), 0)
    lane = lax.broadcasted_iota(jnp.int32, (sz.big, sz.half), 1)
    pick = jnp.where(lane == start + chan, 1.0, 0.0).astype(BF16)
    parts = [nt(pick, filters[way].astype(BF16)) for way in range(2)]
    return jnp.concatenate(parts, axis=0).astype(BF16)


def own_envelope(sz, env):
    first_chan = lax.axis_index("hid") * sz.half + first_channel(sz)
    channel = first_chan + lax.broadcasted_iota(jnp.int32, (sz.big, LANES), 0)
    fraction = lax.rem(channel * 37, sz.width).astype(F32) / (sz.width - 1)
    start_log = math.log(1.0 / 40.0)
    rate = jnp.exp(start_log + (math.log(1.5 / sz.length) - start_log) * fraction)
    lane = lax.broadcasted_iota(jnp.int32, (sz.big, LANES), 1)
    power = jnp.zeros((sz.big, LANES), F32)
    for step in range(sz.steps):
        decay = jnp.exp(-(lane + step * LANES).astype(F32) * rate)
        env[0 : sz.big, step * LANES : (step + 1) * LANES] = decay
        power += decay * decay
    scale = lax.rsqrt(2.0 * jnp.sum(power, axis=1, keepdims=True))
    for step in range(sz.steps):
        lanes = slice(step * LANES, (step + 1) * LANES)
        value = env[0 : sz.big, lanes] * scale
        env[0 : sz.big, lanes] = value
        env[sz.big :, lanes] = jnp.where(lane + step * LANES > 0, value, 0.0)


def filter_spectrum(sz, b, layer):
    piece, steps, outer = sz.big, sz.steps, sz.outer
    taps = own_taps(sz, b.filters[layer])
    chunk = 4
    for start in range(0, steps, chunk):
        span = slice(start * LANES, (start + chunk) * LANES)
        kernels = nn(taps, b.pos[:, span]) * b.env[:, span]
        for step in range(chunk):
            b.tall[pl.ds((start + step) * 2 * piece, 2 * piece), :] = kernels[
                :, step * LANES : (step + 1) * LANES
            ]
    spec = b.filt_spec[layer]
    span = sz.big * outer
    for way in range(2):
        lines = [way * piece + chan for chan in range(sz.big)]
        spread_in(b.tall, b.wide, lines, 2 * piece, steps)
        dft(b, sz.big, outer, b.spec)
        if way == 0:
            spec[...] = b.spec[0:span, :].astype(BF16)
        else:
            spec[:, :LANES] = (spec[:, :LANES].astype(F32) + b.spec[0:span, :LANES]).astype(BF16)
            spec[:, LANES:] = (spec[:, LANES:].astype(F32) - b.spec[0:span, LANES:]).astype(BF16)


def conv_forward(sz, b, layer, landed):
    b.tall[0 : sz.count * sz.big, :] = landed[...].astype(F32)
    lines = signal_lines(sz)
    spread_in(b.tall, b.wide, lines, sz.big, sz.steps)
    dft(b, sz.pairs, sz.outer, b.spec)
    span = sz.big * sz.outer
    filt = b.filt_spec[layer]
    for seq in range(sz.seqs):
        rows = slice(seq * span, (seq + 1) * span)
        re, im = b.spec[rows, :LANES], b.spec[rows, LANES:]
        b.sig_spec[layer][rows, :LANES] = re.astype(BF16)
        b.sig_spec[layer][rows, LANES:] = im.astype(BF16)
        fil_re, fil_im = filt[:, :LANES].astype(F32), filt[:, LANES:].astype(F32)
        b.flat[rows, :LANES] = (re * fil_re - im * fil_im).astype(BF16)
        b.flat[rows, LANES:] = (re * fil_im + im * fil_re).astype(BF16)
    inverse_dft(b, sz.pairs, sz.outer, put_lines(b.tall, lines, sz.big, sz.steps))
    b.staged[...] = b.tall[0 : sz.count * sz.big, :].astype(BF16)


def conv_backward(sz, b, layer, landed):
    b.tall[0 : sz.count * sz.big, :] = landed[...].astype(F32)
    lines = signal_lines(sz)
    spread_in(b.tall, b.wide, lines, sz.big, sz.steps)
    dft(b, sz.pairs, sz.outer, b.spec)
    span = sz.big * sz.outer
    filt = b.filt_spec[layer]
    for seq in range(sz.seqs):
        rows = slice(seq * span, (seq + 1) * span)
        re, im = b.spec[rows, :LANES], b.spec[rows, LANES:]
        fil_re, fil_im = filt[:, :LANES].astype(F32), filt[:, LANES:].astype(F32)
        b.flat[rows, :LANES] = (re * fil_re + im * fil_im).astype(BF16)
        b.flat[rows, LANES:] = (im * fil_re - re * fil_im).astype(BF16)
    inverse_dft(b, sz.pairs, sz.outer, put_lines(b.tall, lines, sz.big, sz.steps))
    b.staged[...] = b.tall[0 : sz.count * sz.big, :].astype(BF16)


def taps_gradient(sz, b, layer, landed, signal):
    span = sz.big * sz.outer
    total_re = jnp.zeros((span, LANES), F32)
    total_im = jnp.zeros((span, LANES), F32)
    for seq in range(sz.seqs):
        rows = slice(seq * span, (seq + 1) * span)
        re, im = b.spec[rows, :LANES], b.spec[rows, LANES:]
        sig = b.sig_spec[layer]
        sig_re, sig_im = sig[rows, :LANES].astype(F32), sig[rows, LANES:].astype(F32)
        total_re += re * sig_re + im * sig_im
        total_im += im * sig_re - re * sig_im
    piece = sz.big
    b.tall[...] = jnp.zeros_like(b.tall)
    for way in range(2):
        b.flat[0:span, :LANES] = total_re.astype(BF16)
        b.flat[0:span, LANES:] = (total_im if way == 0 else -total_im).astype(BF16)
        lines = [way * piece + chan for chan in range(sz.big)]
        inverse_dft(b, sz.big, sz.outer, put_lines(b.tall, lines, 2 * piece, sz.steps))
    taps = own_taps(sz, b.filters[layer])
    total = jnp.zeros((2 * piece, ORDER), F32)
    chunk = 4
    for start in range(0, sz.steps, chunk):
        lanes = slice(start * LANES, (start + chunk) * LANES)
        raw = nn(taps, b.pos[:, lanes])
        grads = jnp.concatenate(
            [b.tall[pl.ds((start + step) * 2 * piece, 2 * piece), :] for step in range(chunk)],
            axis=1,
        )
        grads = grads * b.env[:, lanes] + (2.0 * DECAY) * raw
        total += nt(grads.astype(BF16), b.pos[:, lanes])
    products = jnp.zeros((piece, LANES), F32)
    for block in range(sz.count):
        rows = slice(block * piece, (block + 1) * piece)
        products += landed[rows, :].astype(F32) * signal[rows, :].astype(F32)
    column = jnp.sum(products, axis=1, keepdims=True)
    row = jnp.transpose(jnp.broadcast_to(column, (piece, LANES)))[0:8, :]
    b.taps_work[...] = jnp.zeros_like(b.taps_work)
    b.taps_work[0 : sz.big, :] = total[0 : sz.big, :]
    b.taps_work[sz.big : 2 * sz.big, :] = total[piece : piece + sz.big, :]
    b.taps_work[2 * sz.big : 2 * sz.big + 1, 0:piece] = row[0:1, :]


def block_of(sz, block):
    return slice(block * sz.size, (block + 1) * sz.size)


def project(sz, b, layer):
    for block in range(sz.blocks):
        rows = block_of(sz, block)
        part = b.normed[layer][:, rows]
        b.inner[layer][rows, :] = nt(b.mixer[layer, 0, block], part).astype(BF16)
        b.gate[layer][rows, :] = nt(b.mixer[layer, 1, block], part)


def mix(sz, b, layer, conv):
    summed, mixed, middle = b.summed[layer], b.mixed[layer], b.middle[layer]
    summed[...] = conv[...].astype(F32) + b.skip[layer][...] * b.inner[layer][...].astype(F32)
    mixed[...] = (b.gate[layer][...] * summed[...]).astype(BF16)
    for block in range(sz.blocks):
        rows = block_of(sz, block)
        middle[:, rows] = tn(mixed[rows, :], b.mixer[layer, 2, block])
    middle[...] = middle[...] + b.stream[layer][...]


def mixer_gradient(sz, b, kind_row, values, mine, give):
    low = lax.axis_index("hid") == 0
    left = jnp.concatenate(values[: sz.side_blocks], axis=1)
    right = jnp.concatenate(values[sz.side_blocks :], axis=1)
    rows = slice(kind_row * sz.size, (kind_row + 1) * sz.size)
    mine[rows, :] = jnp.where(low, left, right).astype(BF16)
    give[rows, :] = jnp.where(low, right, left).astype(BF16)


def gain_gradient(sz, b, row, value, mine, give):
    low = lax.axis_index("hid") == 0
    left, right = value[:, : sz.half], value[:, sz.half :]
    mine[row : row + 1, :] = jnp.where(low, left, right)
    give[row : row + 1, :] = jnp.where(low, right, left)


def mixer_backward(sz, b, layer, grad_next, total):
    normal, inv = normalize(b.middle[layer][...])
    gain = b.gain[layer, 1:2, :]
    back, gain_grad = norm_back(total, normal, inv, gain)
    result = grad_next + back
    b.grad_middle[...] = result
    b.grad_o[...] = result.astype(BF16)
    for block in range(sz.blocks):
        rows = block_of(sz, block)
        grad_mixed = nt(b.mixer[layer, 2, block], b.grad_o[:, rows])
        b.gate_grad[rows, :] = (grad_mixed * b.summed[layer][rows, :]).astype(BF16)
        through = grad_mixed * b.gate[layer][rows, :]
        b.summed_grad[rows, :] = through
        b.conv_grad[rows, :] = through.astype(BF16)
    return gain_grad


def out_gradient(sz, b, layer):
    return [
        nn(b.mixed[layer][block_of(sz, block), :], b.grad_o[:, block_of(sz, block)])
        for block in range(sz.blocks)
    ]


def in_gradient(sz, b, layer, grads):
    return [
        jnp.transpose(
            nn(grads[block_of(sz, block), :], b.normed[layer][:, block_of(sz, block)])
        )
        for block in range(sz.blocks)
    ]


def input_backward(sz, b, layer, back):
    direct = b.skip[layer][...] * b.summed_grad[...]
    b.inner_grad[...] = (direct + back[...].astype(F32)).astype(BF16)
    for block in range(sz.blocks):
        rows = block_of(sz, block)
        b.grad_sum[0 : sz.own, rows] = tn(b.inner_grad[rows, :], b.mixer[layer, 0, block]) + tn(
            b.gate_grad[rows, :], b.mixer[layer, 1, block]
        )
    normal, inv = normalize(b.stream[layer][...])
    result, gain_grad = norm_back(
        b.grad_sum[0 : sz.own, :], normal, inv, b.gain[layer, 0:1, :]
    )
    return b.grad_middle[...] + result, gain_grad


def ff_forward(sz, b, layer):
    tile = 512
    rows = slice(0, 2 * sz.own)
    b.out_sum[...] = jnp.zeros_like(b.out_sum)

    def body(step, carry):
        lanes = pl.ds(pl.multiple_of(step * tile, tile), tile)
        normed = b.nbuf[layer][rows, :]
        gate = nn(normed, b.up[layer, 0, :, lanes])
        up = nn(normed, b.up[layer, 1, :, lanes])
        value, _ = gelu_parts(gate)
        b.out_sum[...] += nt((value * up).astype(BF16), b.down[layer, :, lanes])
        return carry

    lax.fori_loop(0, sz.units // tile, body, 0)


def ff_backward(sz, b, layer, with_out):
    tile = 512
    rows = slice(0, 2 * sz.own)
    b.grad_sum[...] = jnp.zeros_like(b.grad_sum)
    if with_out:
        b.out_sum[...] = jnp.zeros_like(b.out_sum)

    def body(step, carry):
        lanes = pl.ds(pl.multiple_of(step * tile, tile), tile)
        normed = b.nbuf[layer][rows, :]
        gate = nn(normed, b.up[layer, 0, :, lanes])
        up = nn(normed, b.up[layer, 1, :, lanes])
        through = nn(b.gbuf[layer][rows, :], b.down[layer, :, lanes])
        value, slope = gelu_parts(gate)
        if with_out:
            b.out_sum[...] += nt((value * up).astype(BF16), b.down[layer, :, lanes])
        gate_grad = (slope * up * through).astype(BF16)
        up_grad = (value * through).astype(BF16)
        b.grad_sum[...] += nt(gate_grad, b.up[layer, 0, :, lanes]) + nt(
            up_grad, b.up[layer, 1, :, lanes]
        )
        return carry

    lax.fori_loop(0, sz.units // tile, body, 0)


def ff_gradients(sz, b, layer, links, between=(None, None, None)):
    start = pl.multiple_of(links.line * sz.part, LANES)
    units = pl.ds(start, sz.part)
    chunk = 2 * sz.own

    def body(step, carry):
        rows = pl.ds(pl.multiple_of(step * chunk, chunk), chunk)
        normed = b.nbuf[layer][rows, :]
        gate = nn(normed, b.up[layer, 0, :, units])
        up = nn(normed, b.up[layer, 1, :, units])
        through = nn(b.gbuf[layer][rows, :], b.down[layer, :, units])
        value, slope = gelu_parts(gate)
        b.unit_grad[0, rows, :] = (slope * up * through).astype(BF16)
        b.unit_grad[1, rows, :] = (value * through).astype(BF16)
        b.unit_grad[2, rows, :] = (value * up).astype(BF16)
        return carry

    lax.fori_loop(0, sz.group, body, 0)
    split = sz.width // 2
    moving = []
    for kind in range(3):
        if between[kind] is not None:
            between[kind]()
        left = b.gbuf[layer] if kind == 2 else b.nbuf[layer]
        for begin in (0, split):
            b.product[...] = tn(left[:, begin : begin + split], b.unit_grad[kind])
            for first in range(0, split, sz.depth):
                owner = (begin + first) // sz.depth
                line, peer = owner // sz.peers, owner % sz.peers
                b.pieces[kind, peer, line, 0 : sz.depth, :] = b.product[
                    first : first + sz.depth, :
                ].astype(BF16)
        half = lambda which: pl.ds(which * (sz.group // 2), sz.group // 2)
        plane = PlaneSum(
            links,
            lambda member, which, kind=kind: b.pieces.at[kind, member, half(which)],
            b.plane_first[layer].at[kind],
            b.plane_give[layer].at[kind],
            b.plane_second[layer].at[kind],
        )
        plane.start()
        moving.append(plane)
    return moving


def done(copy):
    copy.wait()


class Named:
    pass


def layout(sz):
    layers, own, width = sz.layers, sz.own, sz.width
    wide = 2 * sz.big * sz.steps
    late = sz.late_rows * sz.rows
    per_layer = dict(
        stream=((own, width), F32),
        normed=((own, width), BF16),
        inner=((width, own), BF16),
        gate=((width, own), F32),
        summed=((width, own), F32),
        mixed=((width, own), BF16),
        middle=((own, width), F32),
        nbuf=((2 * sz.group * own, width), BF16),
        gbuf=((2 * sz.group * own, width), BF16),
        skip=((width, LANES), F32),
        filt_spec=((sz.big * sz.outer, 2 * LANES), BF16),
        sig_spec=((sz.pairs * sz.outer, 2 * LANES), BF16),
        fore_in=((sz.count * sz.big, LANES), BF16),
        fore_out=((width, own), BF16),
        back_in=((sz.count * sz.big, LANES), BF16),
        back_out=((width, own), BF16),
        plane_first=((3, 2, 2, sz.group // 2, sz.deep, sz.part), BF16),
        plane_give=((3, 2, sz.group // 2, sz.deep, sz.part), BF16),
        plane_second=((3, 2, sz.group // 2, sz.deep, sz.part), BF16),
        grad_got=((own, width), BF16),
        out_got=((own, width), BF16),
    )
    single = dict(
        x=((own, width), BF16),
        gain=((layers, 2, width), F32),
        skip_rows=((layers, width), F32),
        mixer=((layers, 3, sz.blocks, sz.size, sz.size), BF16),
        filters=((layers, 2, ORDER, sz.half), F32),
        pos=((ORDER, sz.length), BF16),
        outer_fwd=((2 * sz.outer, sz.steps), BF16),
        outer_inv=((sz.steps, 2 * sz.outer), BF16),
        inner_fwd=((2 * LANES, 2 * LANES), BF16),
        inner_inv=((2 * LANES, 2 * LANES), BF16),
        twist=((sz.outer, 2 * LANES), F32),
        up=((layers, 2, width, sz.units), BF16),
        down=((layers, width, sz.units), BF16),
        env=((2 * sz.big, sz.length), F32),
        tall=((max(wide, sz.count * sz.big), LANES), F32),
        wide=((sz.steps, sz.pairs * LANES), BF16),
        mid=((2 * sz.outer, CHUNK * LANES), F32),
        flat=((sz.pairs * sz.outer, 2 * LANES), BF16),
        mid_half=((2 * sz.outer, CHUNK * LANES), BF16),
        spec=((sz.pairs * sz.outer, 2 * LANES), F32),
        conv_grad=((width, own), BF16),
        staged=((sz.count * sz.big, LANES), BF16),
        grad_middle=((own, width), F32),
        grad_o=((own, width), BF16),
        gate_grad=((width, own), BF16),
        summed_grad=((width, own), F32),
        inner_grad=((width, own), BF16),
        out_sum=((2 * own, width), F32),
        grad_sum=((2 * own, width), F32),
        out_give=((own, width), BF16),
        sum_give=((own, width), BF16),
        unit_grad=((3, 2 * sz.group * own, sz.part), BF16),
        product=((width // 2, sz.part), F32),
        pieces=((3, sz.peers, sz.group, sz.deep, sz.part), BF16),
        taps_work=((sz.taps_rows, ORDER), F32),
        gain_mine=((16, sz.half), F32),
        gain_give=((16, sz.half), F32),
        late_gain_mine=((16, sz.half), F32),
        late_gain_give=((16, sz.half), F32),
        late_mine=((late, sz.half), BF16),
        late_give=((late, sz.half), BF16),
        late_got=((late, sz.half), BF16),
        late_in=((sz.rows, sz.late_rows, sz.half), BF16),
        late_sum=((sz.late_rows, sz.half), BF16),
        out_keep=((2, own, sz.half), BF16),
        taps_line=((layers, sz.group, sz.taps_rows, ORDER), BF16),
        late_out=((sz.late_rows, sz.half), BF16),
    )
    names, specs = [], []
    for name, (shape, kind) in per_layer.items():
        for layer in range(layers):
            names.append((name, layer))
            specs.append(pltpu.VMEM(shape, kind))
    for index, deep in enumerate(sz.deeps):
        part = (sz.group // 2, deep, sz.half)
        whole_load = (sz.peers, sz.group, deep, sz.half)
        line = (sz.group, deep, sz.half)
        shapes = (whole_load,) * 3 + ((2, 2) + part, (2,) + part, (2,) + part, line, line[1:])
        for name, shape in zip(LOAD_BUFFERS, shapes):
            names.append(("load_" + name, index))
            specs.append(pltpu.VMEM(shape, BF16))
    for name, (shape, kind) in single.items():
        names.append((name, None))
        specs.append(pltpu.VMEM(shape, kind))
    return names, specs


TABLES = ("pos", "outer_fwd", "outer_inv", "inner_fwd", "inner_inv", "twist")
INPUTS = ("hidden_in", "d_out", "gains", "mixer", "skip", "filters", "gate_up", "down") + TABLES
OUTPUTS = ("hidden_out", "grad_in", "upper", "lower", "late", "taps", "units")


def program_kernel(sz, *refs):
    names, _ = layout(sz)
    inputs = dict(zip(INPUTS, refs))
    outputs = dict(zip(OUTPUTS, refs[len(INPUTS) :]))
    scratch = refs[len(INPUTS) + len(OUTPUTS) :]
    b = Named()
    for (name, layer), ref in zip(names, scratch):
        if layer is None:
            setattr(b, name, ref)
        else:
            setattr(b, name, getattr(b, name, ()) + (ref,))
    links = Links(sz, scratch[len(names)], scratch[len(names) + 1])
    own = sz.own
    top = sz.layers - 1
    col = links.col
    low = col == 0
    mine_rows = pl.ds(pl.multiple_of(col * own, own), own)
    other_rows = pl.ds(pl.multiple_of((1 - col) * own, own), own)

    barrier = greet_all(sz)
    lanes = pl.ds(pl.multiple_of(col * sz.half, sz.half), sz.half)
    sides = pl.ds(col * sz.side_blocks, sz.side_blocks)
    slots = lambda first, count: pl.ds(first * own, count * own)
    near_slots, line_slots, far_slots = slots(0, 2), slots(2, 3), slots(5, 3)
    halves = {
        "x": (inputs["hidden_in"].at[mine_rows], b.x.at[:, lanes]),
        "gains": (inputs["gains"], b.gain.at[:, :, lanes]),
        "mixer": (inputs["mixer"].at[0, pl.ds(0, 2)], b.mixer.at[0, pl.ds(0, 2), sides]),
        "skip": (inputs["skip"], b.skip_rows.at[:, lanes]),
        "out_mixer": (inputs["mixer"].at[0, pl.ds(2, 1)], b.mixer.at[0, pl.ds(2, 1), sides]),
    }
    if sz.layers > 1:
        above = pl.ds(1, sz.layers - 1)
        halves["mixers"] = (inputs["mixer"].at[above], b.mixer.at[above, :, sides])
    loads = {name: links.load(*pair) for name, pair in halves.items()}
    for name in ("filters",) + TABLES:
        loads[name] = links.load(inputs[name], getattr(b, name))
    grads = b.gbuf[top]
    loads["g"] = links.load(inputs["d_out"].at[mine_rows], grads.at[slots(0, 1), lanes])
    loads["g_near"] = links.load(inputs["d_out"].at[other_rows], grads.at[slots(1, 1), lanes])
    b.gain_mine[...] = jnp.zeros_like(b.gain_mine)
    b.gain_give[...] = jnp.zeros_like(b.gain_give)
    b.late_gain_mine[...] = jnp.zeros_like(b.late_gain_mine)
    b.late_gain_give[...] = jnp.zeros_like(b.late_gain_give)
    pl.semaphore_wait(barrier, sz.count - 1)
    got = {}
    for name, (source, target) in halves.items():
        if name == "x":
            source = inputs["hidden_in"].at[other_rows]
        got[name] = links.sibling(source, target)
    got["g"] = links.sibling(inputs["d_out"].at[other_rows], grads.at[slots(0, 1), lanes])
    got["g_near"] = links.sibling(inputs["d_out"].at[mine_rows], grads.at[slots(1, 1), lanes])

    def both(*wanted):
        for name in wanted:
            done(loads[name])
            done(got[name])

    def turn_mixer(layer, kind):
        for block in range(sz.blocks):
            b.mixer[layer, kind, block] = jnp.transpose(b.mixer[layer, kind, block])

    def norm_to(source, target, layer, which):
        normal, _ = normalize(source)
        target[...] = (normal * b.gain[layer, which : which + 1, :]).astype(BF16)

    def slot_of(place, member):
        return 2 + (member if member < place else member - 1)

    class Gather:
        moves = (
            {0: [(0, 1)], 1: [(1, 0), (1, 2)], 2: [(2, 1), (2, 3)], 3: [(3, 2)]},
            {1: [(2, 0), (0, 2)], 2: [(3, 1), (1, 3)]},
            {1: [(3, 0)], 2: [(0, 3)]},
        )
        coming = ((1, 2, 2, 1), (1, 1, 1, 1), (1, 0, 0, 1))

        def __init__(self, buffer):
            self.buffer = buffer
            self.pairs = [None] * 3

        def near(self):
            return links.sibling(self.buffer.at[slots(0, 1)], self.buffer.at[slots(1, 1)])

        def views(self, place, whose, target):
            here = 0 if whose == place else slot_of(place, whose)
            there = slot_of(target, whose)
            return [(self.buffer.at[slots(here, 1)], self.buffer.at[slots(there, 1)])]

        def span(self, count):
            return self.buffer.at[slots(0, count)]

        def step(self, index):
            if index > 0:
                self.wait(index - 1)
            pair = links.pair()
            for place, moves in self.moves[index].items():

                @pl.when(links.line == place)
                def _():
                    for whose, target in moves:
                        for source, there in self.views(place, whose, target):
                            row = target * sz.peers + links.plane
                            links.copy(source, there, pair, row, col).start()

            self.pairs[index] = pair

        def wait(self, index):
            pair = self.pairs[index]
            if True:
                for place in range(sz.group):
                    came = self.coming[index][place]
                    sent = len(self.moves[index].get(place, ()))

                    @pl.when(links.line == place)
                    def _():
                        if came:
                            span = self.span(came)
                            links.copy(span, span, pair, links.row, 1 - col).wait_recv()
                        if sent:
                            span = self.span(sent)
                            links.copy(span, span, pair, links.row, 1 - col).wait_send()

        def rest(self):
            self.wait(2)
            self.copies = [links.sibling(self.buffer.at[line_slots], self.buffer.at[far_slots])]

        def finish(self):
            for copy in self.copies:
                done(copy)

    class ArgumentGather(Gather):
        def views(self, place, whose, target):
            there = slot_of(target, whose)
            pairs = []
            for rows, shift in ((mine_rows, 0), (other_rows, 3)):
                if whose == place:
                    source = inputs["d_out"].at[rows]
                else:
                    source = self.buffer.at[slots(slot_of(place, whose) + shift, 1), lanes]
                pairs.append((source, self.buffer.at[slots(there + shift, 1), lanes]))
            return pairs

        def span(self, count):
            return self.buffer.at[slots(0, 2 * count), lanes]

        def rest(self):
            self.wait(2)
            self.copies = [
                links.sibling(self.buffer.at[line_slots, lanes], self.buffer.at[far_slots, lanes]),
                links.sibling(self.buffer.at[far_slots, lanes], self.buffer.at[line_slots, lanes]),
            ]

    top_grads = ArgumentGather(grads)
    top_grads.step(0)
    both("x", "gains")
    b.stream[0][...] = b.x[...].astype(F32)
    norm_to(b.stream[0][...], b.normed[0], 0, 0)
    both("mixer")
    turn_mixer(0, 0)
    turn_mixer(0, 1)

    exchange = Exchange(sz, links)
    project(sz, b, 0)
    normed_parts = []
    for layer in range(sz.layers):
        moving = exchange.to_owners(b.inner[layer], b.fore_in[layer])
        if layer == 0:
            for each in range(sz.layers):
                loads["up", each] = links.load(inputs["gate_up"].at[each], b.up.at[each])
                loads["down", each] = links.load(inputs["down"].at[each], b.down.at[each])
            for name in ("filters", "pos", "outer_fwd", "inner_fwd", "twist"):
                done(loads[name])
            own_envelope(sz, b.env)
            filter_spectrum(sz, b, 0)
            for name in ("outer_inv", "inner_inv"):
                done(loads[name])
            both("skip", "g", "g_near")
            for each in range(sz.layers):
                row = b.skip_rows[each : each + 1, :]
                b.skip[each][...] = jnp.transpose(jnp.broadcast_to(row, (LANES, sz.width)))
        exchange.owners_wait(moving, b.inner[layer], b.fore_in[layer])
        if layer == 0:
            top_grads.step(1)
        else:
            top_grads.rest()
        conv_forward(sz, b, layer, b.fore_in[layer])
        moving = exchange.to_tokens(b.staged, b.fore_out[layer])
        if layer == 0:
            both("out_mixer")
            if sz.layers > 1:
                both("mixers")
            for each in range(1, sz.layers):
                turn_mixer(each, 0)
                turn_mixer(each, 1)
        if layer < top:
            filter_spectrum(sz, b, layer + 1)
        done(loads["up", layer])
        done(loads["down", layer])
        if layer == 0:
            top_grads.step(2)
        exchange.tokens_wait(moving, b.staged, b.fore_out[layer])
        mix(sz, b, layer, b.fore_out[layer])
        norm_to(b.middle[layer][...], b.nbuf[layer].at[slots(0, 1)], layer, 1)
        normed_parts.append(Gather(b.nbuf[layer]))
        near = normed_parts[layer].near()
        if layer == top:
            normed_parts[layer].step(0)
        done(near)
        if layer < top:
            ff_forward(sz, b, layer)
            b.out_give[...] = b.out_sum[own:, :].astype(BF16)
            moving = links.sibling(b.out_give, b.out_got[layer])
            done(moving)
            value = b.middle[layer][...] + b.out_sum[0:own, :] + b.out_got[layer][...].astype(F32)
            b.stream[layer + 1][...] = value
            norm_to(value, b.normed[layer + 1], layer + 1, 0)
            project(sz, b, layer + 1)

    ff_backward(sz, b, top, True)
    b.sum_give[...] = b.grad_sum[own:, :].astype(BF16)
    moving = links.sibling(b.sum_give, b.grad_got[top])
    b.out_give[...] = b.out_sum[own:, :].astype(BF16)
    out_moving = links.sibling(b.out_give, b.out_got[top])
    normed_parts[top].step(1)
    done(moving)
    total = b.grad_sum[0:own, :] + b.grad_got[top][...].astype(F32)
    grad_next = b.gbuf[top][0:own, :].astype(F32)
    gain_grad = mixer_backward(sz, b, top, grad_next, total)
    moving = exchange.to_owners(b.conv_grad, b.back_in[top])
    gain_gradient(sz, b, 2 * top, gain_grad, b.gain_mine, b.gain_give)
    upper = Payload(sz, b, links, 0, outputs["upper"])
    lower = Payload(sz, b, links, 1, outputs["lower"])
    upper.matrix(0, out_gradient(sz, b, top))
    done(out_moving)
    value = b.middle[top][...] + b.out_sum[0:own, :] + b.out_got[top][...].astype(F32)
    value = value.astype(BF16)
    left, right = value[:, : sz.half], value[:, sz.half :]
    b.out_keep[0] = jnp.where(low, left, right)
    b.out_keep[1] = jnp.where(low, right, left)
    place = outputs["hidden_out"].at[mine_rows]
    ending = [links.load(b.out_keep.at[0], place), links.sibling(b.out_keep.at[1], place)]
    top_grads.finish()
    normed_parts[top].step(2)

    plane_moving = {}
    taps_moving = {}
    units_moving = []

    def taps_to_line(layer):
        taps_gradient(sz, b, layer, b.back_in[layer], b.fore_in[layer])
        place = b.taps_line.at[layer, links.line]
        b.taps_line[layer, links.line] = b.taps_work[...].astype(BF16)
        taps_moving[layer] = links.in_line(lambda member: place, place)

    def taps_to_plane(layer):
        links.wait(taps_moving[layer], b.taps_line.at[layer, pl.ds(0, sz.group - 1)])
        place = outputs["taps"].at[layer, links.plane]
        ending.append(links.load(b.taps_line.at[layer], place))
        taps_moving[layer] = links.in_plane(lambda member: b.taps_line.at[layer], place)

    def units_middle(layer, kinds=(0, 1, 2)):
        for kind in kinds:
            plane_moving[layer][kind].middle()

    def units_end(layer, kinds=(0, 1, 2)):
        for kind in kinds:
            plane = plane_moving[layer][kind]
            plane.end()
            part = plane.sums()
            target = outputs["units"].at[layer, kind, links.line]
            ending.append(links.load(part(links.line), target))
            pair = links.in_line(part, target)
            units_moving.append((layer, kind, pair))

    exchange.owners_wait(moving, b.conv_grad, b.back_in[top])
    conv_backward(sz, b, top, b.back_in[top])
    moving = exchange.to_tokens(b.staged, b.back_out[top])
    normed_parts[top].rest()
    normed_parts[0].step(0)
    normed_parts[top].finish()
    plane_moving[top] = ff_gradients(sz, b, top, links)
    exchange.tokens_wait(moving, b.staged, b.back_out[top])
    value, gain_grad = input_backward(sz, b, top, b.back_out[top])
    b.out_sum[0:own, :] = value
    b.gbuf[0][0:own, :] = value.astype(BF16)
    gather = Gather(b.gbuf[0])
    near = gather.near()
    gather.step(0)
    normed_parts[0].step(1)
    gain_gradient(sz, b, 2 * top - 1, gain_grad, b.gain_mine, b.gain_give)
    upper.matrix(1, in_gradient(sz, b, top, b.inner_grad))
    upper.matrix(2, in_gradient(sz, b, top, b.gate_grad))
    upper.to_partner()
    done(near)
    ff_backward(sz, b, 0, False)
    b.sum_give[...] = b.grad_sum[own:, :].astype(BF16)
    moving = links.sibling(b.sum_give, b.grad_got[0])
    gather.step(1)
    normed_parts[0].step(2)
    done(moving)
    total = b.grad_sum[0:own, :] + b.grad_got[0][...].astype(F32)
    gain_grad = mixer_backward(sz, b, 0, b.out_sum[0:own, :], total)

    moving = exchange.to_owners(b.conv_grad, b.back_in[0])
    units_middle(top)
    upper.to_plane()
    taps_to_line(top)
    gain_gradient(sz, b, 0, gain_grad, b.gain_mine, b.gain_give)
    lower.matrix(0, out_gradient(sz, b, 0))
    lower.matrix(1, in_gradient(sz, b, 0, b.gate_grad))
    lower.rows16(2, b.gain_mine[...], b.gain_give[...])
    lower.to_partner()
    gather.step(2)
    exchange.owners_wait(moving, b.conv_grad, b.back_in[0])
    lower.to_plane()
    conv_backward(sz, b, 0, b.back_in[0])
    moving = exchange.to_tokens(b.staged, b.back_out[0])
    units_end(top)
    normed_parts[0].rest()
    gather.rest()
    upper.middle()
    taps_to_plane(top)
    normed_parts[0].finish()
    gather.finish()
    between = (lower.middle, upper.to_line, None)
    plane_moving[0] = ff_gradients(sz, b, 0, links, between)
    exchange.tokens_wait(moving, b.staged, b.back_out[0])
    value, gain_grad = input_backward(sz, b, 0, b.back_out[0])

    left, right = value[:, : sz.half], value[:, sz.half :]
    keep, give = b.out_sum.at[0:own, 0 : sz.half], b.out_sum.at[own:, 0 : sz.half]
    keep[...] = jnp.where(low, left, right)
    give[...] = jnp.where(low, right, left)
    mixer_gradient(sz, b, 0, in_gradient(sz, b, 0, b.inner_grad), b.late_mine, b.late_give)
    gain_gradient(sz, b, 0, gain_grad, b.late_gain_mine, b.late_gain_give)
    rows = slice(sz.size, sz.size + 16)
    b.late_mine[rows, :] = b.late_gain_mine[...].astype(BF16)
    b.late_give[rows, :] = b.late_gain_give[...].astype(BF16)
    last = slice(sz.size + 16, sz.rows * sz.late_rows)
    b.late_mine[last, :] = jnp.zeros_like(b.late_mine[last, :])
    b.late_give[last, :] = jnp.zeros_like(b.late_give[last, :])
    late_pair = links.sibling(b.late_give, b.late_got)
    place = outputs["grad_in"].at[mine_rows]
    ending += [links.load(keep, place), links.sibling(give, place)]

    done(late_pair)
    b.late_mine[...] = (b.late_mine[...].astype(F32) + b.late_got[...].astype(F32)).astype(BF16)
    few = lambda index: pl.ds(pl.multiple_of(index * sz.late_rows, sz.late_rows), sz.late_rows)
    rows_pair = links.in_rows(
        lambda member: b.late_mine.at[few(member)], b.late_in.at[links.row]
    )
    lower.to_line()
    units_middle(0, (0, 1))
    taps_to_line(0)
    units_middle(0, (2,))
    upper.back_line()
    lower.back_line()
    units_end(0, (0,))
    links.wait(rows_pair, b.late_in.at[pl.ds(0, sz.rows - 1)])
    b.late_in[links.row] = b.late_mine[few(links.row), :]
    late = outputs["late"]
    b.late_out[...] = jnp.sum(b.late_in[...].astype(F32), axis=0).astype(BF16)
    place = late.at[few(links.row)]
    ending.append(links.load(b.late_out, place))
    spread_rows = links.in_rows(lambda member: b.late_out, place)
    units_end(0, (1,))
    upper.back_plane()
    units_end(0, (2,))
    lower.back_plane()
    upper.spread.middle()
    lower.spread.middle()
    taps_to_plane(0)
    ending += [upper.finish(), lower.finish()]
    for layer, kind, pair in units_moving:
        links.wait(pair, outputs["units"].at[layer, kind, pl.ds(0, sz.group - 1)])
    links.wait(spread_rows, late.at[pl.ds(0, (sz.rows - 1) * sz.late_rows)])
    for layer, pair in taps_moving.items():
        links.wait(pair, outputs["taps"].at[layer, pl.ds(0, sz.peers - 1)])
    for copy in ending:
        done(copy)


def results_kernel(sz, *refs):
    raw, outs, scratch = refs[:7], refs[7:15], refs[15:]
    targets, held = scratch[:7], scratch[7:15]
    hidden_out, grad_in, gain_out, mixer_out, skip_out, taps_out, pair_out, down_out = held
    upper, lower, late, taps, units = targets[2:]
    channels, sems = scratch[15:]
    targets = (hidden_out, grad_in) + targets[2:]
    copies = [
        pltpu.make_async_copy(source, target, sems.at[index])
        for index, (source, target) in enumerate(zip(raw, targets))
    ]
    for copy in reversed(copies):
        copy.start()
    leaving = []

    def leave(index):
        copy = pltpu.make_async_copy(held[index], outs[index], sems.at[7 + index])
        copy.start()
        leaving.append(copy)

    layers = sz.layers
    copies[6].wait()
    for kind in range(3):
        for layer in range(layers):
            for line in range(sz.group):
                lanes = slice(line * sz.part, (line + 1) * sz.part)
                value = units[layer, kind, line].astype(F32)
                if kind < 2:
                    pair_out[layer, kind, :, lanes] = value
                else:
                    down_out[layer, :, lanes] = value
    leave(6)
    leave(7)
    copies[5].wait()
    for layer in range(layers):
        for way in range(3):
            for row in range(sz.rows):
                part = taps[layer, row % sz.peers, row // sz.peers]
                begin = (row // 2) * sz.couple + (row % 2) * sz.big
                size = sz.small if row % 2 else sz.big
                if way < 2:
                    value = part[way * sz.big : way * sz.big + size, :].astype(F32)
                else:
                    line = part[2 * sz.big : 2 * sz.big + 16, :].astype(F32)[0:1, :]
                    value = jnp.transpose(jnp.broadcast_to(line, (LANES, ORDER)))[0:size, :]
                channels[begin : begin + size, :] = value
            turned = jnp.transpose(channels[...])
            if way < 2:
                taps_out[layer, way] = turned
            else:
                skip_out[layer : layer + 1, :] = turned[0:1, :]
    leave(4)
    leave(5)
    for copy in copies[2:5]:
        copy.wait()

    def matrix(payload, place, layer, kind):
        deep = payload.shape[2]
        count = sz.size // deep
        for part in range(count):
            index = place * count + part
            rows = payload[index // sz.group, index % sz.group].astype(F32)
            for block in range(sz.side_blocks):
                mixer_out[layer, kind, block, part * deep : (part + 1) * deep, :] = rows[
                    :, block_of(sz, block)
                ]

    for place, kind in enumerate((2, 0, 1)):
        matrix(upper, place, 1, kind)
    for place, kind in enumerate((2, 1)):
        matrix(lower, place, 0, kind)
    rows = late[0 : sz.size, :].astype(F32)
    for block in range(sz.side_blocks):
        mixer_out[0, 0, block] = rows[:, block_of(sz, block)]
    index = 2 * (sz.size // sz.deeps[1])
    gains = lower[index // sz.group, index % sz.group].astype(F32)
    gain_out[0, 0:1, :] = late[sz.size : sz.size + 16, :].astype(F32)[0:1, :]
    for row in range(1, 2 * layers):
        gain_out[row // 2, row % 2 : row % 2 + 1, :] = gains[row - 1 : row, :]
    leave(2)
    leave(3)
    for index in range(2):
        copies[index].wait()
        leave(index)
    for copy in leaving:
        copy.wait()


def results(sz, *arrays):
    layers = sz.layers
    outs = (
        ((2 * sz.own, sz.half), BF16),
        ((2 * sz.own, sz.half), F32),
        ((layers, 2, sz.half), F32),
        ((layers, 3, sz.side_blocks, sz.size, sz.size), F32),
        ((layers, sz.half), F32),
        ((layers, 2, ORDER, sz.half), F32),
        ((layers, 2, sz.depth, sz.units), F32),
        ((layers, sz.depth, sz.units), F32),
    )
    anywhere = pl.BlockSpec(memory_space=pl.ANY)
    return pl.pallas_call(
        functools.partial(results_kernel, sz),
        out_shape=tuple(jax.ShapeDtypeStruct(shape, kind) for shape, kind in outs),
        in_specs=[anywhere] * len(arrays),
        out_specs=(anywhere,) * len(outs),
        scratch_shapes=[pltpu.VMEM(entry.shape, entry.dtype) for entry in arrays]
        + [pltpu.VMEM(shape, kind) for shape, kind in outs]
        + [pltpu.VMEM((sz.half, ORDER), F32), pltpu.SemaphoreType.DMA((15,))],
        compiler_params=pltpu.CompilerParams(vmem_limit_bytes=62 * MIB),
        name="results",
    )(*arrays)


def program(sz, arrays):
    names, scratch = layout(sz)
    outs = (
        ((2 * sz.own, sz.half), BF16),
        ((2 * sz.own, sz.half), F32),
        ((sz.peers, sz.group, sz.deeps[0], sz.half), BF16),
        ((sz.peers, sz.group, sz.deeps[1], sz.half), BF16),
        ((sz.rows * sz.late_rows, sz.half), BF16),
        ((sz.layers, sz.peers, sz.group, sz.taps_rows, ORDER), BF16),
        ((sz.layers, 3, sz.group, sz.deep, sz.part), BF16),
    )
    return pl.pallas_call(
        functools.partial(program_kernel, sz),
        out_shape=tuple(jax.ShapeDtypeStruct(shape, kind) for shape, kind in outs),
        in_specs=[pl.BlockSpec(memory_space=pl.ANY)] * len(arrays),
        out_specs=(pl.BlockSpec(memory_space=pl.ANY),) * len(outs),
        scratch_shapes=scratch
        + [pltpu.SemaphoreType.DMA((220,)), pltpu.SemaphoreType.DMA((80,))],
        compiler_params=pltpu.CompilerParams(
            collective_id=0, has_side_effects=True, vmem_limit_bytes=63 * MIB
        ),
        name="program",
    )(*arrays)


def together(sz, hidden_in, d_out, gains, mixer, skip, filters, gate_up, down):
    pos = jnp.asarray(position_table(sz.length).T, F32).astype(BF16)
    arrays = (hidden_in, d_out, gains, mixer, skip, filters, gate_up, down, pos)
    raw = program(sz, arrays + dft_tables(sz.length))

    return results(sz, *raw)


def apart_enter(count, hid):
    me = lax.axis_index("rows") * hid + lax.axis_index("hid")
    barrier = pltpu.get_barrier_semaphore()

    def greet(step, carry):
        peer = lax.rem(me + step, count)
        pl.semaphore_signal(
            barrier, inc=1, device_id=(peer // hid, lax.rem(peer, hid)), device_id_type=MESH
        )
        return carry

    lax.fori_loop(1, count, greet, 0)
    return barrier


def apart_exchange_start(source, target, sems, count, rows, hid, piece, by_owner):
    send, recv, local = sems
    row = lax.axis_index("rows")
    col = lax.axis_index("hid")
    token_id = row * hid + col
    owner_id = col * rows + row
    mine_there = token_id if by_owner else owner_id
    mine_here = owner_id if by_owner else token_id
    at = lambda index: pl.ds(pl.multiple_of(index * piece, piece), piece)
    pltpu.make_async_copy(source.at[at(mine_here)], target.at[at(mine_there)], local).start()

    def post(step, carry):
        peer = lax.rem(token_id + step, count)
        peer_row = peer // hid
        peer_col = lax.rem(peer, hid)
        there = (peer_col * rows + peer_row) if by_owner else peer
        pltpu.make_async_remote_copy(
            src_ref=source.at[at(there)],
            dst_ref=target.at[at(mine_there)],
            send_sem=send,
            recv_sem=recv,
            device_id=(peer_row, peer_col),
            device_id_type=MESH,
        ).start()
        return carry

    lax.fori_loop(1, count, post, 0)


def apart_exchange_wait(source, target, sems, count, rows, hid, piece):
    send, recv, local = sems
    row = lax.axis_index("rows")
    col = lax.axis_index("hid")
    pltpu.make_async_copy(
        source.at[pl.ds(0, piece)], target.at[pl.ds(0, piece)], local
    ).wait()
    span = pl.ds(0, (count - 1) * piece)
    pltpu.make_async_remote_copy(
        src_ref=source.at[span],
        dst_ref=target.at[span],
        send_sem=send,
        recv_sem=recv,
        device_id=(row, hid - 1 - col),
        device_id_type=MESH,
    ).wait()


class apart_Sizes:
    def __init__(self, rows, hid, width, hidden, tokens):
        self.rows, self.hid, self.width, self.hidden = rows, hid, width, hidden
        self.count = rows * hid
        self.chans = width // self.count
        self.piece = round_up(self.chans, 16)
        self.length = min(SEQ_LEN, tokens)
        self.seqs = tokens // self.length
        self.blocks = self.length // LANES
        self.outer = 2 * self.blocks
        self.pairs = self.seqs * self.chans
        self.half = width // hid
        self.padded = rows * self.piece
        self.channels = self.count * self.piece


def apart_spread_in(source, wide, lines, stride, blocks):
    for place, line in enumerate(lines):
        wide[:, place * LANES : (place + 1) * LANES] = source[
            pl.ds(line, blocks, stride=stride), :
        ].astype(wide.dtype)


def apart_dft(wide, spectrum, tables, mid, flat, lines, outer, offset=0):
    outer_fwd, inner_fwd, twist = tables
    mid[:, : lines * LANES] = nn(outer_fwd[...], wide[:, : lines * LANES])
    cos = twist[:, :LANES]
    sin = twist[:, LANES:]
    for line in range(lines):
        lanes = pl.ds(line * LANES, LANES)
        real = mid[0:outer, lanes]
        imag = mid[outer : 2 * outer, lanes]
        rows = pl.ds(line * outer, outer)
        flat[rows, 0:LANES] = (real * cos + imag * sin).astype(BF16)
        flat[rows, LANES:] = (imag * cos - real * sin).astype(BF16)
    spectrum[0 : lines * outer, :] = nn(flat[0 : lines * outer, :], inner_fwd[...])


def apart_inverse_dft(flat, tables, mid_half, lines, outer):
    outer_inv, inner_inv, twist = tables
    cos = twist[:, :LANES]
    sin = twist[:, LANES:]
    for line in range(lines):
        rows = pl.ds(line * outer, outer)
        lanes = pl.ds(line * LANES, LANES)
        part = nn(flat[rows, :], inner_inv[...])
        real = part[:, :LANES]
        imag = part[:, LANES:]
        mid_half[0:outer, lanes] = (real * cos - imag * sin).astype(BF16)
        mid_half[outer : 2 * outer, lanes] = (imag * cos + real * sin).astype(BF16)
    return nn(outer_inv[...], mid_half[:, : lines * LANES])


def apart_spread_out(value, target, lines, stride, blocks):
    for place, line in enumerate(lines):
        target[pl.ds(line, blocks, stride=stride), :] = value[
            :, place * LANES : (place + 1) * LANES
        ]


def apart_signal_lines(sz):
    return [seq * sz.blocks * sz.piece + chan for seq in range(sz.seqs) for chan in range(sz.chans)]


def apart_conv_forward_kernel(
    sz,
    inner_ref,
    taps_ref,
    pos_ref,
    env_ref,
    outer_fwd,
    outer_inv,
    inner_fwd,
    inner_inv,
    twist,
    conv_ref,
    filt_spec,
    sig_spec,
    landed,
    staged,
    tall,
    wide,
    mid,
    flat,
    mid_half,
    sems_in,
    sems_out,
):
    barrier = apart_enter(sz.count, sz.hid)
    pl.semaphore_wait(barrier, sz.count - 1)
    into = tuple(sems_in.at[i] for i in range(3))
    back = tuple(sems_out.at[i] for i in range(3))
    apart_exchange_start(inner_ref, landed, into, sz.count, sz.rows, sz.hid, sz.piece, True)

    piece, blocks, outer = sz.piece, sz.blocks, sz.outer
    step = 4
    for start in range(0, blocks, step):
        span = slice(start * LANES, (start + step) * LANES)
        raw = nn(taps_ref[...], pos_ref[:, span])
        kernels = raw * env_ref[:, span]
        for block in range(step):
            tall[pl.ds((start + block) * 2 * piece, 2 * piece), :] = kernels[
                :, block * LANES : (block + 1) * LANES
            ]
    lines = [way * piece + chan for way in range(2) for chan in range(sz.chans)]
    apart_spread_in(tall, wide, lines, 2 * piece, blocks)
    apart_dft(wide, sig_spec, (outer_fwd, inner_fwd, twist), mid, flat, len(lines), outer)
    span = sz.chans * outer
    filt_spec[:, :LANES] = sig_spec[0:span, :LANES] + sig_spec[span : 2 * span, :LANES]
    filt_spec[:, LANES:] = sig_spec[0:span, LANES:] - sig_spec[span : 2 * span, LANES:]

    apart_exchange_wait(inner_ref, landed, into, sz.count, sz.rows, sz.hid, piece)
    tall[0 : sz.channels, :] = landed[...].astype(F32)
    lines = apart_signal_lines(sz)
    apart_spread_in(tall, wide, lines, piece, blocks)
    apart_dft(wide, sig_spec, (outer_fwd, inner_fwd, twist), mid, flat, sz.pairs, outer)
    for seq in range(sz.seqs):
        rows = pl.ds(seq * span, span)
        sig_re, sig_im = sig_spec[rows, :LANES], sig_spec[rows, LANES:]
        fil_re, fil_im = filt_spec[:, :LANES], filt_spec[:, LANES:]
        flat[rows, :LANES] = (sig_re * fil_re - sig_im * fil_im).astype(BF16)
        flat[rows, LANES:] = (sig_re * fil_im + sig_im * fil_re).astype(BF16)
    result = apart_inverse_dft(flat, (outer_inv, inner_inv, twist), mid_half, sz.pairs, outer)
    apart_spread_out(result, tall, lines, piece, blocks)
    staged[...] = tall[0 : sz.channels, :].astype(BF16)
    apart_exchange_start(staged, conv_ref, back, sz.count, sz.rows, sz.hid, piece, False)
    apart_exchange_wait(staged, conv_ref, back, sz.count, sz.rows, sz.hid, piece)


def apart_conv_forward(sz, inner, taps, pos, env, tables, cid):
    outer_fwd, outer_inv, inner_fwd, inner_inv, twist = tables
    wide_lines = max(2 * sz.chans, sz.pairs)
    return pl.pallas_call(
        functools.partial(apart_conv_forward_kernel, sz),
        out_shape=(
            jax.ShapeDtypeStruct((sz.channels, LANES), BF16),
            jax.ShapeDtypeStruct((sz.chans * sz.outer, 2 * LANES), F32),
            jax.ShapeDtypeStruct((wide_lines * sz.outer, 2 * LANES), F32),
        ),
        in_specs=[whole()] * 9,
        out_specs=(whole(),) * 3,
        scratch_shapes=[
            pltpu.VMEM((sz.channels, LANES), BF16),
            pltpu.VMEM((sz.channels, LANES), BF16),
            pltpu.VMEM((max(2 * sz.piece * sz.blocks, sz.channels), LANES), F32),
            pltpu.VMEM((sz.blocks, wide_lines * LANES), BF16),
            pltpu.VMEM((2 * sz.outer, wide_lines * LANES), F32),
            pltpu.VMEM((wide_lines * sz.outer, 2 * LANES), BF16),
            pltpu.VMEM((2 * sz.outer, sz.pairs * LANES), BF16),
            pltpu.SemaphoreType.DMA((3,)),
            pltpu.SemaphoreType.DMA((3,)),
        ],
        compiler_params=pltpu.CompilerParams(
            collective_id=cid, has_side_effects=True, vmem_limit_bytes=48 * MIB
        ),
        name="conv_forward",
    )(inner, taps, pos, env, outer_fwd, outer_inv, inner_fwd, inner_inv, twist)


def apart_conv_backward_kernel(
    sz,
    grad_ref,
    filt_spec,
    sig_spec,
    taps_ref,
    pos_ref,
    env_ref,
    outer_fwd,
    outer_inv,
    inner_fwd,
    inner_inv,
    twist,
    back_ref,
    taps_grad,
    landed,
    staged,
    tall,
    wide,
    mid,
    flat,
    mid_half,
    grad_spec,
    sems_in,
    sems_out,
):
    barrier = apart_enter(sz.count, sz.hid)
    pl.semaphore_wait(barrier, sz.count - 1)
    into = tuple(sems_in.at[i] for i in range(3))
    back = tuple(sems_out.at[i] for i in range(3))
    piece, blocks, outer = sz.piece, sz.blocks, sz.outer
    apart_exchange_start(grad_ref, landed, into, sz.count, sz.rows, sz.hid, piece, True)
    apart_exchange_wait(grad_ref, landed, into, sz.count, sz.rows, sz.hid, piece)
    tall[0 : sz.channels, :] = landed[...].astype(F32)
    lines = apart_signal_lines(sz)
    apart_spread_in(tall, wide, lines, piece, blocks)
    apart_dft(wide, grad_spec, (outer_fwd, inner_fwd, twist), mid, flat, sz.pairs, outer)
    span = sz.chans * outer
    for seq in range(sz.seqs):
        rows = pl.ds(seq * span, span)
        re, im = grad_spec[rows, :LANES], grad_spec[rows, LANES:]
        fil_re, fil_im = filt_spec[:, :LANES], filt_spec[:, LANES:]
        flat[rows, :LANES] = (re * fil_re + im * fil_im).astype(BF16)
        flat[rows, LANES:] = (im * fil_re - re * fil_im).astype(BF16)
    inv_tables = (outer_inv, inner_inv, twist)
    result = apart_inverse_dft(flat, inv_tables, mid_half, sz.pairs, outer)
    apart_spread_out(result, tall, lines, piece, blocks)
    staged[...] = tall[0 : sz.channels, :].astype(BF16)
    apart_exchange_start(staged, back_ref, back, sz.count, sz.rows, sz.hid, piece, False)

    total_re = jnp.zeros((span, LANES), F32)
    total_im = jnp.zeros((span, LANES), F32)
    for seq in range(sz.seqs):
        rows = pl.ds(seq * span, span)
        re, im = grad_spec[rows, :LANES], grad_spec[rows, LANES:]
        sig_re, sig_im = sig_spec[rows, :LANES], sig_spec[rows, LANES:]
        total_re += re * sig_re + im * sig_im
        total_im += im * sig_re - re * sig_im
    flat[0:span, :LANES] = total_re.astype(BF16)
    flat[span : 2 * span, :LANES] = total_re.astype(BF16)
    flat[0:span, LANES:] = total_im.astype(BF16)
    flat[span : 2 * span, LANES:] = (-total_im).astype(BF16)
    result = apart_inverse_dft(flat, inv_tables, mid_half, 2 * sz.chans, outer)
    lines = [way * piece + chan for way in range(2) for chan in range(sz.chans)]
    if sz.chans < piece:
        tall[...] = jnp.zeros_like(tall)
    apart_spread_out(result, tall, lines, 2 * piece, blocks)
    total = jnp.zeros((2 * piece, ORDER), F32)
    step = 4
    for start in range(0, blocks, step):
        span = slice(start * LANES, (start + step) * LANES)
        raw = nn(taps_ref[...], pos_ref[:, span])
        grads = jnp.concatenate(
            [
                tall[pl.ds((start + block) * 2 * piece, 2 * piece), :]
                for block in range(step)
            ],
            axis=1,
        )
        grads = grads * env_ref[:, span] + (2.0 * DECAY) * raw
        total += nt(grads.astype(BF16), pos_ref[:, span])
    taps_grad[...] = total

    apart_exchange_wait(staged, back_ref, back, sz.count, sz.rows, sz.hid, piece)


def apart_conv_backward(sz, grad, filt_spec, sig_spec, taps, pos, env, tables, cid):
    outer_fwd, outer_inv, inner_fwd, inner_inv, twist = tables
    wide_lines = max(2 * sz.chans, sz.pairs)
    return pl.pallas_call(
        functools.partial(apart_conv_backward_kernel, sz),
        out_shape=(
            jax.ShapeDtypeStruct((sz.channels, LANES), BF16),
            jax.ShapeDtypeStruct((2 * sz.piece, ORDER), F32),
        ),
        in_specs=[whole()] * 11,
        out_specs=(whole(),) * 2,
        scratch_shapes=[
            pltpu.VMEM((sz.channels, LANES), BF16),
            pltpu.VMEM((sz.channels, LANES), BF16),
            pltpu.VMEM((max(2 * sz.piece * sz.blocks, sz.channels), LANES), F32),
            pltpu.VMEM((sz.blocks, wide_lines * LANES), BF16),
            pltpu.VMEM((2 * sz.outer, wide_lines * LANES), F32),
            pltpu.VMEM((wide_lines * sz.outer, 2 * LANES), BF16),
            pltpu.VMEM((2 * sz.outer, wide_lines * LANES), BF16),
            pltpu.VMEM((sz.pairs * sz.outer, 2 * LANES), F32),
            pltpu.SemaphoreType.DMA((3,)),
            pltpu.SemaphoreType.DMA((3,)),
        ],
        compiler_params=pltpu.CompilerParams(
            collective_id=cid, has_side_effects=True, vmem_limit_bytes=48 * MIB
        ),
        name="conv_backward",
    )(grad, filt_spec, sig_spec, taps, pos, env, outer_fwd, outer_inv, inner_fwd, inner_inv, twist)


def apart_project(sz, normed, w_in, w_gate, inner_ref, gate_ref):
    for side in range(sz.hid):
        rows = slice(side * sz.padded, (side + 1) * sz.padded)
        part = normed[:, side * sz.half : (side + 1) * sz.half]
        inner_ref[rows, :] = nt(w_in[side], part).astype(BF16)
        gate_ref[rows, :] = nt(w_gate[side], part)


def apart_first_kernel(sz, x_ref, gain_ref, w_in, w_gate, normed_ref, inner_ref, gate_ref):
    normal, _ = normalize(x_ref[...].astype(F32))
    normed = (normal * gain_ref[0:1, :]).astype(BF16)
    normed_ref[...] = normed
    apart_project(sz, normed, w_in, w_gate, inner_ref, gate_ref)


def apart_first(sz, x, gains, w_in, w_gate):
    tokens = x.shape[0]
    return pl.pallas_call(
        functools.partial(apart_first_kernel, sz),
        out_shape=(
            jax.ShapeDtypeStruct((tokens, sz.width), BF16),
            jax.ShapeDtypeStruct((sz.channels, tokens), BF16),
            jax.ShapeDtypeStruct((sz.channels, tokens), F32),
        ),
        in_specs=[whole()] * 4,
        out_specs=(whole(),) * 3,
        compiler_params=pltpu.CompilerParams(vmem_limit_bytes=32 * MIB),
        name="first_projection",
    )(x, gains, w_in, w_gate)


def apart_mix_out(sz, mixed, w_out):
    parts = []
    for side in range(sz.hid):
        rows = slice(side * sz.padded, (side + 1) * sz.padded)
        parts.append(tn(mixed[rows, :], w_out[side]))
    return jnp.concatenate(parts, axis=1)


def apart_ff_specs(sz, layer, tile):
    steps = sz.hidden // sz.hid // tile
    first_half = lambda i: jnp.minimum(i, steps - 1)
    second = lambda i: jnp.maximum(i - steps, 0)
    specs = []
    for place in (first_half, second):
        specs.append(
            pl.BlockSpec((1, 2, sz.width, tile), lambda i, place=place: (layer, 0, 0, place(i)))
        )
        specs.append(pl.BlockSpec((1, sz.width, tile), lambda i, place=place: (layer, 0, place(i))))
    return specs, steps


def apart_forward_kernel(
    sz,
    steps,
    conv_ref,
    inner_ref,
    gate_ref,
    skip_ref,
    x_ref,
    gain_ref,
    next_gain,
    w_out,
    w_in,
    w_gate,
    up_a,
    down_a,
    up_b,
    down_b,
    summed_ref,
    mixed_ref,
    middle_ref,
    normed_two,
    next_x,
    next_normed,
    next_inner,
    next_gate,
):
    index = pl.program_id(0)

    @pl.when(index == 0)
    def _():
        summed = conv_ref[...].astype(F32) + skip_ref[...] * inner_ref[...].astype(F32)
        summed_ref[...] = summed
        mixed_ref[...] = (gate_ref[...] * summed).astype(BF16)
        middle = x_ref[...].astype(F32) + apart_mix_out(sz, mixed_ref, w_out)
        middle_ref[...] = middle
        normal, _ = normalize(middle)
        normed_two[...] = (normal * gain_ref[1:2, :]).astype(BF16)
        next_x[...] = middle

    def accumulate(up_ref, down_ref):
        gate = nn(normed_two[...], up_ref[0, 0])
        up = nn(normed_two[...], up_ref[0, 1])
        value, _ = gelu_parts(gate)
        next_x[...] += nt((value * up).astype(BF16), down_ref[0])

    pl.when(index < steps)(lambda: accumulate(up_a, down_a))
    pl.when(index >= steps)(lambda: accumulate(up_b, down_b))

    @pl.when(index == 2 * steps - 1)
    def _():
        normal, _ = normalize(next_x[...])
        normed = (normal * next_gain[0:1, :]).astype(BF16)
        next_normed[...] = normed
        apart_project(sz, normed, w_in, w_gate, next_inner, next_gate)


def apart_full(shape):
    return pl.BlockSpec(shape, lambda i: (0,) * len(shape))


def apart_forward(sz, layer, conv, inner, gate, skip, x, gains, next_gains, w_out, w_in, w_gate, ff):
    tokens = x.shape[0]
    tile = 512
    specs, steps = apart_ff_specs(sz, layer, tile)
    small = (conv, inner, gate, skip, x, gains, next_gains, w_out, w_in, w_gate)
    outs = (
        ((sz.channels, tokens), F32),
        ((sz.channels, tokens), BF16),
        ((tokens, sz.width), F32),
        ((tokens, sz.width), BF16),
        ((tokens, sz.width), F32),
        ((tokens, sz.width), BF16),
        ((sz.channels, tokens), BF16),
        ((sz.channels, tokens), F32),
    )
    return pl.pallas_call(
        functools.partial(apart_forward_kernel, sz, steps),
        grid=(2 * steps,),
        out_shape=tuple(jax.ShapeDtypeStruct(shape, kind) for shape, kind in outs),
        in_specs=[apart_full(entry.shape) for entry in small] + specs,
        out_specs=tuple(apart_full(shape) for shape, kind in outs),
        compiler_params=pltpu.CompilerParams(
            dimension_semantics=("arbitrary",), vmem_limit_bytes=48 * MIB
        ),
        name="token_forward",
    )(*small, *ff)


def apart_block_grads(sz, tall, flat, target, slot):
    blocks_side = target.shape[1] // sz.hid
    size = sz.half // blocks_side
    rows = sz.padded // blocks_side
    for side in range(sz.hid):
        for block in range(blocks_side):
            begin = side * sz.padded + block * rows
            place = side * sz.half + block * size
            target[slot, side * blocks_side + block] = nn(
                tall[begin : begin + rows, :], flat[:, place : place + size]
            ).astype(target.dtype)


def apart_ff_backward_tile(normed, grad, up_ref, down_ref, total, out_total):
    gate = nn(normed, up_ref[0, 0])
    up = nn(normed, up_ref[0, 1])
    grad_hidden = nn(grad, down_ref[0])
    value, slope = gelu_parts(gate)
    if out_total is not None:
        out_total[...] += nt((value * up).astype(BF16), down_ref[0])
    grad_gate = (slope * up * grad_hidden).astype(BF16)
    grad_up = (value * grad_hidden).astype(BF16)
    total[...] += nt(grad_gate, up_ref[0, 0]) + nt(grad_up, up_ref[0, 1])


def apart_mixer_backward(
    sz, grad_next, middle, total, gain, mixed, summed, gate, w_out, outs
):
    grad_middle, mixer_grad, grad_gate, grad_summed, grad_conv, gain_grad = outs
    normal, inv = normalize(middle)
    back, gain_grad[...] = norm_back(total, normal, inv, gain)
    result = grad_next + back
    grad_middle[...] = result
    grad_o = result.astype(BF16)
    apart_block_grads(sz, mixed, grad_o, mixer_grad, 0)
    for side in range(sz.hid):
        rows = slice(side * sz.padded, (side + 1) * sz.padded)
        grad_mixed = nt(w_out[side], grad_o[:, side * sz.half : (side + 1) * sz.half])
        grad_gate[rows, :] = (grad_mixed * summed[rows, :]).astype(BF16)
        through = grad_mixed * gate[rows, :]
        grad_summed[rows, :] = through
        grad_conv[rows, :] = through.astype(BF16)


def apart_mixer_outs(sz, tokens, blocks):
    size = sz.width // blocks
    return (
        ((tokens, sz.width), F32),
        ((1, blocks, sz.channels // blocks, size), BF16),
        ((sz.channels, tokens), BF16),
        ((sz.channels, tokens), F32),
        ((sz.channels, tokens), BF16),
        ((1, sz.width), F32),
    )


def apart_turn_kernel(
    sz,
    steps,
    conv_ref,
    inner_ref,
    gate_ref,
    skip_ref,
    x_ref,
    gain_ref,
    grad_ref,
    w_out,
    up_a,
    down_a,
    up_b,
    down_b,
    hidden_out,
    normed_two,
    grad_middle,
    mixer_grad,
    grad_gate,
    grad_summed,
    grad_conv,
    gain_grad,
    summed,
    mixed,
    middle,
    out_total,
    total,
):
    index = pl.program_id(0)

    @pl.when(index == 0)
    def _():
        summed[...] = conv_ref[...].astype(F32) + skip_ref[...] * inner_ref[...].astype(F32)
        mixed[...] = (gate_ref[...] * summed[...]).astype(BF16)
        middle[...] = x_ref[...].astype(F32) + apart_mix_out(sz, mixed, w_out)
        normal, _ = normalize(middle[...])
        normed_two[...] = (normal * gain_ref[1:2, :]).astype(BF16)
        out_total[...] = middle[...]
        total[...] = jnp.zeros_like(total)

    def accumulate(up_ref, down_ref):
        apart_ff_backward_tile(normed_two[...], grad_ref[...], up_ref, down_ref, total, out_total)

    pl.when(index < steps)(lambda: accumulate(up_a, down_a))
    pl.when(index >= steps)(lambda: accumulate(up_b, down_b))

    @pl.when(index == 2 * steps - 1)
    def _():
        hidden_out[...] = out_total[...].astype(BF16)
        outs = (grad_middle, mixer_grad, grad_gate, grad_summed, grad_conv, gain_grad)
        apart_mixer_backward(
            sz,
            grad_ref[...].astype(F32),
            middle[...],
            total[...],
            gain_ref[1:2, :],
            mixed,
            summed,
            gate_ref,
            w_out,
            outs,
        )


def apart_turn(sz, layer, blocks, conv, inner, gate, skip, x, gains, grad, w_out, ff):
    tokens = x.shape[0]
    specs, steps = apart_ff_specs(sz, layer, 512)
    small = (conv, inner, gate, skip, x, gains, grad, w_out)
    outs = (((tokens, sz.width), BF16), ((tokens, sz.width), BF16)) + apart_mixer_outs(sz, tokens, blocks)
    return pl.pallas_call(
        functools.partial(apart_turn_kernel, sz, steps),
        grid=(2 * steps,),
        out_shape=tuple(jax.ShapeDtypeStruct(shape, kind) for shape, kind in outs),
        in_specs=[apart_full(entry.shape) for entry in small] + specs,
        out_specs=tuple(apart_full(shape) for shape, kind in outs),
        scratch_shapes=[
            pltpu.VMEM((sz.channels, tokens), F32),
            pltpu.VMEM((sz.channels, tokens), BF16),
            pltpu.VMEM((tokens, sz.width), F32),
            pltpu.VMEM((tokens, sz.width), F32),
            pltpu.VMEM((tokens, sz.width), F32),
        ],
        compiler_params=pltpu.CompilerParams(
            dimension_semantics=("arbitrary",), vmem_limit_bytes=48 * MIB
        ),
        name="token_turn",
    )(*small, *ff)


def apart_input_backward(
    sz, back, through, grad_gate, skip, normed, x, gain, w_in, w_gate, grad_middle, mixer_grad
):
    inner_grad = (skip * through + back.astype(F32)).astype(BF16)
    apart_block_grads(sz, inner_grad, normed, mixer_grad, 0)
    apart_block_grads(sz, grad_gate, normed, mixer_grad, 1)
    parts = []
    for side in range(sz.hid):
        rows = slice(side * sz.padded, (side + 1) * sz.padded)
        parts.append(tn(inner_grad[rows, :], w_in[side]) + tn(grad_gate[rows, :], w_gate[side]))
    normal, inv = normalize(x)
    result, gain_grad = norm_back(jnp.concatenate(parts, axis=1), normal, inv, gain)
    return grad_middle + result, gain_grad


def apart_backward_kernel(
    sz,
    steps,
    back_ref,
    through_ref,
    gate_grad_ref,
    skip_ref,
    normed_ref,
    x_ref,
    gain_ref,
    w_in,
    w_gate,
    grad_middle_ref,
    normed_two,
    middle_ref,
    summed_ref,
    gate_ref,
    mixed_ref,
    low_gain,
    w_out,
    up_a,
    down_a,
    up_b,
    down_b,
    input_grad,
    input_gain,
    grad_ff,
    grad_middle,
    mixer_grad,
    grad_gate,
    grad_summed,
    grad_conv,
    gain_grad,
    grad_next,
    total,
):
    index = pl.program_id(0)

    @pl.when(index == 0)
    def _():
        result, input_gain[...] = apart_input_backward(
            sz,
            back_ref[...],
            through_ref[...],
            gate_grad_ref[...],
            skip_ref[...],
            normed_ref[...],
            x_ref[...],
            gain_ref[0:1, :],
            w_in,
            w_gate,
            grad_middle_ref[...],
            input_grad,
        )
        grad_next[...] = result
        grad_ff[...] = result.astype(BF16)
        total[...] = jnp.zeros_like(total)

    def accumulate(up_ref, down_ref):
        apart_ff_backward_tile(normed_two[...], grad_ff[...], up_ref, down_ref, total, None)

    pl.when(index < steps)(lambda: accumulate(up_a, down_a))
    pl.when(index >= steps)(lambda: accumulate(up_b, down_b))

    @pl.when(index == 2 * steps - 1)
    def _():
        outs = (grad_middle, mixer_grad, grad_gate, grad_summed, grad_conv, gain_grad)
        apart_mixer_backward(
            sz,
            grad_next[...],
            middle_ref[...],
            total[...],
            low_gain[1:2, :],
            mixed_ref,
            summed_ref,
            gate_ref,
            w_out,
            outs,
        )


def apart_input_outs(sz, blocks):
    size = sz.width // blocks
    return (((2, blocks, sz.channels // blocks, size), BF16), ((1, sz.width), F32))


def apart_backward(
    sz,
    layer,
    blocks,
    back,
    through,
    gate_grad,
    skip,
    normed,
    x,
    gains,
    w_in,
    w_gate,
    grad_middle,
    normed_two,
    middle,
    summed,
    gate,
    mixed,
    low_gains,
    w_out,
    ff,
):
    tokens = x.shape[0]
    specs, steps = apart_ff_specs(sz, layer, 512)
    small = (
        back,
        through,
        gate_grad,
        skip,
        normed,
        x,
        gains,
        w_in,
        w_gate,
        grad_middle,
        normed_two,
        middle,
        summed,
        gate,
        mixed,
        low_gains,
        w_out,
    )
    outs = (
        apart_input_outs(sz, blocks) + (((tokens, sz.width), BF16),) + apart_mixer_outs(sz, tokens, blocks)
    )
    return pl.pallas_call(
        functools.partial(apart_backward_kernel, sz, steps),
        grid=(2 * steps,),
        out_shape=tuple(jax.ShapeDtypeStruct(shape, kind) for shape, kind in outs),
        in_specs=[apart_full(entry.shape) for entry in small] + specs,
        out_specs=tuple(apart_full(shape) for shape, kind in outs),
        scratch_shapes=[
            pltpu.VMEM((tokens, sz.width), F32),
            pltpu.VMEM((tokens, sz.width), F32),
        ],
        compiler_params=pltpu.CompilerParams(
            dimension_semantics=("arbitrary",), vmem_limit_bytes=48 * MIB
        ),
        name="token_backward",
    )(*small, *ff)


def apart_last_kernel(
    sz,
    back_ref,
    through_ref,
    gate_grad_ref,
    skip_ref,
    normed_ref,
    x_ref,
    gain_ref,
    w_in,
    w_gate,
    grad_middle_ref,
    input_grad,
    input_gain,
    grad_in,
):
    grad_in[...], input_gain[...] = apart_input_backward(
        sz,
        back_ref[...],
        through_ref[...],
        gate_grad_ref[...],
        skip_ref[...],
        normed_ref[...],
        x_ref[...].astype(F32),
        gain_ref[0:1, :],
        w_in,
        w_gate,
        grad_middle_ref[...],
        input_grad,
    )


def apart_last(sz, blocks, *args):
    tokens = args[5].shape[0]
    outs = apart_input_outs(sz, blocks) + (((tokens, sz.width), F32),)
    return pl.pallas_call(
        functools.partial(apart_last_kernel, sz),
        out_shape=tuple(jax.ShapeDtypeStruct(shape, kind) for shape, kind in outs),
        in_specs=[whole()] * len(args),
        out_specs=(whole(),) * len(outs),
        compiler_params=pltpu.CompilerParams(vmem_limit_bytes=32 * MIB),
        name="last_projection",
    )(*args)


def apart_ff_grads_kernel(normed_ref, grad_ref, up_ref, down_ref, out_ref, hidden, grad_gate, grad_up):
    tokens = normed_ref.shape[0]
    chunk = 256
    for start in range(0, tokens, chunk):
        rows = pl.ds(start, chunk)
        normed = normed_ref[rows, :]
        gate = nn(normed, up_ref[0])
        up = nn(normed, up_ref[1])
        through = nn(grad_ref[rows, :], down_ref[...])
        value, slope = gelu_parts(gate)
        hidden[rows, :] = (value * up).astype(BF16)
        grad_gate[rows, :] = (slope * up * through).astype(BF16)
        grad_up[rows, :] = (value * through).astype(BF16)
    out_ref[0] = tn(normed_ref[...], grad_gate[...]).astype(BF16)
    out_ref[1] = tn(normed_ref[...], grad_up[...]).astype(BF16)
    out_ref[2] = tn(grad_ref[...], hidden[...]).astype(BF16)


def apart_ff_grads(normed, grad, up, down):
    tokens, width = normed.shape
    units = down.shape[1]
    return pl.pallas_call(
        apart_ff_grads_kernel,
        out_shape=jax.ShapeDtypeStruct((3, width, units), BF16),
        in_specs=[whole()] * 4,
        out_specs=whole(),
        scratch_shapes=[pltpu.VMEM((tokens, units), BF16)] * 3,
        compiler_params=pltpu.CompilerParams(vmem_limit_bytes=48 * MIB),
        name="ff_weight_grads",
    )(normed, grad, up, down)


def apart_row_exchange_kernel(rows, parts, *refs):
    sources, targets, sems = refs[:parts], refs[parts : 2 * parts], refs[2 * parts]
    row = lax.axis_index("rows")
    col = lax.axis_index("hid")
    barrier = pltpu.get_barrier_semaphore()

    def greet(step, carry):
        peer = lax.rem(row + step, rows)
        pl.semaphore_signal(barrier, inc=1, device_id=(peer, col), device_id_type=MESH)
        return carry

    lax.fori_loop(1, rows, greet, 0)
    for part in range(parts):
        pltpu.make_async_copy(
            sources[part].at[row], targets[part].at[row], sems.at[part, 2]
        ).start()
    pl.semaphore_wait(barrier, rows - 1)

    def post(step, carry):
        peer = lax.rem(row + step, rows)
        for part in range(parts):
            pltpu.make_async_remote_copy(
                src_ref=sources[part].at[peer],
                dst_ref=targets[part].at[row],
                send_sem=sems.at[part, 0],
                recv_sem=sems.at[part, 1],
                device_id=(peer, col),
                device_id_type=MESH,
            ).start()
        return carry

    lax.fori_loop(1, rows, post, 0)
    for part in range(parts):
        pltpu.make_async_copy(
            sources[part].at[0], targets[part].at[0], sems.at[part, 2]
        ).wait()
        span = pl.ds(0, rows - 1)
        pltpu.make_async_remote_copy(
            src_ref=sources[part].at[span],
            dst_ref=targets[part].at[span],
            send_sem=sems.at[part, 0],
            recv_sem=sems.at[part, 1],
            device_id=(lax.rem(row + 1, rows), col),
            device_id_type=MESH,
        ).wait()


def apart_row_exchange(arrays, rows, cid):
    parts = len(arrays)
    return pl.pallas_call(
        functools.partial(apart_row_exchange_kernel, rows, parts),
        out_shape=tuple(jax.ShapeDtypeStruct(entry.shape, entry.dtype) for entry in arrays),
        in_specs=[pl.BlockSpec(memory_space=pl.ANY)] * parts,
        out_specs=(pl.BlockSpec(memory_space=pl.ANY),) * parts,
        scratch_shapes=[pltpu.SemaphoreType.DMA((parts, 3))],
        compiler_params=pltpu.CompilerParams(collective_id=cid, has_side_effects=True),
        name="row_exchange",
    )(*arrays)


def apart_swap(value):
    return lax.ppermute(value, "hid", [(0, 1), (1, 0)])


def apart_both_halves(own, axis):
    other = apart_swap(own)
    low = lax.axis_index("hid") == 0
    return jnp.concatenate([jnp.where(low, own, other), jnp.where(low, other, own)], axis=axis)


def apart_own_tokens(part):
    tokens = part.shape[0] // 2
    side = lax.axis_index("hid")
    keep = lax.dynamic_slice_in_dim(part, side * tokens, tokens, 0)
    other = apart_swap(lax.dynamic_slice_in_dim(part, (1 - side) * tokens, tokens, 0))
    low = side == 0
    return jnp.concatenate([jnp.where(low, keep, other), jnp.where(low, other, keep)], axis=1)


def apart_own_features(part):
    half = part.shape[1] // 2
    side = lax.axis_index("hid")
    keep = lax.dynamic_slice_in_dim(part, side * half, half, 1)
    other = apart_swap(lax.dynamic_slice_in_dim(part, (1 - side) * half, half, 1))
    low = side == 0
    return jnp.concatenate([jnp.where(low, keep, other), jnp.where(low, other, keep)], axis=0)


def apart_padded_mixer(sz, mixer):
    layers, kinds, blocks, size, _ = mixer.shape
    chan_first = jnp.concatenate([jnp.swapaxes(mixer[:, :2], 3, 4), mixer[:, 2:]], axis=1)
    grouped = chan_first.reshape(layers, kinds, blocks, size // sz.chans, sz.chans, size)
    grouped = jnp.pad(grouped, ((0, 0),) * 4 + ((0, sz.piece - sz.chans), (0, 0)))
    grouped = grouped.reshape(layers, kinds, blocks, -1, size)
    parts = [
        jnp.pad(grouped[:, :, block], ((0, 0),) * 3 + ((block * size, (blocks - 1 - block) * size),))
        for block in range(blocks)
    ]
    return jnp.concatenate(parts, axis=2)


def apart_padded_channels(sz, values):
    lead = values.shape[:-1]
    grouped = values.reshape(lead + (sz.rows, sz.chans))
    grouped = jnp.pad(grouped, ((0, 0),) * (len(lead) + 1) + ((0, sz.piece - sz.chans),))
    return grouped.reshape(lead + (sz.padded,))


def apart_envelopes(sz):
    row = lax.axis_index("rows")
    first_chan = lax.axis_index("hid") * sz.half + row * sz.chans
    channels = first_chan + jnp.arange(sz.piece, dtype=jnp.int32)
    fraction = (channels * 37 % sz.width).astype(F32) / (sz.width - 1)
    start_log = math.log(1.0 / 40.0)
    rate = jnp.exp(start_log + (math.log(1.5 / sz.length) - start_log) * fraction)
    steps = jnp.arange(sz.length, dtype=jnp.int32).astype(F32)
    decay = jnp.exp(-steps[None, :] * rate[:, None])
    shape = decay * lax.rsqrt(2.0 * jnp.sum(decay * decay, axis=1, keepdims=True))
    return jnp.concatenate([shape, shape * (steps > 0)[None, :]], axis=0)


def apart_plane_gather(value):
    size = lax.axis_size("rows")
    for bit in (1, 2):
        other = lax.ppermute(value, "rows", [(r, r ^ bit) for r in range(size)])
        value = jnp.concatenate([value, other], axis=0)
    return jnp.concatenate([value, apart_swap(value)], axis=0)


def apart_on_device(hidden_in, d_out, gains, mixer, skip, filters, gate_up, down):
    layers = gate_up.shape[0]
    rows = lax.axis_size("rows")
    hid = lax.axis_size("hid")
    width = gate_up.shape[2]
    hidden = gate_up.shape[3] * hid
    blocks = mixer.shape[2] * hid
    block_size = mixer.shape[3]
    sz = apart_Sizes(rows, hid, width, hidden, hidden_in.shape[0] * rows)
    row = lax.axis_index("rows")

    x = apart_own_tokens(hidden_in)
    gains_all = apart_both_halves(gains, 2)
    skip_all = apart_both_halves(apart_padded_channels(sz, skip), 1)[:, :, None]
    weights = apart_both_halves(apart_padded_mixer(sz, mixer)[:, :, None], 2)
    gate_up_b = apart_swap(gate_up)
    down_b = apart_swap(down)
    ff = (gate_up, down, gate_up_b, down_b)
    grad_out = apart_own_tokens(d_out)

    tables = dft_tables(sz.length)
    pos = jnp.asarray(position_table(sz.length).T, F32).astype(BF16)
    env = apart_envelopes(sz)
    taps = lax.dynamic_slice_in_dim(filters, row * sz.chans, sz.chans, 3)
    taps = jnp.pad(taps, ((0, 0),) * 3 + ((0, sz.piece - sz.chans),))
    taps = jnp.swapaxes(taps, 2, 3).reshape(layers, 2 * sz.piece, ORDER).astype(BF16)

    normed, inner, gate = apart_first(sz, x, gains_all[0], weights[0, 0], weights[0, 1])
    stored = []
    for layer in range(layers):
        conv, filt_spec, sig_spec = apart_conv_forward(sz, inner, taps[layer], pos, env, tables, 0)
        stored.append(dict(x=x, normed=normed, inner=inner, gate=gate, f=filt_spec, s=sig_spec))
        if layer < layers - 1:
            summed, mixed, middle, normed_two, x, normed, next_inner, next_gate = apart_forward(
                sz,
                layer,
                conv,
                inner,
                gate,
                skip_all[layer],
                x,
                gains_all[layer],
                gains_all[layer + 1],
                weights[layer, 2],
                weights[layer + 1, 0],
                weights[layer + 1, 1],
                ff,
            )
            stored[-1].update(summed=summed, mixed=mixed, middle=middle, normed_two=normed_two)
            inner, gate = next_inner, next_gate

    top = layers - 1
    hidden_out, normed_two, *rest = apart_turn(
        sz,
        top,
        blocks,
        conv,
        inner,
        gate,
        skip_all[top],
        x,
        gains_all[top],
        grad_out,
        weights[top, 2],
        ff,
    )
    stored[top].update(normed_two=normed_two)
    grad_ff = grad_out
    units = sz.hidden // hid // 4
    unit_start = lax.rem(row, 4) * units
    ff_parts, mixer_parts, gain_parts, skip_parts, taps_parts = [], [], [], [], []
    for layer in reversed(range(layers)):
        kept = stored[layer]
        grad_middle, out_grad, grad_gate, grad_summed, grad_conv, gain_two = rest
        ff_parts.insert(
            0,
            apart_ff_grads(
                apart_plane_gather(kept["normed_two"]),
                apart_plane_gather(grad_ff),
                lax.dynamic_slice_in_dim(gate_up[layer], unit_start, units, 2),
                lax.dynamic_slice_in_dim(down[layer], unit_start, units, 1),
            ),
        )
        back, taps_grad = apart_conv_backward(
            sz, grad_conv, kept["f"], kept["s"], taps[layer], pos, env, tables, 1
        )
        skip_parts.insert(0, jnp.sum(grad_summed * kept["inner"].astype(F32), axis=1))
        taps_parts.insert(0, taps_grad)
        common = (
            back,
            grad_summed,
            grad_gate,
            skip_all[layer],
            kept["normed"],
            kept["x"],
            gains_all[layer],
            weights[layer, 0],
            weights[layer, 1],
            grad_middle,
        )
        if layer > 0:
            low = stored[layer - 1]
            in_grad, gain_one, grad_ff, *rest = apart_backward(
                sz,
                layer - 1,
                blocks,
                *common,
                low["normed_two"],
                low["middle"],
                low["summed"],
                low["gate"],
                low["mixed"],
                gains_all[layer - 1],
                weights[layer - 1, 2],
                ff,
            )
        else:
            in_grad, gain_one, grad_in = apart_last(sz, blocks, *common)
        mixer_parts.insert(0, jnp.concatenate([in_grad, out_grad], axis=0))
        gain_parts.insert(0, jnp.concatenate([gain_one, gain_two], axis=0))

    piece_rows = width // rows
    padded_rows = round_up(piece_rows, 16)
    pieces = jnp.stack(ff_parts).reshape(layers, 3, rows, piece_rows, units)
    pieces = jnp.pad(pieces, ((0, 0),) * 3 + ((0, padded_rows - piece_rows), (0, 0)))
    pieces = jnp.moveaxis(pieces, 2, 0)
    (arrived,) = apart_row_exchange((pieces,), rows, 2)
    arrived = arrived.reshape(rows // 4, 4, layers, 3, padded_rows, units)[:, :, :, :, :piece_rows]
    summed_ff = jnp.sum(arrived.astype(F32), axis=0)
    summed_ff = jnp.moveaxis(summed_ff, 0, 3).reshape(layers, 3, piece_rows, 4 * units)

    mixers = jnp.stack(mixer_parts).reshape(layers, 3, blocks, -1, sz.piece, block_size)
    mixers = mixers[:, :, :, :, : sz.chans].reshape(layers, 3, blocks, block_size, block_size)
    small = jnp.concatenate(
        [jnp.stack(gain_parts).reshape(-1), jnp.stack(skip_parts).reshape(-1)]
    )
    mixers, small = lax.psum((mixers.astype(F32), small), ("rows", "hid"))
    side = lax.axis_index("hid")
    mixers = lax.dynamic_slice_in_dim(mixers, side * (blocks // hid), blocks // hid, 2)
    mixers = jnp.concatenate([jnp.swapaxes(mixers[:, :2], 3, 4), mixers[:, 2:]], axis=1)
    gain_size = layers * 2 * width
    gain_out = lax.dynamic_slice_in_dim(
        small[:gain_size].reshape(layers, 2, width), side * sz.half, sz.half, 2
    )
    skip_out = small[gain_size:].reshape(layers, hid, rows, sz.piece)[..., : sz.chans]
    skip_out = lax.dynamic_index_in_dim(skip_out, side, 1, False).reshape(layers, sz.half)
    taps_out = jnp.stack(taps_parts).reshape(layers, 2, sz.piece, ORDER)[:, :, : sz.chans]
    taps_out = lax.all_gather(taps_out, "rows", axis=2, tiled=True)
    return (
        apart_own_features(hidden_out),
        apart_own_features(grad_in),
        gain_out,
        mixers,
        skip_out,
        jnp.swapaxes(taps_out, 2, 3),
        summed_ff[:, :2],
        summed_ff[:, 2],
    )


def on_device(*arrays):
    sz = Sizes.of(*arrays)
    return together(sz, *arrays) if sz.fits() else apart_on_device(*arrays)


def solution(mesh):
    placed = (
        P("rows", "hid"),
        P("rows", "hid"),
        P(None, None, "hid"),
        P(None, None, "hid", None, None),
        P(None, "hid"),
        P(None, None, None, "hid"),
        P(None, None, None, "hid"),
        P(None, None, "hid"),
    )
    return jax.shard_map(
        on_device,
        mesh=mesh,
        in_specs=placed,
        out_specs=(
            P("rows", "hid"),
            P("rows", "hid"),
            P(None, None, "hid"),
            P(None, None, "hid", None, None),
            P(None, "hid"),
            P(None, None, None, "hid"),
            P(None, None, "rows", "hid"),
            P(None, "rows", "hid"),
        ),
        check_vma=False,
    )
```

```python
import functools
import math

import jax
import jax.numpy as jnp
import numpy as np
from jax import lax
from jax.experimental import pallas as pl
from jax.experimental.pallas import tpu as pltpu
from jax.sharding import PartitionSpec as P

ORDER = 128
SEQ_LEN = 8192
LANES = 128
NORM_EPS = 1e-05
DECAY = 0.02
MESH = pl.DeviceIdType.MESH
BF16 = jnp.bfloat16
F32 = jnp.float32
MIB = 2**20
GELU_C = math.sqrt(2.0 / math.pi)


def round_up(value, step):
    return -(-value // step) * step


def whole():
    return pl.BlockSpec(memory_space=pltpu.VMEM)


def nn(a, b):
    return lax.dot_general(a, b, (((1,), (0,)), ((), ())), preferred_element_type=F32)


def nt(a, b):
    return lax.dot_general(a, b, (((1,), (1,)), ((), ())), preferred_element_type=F32)


def tn(a, b):
    return lax.dot_general(a, b, (((0,), (0,)), ((), ())), preferred_element_type=F32)


def position_table(length):
    half_order = ORDER // 2
    index_list = np.arange(half_order)
    multiple = 1 + index_list * index_list * (length // 4) // (half_order * half_order)
    phase = (np.arange(length)[:, None] * multiple[None, :] % length) * (2.0 * math.pi / length)
    return np.concatenate([np.sin(phase), np.cos(phase)], axis=1)


def dft_tables(length):
    blocks = length // LANES
    size = 2 * length
    outer = 2 * blocks
    k = np.arange(outer)
    n = np.arange(blocks)
    m = np.arange(LANES)
    angle = 2.0 * math.pi * (np.outer(k, n) % outer) / outer
    outer_fwd = np.concatenate([np.cos(angle), -np.sin(angle)], axis=0)
    outer_inv = np.concatenate([np.cos(angle), -np.sin(angle)], axis=0).T / size
    angle = 2.0 * math.pi * (np.outer(m, m) % LANES) / LANES
    cos, sin = np.cos(angle), np.sin(angle)
    inner_fwd = np.block([[cos, -sin], [sin, cos]])
    inner_inv = np.block([[cos, sin], [-sin, cos]])
    angle = 2.0 * math.pi * np.outer(k, m) / size
    twist = np.concatenate([np.cos(angle), np.sin(angle)], axis=1)
    half = lambda table: jnp.asarray(table, F32).astype(BF16)
    return (half(outer_fwd), half(outer_inv), half(inner_fwd), half(inner_inv), jnp.asarray(twist, F32))


def normalize(values):
    mean = jnp.mean(values, axis=1, keepdims=True)
    square = jnp.mean(values * values, axis=1, keepdims=True)
    inv = lax.rsqrt(square - mean * mean + NORM_EPS)
    return (values - mean) * inv, inv


def norm_back(grad, normal, inv, gain):
    scaled = grad * gain
    mean = jnp.mean(scaled, axis=1, keepdims=True)
    cross = jnp.mean(scaled * normal, axis=1, keepdims=True)
    return inv * (scaled - mean - normal * cross), jnp.sum(grad * normal, axis=0, keepdims=True)


def gelu_parts(gate):
    square = gate * gate
    tanh = jnp.tanh(GELU_C * gate * (1.0 + 0.044715 * square))
    half = 0.5 * (1.0 + tanh)
    value = gate * half
    slope = half + 0.5 * gate * (1.0 - tanh * tanh) * (GELU_C * (1.0 + 3.0 * 0.044715 * square))
    return value, slope


class Sizes:
    def __init__(self, rows, hid, tokens, width, hidden, layers, blocks):
        self.rows, self.hid, self.width, self.layers = rows, hid, width, layers
        self.count = rows * hid
        self.own = tokens // self.count
        self.half = width // hid
        self.units = hidden // hid
        self.blocks = blocks
        self.size = width // blocks
        self.side_blocks = blocks // hid
        self.couple = 2 * width // self.count
        self.big = round_up(self.couple // 2, 16)
        self.small = self.couple - self.big
        self.length = min(SEQ_LEN, tokens)
        self.seqs = tokens // self.length
        self.steps = self.length // LANES
        self.outer = 2 * self.steps
        self.pairs = self.seqs * self.big
        self.group = 4
        self.peers = rows // self.group
        self.part = self.units // self.group
        self.depth = width // rows
        self.deep = round_up(self.depth, 16)
        self.deeps = tuple(
            round_up(-(-rows_needed // rows), 16)
            for rows_needed in (3 * (layers - 1) * self.size, 2 * self.size + 16)
        )
        self.late_rows = round_up(-(-(self.size + 16) // rows), 16)
        self.taps_rows = round_up(2 * self.big + 1, 16)


    @classmethod
    def of(cls, hidden_in, d_out, gains, mixer, skip, filters, gate_up, down):
        rows, hid = lax.axis_size("rows"), lax.axis_size("hid")
        layers, _, width, units = gate_up.shape
        tokens = hidden_in.shape[0] * rows
        return cls(rows, hid, tokens, width, units * hid, layers, mixer.shape[2] * hid)


    def fits(self):
        whole_tiles = self.small > 0 and self.small % 16 == 0 and self.rows % 8 == 0
        whole_tiles = whole_tiles and self.own == LANES and self.depth % 16 == 0
        whole_tiles = whole_tiles and self.peers == 4 and self.layers == 2 and self.seqs == 1
        whole_tiles = whole_tiles and all(self.size % deep == 0 for deep in self.deeps)
        total = 0
        for spec in layout(self)[1]:
            size = jnp.dtype(spec.dtype).itemsize
            *lead, rows, lanes = spec.shape
            total += math.prod(lead) * round_up(rows, 32 // size) * round_up(lanes, LANES) * size
        return whole_tiles and total <= 60 * MIB


class Links:
    def __init__(self, sz, sems, local_sems):
        self.sz, self.sems, self.local_sems = sz, sems, local_sems
        self.used = 0
        self.used_local = 0
        self.row = lax.axis_index("rows")
        self.col = lax.axis_index("hid")
        self.plane = lax.rem(self.row, sz.peers)
        self.line = self.row // sz.peers

    def pair(self):
        first = self.used
        self.used += 2
        return self.sems.at[first], self.sems.at[first + 1]

    def copy(self, source, target, pair, row, col):
        return pltpu.make_async_remote_copy(
            src_ref=source,
            dst_ref=target,
            send_sem=pair[0],
            recv_sem=pair[1],
            device_id=(row, col),
            device_id_type=MESH,
        )

    def sibling(self, source, target):
        copy = self.copy(source, target, self.pair(), self.row, self.sz.hid - 1 - self.col)
        copy.start()
        return copy

    def load(self, source, target):
        copy = pltpu.make_async_copy(source, target, self.local_sems.at[self.used_local])
        self.used_local += 1
        copy.start()
        return copy

    def groups(self, count, me, row_of, source_of, target):
        pair = self.pair()

        def post(step, carry):
            member = lax.rem(me + step, count)
            self.copy(source_of(member), target, pair, row_of(member), self.col).start()
            return carry

        lax.fori_loop(1, count, post, 0)
        return pair

    def in_plane(self, source_of, target):
        row_of = lambda member: self.line * self.sz.peers + member
        return self.groups(self.sz.peers, self.plane, row_of, source_of, target)

    def in_line(self, source_of, target):
        row_of = lambda member: member * self.sz.peers + self.plane
        return self.groups(self.sz.group, self.line, row_of, source_of, target)

    def in_rows(self, source_of, target):
        return self.groups(self.sz.rows, self.row, lambda member: member, source_of, target)

    def wait(self, pair, span):
        self.copy(span, span, pair, self.row, self.sz.hid - 1 - self.col).wait()


class Plane:
    def __init__(self, links):
        self.links = links
        self.me = links.plane
        along_x = self.me + 1 - 2 * lax.rem(self.me, 2)
        along_y = self.me + 2 - 4 * (self.me // 2)
        self.near = (along_x, along_y)
        self.far = (along_y, along_x)
        self.across = 3 - self.me

    def send(self, copies):
        links = self.links
        pair = links.pair()
        for source, target, member in copies:
            row = links.line * links.sz.peers + member
            links.copy(source, target, pair, row, links.col).start()
        return pair


class PlaneSum(Plane):
    def __init__(self, links, source, first, give, second):
        super().__init__(links)
        self.source, self.first, self.give, self.second = source, first, give, second

    def start(self):
        copies = []
        for half in range(2):
            for which, member in enumerate((self.near[half], self.across)):
                target = self.first.at[half, which]
                copies.append((self.source(member, half), target, self.near[half]))
        self.pair = self.send(copies)

    def middle(self):
        self.links.wait(self.pair, self.first)
        copies = []
        for half in range(2):
            theirs = self.source(self.far[half], half)[...].astype(F32)
            self.give[half] = (theirs + self.first[half, 1].astype(F32)).astype(BF16)
            mine = self.source(self.me, half)[...].astype(F32)
            self.first[half, 0] = (mine + self.first[half, 0].astype(F32)).astype(BF16)
            copies.append((self.give.at[half], self.second.at[half], self.far[half]))
        self.pair = self.send(copies)

    def end(self):
        self.links.wait(self.pair, self.second)

    def sums(self):
        for half in range(2):
            total = self.first[half, 0].astype(F32) + self.second[half].astype(F32)
            self.second[half] = total.astype(BF16)
        count = self.links.sz.group // 2
        return lambda member: self.second.at[member // count, lax.rem(member, count)]


class PlaneSpread(Plane):
    def __init__(self, links, place, span):
        super().__init__(links)
        self.place, self.span = place, span

    def start(self):
        copies = []
        for half in range(2):
            here = self.place(self.me, half)
            copies.append((here, here, self.near[half]))
        self.pair = self.send(copies)

    def middle(self):
        self.links.wait(self.pair, self.span(1))
        copies = []
        for half in range(2):
            for member in (self.me, self.near[half]):
                here = self.place(member, half)
                copies.append((here, here, self.far[half]))
        self.pair = self.send(copies)

    def end(self):
        self.links.wait(self.pair, self.span(2))


LOAD_BUFFERS = ("mine", "give", "got", "first", "second_give", "second", "line_in", "out")


class Payload:
    def __init__(self, sz, b, links, index, output):
        self.sz, self.links, self.output = sz, links, output
        self.deep = sz.deeps[index]
        for name in LOAD_BUFFERS:
            setattr(self, name, getattr(b, "load_" + name)[index])
        half = lambda which: pl.ds(which * (sz.group // 2), sz.group // 2)
        self.plane = PlaneSum(
            links,
            lambda member, which: self.mine.at[member, half(which)],
            self.first,
            self.second_give,
            self.second,
        )
        self.spread = PlaneSpread(
            links,
            lambda member, which: self.got.at[member, half(which)],
            lambda count: self.got.at[pl.ds(0, count)],
        )
        self.half = half

    def matrix(self, place, values):
        sz = self.sz
        low = lax.axis_index("hid") == 0
        left = jnp.concatenate(values[: sz.side_blocks], axis=1)
        right = jnp.concatenate(values[sz.side_blocks :], axis=1)
        mine = jnp.where(low, left, right).astype(BF16)
        give = jnp.where(low, right, left).astype(BF16)
        count = sz.size // self.deep
        for part in range(count):
            index = place * count + part
            rows = slice(part * self.deep, (part + 1) * self.deep)
            self.mine[index // sz.group, index % sz.group] = mine[rows, :]
            self.give[index // sz.group, index % sz.group] = give[rows, :]

    def rows16(self, place, mine, give):
        index = place * (self.sz.size // self.deep)
        self.mine[index // self.sz.group, index % self.sz.group, 0:16] = mine.astype(BF16)
        self.give[index // self.sz.group, index % self.sz.group, 0:16] = give.astype(BF16)

    def to_partner(self):
        self.copy = self.links.sibling(self.give, self.got)

    def to_plane(self):
        done(self.copy)
        self.mine[...] = (self.mine[...].astype(F32) + self.got[...].astype(F32)).astype(BF16)
        self.plane.start()

    def middle(self):
        self.plane.middle()

    def to_line(self):
        self.plane.end()
        self.sums = self.plane.sums()
        links = self.links
        self.pair = links.in_line(self.sums, self.line_in.at[links.line])

    def back_line(self):
        links, sz = self.links, self.sz
        links.wait(self.pair, self.line_in.at[pl.ds(0, sz.group - 1)])
        self.line_in[links.line] = self.sums(links.line)[...]
        total = self.line_in[0].astype(F32)
        for member in range(1, sz.group):
            total += self.line_in[member].astype(F32)
        self.out[...] = total.astype(BF16)
        self.got[links.plane, links.line] = self.out[...]
        self.pair = links.in_line(lambda member: self.out, self.got.at[links.plane, links.line])

    def back_plane(self):
        self.links.wait(self.pair, self.got.at[0, pl.ds(0, self.sz.group - 1)])
        self.spread.start()

    def finish(self):
        self.spread.end()
        return self.links.load(self.got, self.output)


def greet_all(sz):
    me = lax.axis_index("rows") * sz.hid + lax.axis_index("hid")
    barrier = pltpu.get_barrier_semaphore()

    def greet(step, carry):
        peer = lax.rem(me + step, sz.count)
        pl.semaphore_signal(
            barrier,
            inc=1,
            device_id=(peer // sz.hid, lax.rem(peer, sz.hid)),
            device_id_type=MESH,
        )
        return carry

    lax.fori_loop(1, sz.count, greet, 0)
    return barrier


class Exchange:
    def __init__(self, sz, links):
        self.sz, self.links = sz, links
        self.odd = lax.rem(links.row, 2)
        self.token = links.row * sz.hid + links.col

    def channels(self, row, col, size):
        sz = self.sz
        start = col * sz.half + (row // 2) * sz.couple + lax.rem(row, 2) * sz.big
        return pl.ds(pl.multiple_of(start, 16), size)

    def block(self, token, size):
        return pl.ds(pl.multiple_of(token * self.sz.big, 16), size)

    def far_first(self):
        line = self.links.line
        odd = lax.rem(line, 2)
        across = 2 * (1 - line // 2)
        return across + odd, across + 1 - odd, line + 1 - 2 * odd, line

    def by_size(self, body):
        pl.when(self.odd == 0)(lambda: body(self.sz.big))
        pl.when(self.odd == 1)(lambda: body(self.sz.small))

    def local(self):
        local = self.links.local_sems.at[self.links.used_local]
        self.links.used_local += 1
        return local

    def to_owners(self, source, target):
        sz, links = self.sz, self.links
        pair, local = links.pair(), self.local()

        def own(size):
            pltpu.make_async_copy(
                source.at[self.channels(links.row, links.col, size)],
                target.at[self.block(self.token, size)],
                local,
            ).start()

        self.by_size(own)
        half = sz.peers * sz.hid // 2
        first = (links.plane // 2) * sz.hid + links.col

        for turn, line in enumerate(self.far_first()):

            def post(step, carry):
                index = lax.rem(first + step, half)
                col = lax.rem(index, sz.hid)
                for odd, size in ((0, sz.big), (1, sz.small)):
                    row = line * sz.peers + 2 * (index // sz.hid) + odd

                    def send():
                        links.copy(
                            source.at[self.channels(row, col, size)],
                            target.at[self.block(self.token, size)],
                            pair,
                            row,
                            col,
                        ).start()

                    if turn < sz.group - 1:
                        send()
                    else:
                        pl.when((step > 0) | (self.odd != odd))(send)
                return carry

            lax.fori_loop(0, half, post, 0)
        return pair, local

    def to_tokens(self, source, target):
        sz, links = self.sz, self.links
        pair, local = links.pair(), self.local()

        def send(size):
            mine = target.at[self.channels(links.row, links.col, size)]
            pltpu.make_async_copy(source.at[self.block(self.token, size)], mine, local).start()

            devices = sz.peers * sz.hid
            first = links.plane * sz.hid + links.col

            for turn, line in enumerate(self.far_first()):

                def post(step, carry):
                    index = lax.rem(first + step, devices)
                    row, col = line * sz.peers + index // sz.hid, lax.rem(index, sz.hid)
                    peer = row * sz.hid + col
                    links.copy(source.at[self.block(peer, size)], mine, pair, row, col).start()
                    return carry

                lax.fori_loop(0 if turn < sz.group - 1 else 1, devices, post, 0)

        self.by_size(send)
        return pair, local

    def wait(self, tokens, by_tokens, by_owners, sent_by_tokens):
        sz, links = self.sz, self.links
        pair, local = tokens

        def wait(size):
            first = by_owners.at[pl.ds(0, size)]
            pltpu.make_async_copy(first, first, local).wait()
            all_tokens = by_owners.at[pl.ds(0, (sz.count - 1) * size)]
            all_channels = by_tokens.at[pl.ds(0, sz.width - size)]
            sent, came = all_tokens, all_channels
            if sent_by_tokens:
                sent, came = came, sent
            links.copy(came, came, pair, links.row, 1 - links.col).wait_recv()
            links.copy(sent, sent, pair, links.row, 1 - links.col).wait_send()

        self.by_size(wait)

    def owners_wait(self, tokens, source, target):
        self.wait(tokens, source, target, True)

    def tokens_wait(self, tokens, source, target):
        self.wait(tokens, target, source, False)


CHUNK = 8


def place(index, size):
    return pl.ds(pl.multiple_of(index * size, size), size)


def dft(sz, b, source, base, stride, target, unroll=2):
    steps, outer = sz.steps, sz.outer

    def chunk(index, carry):
        cos = b.twist[:, :LANES]
        sin = b.twist[:, LANES:]
        for line in range(CHUNK):
            start = base + index * CHUNK + line
            b.wide[:, line * LANES : (line + 1) * LANES] = source[
                pl.ds(start, steps, stride=stride), :
            ].astype(BF16)
        b.mid[...] = nn(b.outer_fwd[...], b.wide[...])
        for line in range(CHUNK):
            lanes = slice(line * LANES, (line + 1) * LANES)
            real = b.mid[0:outer, lanes]
            imag = b.mid[outer : 2 * outer, lanes]
            rows = slice(line * outer, (line + 1) * outer)
            b.turned[rows, 0:LANES] = (real * cos + imag * sin).astype(BF16)
            b.turned[rows, LANES:] = (imag * cos - real * sin).astype(BF16)
        target[place(index, CHUNK * outer), :] = nn(b.turned[...], b.inner_fwd[...])
        return carry

    lax.fori_loop(0, sz.big // CHUNK, chunk, 0, unroll=unroll)


def inverse_dft(sz, b, target, base, stride, unroll=2):
    steps, outer = sz.steps, sz.outer

    def chunk(index, carry):
        cos = b.twist[:, :LANES]
        sin = b.twist[:, LANES:]
        part = nn(b.flat[place(index, CHUNK * outer), :], b.inner_inv[...])
        for line in range(CHUNK):
            rows = slice(line * outer, (line + 1) * outer)
            lanes = slice(line * LANES, (line + 1) * LANES)
            real = part[rows, :LANES]
            imag = part[rows, LANES:]
            b.mid_half[0:outer, lanes] = (real * cos - imag * sin).astype(BF16)
            b.mid_half[outer : 2 * outer, lanes] = (imag * cos + real * sin).astype(BF16)
        value = nn(b.outer_inv[...], b.mid_half[...])
        for line in range(CHUNK):
            start = base + index * CHUNK + line
            target[pl.ds(start, steps, stride=stride), :] = value[
                :, line * LANES : (line + 1) * LANES
            ]
        return carry

    lax.fori_loop(0, sz.big // CHUNK, chunk, 0, unroll=unroll)


def first_channel(sz):
    row = lax.axis_index("rows")
    return (row // 2) * sz.couple + lax.rem(row, 2) * sz.big


def own_taps(sz, filters):
    start = first_channel(sz)
    chan = lax.broadcasted_iota(jnp.int32, (sz.big, sz.half), 0)
    lane = lax.broadcasted_iota(jnp.int32, (sz.big, sz.half), 1)
    pick = jnp.where(lane == start + chan, 1.0, 0.0).astype(BF16)
    parts = [nt(pick, filters[way].astype(BF16)) for way in range(2)]
    return jnp.concatenate(parts, axis=0).astype(BF16)


def own_envelope(sz, env):
    first_chan = lax.axis_index("hid") * sz.half + first_channel(sz)
    channel = first_chan + lax.broadcasted_iota(jnp.int32, (sz.big, LANES), 0)
    fraction = lax.rem(channel * 37, sz.width).astype(F32) / (sz.width - 1)
    start_log = math.log(1.0 / 40.0)
    rate = jnp.exp(start_log + (math.log(1.5 / sz.length) - start_log) * fraction)
    lane = lax.broadcasted_iota(jnp.int32, (sz.big, LANES), 1)

    def decays(step, power):
        decay = jnp.exp(-(lane + step * LANES).astype(F32) * rate)
        env[0 : sz.big, place(step, LANES)] = decay
        return power + decay * decay

    power = lax.fori_loop(0, sz.steps, decays, jnp.zeros((sz.big, LANES), F32), unroll=4)
    scale = lax.rsqrt(2.0 * jnp.sum(power, axis=1, keepdims=True))

    def scaled(step, carry):
        value = env[0 : sz.big, place(step, LANES)] * scale
        env[0 : sz.big, place(step, LANES)] = value
        env[sz.big :, place(step, LANES)] = jnp.where(lane + step * LANES > 0, value, 0.0)
        return carry

    lax.fori_loop(0, sz.steps, scaled, 0, unroll=4)


def filter_spectrum(sz, b, layer):
    piece, steps, outer = sz.big, sz.steps, sz.outer
    taps = own_taps(sz, b.filters[layer])
    count = 4

    def chunk(index, carry):
        lanes = place(index, count * LANES)
        kernels = nn(taps, b.pos[:, lanes]) * b.env[:, lanes]
        rows = pl.multiple_of(index * count * 2 * piece, 2 * piece)
        for step in range(count):
            b.tall[pl.ds(rows + step * 2 * piece, 2 * piece), :] = kernels[
                :, step * LANES : (step + 1) * LANES
            ]
        return carry

    lax.fori_loop(0, steps // count, chunk, 0, unroll=2)
    spec = b.filt_spec[layer]
    span = sz.big * outer
    for way in range(2):
        dft(sz, b, b.tall, way * piece, 2 * piece, b.spec)
        if way == 0:
            spec[...] = b.spec[0:span, :].astype(BF16)
        else:
            spec[:, :LANES] = (spec[:, :LANES].astype(F32) + b.spec[0:span, :LANES]).astype(BF16)
            spec[:, LANES:] = (spec[:, LANES:].astype(F32) - b.spec[0:span, LANES:]).astype(BF16)


def conv_forward(sz, b, layer, landed):
    b.tall[0 : sz.count * sz.big, :] = landed[...].astype(F32)
    dft(sz, b, b.tall, 0, sz.big, b.spec, True)
    span = sz.big * sz.outer
    filt = b.filt_spec[layer]
    for seq in range(sz.seqs):
        rows = slice(seq * span, (seq + 1) * span)
        re, im = b.spec[rows, :LANES], b.spec[rows, LANES:]
        b.sig_spec[layer][rows, :LANES] = re.astype(BF16)
        b.sig_spec[layer][rows, LANES:] = im.astype(BF16)
        fil_re, fil_im = filt[:, :LANES].astype(F32), filt[:, LANES:].astype(F32)
        b.flat[rows, :LANES] = (re * fil_re - im * fil_im).astype(BF16)
        b.flat[rows, LANES:] = (re * fil_im + im * fil_re).astype(BF16)
    inverse_dft(sz, b, b.tall, 0, sz.big, True)
    b.staged[...] = b.tall[0 : sz.count * sz.big, :].astype(BF16)


def conv_backward(sz, b, layer, landed):
    b.tall[0 : sz.count * sz.big, :] = landed[...].astype(F32)
    dft(sz, b, b.tall, 0, sz.big, b.spec, True)
    span = sz.big * sz.outer
    filt = b.filt_spec[layer]
    for seq in range(sz.seqs):
        rows = slice(seq * span, (seq + 1) * span)
        re, im = b.spec[rows, :LANES], b.spec[rows, LANES:]
        fil_re, fil_im = filt[:, :LANES].astype(F32), filt[:, LANES:].astype(F32)
        b.flat[rows, :LANES] = (re * fil_re + im * fil_im).astype(BF16)
        b.flat[rows, LANES:] = (im * fil_re - re * fil_im).astype(BF16)
    inverse_dft(sz, b, b.tall, 0, sz.big, True)
    b.staged[...] = b.tall[0 : sz.count * sz.big, :].astype(BF16)


def taps_gradient(sz, b, layer, landed, signal):
    span = sz.big * sz.outer
    total_re = jnp.zeros((span, LANES), F32)
    total_im = jnp.zeros((span, LANES), F32)
    for seq in range(sz.seqs):
        rows = slice(seq * span, (seq + 1) * span)
        re, im = b.spec[rows, :LANES], b.spec[rows, LANES:]
        sig = b.sig_spec[layer]
        sig_re, sig_im = sig[rows, :LANES].astype(F32), sig[rows, LANES:].astype(F32)
        total_re += re * sig_re + im * sig_im
        total_im += im * sig_re - re * sig_im
    piece = sz.big
    b.tall[...] = jnp.zeros_like(b.tall)
    for way in range(2):
        b.flat[0:span, :LANES] = total_re.astype(BF16)
        b.flat[0:span, LANES:] = (total_im if way == 0 else -total_im).astype(BF16)
        inverse_dft(sz, b, b.tall, way * piece, 2 * piece)
    taps = own_taps(sz, b.filters[layer])
    count = 4

    def chunk(index, total):
        lanes = place(index, count * LANES)
        rows = pl.multiple_of(index * count * 2 * piece, 2 * piece)
        raw = nn(taps, b.pos[:, lanes])
        grads = jnp.concatenate(
            [b.tall[pl.ds(rows + step * 2 * piece, 2 * piece), :] for step in range(count)],
            axis=1,
        )
        grads = grads * b.env[:, lanes] + (2.0 * DECAY) * raw
        return total + nt(grads.astype(BF16), b.pos[:, lanes])

    start = jnp.zeros((2 * piece, ORDER), F32)
    total = lax.fori_loop(0, sz.steps // count, chunk, start, unroll=2)

    def product(block, products):
        rows = place(block, piece)
        return products + landed[rows, :].astype(F32) * signal[rows, :].astype(F32)

    start = jnp.zeros((piece, LANES), F32)
    products = lax.fori_loop(0, sz.count, product, start, unroll=8)
    column = jnp.sum(products, axis=1, keepdims=True)
    row = jnp.transpose(jnp.broadcast_to(column, (piece, LANES)))[0:8, :]
    b.taps_work[...] = jnp.zeros_like(b.taps_work)
    b.taps_work[0 : sz.big, :] = total[0 : sz.big, :]
    b.taps_work[sz.big : 2 * sz.big, :] = total[piece : piece + sz.big, :]
    b.taps_work[2 * sz.big : 2 * sz.big + 1, 0:piece] = row[0:1, :]


def block_of(sz, block):
    return slice(block * sz.size, (block + 1) * sz.size)


def project(sz, b, layer):
    for block in range(sz.blocks):
        rows = block_of(sz, block)
        part = b.normed[layer][:, rows]
        b.inner[layer][rows, :] = nt(b.mixer[layer, 0, block], part).astype(BF16)
        b.gate[layer][rows, :] = nt(b.mixer[layer, 1, block], part)


def mix(sz, b, layer, conv):
    summed, mixed, middle = b.summed[layer], b.mixed[layer], b.middle[layer]
    summed[...] = conv[...].astype(F32) + b.skip[layer][...] * b.inner[layer][...].astype(F32)
    mixed[...] = (b.gate[layer][...] * summed[...]).astype(BF16)
    for block in range(sz.blocks):
        rows = block_of(sz, block)
        middle[:, rows] = tn(mixed[rows, :], b.mixer[layer, 2, block])
    middle[...] = middle[...] + b.stream[layer][...]


def mixer_gradient(sz, b, kind_row, values, mine, give):
    low = lax.axis_index("hid") == 0
    left = jnp.concatenate(values[: sz.side_blocks], axis=1)
    right = jnp.concatenate(values[sz.side_blocks :], axis=1)
    rows = slice(kind_row * sz.size, (kind_row + 1) * sz.size)
    mine[rows, :] = jnp.where(low, left, right).astype(BF16)
    give[rows, :] = jnp.where(low, right, left).astype(BF16)


def gain_gradient(sz, b, row, value, mine, give):
    low = lax.axis_index("hid") == 0
    left, right = value[:, : sz.half], value[:, sz.half :]
    mine[row : row + 1, :] = jnp.where(low, left, right)
    give[row : row + 1, :] = jnp.where(low, right, left)


def mixer_backward(sz, b, layer, grad_next, total):
    normal, inv = normalize(b.middle[layer][...])
    gain = b.gain[layer, 1:2, :]
    back, gain_grad = norm_back(total, normal, inv, gain)
    result = grad_next + back
    b.grad_middle[...] = result
    b.grad_o[...] = result.astype(BF16)
    for block in range(sz.blocks):
        rows = block_of(sz, block)
        grad_mixed = nt(b.mixer[layer, 2, block], b.grad_o[:, rows])
        b.gate_grad[rows, :] = (grad_mixed * b.summed[layer][rows, :]).astype(BF16)
        through = grad_mixed * b.gate[layer][rows, :]
        b.summed_grad[rows, :] = through
        b.conv_grad[rows, :] = through.astype(BF16)
    return gain_grad


def out_gradient(sz, b, layer):
    return [
        nn(b.mixed[layer][block_of(sz, block), :], b.grad_o[:, block_of(sz, block)])
        for block in range(sz.blocks)
    ]


def in_gradient(sz, b, layer, grads):
    return [
        jnp.transpose(
            nn(grads[block_of(sz, block), :], b.normed[layer][:, block_of(sz, block)])
        )
        for block in range(sz.blocks)
    ]


def input_backward(sz, b, layer, back):
    direct = b.skip[layer][...] * b.summed_grad[...]
    b.inner_grad[...] = (direct + back[...].astype(F32)).astype(BF16)
    for block in range(sz.blocks):
        rows = block_of(sz, block)
        b.grad_sum[0 : sz.own, rows] = tn(b.inner_grad[rows, :], b.mixer[layer, 0, block]) + tn(
            b.gate_grad[rows, :], b.mixer[layer, 1, block]
        )
    normal, inv = normalize(b.stream[layer][...])
    result, gain_grad = norm_back(
        b.grad_sum[0 : sz.own, :], normal, inv, b.gain[layer, 0:1, :]
    )
    return b.grad_middle[...] + result, gain_grad


def ff_forward(sz, b, layer):
    tile = 512
    rows = slice(0, 2 * sz.own)
    b.out_sum[...] = jnp.zeros_like(b.out_sum)

    def body(step, carry):
        lanes = pl.ds(pl.multiple_of(step * tile, tile), tile)
        normed = b.nbuf[layer][rows, :]
        gate = nn(normed, b.up[layer, 0, :, lanes])
        up = nn(normed, b.up[layer, 1, :, lanes])
        value, _ = gelu_parts(gate)
        b.out_sum[...] += nt((value * up).astype(BF16), b.down[layer, :, lanes])
        return carry

    lax.fori_loop(0, sz.units // tile, body, 0)


def ff_backward(sz, b, layer, with_out):
    tile = 512
    rows = slice(0, 2 * sz.own)
    b.grad_sum[...] = jnp.zeros_like(b.grad_sum)
    if with_out:
        b.out_sum[...] = jnp.zeros_like(b.out_sum)

    def body(step, carry):
        lanes = pl.ds(pl.multiple_of(step * tile, tile), tile)
        normed = b.nbuf[layer][rows, :]
        gate = nn(normed, b.up[layer, 0, :, lanes])
        up = nn(normed, b.up[layer, 1, :, lanes])
        through = nn(b.gbuf[layer][rows, :], b.down[layer, :, lanes])
        value, slope = gelu_parts(gate)
        if with_out:
            b.out_sum[...] += nt((value * up).astype(BF16), b.down[layer, :, lanes])
        gate_grad = (slope * up * through).astype(BF16)
        up_grad = (value * through).astype(BF16)
        b.grad_sum[...] += nt(gate_grad, b.up[layer, 0, :, lanes]) + nt(
            up_grad, b.up[layer, 1, :, lanes]
        )
        return carry

    lax.fori_loop(0, sz.units // tile, body, 0)


def ff_gradients(sz, b, layer, links, between=(None, None, None)):
    start = pl.multiple_of(links.line * sz.part, LANES)
    units = pl.ds(start, sz.part)
    chunk = 2 * sz.own

    def body(step, carry):
        rows = pl.ds(pl.multiple_of(step * chunk, chunk), chunk)
        normed = b.nbuf[layer][rows, :]
        gate = nn(normed, b.up[layer, 0, :, units])
        up = nn(normed, b.up[layer, 1, :, units])
        through = nn(b.gbuf[layer][rows, :], b.down[layer, :, units])
        value, slope = gelu_parts(gate)
        b.unit_grad[0, rows, :] = (slope * up * through).astype(BF16)
        b.unit_grad[1, rows, :] = (value * through).astype(BF16)
        b.unit_grad[2, rows, :] = (value * up).astype(BF16)
        return carry

    lax.fori_loop(0, sz.group, body, 0)
    split = sz.width // 2
    moving = []
    for kind in range(3):
        if between[kind] is not None:
            between[kind]()
        left = b.gbuf[layer] if kind == 2 else b.nbuf[layer]

        def part(index, carry):
            lanes = place(index, split)
            b.product[...] = tn(left[:, lanes], b.unit_grad[kind])
            count = split // sz.depth
            for each in range(count):
                line = index * (count // sz.peers) + each // sz.peers
                rows = slice(each * sz.depth, (each + 1) * sz.depth)
                b.pieces[kind, each % sz.peers, line, 0 : sz.depth, :] = b.product[rows, :].astype(
                    BF16
                )
            return carry

        lax.fori_loop(0, 2, part, 0)
        half = lambda which: pl.ds(which * (sz.group // 2), sz.group // 2)
        plane = PlaneSum(
            links,
            lambda member, which, kind=kind: b.pieces.at[kind, member, half(which)],
            b.plane_first[layer].at[kind],
            b.plane_give[layer].at[kind],
            b.plane_second[layer].at[kind],
        )
        plane.start()
        moving.append(plane)
    return moving


def done(copy):
    copy.wait()


class Named:
    pass


def layout(sz):
    layers, own, width = sz.layers, sz.own, sz.width
    wide = 2 * sz.big * sz.steps
    late = sz.late_rows * sz.rows
    per_layer = dict(
        stream=((own, width), F32),
        normed=((own, width), BF16),
        inner=((width, own), BF16),
        gate=((width, own), F32),
        summed=((width, own), F32),
        mixed=((width, own), BF16),
        middle=((own, width), F32),
        nbuf=((2 * sz.group * own, width), BF16),
        gbuf=((2 * sz.group * own, width), BF16),
        skip=((width, LANES), F32),
        filt_spec=((sz.big * sz.outer, 2 * LANES), BF16),
        sig_spec=((sz.pairs * sz.outer, 2 * LANES), BF16),
        fore_in=((sz.count * sz.big, LANES), BF16),
        fore_out=((width, own), BF16),
        back_in=((sz.count * sz.big, LANES), BF16),
        back_out=((width, own), BF16),
        plane_first=((3, 2, 2, sz.group // 2, sz.deep, sz.part), BF16),
        plane_give=((3, 2, sz.group // 2, sz.deep, sz.part), BF16),
        plane_second=((3, 2, sz.group // 2, sz.deep, sz.part), BF16),
        grad_got=((own, width), BF16),
        out_got=((own, width), BF16),
    )
    single = dict(
        x=((own, width), BF16),
        gain=((layers, 2, width), F32),
        skip_rows=((layers, width), F32),
        mixer=((layers, 3, sz.blocks, sz.size, sz.size), BF16),
        filters=((layers, 2, ORDER, sz.half), F32),
        pos=((ORDER, sz.length), BF16),
        outer_fwd=((2 * sz.outer, sz.steps), BF16),
        outer_inv=((sz.steps, 2 * sz.outer), BF16),
        inner_fwd=((2 * LANES, 2 * LANES), BF16),
        inner_inv=((2 * LANES, 2 * LANES), BF16),
        twist=((sz.outer, 2 * LANES), F32),
        up=((layers, 2, width, sz.units), BF16),
        down=((layers, width, sz.units), BF16),
        env=((2 * sz.big, sz.length), F32),
        tall=((max(wide, sz.count * sz.big), LANES), F32),
        wide=((sz.steps, CHUNK * LANES), BF16),
        turned=((CHUNK * sz.outer, 2 * LANES), BF16),
        mid=((2 * sz.outer, CHUNK * LANES), F32),
        flat=((sz.pairs * sz.outer, 2 * LANES), BF16),
        mid_half=((2 * sz.outer, CHUNK * LANES), BF16),
        spec=((sz.pairs * sz.outer, 2 * LANES), F32),
        conv_grad=((width, own), BF16),
        staged=((sz.count * sz.big, LANES), BF16),
        grad_middle=((own, width), F32),
        grad_o=((own, width), BF16),
        gate_grad=((width, own), BF16),
        summed_grad=((width, own), F32),
        inner_grad=((width, own), BF16),
        out_sum=((2 * own, width), F32),
        grad_sum=((2 * own, width), F32),
        out_give=((own, width), BF16),
        sum_give=((own, width), BF16),
        unit_grad=((3, 2 * sz.group * own, sz.part), BF16),
        product=((width // 2, sz.part), F32),
        pieces=((3, sz.peers, sz.group, sz.deep, sz.part), BF16),
        taps_work=((sz.taps_rows, ORDER), F32),
        gain_mine=((16, sz.half), F32),
        gain_give=((16, sz.half), F32),
        late_gain_mine=((16, sz.half), F32),
        late_gain_give=((16, sz.half), F32),
        late_mine=((late, sz.half), BF16),
        late_give=((late, sz.half), BF16),
        late_got=((late, sz.half), BF16),
        late_in=((sz.rows, sz.late_rows, sz.half), BF16),
        late_sum=((sz.late_rows, sz.half), BF16),
        out_keep=((2, own, sz.half), BF16),
        taps_line=((layers, sz.group, sz.taps_rows, ORDER), BF16),
        late_out=((sz.late_rows, sz.half), BF16),
    )
    names, specs = [], []
    for name, (shape, kind) in per_layer.items():
        for layer in range(layers):
            names.append((name, layer))
            specs.append(pltpu.VMEM(shape, kind))
    for index, deep in enumerate(sz.deeps):
        part = (sz.group // 2, deep, sz.half)
        whole_load = (sz.peers, sz.group, deep, sz.half)
        line = (sz.group, deep, sz.half)
        shapes = (whole_load,) * 3 + ((2, 2) + part, (2,) + part, (2,) + part, line, line[1:])
        for name, shape in zip(LOAD_BUFFERS, shapes):
            names.append(("load_" + name, index))
            specs.append(pltpu.VMEM(shape, BF16))
    for name, (shape, kind) in single.items():
        names.append((name, None))
        specs.append(pltpu.VMEM(shape, kind))
    return names, specs


TABLES = ("pos", "outer_fwd", "outer_inv", "inner_fwd", "inner_inv", "twist")
INPUTS = ("hidden_in", "d_out", "gains", "mixer", "skip", "filters", "gate_up", "down") + TABLES
OUTPUTS = ("hidden_out", "grad_in", "upper", "lower", "late", "taps", "units")


def program_kernel(sz, *refs):
    names, _ = layout(sz)
    inputs = dict(zip(INPUTS, refs))
    outputs = dict(zip(OUTPUTS, refs[len(INPUTS) :]))
    scratch = refs[len(INPUTS) + len(OUTPUTS) :]
    b = Named()
    for (name, layer), ref in zip(names, scratch):
        if layer is None:
            setattr(b, name, ref)
        else:
            setattr(b, name, getattr(b, name, ()) + (ref,))
    links = Links(sz, scratch[len(names)], scratch[len(names) + 1])
    own = sz.own
    top = sz.layers - 1
    col = links.col
    low = col == 0
    mine_rows = pl.ds(pl.multiple_of(col * own, own), own)
    other_rows = pl.ds(pl.multiple_of((1 - col) * own, own), own)

    barrier = greet_all(sz)
    lanes = pl.ds(pl.multiple_of(col * sz.half, sz.half), sz.half)
    sides = pl.ds(col * sz.side_blocks, sz.side_blocks)
    slots = lambda first, count: pl.ds(first * own, count * own)
    near_slots, line_slots, far_slots = slots(0, 2), slots(2, 3), slots(5, 3)
    halves = {
        "x": (inputs["hidden_in"].at[mine_rows], b.x.at[:, lanes]),
        "gains": (inputs["gains"], b.gain.at[:, :, lanes]),
        "mixer": (inputs["mixer"].at[0, pl.ds(0, 2)], b.mixer.at[0, pl.ds(0, 2), sides]),
        "skip": (inputs["skip"], b.skip_rows.at[:, lanes]),
        "out_mixer": (inputs["mixer"].at[0, pl.ds(2, 1)], b.mixer.at[0, pl.ds(2, 1), sides]),
    }
    if sz.layers > 1:
        above = pl.ds(1, sz.layers - 1)
        halves["mixers"] = (inputs["mixer"].at[above], b.mixer.at[above, :, sides])
    loads = {name: links.load(*pair) for name, pair in halves.items()}
    for name in ("filters",) + TABLES:
        loads[name] = links.load(inputs[name], getattr(b, name))
    grads = b.gbuf[top]
    loads["g"] = links.load(inputs["d_out"].at[mine_rows], grads.at[slots(0, 1), lanes])
    loads["g_near"] = links.load(inputs["d_out"].at[other_rows], grads.at[slots(1, 1), lanes])
    b.gain_mine[...] = jnp.zeros_like(b.gain_mine)
    b.gain_give[...] = jnp.zeros_like(b.gain_give)
    b.late_gain_mine[...] = jnp.zeros_like(b.late_gain_mine)
    b.late_gain_give[...] = jnp.zeros_like(b.late_gain_give)
    pl.semaphore_wait(barrier, sz.count - 1)
    got = {}
    for name, (source, target) in halves.items():
        if name == "x":
            source = inputs["hidden_in"].at[other_rows]
        got[name] = links.sibling(source, target)
    got["g"] = links.sibling(inputs["d_out"].at[other_rows], grads.at[slots(0, 1), lanes])
    got["g_near"] = links.sibling(inputs["d_out"].at[mine_rows], grads.at[slots(1, 1), lanes])

    def both(*wanted):
        for name in wanted:
            done(loads[name])
            done(got[name])

    def turn_mixer(layer, kind):
        for block in range(sz.blocks):
            b.mixer[layer, kind, block] = jnp.transpose(b.mixer[layer, kind, block])

    def norm_to(source, target, layer, which):
        normal, _ = normalize(source)
        target[...] = (normal * b.gain[layer, which : which + 1, :]).astype(BF16)

    def slot_of(place, member):
        return 2 + (member if member < place else member - 1)

    class Gather:
        moves = (
            {0: [(0, 1)], 1: [(1, 0), (1, 2)], 2: [(2, 1), (2, 3)], 3: [(3, 2)]},
            {1: [(2, 0), (0, 2)], 2: [(3, 1), (1, 3)]},
            {1: [(3, 0)], 2: [(0, 3)]},
        )
        coming = ((1, 2, 2, 1), (1, 1, 1, 1), (1, 0, 0, 1))

        def __init__(self, buffer):
            self.buffer = buffer
            self.pairs = [None] * 3

        def near(self):
            return links.sibling(self.buffer.at[slots(0, 1)], self.buffer.at[slots(1, 1)])

        def views(self, place, whose, target):
            here = 0 if whose == place else slot_of(place, whose)
            there = slot_of(target, whose)
            return [(self.buffer.at[slots(here, 1)], self.buffer.at[slots(there, 1)])]

        def span(self, count):
            return self.buffer.at[slots(0, count)]

        def step(self, index):
            if index > 0:
                self.wait(index - 1)
            pair = links.pair()
            for place, moves in self.moves[index].items():

                @pl.when(links.line == place)
                def _():
                    for whose, target in moves:
                        for source, there in self.views(place, whose, target):
                            row = target * sz.peers + links.plane
                            links.copy(source, there, pair, row, col).start()

            self.pairs[index] = pair

        def wait(self, index):
            pair = self.pairs[index]
            if True:
                for place in range(sz.group):
                    came = self.coming[index][place]
                    sent = len(self.moves[index].get(place, ()))

                    @pl.when(links.line == place)
                    def _():
                        if came:
                            span = self.span(came)
                            links.copy(span, span, pair, links.row, 1 - col).wait_recv()
                        if sent:
                            span = self.span(sent)
                            links.copy(span, span, pair, links.row, 1 - col).wait_send()

        def rest(self):
            self.wait(2)
            self.copies = [links.sibling(self.buffer.at[line_slots], self.buffer.at[far_slots])]

        def finish(self):
            for copy in self.copies:
                done(copy)

    class ArgumentGather(Gather):
        def views(self, place, whose, target):
            there = slot_of(target, whose)
            pairs = []
            for rows, shift in ((mine_rows, 0), (other_rows, 3)):
                if whose == place:
                    source = inputs["d_out"].at[rows]
                else:
                    source = self.buffer.at[slots(slot_of(place, whose) + shift, 1), lanes]
                pairs.append((source, self.buffer.at[slots(there + shift, 1), lanes]))
            return pairs

        def span(self, count):
            return self.buffer.at[slots(0, 2 * count), lanes]

        def rest(self):
            self.wait(2)
            self.copies = [
                links.sibling(self.buffer.at[line_slots, lanes], self.buffer.at[far_slots, lanes]),
                links.sibling(self.buffer.at[far_slots, lanes], self.buffer.at[line_slots, lanes]),
            ]

    top_grads = ArgumentGather(grads)
    top_grads.step(0)
    both("x", "gains")
    b.stream[0][...] = b.x[...].astype(F32)
    norm_to(b.stream[0][...], b.normed[0], 0, 0)
    both("mixer")
    turn_mixer(0, 0)
    turn_mixer(0, 1)

    exchange = Exchange(sz, links)
    project(sz, b, 0)
    normed_parts = []
    for layer in range(sz.layers):
        moving = exchange.to_owners(b.inner[layer], b.fore_in[layer])
        if layer == 0:
            for each in range(sz.layers):
                loads["up", each] = links.load(inputs["gate_up"].at[each], b.up.at[each])
                loads["down", each] = links.load(inputs["down"].at[each], b.down.at[each])
            for name in ("filters", "pos", "outer_fwd", "inner_fwd", "twist"):
                done(loads[name])
            own_envelope(sz, b.env)
            filter_spectrum(sz, b, 0)
            for name in ("outer_inv", "inner_inv"):
                done(loads[name])
            both("skip", "g", "g_near")
            for each in range(sz.layers):
                row = b.skip_rows[each : each + 1, :]
                b.skip[each][...] = jnp.transpose(jnp.broadcast_to(row, (LANES, sz.width)))
        exchange.owners_wait(moving, b.inner[layer], b.fore_in[layer])
        if layer == 0:
            top_grads.step(1)
        else:
            top_grads.rest()
        conv_forward(sz, b, layer, b.fore_in[layer])
        moving = exchange.to_tokens(b.staged, b.fore_out[layer])
        if layer == 0:
            both("out_mixer")
            if sz.layers > 1:
                both("mixers")
            for each in range(1, sz.layers):
                turn_mixer(each, 0)
                turn_mixer(each, 1)
        if layer < top:
            filter_spectrum(sz, b, layer + 1)
        done(loads["up", layer])
        done(loads["down", layer])
        if layer == 0:
            top_grads.step(2)
        exchange.tokens_wait(moving, b.staged, b.fore_out[layer])
        mix(sz, b, layer, b.fore_out[layer])
        norm_to(b.middle[layer][...], b.nbuf[layer].at[slots(0, 1)], layer, 1)
        normed_parts.append(Gather(b.nbuf[layer]))
        near = normed_parts[layer].near()
        if layer == top:
            normed_parts[layer].step(0)
        done(near)
        if layer < top:
            ff_forward(sz, b, layer)
            b.out_give[...] = b.out_sum[own:, :].astype(BF16)
            moving = links.sibling(b.out_give, b.out_got[layer])
            done(moving)
            value = b.middle[layer][...] + b.out_sum[0:own, :] + b.out_got[layer][...].astype(F32)
            b.stream[layer + 1][...] = value
            norm_to(value, b.normed[layer + 1], layer + 1, 0)
            project(sz, b, layer + 1)

    ff_backward(sz, b, top, True)
    b.sum_give[...] = b.grad_sum[own:, :].astype(BF16)
    moving = links.sibling(b.sum_give, b.grad_got[top])
    b.out_give[...] = b.out_sum[own:, :].astype(BF16)
    out_moving = links.sibling(b.out_give, b.out_got[top])
    normed_parts[top].step(1)
    done(moving)
    total = b.grad_sum[0:own, :] + b.grad_got[top][...].astype(F32)
    grad_next = b.gbuf[top][0:own, :].astype(F32)
    gain_grad = mixer_backward(sz, b, top, grad_next, total)
    moving = exchange.to_owners(b.conv_grad, b.back_in[top])
    gain_gradient(sz, b, 2 * top, gain_grad, b.gain_mine, b.gain_give)
    upper = Payload(sz, b, links, 0, outputs["upper"])
    lower = Payload(sz, b, links, 1, outputs["lower"])
    upper.matrix(0, out_gradient(sz, b, top))
    done(out_moving)
    value = b.middle[top][...] + b.out_sum[0:own, :] + b.out_got[top][...].astype(F32)
    value = value.astype(BF16)
    left, right = value[:, : sz.half], value[:, sz.half :]
    b.out_keep[0] = jnp.where(low, left, right)
    b.out_keep[1] = jnp.where(low, right, left)
    place = outputs["hidden_out"].at[mine_rows]
    ending = [links.load(b.out_keep.at[0], place), links.sibling(b.out_keep.at[1], place)]
    top_grads.finish()
    normed_parts[top].step(2)

    plane_moving = {}
    taps_moving = {}
    units_moving = []

    def taps_to_line(layer):
        taps_gradient(sz, b, layer, b.back_in[layer], b.fore_in[layer])
        place = b.taps_line.at[layer, links.line]
        b.taps_line[layer, links.line] = b.taps_work[...].astype(BF16)
        taps_moving[layer] = links.in_line(lambda member: place, place)

    def taps_to_plane(layer):
        links.wait(taps_moving[layer], b.taps_line.at[layer, pl.ds(0, sz.group - 1)])
        place = outputs["taps"].at[layer, links.plane]
        ending.append(links.load(b.taps_line.at[layer], place))
        taps_moving[layer] = links.in_plane(lambda member: b.taps_line.at[layer], place)

    def units_middle(layer, kinds=(0, 1, 2)):
        for kind in kinds:
            plane_moving[layer][kind].middle()

    def units_end(layer, kinds=(0, 1, 2)):
        for kind in kinds:
            plane = plane_moving[layer][kind]
            plane.end()
            part = plane.sums()
            target = outputs["units"].at[layer, kind, links.line]
            ending.append(links.load(part(links.line), target))
            pair = links.in_line(part, target)
            units_moving.append((layer, kind, pair))

    exchange.owners_wait(moving, b.conv_grad, b.back_in[top])
    conv_backward(sz, b, top, b.back_in[top])
    moving = exchange.to_tokens(b.staged, b.back_out[top])
    normed_parts[top].rest()
    normed_parts[0].step(0)
    normed_parts[top].finish()
    plane_moving[top] = ff_gradients(sz, b, top, links)
    exchange.tokens_wait(moving, b.staged, b.back_out[top])
    value, gain_grad = input_backward(sz, b, top, b.back_out[top])
    b.out_sum[0:own, :] = value
    b.gbuf[0][0:own, :] = value.astype(BF16)
    gather = Gather(b.gbuf[0])
    near = gather.near()
    gather.step(0)
    normed_parts[0].step(1)
    gain_gradient(sz, b, 2 * top - 1, gain_grad, b.gain_mine, b.gain_give)
    upper.matrix(1, in_gradient(sz, b, top, b.inner_grad))
    upper.matrix(2, in_gradient(sz, b, top, b.gate_grad))
    upper.to_partner()
    done(near)
    ff_backward(sz, b, 0, False)
    b.sum_give[...] = b.grad_sum[own:, :].astype(BF16)
    moving = links.sibling(b.sum_give, b.grad_got[0])
    gather.step(1)
    normed_parts[0].step(2)
    done(moving)
    total = b.grad_sum[0:own, :] + b.grad_got[0][...].astype(F32)
    gain_grad = mixer_backward(sz, b, 0, b.out_sum[0:own, :], total)

    moving = exchange.to_owners(b.conv_grad, b.back_in[0])
    units_middle(top)
    upper.to_plane()
    taps_to_line(top)
    gain_gradient(sz, b, 0, gain_grad, b.gain_mine, b.gain_give)
    lower.matrix(0, out_gradient(sz, b, 0))
    lower.matrix(1, in_gradient(sz, b, 0, b.gate_grad))
    lower.rows16(2, b.gain_mine[...], b.gain_give[...])
    lower.to_partner()
    gather.step(2)
    exchange.owners_wait(moving, b.conv_grad, b.back_in[0])
    lower.to_plane()
    conv_backward(sz, b, 0, b.back_in[0])
    moving = exchange.to_tokens(b.staged, b.back_out[0])
    units_end(top)
    normed_parts[0].rest()
    gather.rest()
    upper.middle()
    taps_to_plane(top)
    normed_parts[0].finish()
    gather.finish()
    between = (lower.middle, upper.to_line, None)
    plane_moving[0] = ff_gradients(sz, b, 0, links, between)
    exchange.tokens_wait(moving, b.staged, b.back_out[0])
    value, gain_grad = input_backward(sz, b, 0, b.back_out[0])

    left, right = value[:, : sz.half], value[:, sz.half :]
    keep, give = b.out_sum.at[0:own, 0 : sz.half], b.out_sum.at[own:, 0 : sz.half]
    keep[...] = jnp.where(low, left, right)
    give[...] = jnp.where(low, right, left)
    mixer_gradient(sz, b, 0, in_gradient(sz, b, 0, b.inner_grad), b.late_mine, b.late_give)
    gain_gradient(sz, b, 0, gain_grad, b.late_gain_mine, b.late_gain_give)
    rows = slice(sz.size, sz.size + 16)
    b.late_mine[rows, :] = b.late_gain_mine[...].astype(BF16)
    b.late_give[rows, :] = b.late_gain_give[...].astype(BF16)
    last = slice(sz.size + 16, sz.rows * sz.late_rows)
    b.late_mine[last, :] = jnp.zeros_like(b.late_mine[last, :])
    b.late_give[last, :] = jnp.zeros_like(b.late_give[last, :])
    late_pair = links.sibling(b.late_give, b.late_got)
    place = outputs["grad_in"].at[mine_rows]
    ending += [links.load(keep, place), links.sibling(give, place)]

    done(late_pair)
    b.late_mine[...] = (b.late_mine[...].astype(F32) + b.late_got[...].astype(F32)).astype(BF16)
    few = lambda index: pl.ds(pl.multiple_of(index * sz.late_rows, sz.late_rows), sz.late_rows)
    rows_pair = links.in_rows(
        lambda member: b.late_mine.at[few(member)], b.late_in.at[links.row]
    )
    lower.to_line()
    units_middle(0, (0, 1))
    taps_to_line(0)
    units_middle(0, (2,))
    upper.back_line()
    lower.back_line()
    units_end(0, (0,))
    links.wait(rows_pair, b.late_in.at[pl.ds(0, sz.rows - 1)])
    b.late_in[links.row] = b.late_mine[few(links.row), :]
    late = outputs["late"]
    b.late_out[...] = jnp.sum(b.late_in[...].astype(F32), axis=0).astype(BF16)
    place = late.at[few(links.row)]
    ending.append(links.load(b.late_out, place))
    spread_rows = links.in_rows(lambda member: b.late_out, place)
    units_end(0, (1,))
    upper.back_plane()
    units_end(0, (2,))
    lower.back_plane()
    upper.spread.middle()
    lower.spread.middle()
    taps_to_plane(0)
    ending += [upper.finish(), lower.finish()]
    for layer, kind, pair in units_moving:
        links.wait(pair, outputs["units"].at[layer, kind, pl.ds(0, sz.group - 1)])
    links.wait(spread_rows, late.at[pl.ds(0, (sz.rows - 1) * sz.late_rows)])
    for layer, pair in taps_moving.items():
        links.wait(pair, outputs["taps"].at[layer, pl.ds(0, sz.peers - 1)])
    for copy in ending:
        done(copy)


def results_kernel(sz, *refs):
    raw, outs, scratch = refs[:7], refs[7:15], refs[15:]
    targets, held = scratch[:7], scratch[7:15]
    hidden_out, grad_in, gain_out, mixer_out, skip_out, taps_out, pair_out, down_out = held
    upper, lower, late, taps, units = targets[2:]
    channels, sems = scratch[15:]
    targets = (hidden_out, grad_in) + targets[2:]
    copies = [
        pltpu.make_async_copy(source, target, sems.at[index])
        for index, (source, target) in enumerate(zip(raw, targets))
    ]
    for copy in reversed(copies):
        copy.start()
    leaving = []

    def leave(index):
        copy = pltpu.make_async_copy(held[index], outs[index], sems.at[7 + index])
        copy.start()
        leaving.append(copy)

    layers = sz.layers
    copies[6].wait()
    for kind in range(3):
        for layer in range(layers):
            for line in range(sz.group):
                lanes = slice(line * sz.part, (line + 1) * sz.part)
                value = units[layer, kind, line].astype(F32)
                if kind < 2:
                    pair_out[layer, kind, :, lanes] = value
                else:
                    down_out[layer, :, lanes] = value
    leave(6)
    leave(7)
    copies[5].wait()
    for layer in range(layers):
        for way in range(3):
            for row in range(sz.rows):
                part = taps[layer, row % sz.peers, row // sz.peers]
                begin = (row // 2) * sz.couple + (row % 2) * sz.big
                size = sz.small if row % 2 else sz.big
                if way < 2:
                    value = part[way * sz.big : way * sz.big + size, :].astype(F32)
                else:
                    line = part[2 * sz.big : 2 * sz.big + 16, :].astype(F32)[0:1, :]
                    value = jnp.transpose(jnp.broadcast_to(line, (LANES, ORDER)))[0:size, :]
                channels[begin : begin + size, :] = value
            turned = jnp.transpose(channels[...])
            if way < 2:
                taps_out[layer, way] = turned
            else:
                skip_out[layer : layer + 1, :] = turned[0:1, :]
    leave(4)
    leave(5)
    for copy in copies[2:5]:
        copy.wait()

    def matrix(payload, place, layer, kind):
        deep = payload.shape[2]
        count = sz.size // deep
        for part in range(count):
            index = place * count + part
            rows = payload[index // sz.group, index % sz.group].astype(F32)
            for block in range(sz.side_blocks):
                mixer_out[layer, kind, block, part * deep : (part + 1) * deep, :] = rows[
                    :, block_of(sz, block)
                ]

    for place, kind in enumerate((2, 0, 1)):
        matrix(upper, place, 1, kind)
    for place, kind in enumerate((2, 1)):
        matrix(lower, place, 0, kind)
    rows = late[0 : sz.size, :].astype(F32)
    for block in range(sz.side_blocks):
        mixer_out[0, 0, block] = rows[:, block_of(sz, block)]
    index = 2 * (sz.size // sz.deeps[1])
    gains = lower[index // sz.group, index % sz.group].astype(F32)
    gain_out[0, 0:1, :] = late[sz.size : sz.size + 16, :].astype(F32)[0:1, :]
    for row in range(1, 2 * layers):
        gain_out[row // 2, row % 2 : row % 2 + 1, :] = gains[row - 1 : row, :]
    leave(2)
    leave(3)
    for index in range(2):
        copies[index].wait()
        leave(index)
    for copy in leaving:
        copy.wait()


def results(sz, *arrays):
    layers = sz.layers
    outs = (
        ((2 * sz.own, sz.half), BF16),
        ((2 * sz.own, sz.half), F32),
        ((layers, 2, sz.half), F32),
        ((layers, 3, sz.side_blocks, sz.size, sz.size), F32),
        ((layers, sz.half), F32),
        ((layers, 2, ORDER, sz.half), F32),
        ((layers, 2, sz.depth, sz.units), F32),
        ((layers, sz.depth, sz.units), F32),
    )
    anywhere = pl.BlockSpec(memory_space=pl.ANY)
    return pl.pallas_call(
        functools.partial(results_kernel, sz),
        out_shape=tuple(jax.ShapeDtypeStruct(shape, kind) for shape, kind in outs),
        in_specs=[anywhere] * len(arrays),
        out_specs=(anywhere,) * len(outs),
        scratch_shapes=[pltpu.VMEM(entry.shape, entry.dtype) for entry in arrays]
        + [pltpu.VMEM(shape, kind) for shape, kind in outs]
        + [pltpu.VMEM((sz.half, ORDER), F32), pltpu.SemaphoreType.DMA((15,))],
        compiler_params=pltpu.CompilerParams(vmem_limit_bytes=62 * MIB),
        name="results",
    )(*arrays)


def program(sz, arrays):
    names, scratch = layout(sz)
    outs = (
        ((2 * sz.own, sz.half), BF16),
        ((2 * sz.own, sz.half), F32),
        ((sz.peers, sz.group, sz.deeps[0], sz.half), BF16),
        ((sz.peers, sz.group, sz.deeps[1], sz.half), BF16),
        ((sz.rows * sz.late_rows, sz.half), BF16),
        ((sz.layers, sz.peers, sz.group, sz.taps_rows, ORDER), BF16),
        ((sz.layers, 3, sz.group, sz.deep, sz.part), BF16),
    )
    return pl.pallas_call(
        functools.partial(program_kernel, sz),
        out_shape=tuple(jax.ShapeDtypeStruct(shape, kind) for shape, kind in outs),
        in_specs=[pl.BlockSpec(memory_space=pl.ANY)] * len(arrays),
        out_specs=(pl.BlockSpec(memory_space=pl.ANY),) * len(outs),
        scratch_shapes=scratch
        + [pltpu.SemaphoreType.DMA((220,)), pltpu.SemaphoreType.DMA((80,))],
        compiler_params=pltpu.CompilerParams(
            collective_id=0, has_side_effects=True, vmem_limit_bytes=63 * MIB
        ),
        name="program",
    )(*arrays)


def together(sz, hidden_in, d_out, gains, mixer, skip, filters, gate_up, down):
    pos = jnp.asarray(position_table(sz.length).T, F32).astype(BF16)
    arrays = (hidden_in, d_out, gains, mixer, skip, filters, gate_up, down, pos)
    raw = program(sz, arrays + dft_tables(sz.length))

    return results(sz, *raw)


def apart_enter(count, hid):
    me = lax.axis_index("rows") * hid + lax.axis_index("hid")
    barrier = pltpu.get_barrier_semaphore()

    def greet(step, carry):
        peer = lax.rem(me + step, count)
        pl.semaphore_signal(
            barrier, inc=1, device_id=(peer // hid, lax.rem(peer, hid)), device_id_type=MESH
        )
        return carry

    lax.fori_loop(1, count, greet, 0)
    return barrier


def apart_exchange_start(source, target, sems, count, rows, hid, piece, by_owner):
    send, recv, local = sems
    row = lax.axis_index("rows")
    col = lax.axis_index("hid")
    token_id = row * hid + col
    owner_id = col * rows + row
    mine_there = token_id if by_owner else owner_id
    mine_here = owner_id if by_owner else token_id
    at = lambda index: pl.ds(pl.multiple_of(index * piece, piece), piece)
    pltpu.make_async_copy(source.at[at(mine_here)], target.at[at(mine_there)], local).start()

    def post(step, carry):
        peer = lax.rem(token_id + step, count)
        peer_row = peer // hid
        peer_col = lax.rem(peer, hid)
        there = (peer_col * rows + peer_row) if by_owner else peer
        pltpu.make_async_remote_copy(
            src_ref=source.at[at(there)],
            dst_ref=target.at[at(mine_there)],
            send_sem=send,
            recv_sem=recv,
            device_id=(peer_row, peer_col),
            device_id_type=MESH,
        ).start()
        return carry

    lax.fori_loop(1, count, post, 0)


def apart_exchange_wait(source, target, sems, count, rows, hid, piece):
    send, recv, local = sems
    row = lax.axis_index("rows")
    col = lax.axis_index("hid")
    pltpu.make_async_copy(
        source.at[pl.ds(0, piece)], target.at[pl.ds(0, piece)], local
    ).wait()
    span = pl.ds(0, (count - 1) * piece)
    pltpu.make_async_remote_copy(
        src_ref=source.at[span],
        dst_ref=target.at[span],
        send_sem=send,
        recv_sem=recv,
        device_id=(row, hid - 1 - col),
        device_id_type=MESH,
    ).wait()


class apart_Sizes:
    def __init__(self, rows, hid, width, hidden, tokens):
        self.rows, self.hid, self.width, self.hidden = rows, hid, width, hidden
        self.count = rows * hid
        self.chans = width // self.count
        self.piece = round_up(self.chans, 16)
        self.length = min(SEQ_LEN, tokens)
        self.seqs = tokens // self.length
        self.blocks = self.length // LANES
        self.outer = 2 * self.blocks
        self.pairs = self.seqs * self.chans
        self.half = width // hid
        self.padded = rows * self.piece
        self.channels = self.count * self.piece


def apart_spread_in(source, wide, lines, stride, blocks):
    for place, line in enumerate(lines):
        wide[:, place * LANES : (place + 1) * LANES] = source[
            pl.ds(line, blocks, stride=stride), :
        ].astype(wide.dtype)


def apart_dft(wide, spectrum, tables, mid, flat, lines, outer, offset=0):
    outer_fwd, inner_fwd, twist = tables
    mid[:, : lines * LANES] = nn(outer_fwd[...], wide[:, : lines * LANES])
    cos = twist[:, :LANES]
    sin = twist[:, LANES:]
    for line in range(lines):
        lanes = pl.ds(line * LANES, LANES)
        real = mid[0:outer, lanes]
        imag = mid[outer : 2 * outer, lanes]
        rows = pl.ds(line * outer, outer)
        flat[rows, 0:LANES] = (real * cos + imag * sin).astype(BF16)
        flat[rows, LANES:] = (imag * cos - real * sin).astype(BF16)
    spectrum[0 : lines * outer, :] = nn(flat[0 : lines * outer, :], inner_fwd[...])


def apart_inverse_dft(flat, tables, mid_half, lines, outer):
    outer_inv, inner_inv, twist = tables
    cos = twist[:, :LANES]
    sin = twist[:, LANES:]
    for line in range(lines):
        rows = pl.ds(line * outer, outer)
        lanes = pl.ds(line * LANES, LANES)
        part = nn(flat[rows, :], inner_inv[...])
        real = part[:, :LANES]
        imag = part[:, LANES:]
        mid_half[0:outer, lanes] = (real * cos - imag * sin).astype(BF16)
        mid_half[outer : 2 * outer, lanes] = (imag * cos + real * sin).astype(BF16)
    return nn(outer_inv[...], mid_half[:, : lines * LANES])


def apart_spread_out(value, target, lines, stride, blocks):
    for place, line in enumerate(lines):
        target[pl.ds(line, blocks, stride=stride), :] = value[
            :, place * LANES : (place + 1) * LANES
        ]


def apart_signal_lines(sz):
    return [seq * sz.blocks * sz.piece + chan for seq in range(sz.seqs) for chan in range(sz.chans)]


def apart_conv_forward_kernel(
    sz,
    inner_ref,
    taps_ref,
    pos_ref,
    env_ref,
    outer_fwd,
    outer_inv,
    inner_fwd,
    inner_inv,
    twist,
    conv_ref,
    filt_spec,
    sig_spec,
    landed,
    staged,
    tall,
    wide,
    mid,
    flat,
    mid_half,
    sems_in,
    sems_out,
):
    barrier = apart_enter(sz.count, sz.hid)
    pl.semaphore_wait(barrier, sz.count - 1)
    into = tuple(sems_in.at[i] for i in range(3))
    back = tuple(sems_out.at[i] for i in range(3))
    apart_exchange_start(inner_ref, landed, into, sz.count, sz.rows, sz.hid, sz.piece, True)

    piece, blocks, outer = sz.piece, sz.blocks, sz.outer
    step = 4
    for start in range(0, blocks, step):
        span = slice(start * LANES, (start + step) * LANES)
        raw = nn(taps_ref[...], pos_ref[:, span])
        kernels = raw * env_ref[:, span]
        for block in range(step):
            tall[pl.ds((start + block) * 2 * piece, 2 * piece), :] = kernels[
                :, block * LANES : (block + 1) * LANES
            ]
    lines = [way * piece + chan for way in range(2) for chan in range(sz.chans)]
    apart_spread_in(tall, wide, lines, 2 * piece, blocks)
    apart_dft(wide, sig_spec, (outer_fwd, inner_fwd, twist), mid, flat, len(lines), outer)
    span = sz.chans * outer
    filt_spec[:, :LANES] = sig_spec[0:span, :LANES] + sig_spec[span : 2 * span, :LANES]
    filt_spec[:, LANES:] = sig_spec[0:span, LANES:] - sig_spec[span : 2 * span, LANES:]

    apart_exchange_wait(inner_ref, landed, into, sz.count, sz.rows, sz.hid, piece)
    tall[0 : sz.channels, :] = landed[...].astype(F32)
    lines = apart_signal_lines(sz)
    apart_spread_in(tall, wide, lines, piece, blocks)
    apart_dft(wide, sig_spec, (outer_fwd, inner_fwd, twist), mid, flat, sz.pairs, outer)
    for seq in range(sz.seqs):
        rows = pl.ds(seq * span, span)
        sig_re, sig_im = sig_spec[rows, :LANES], sig_spec[rows, LANES:]
        fil_re, fil_im = filt_spec[:, :LANES], filt_spec[:, LANES:]
        flat[rows, :LANES] = (sig_re * fil_re - sig_im * fil_im).astype(BF16)
        flat[rows, LANES:] = (sig_re * fil_im + sig_im * fil_re).astype(BF16)
    result = apart_inverse_dft(flat, (outer_inv, inner_inv, twist), mid_half, sz.pairs, outer)
    apart_spread_out(result, tall, lines, piece, blocks)
    staged[...] = tall[0 : sz.channels, :].astype(BF16)
    apart_exchange_start(staged, conv_ref, back, sz.count, sz.rows, sz.hid, piece, False)
    apart_exchange_wait(staged, conv_ref, back, sz.count, sz.rows, sz.hid, piece)


def apart_conv_forward(sz, inner, taps, pos, env, tables, cid):
    outer_fwd, outer_inv, inner_fwd, inner_inv, twist = tables
    wide_lines = max(2 * sz.chans, sz.pairs)
    return pl.pallas_call(
        functools.partial(apart_conv_forward_kernel, sz),
        out_shape=(
            jax.ShapeDtypeStruct((sz.channels, LANES), BF16),
            jax.ShapeDtypeStruct((sz.chans * sz.outer, 2 * LANES), F32),
            jax.ShapeDtypeStruct((wide_lines * sz.outer, 2 * LANES), F32),
        ),
        in_specs=[whole()] * 9,
        out_specs=(whole(),) * 3,
        scratch_shapes=[
            pltpu.VMEM((sz.channels, LANES), BF16),
            pltpu.VMEM((sz.channels, LANES), BF16),
            pltpu.VMEM((max(2 * sz.piece * sz.blocks, sz.channels), LANES), F32),
            pltpu.VMEM((sz.blocks, wide_lines * LANES), BF16),
            pltpu.VMEM((2 * sz.outer, wide_lines * LANES), F32),
            pltpu.VMEM((wide_lines * sz.outer, 2 * LANES), BF16),
            pltpu.VMEM((2 * sz.outer, sz.pairs * LANES), BF16),
            pltpu.SemaphoreType.DMA((3,)),
            pltpu.SemaphoreType.DMA((3,)),
        ],
        compiler_params=pltpu.CompilerParams(
            collective_id=cid, has_side_effects=True, vmem_limit_bytes=48 * MIB
        ),
        name="conv_forward",
    )(inner, taps, pos, env, outer_fwd, outer_inv, inner_fwd, inner_inv, twist)


def apart_conv_backward_kernel(
    sz,
    grad_ref,
    filt_spec,
    sig_spec,
    taps_ref,
    pos_ref,
    env_ref,
    outer_fwd,
    outer_inv,
    inner_fwd,
    inner_inv,
    twist,
    back_ref,
    taps_grad,
    landed,
    staged,
    tall,
    wide,
    mid,
    flat,
    mid_half,
    grad_spec,
    sems_in,
    sems_out,
):
    barrier = apart_enter(sz.count, sz.hid)
    pl.semaphore_wait(barrier, sz.count - 1)
    into = tuple(sems_in.at[i] for i in range(3))
    back = tuple(sems_out.at[i] for i in range(3))
    piece, blocks, outer = sz.piece, sz.blocks, sz.outer
    apart_exchange_start(grad_ref, landed, into, sz.count, sz.rows, sz.hid, piece, True)
    apart_exchange_wait(grad_ref, landed, into, sz.count, sz.rows, sz.hid, piece)
    tall[0 : sz.channels, :] = landed[...].astype(F32)
    lines = apart_signal_lines(sz)
    apart_spread_in(tall, wide, lines, piece, blocks)
    apart_dft(wide, grad_spec, (outer_fwd, inner_fwd, twist), mid, flat, sz.pairs, outer)
    span = sz.chans * outer
    for seq in range(sz.seqs):
        rows = pl.ds(seq * span, span)
        re, im = grad_spec[rows, :LANES], grad_spec[rows, LANES:]
        fil_re, fil_im = filt_spec[:, :LANES], filt_spec[:, LANES:]
        flat[rows, :LANES] = (re * fil_re + im * fil_im).astype(BF16)
        flat[rows, LANES:] = (im * fil_re - re * fil_im).astype(BF16)
    inv_tables = (outer_inv, inner_inv, twist)
    result = apart_inverse_dft(flat, inv_tables, mid_half, sz.pairs, outer)
    apart_spread_out(result, tall, lines, piece, blocks)
    staged[...] = tall[0 : sz.channels, :].astype(BF16)
    apart_exchange_start(staged, back_ref, back, sz.count, sz.rows, sz.hid, piece, False)

    total_re = jnp.zeros((span, LANES), F32)
    total_im = jnp.zeros((span, LANES), F32)
    for seq in range(sz.seqs):
        rows = pl.ds(seq * span, span)
        re, im = grad_spec[rows, :LANES], grad_spec[rows, LANES:]
        sig_re, sig_im = sig_spec[rows, :LANES], sig_spec[rows, LANES:]
        total_re += re * sig_re + im * sig_im
        total_im += im * sig_re - re * sig_im
    flat[0:span, :LANES] = total_re.astype(BF16)
    flat[span : 2 * span, :LANES] = total_re.astype(BF16)
    flat[0:span, LANES:] = total_im.astype(BF16)
    flat[span : 2 * span, LANES:] = (-total_im).astype(BF16)
    result = apart_inverse_dft(flat, inv_tables, mid_half, 2 * sz.chans, outer)
    lines = [way * piece + chan for way in range(2) for chan in range(sz.chans)]
    if sz.chans < piece:
        tall[...] = jnp.zeros_like(tall)
    apart_spread_out(result, tall, lines, 2 * piece, blocks)
    total = jnp.zeros((2 * piece, ORDER), F32)
    step = 4
    for start in range(0, blocks, step):
        span = slice(start * LANES, (start + step) * LANES)
        raw = nn(taps_ref[...], pos_ref[:, span])
        grads = jnp.concatenate(
            [
                tall[pl.ds((start + block) * 2 * piece, 2 * piece), :]
                for block in range(step)
            ],
            axis=1,
        )
        grads = grads * env_ref[:, span] + (2.0 * DECAY) * raw
        total += nt(grads.astype(BF16), pos_ref[:, span])
    taps_grad[...] = total

    apart_exchange_wait(staged, back_ref, back, sz.count, sz.rows, sz.hid, piece)


def apart_conv_backward(sz, grad, filt_spec, sig_spec, taps, pos, env, tables, cid):
    outer_fwd, outer_inv, inner_fwd, inner_inv, twist = tables
    wide_lines = max(2 * sz.chans, sz.pairs)
    return pl.pallas_call(
        functools.partial(apart_conv_backward_kernel, sz),
        out_shape=(
            jax.ShapeDtypeStruct((sz.channels, LANES), BF16),
            jax.ShapeDtypeStruct((2 * sz.piece, ORDER), F32),
        ),
        in_specs=[whole()] * 11,
        out_specs=(whole(),) * 2,
        scratch_shapes=[
            pltpu.VMEM((sz.channels, LANES), BF16),
            pltpu.VMEM((sz.channels, LANES), BF16),
            pltpu.VMEM((max(2 * sz.piece * sz.blocks, sz.channels), LANES), F32),
            pltpu.VMEM((sz.blocks, wide_lines * LANES), BF16),
            pltpu.VMEM((2 * sz.outer, wide_lines * LANES), F32),
            pltpu.VMEM((wide_lines * sz.outer, 2 * LANES), BF16),
            pltpu.VMEM((2 * sz.outer, wide_lines * LANES), BF16),
            pltpu.VMEM((sz.pairs * sz.outer, 2 * LANES), F32),
            pltpu.SemaphoreType.DMA((3,)),
            pltpu.SemaphoreType.DMA((3,)),
        ],
        compiler_params=pltpu.CompilerParams(
            collective_id=cid, has_side_effects=True, vmem_limit_bytes=48 * MIB
        ),
        name="conv_backward",
    )(grad, filt_spec, sig_spec, taps, pos, env, outer_fwd, outer_inv, inner_fwd, inner_inv, twist)


def apart_project(sz, normed, w_in, w_gate, inner_ref, gate_ref):
    for side in range(sz.hid):
        rows = slice(side * sz.padded, (side + 1) * sz.padded)
        part = normed[:, side * sz.half : (side + 1) * sz.half]
        inner_ref[rows, :] = nt(w_in[side], part).astype(BF16)
        gate_ref[rows, :] = nt(w_gate[side], part)


def apart_first_kernel(sz, x_ref, gain_ref, w_in, w_gate, normed_ref, inner_ref, gate_ref):
    normal, _ = normalize(x_ref[...].astype(F32))
    normed = (normal * gain_ref[0:1, :]).astype(BF16)
    normed_ref[...] = normed
    apart_project(sz, normed, w_in, w_gate, inner_ref, gate_ref)


def apart_first(sz, x, gains, w_in, w_gate):
    tokens = x.shape[0]
    return pl.pallas_call(
        functools.partial(apart_first_kernel, sz),
        out_shape=(
            jax.ShapeDtypeStruct((tokens, sz.width), BF16),
            jax.ShapeDtypeStruct((sz.channels, tokens), BF16),
            jax.ShapeDtypeStruct((sz.channels, tokens), F32),
        ),
        in_specs=[whole()] * 4,
        out_specs=(whole(),) * 3,
        compiler_params=pltpu.CompilerParams(vmem_limit_bytes=32 * MIB),
        name="first_projection",
    )(x, gains, w_in, w_gate)


def apart_mix_out(sz, mixed, w_out):
    parts = []
    for side in range(sz.hid):
        rows = slice(side * sz.padded, (side + 1) * sz.padded)
        parts.append(tn(mixed[rows, :], w_out[side]))
    return jnp.concatenate(parts, axis=1)


def apart_ff_specs(sz, layer, tile):
    steps = sz.hidden // sz.hid // tile
    first_half = lambda i: jnp.minimum(i, steps - 1)
    second = lambda i: jnp.maximum(i - steps, 0)
    specs = []
    for place in (first_half, second):
        specs.append(
            pl.BlockSpec((1, 2, sz.width, tile), lambda i, place=place: (layer, 0, 0, place(i)))
        )
        specs.append(pl.BlockSpec((1, sz.width, tile), lambda i, place=place: (layer, 0, place(i))))
    return specs, steps


def apart_forward_kernel(
    sz,
    steps,
    conv_ref,
    inner_ref,
    gate_ref,
    skip_ref,
    x_ref,
    gain_ref,
    next_gain,
    w_out,
    w_in,
    w_gate,
    up_a,
    down_a,
    up_b,
    down_b,
    summed_ref,
    mixed_ref,
    middle_ref,
    normed_two,
    next_x,
    next_normed,
    next_inner,
    next_gate,
):
    index = pl.program_id(0)

    @pl.when(index == 0)
    def _():
        summed = conv_ref[...].astype(F32) + skip_ref[...] * inner_ref[...].astype(F32)
        summed_ref[...] = summed
        mixed_ref[...] = (gate_ref[...] * summed).astype(BF16)
        middle = x_ref[...].astype(F32) + apart_mix_out(sz, mixed_ref, w_out)
        middle_ref[...] = middle
        normal, _ = normalize(middle)
        normed_two[...] = (normal * gain_ref[1:2, :]).astype(BF16)
        next_x[...] = middle

    def accumulate(up_ref, down_ref):
        gate = nn(normed_two[...], up_ref[0, 0])
        up = nn(normed_two[...], up_ref[0, 1])
        value, _ = gelu_parts(gate)
        next_x[...] += nt((value * up).astype(BF16), down_ref[0])

    pl.when(index < steps)(lambda: accumulate(up_a, down_a))
    pl.when(index >= steps)(lambda: accumulate(up_b, down_b))

    @pl.when(index == 2 * steps - 1)
    def _():
        normal, _ = normalize(next_x[...])
        normed = (normal * next_gain[0:1, :]).astype(BF16)
        next_normed[...] = normed
        apart_project(sz, normed, w_in, w_gate, next_inner, next_gate)


def apart_full(shape):
    return pl.BlockSpec(shape, lambda i: (0,) * len(shape))


def apart_forward(sz, layer, conv, inner, gate, skip, x, gains, next_gains, w_out, w_in, w_gate, ff):
    tokens = x.shape[0]
    tile = 512
    specs, steps = apart_ff_specs(sz, layer, tile)
    small = (conv, inner, gate, skip, x, gains, next_gains, w_out, w_in, w_gate)
    outs = (
        ((sz.channels, tokens), F32),
        ((sz.channels, tokens), BF16),
        ((tokens, sz.width), F32),
        ((tokens, sz.width), BF16),
        ((tokens, sz.width), F32),
        ((tokens, sz.width), BF16),
        ((sz.channels, tokens), BF16),
        ((sz.channels, tokens), F32),
    )
    return pl.pallas_call(
        functools.partial(apart_forward_kernel, sz, steps),
        grid=(2 * steps,),
        out_shape=tuple(jax.ShapeDtypeStruct(shape, kind) for shape, kind in outs),
        in_specs=[apart_full(entry.shape) for entry in small] + specs,
        out_specs=tuple(apart_full(shape) for shape, kind in outs),
        compiler_params=pltpu.CompilerParams(
            dimension_semantics=("arbitrary",), vmem_limit_bytes=48 * MIB
        ),
        name="token_forward",
    )(*small, *ff)


def apart_block_grads(sz, tall, flat, target, slot):
    blocks_side = target.shape[1] // sz.hid
    size = sz.half // blocks_side
    rows = sz.padded // blocks_side
    for side in range(sz.hid):
        for block in range(blocks_side):
            begin = side * sz.padded + block * rows
            place = side * sz.half + block * size
            target[slot, side * blocks_side + block] = nn(
                tall[begin : begin + rows, :], flat[:, place : place + size]
            ).astype(target.dtype)


def apart_ff_backward_tile(normed, grad, up_ref, down_ref, total, out_total):
    gate = nn(normed, up_ref[0, 0])
    up = nn(normed, up_ref[0, 1])
    grad_hidden = nn(grad, down_ref[0])
    value, slope = gelu_parts(gate)
    if out_total is not None:
        out_total[...] += nt((value * up).astype(BF16), down_ref[0])
    grad_gate = (slope * up * grad_hidden).astype(BF16)
    grad_up = (value * grad_hidden).astype(BF16)
    total[...] += nt(grad_gate, up_ref[0, 0]) + nt(grad_up, up_ref[0, 1])


def apart_mixer_backward(
    sz, grad_next, middle, total, gain, mixed, summed, gate, w_out, outs
):
    grad_middle, mixer_grad, grad_gate, grad_summed, grad_conv, gain_grad = outs
    normal, inv = normalize(middle)
    back, gain_grad[...] = norm_back(total, normal, inv, gain)
    result = grad_next + back
    grad_middle[...] = result
    grad_o = result.astype(BF16)
    apart_block_grads(sz, mixed, grad_o, mixer_grad, 0)
    for side in range(sz.hid):
        rows = slice(side * sz.padded, (side + 1) * sz.padded)
        grad_mixed = nt(w_out[side], grad_o[:, side * sz.half : (side + 1) * sz.half])
        grad_gate[rows, :] = (grad_mixed * summed[rows, :]).astype(BF16)
        through = grad_mixed * gate[rows, :]
        grad_summed[rows, :] = through
        grad_conv[rows, :] = through.astype(BF16)


def apart_mixer_outs(sz, tokens, blocks):
    size = sz.width // blocks
    return (
        ((tokens, sz.width), F32),
        ((1, blocks, sz.channels // blocks, size), BF16),
        ((sz.channels, tokens), BF16),
        ((sz.channels, tokens), F32),
        ((sz.channels, tokens), BF16),
        ((1, sz.width), F32),
    )


def apart_turn_kernel(
    sz,
    steps,
    conv_ref,
    inner_ref,
    gate_ref,
    skip_ref,
    x_ref,
    gain_ref,
    grad_ref,
    w_out,
    up_a,
    down_a,
    up_b,
    down_b,
    hidden_out,
    normed_two,
    grad_middle,
    mixer_grad,
    grad_gate,
    grad_summed,
    grad_conv,
    gain_grad,
    summed,
    mixed,
    middle,
    out_total,
    total,
):
    index = pl.program_id(0)

    @pl.when(index == 0)
    def _():
        summed[...] = conv_ref[...].astype(F32) + skip_ref[...] * inner_ref[...].astype(F32)
        mixed[...] = (gate_ref[...] * summed[...]).astype(BF16)
        middle[...] = x_ref[...].astype(F32) + apart_mix_out(sz, mixed, w_out)
        normal, _ = normalize(middle[...])
        normed_two[...] = (normal * gain_ref[1:2, :]).astype(BF16)
        out_total[...] = middle[...]
        total[...] = jnp.zeros_like(total)

    def accumulate(up_ref, down_ref):
        apart_ff_backward_tile(normed_two[...], grad_ref[...], up_ref, down_ref, total, out_total)

    pl.when(index < steps)(lambda: accumulate(up_a, down_a))
    pl.when(index >= steps)(lambda: accumulate(up_b, down_b))

    @pl.when(index == 2 * steps - 1)
    def _():
        hidden_out[...] = out_total[...].astype(BF16)
        outs = (grad_middle, mixer_grad, grad_gate, grad_summed, grad_conv, gain_grad)
        apart_mixer_backward(
            sz,
            grad_ref[...].astype(F32),
            middle[...],
            total[...],
            gain_ref[1:2, :],
            mixed,
            summed,
            gate_ref,
            w_out,
            outs,
        )


def apart_turn(sz, layer, blocks, conv, inner, gate, skip, x, gains, grad, w_out, ff):
    tokens = x.shape[0]
    specs, steps = apart_ff_specs(sz, layer, 512)
    small = (conv, inner, gate, skip, x, gains, grad, w_out)
    outs = (((tokens, sz.width), BF16), ((tokens, sz.width), BF16)) + apart_mixer_outs(sz, tokens, blocks)
    return pl.pallas_call(
        functools.partial(apart_turn_kernel, sz, steps),
        grid=(2 * steps,),
        out_shape=tuple(jax.ShapeDtypeStruct(shape, kind) for shape, kind in outs),
        in_specs=[apart_full(entry.shape) for entry in small] + specs,
        out_specs=tuple(apart_full(shape) for shape, kind in outs),
        scratch_shapes=[
            pltpu.VMEM((sz.channels, tokens), F32),
            pltpu.VMEM((sz.channels, tokens), BF16),
            pltpu.VMEM((tokens, sz.width), F32),
            pltpu.VMEM((tokens, sz.width), F32),
            pltpu.VMEM((tokens, sz.width), F32),
        ],
        compiler_params=pltpu.CompilerParams(
            dimension_semantics=("arbitrary",), vmem_limit_bytes=48 * MIB
        ),
        name="token_turn",
    )(*small, *ff)


def apart_input_backward(
    sz, back, through, grad_gate, skip, normed, x, gain, w_in, w_gate, grad_middle, mixer_grad
):
    inner_grad = (skip * through + back.astype(F32)).astype(BF16)
    apart_block_grads(sz, inner_grad, normed, mixer_grad, 0)
    apart_block_grads(sz, grad_gate, normed, mixer_grad, 1)
    parts = []
    for side in range(sz.hid):
        rows = slice(side * sz.padded, (side + 1) * sz.padded)
        parts.append(tn(inner_grad[rows, :], w_in[side]) + tn(grad_gate[rows, :], w_gate[side]))
    normal, inv = normalize(x)
    result, gain_grad = norm_back(jnp.concatenate(parts, axis=1), normal, inv, gain)
    return grad_middle + result, gain_grad


def apart_backward_kernel(
    sz,
    steps,
    back_ref,
    through_ref,
    gate_grad_ref,
    skip_ref,
    normed_ref,
    x_ref,
    gain_ref,
    w_in,
    w_gate,
    grad_middle_ref,
    normed_two,
    middle_ref,
    summed_ref,
    gate_ref,
    mixed_ref,
    low_gain,
    w_out,
    up_a,
    down_a,
    up_b,
    down_b,
    input_grad,
    input_gain,
    grad_ff,
    grad_middle,
    mixer_grad,
    grad_gate,
    grad_summed,
    grad_conv,
    gain_grad,
    grad_next,
    total,
):
    index = pl.program_id(0)

    @pl.when(index == 0)
    def _():
        result, input_gain[...] = apart_input_backward(
            sz,
            back_ref[...],
            through_ref[...],
            gate_grad_ref[...],
            skip_ref[...],
            normed_ref[...],
            x_ref[...],
            gain_ref[0:1, :],
            w_in,
            w_gate,
            grad_middle_ref[...],
            input_grad,
        )
        grad_next[...] = result
        grad_ff[...] = result.astype(BF16)
        total[...] = jnp.zeros_like(total)

    def accumulate(up_ref, down_ref):
        apart_ff_backward_tile(normed_two[...], grad_ff[...], up_ref, down_ref, total, None)

    pl.when(index < steps)(lambda: accumulate(up_a, down_a))
    pl.when(index >= steps)(lambda: accumulate(up_b, down_b))

    @pl.when(index == 2 * steps - 1)
    def _():
        outs = (grad_middle, mixer_grad, grad_gate, grad_summed, grad_conv, gain_grad)
        apart_mixer_backward(
            sz,
            grad_next[...],
            middle_ref[...],
            total[...],
            low_gain[1:2, :],
            mixed_ref,
            summed_ref,
            gate_ref,
            w_out,
            outs,
        )


def apart_input_outs(sz, blocks):
    size = sz.width // blocks
    return (((2, blocks, sz.channels // blocks, size), BF16), ((1, sz.width), F32))


def apart_backward(
    sz,
    layer,
    blocks,
    back,
    through,
    gate_grad,
    skip,
    normed,
    x,
    gains,
    w_in,
    w_gate,
    grad_middle,
    normed_two,
    middle,
    summed,
    gate,
    mixed,
    low_gains,
    w_out,
    ff,
):
    tokens = x.shape[0]
    specs, steps = apart_ff_specs(sz, layer, 512)
    small = (
        back,
        through,
        gate_grad,
        skip,
        normed,
        x,
        gains,
        w_in,
        w_gate,
        grad_middle,
        normed_two,
        middle,
        summed,
        gate,
        mixed,
        low_gains,
        w_out,
    )
    outs = (
        apart_input_outs(sz, blocks) + (((tokens, sz.width), BF16),) + apart_mixer_outs(sz, tokens, blocks)
    )
    return pl.pallas_call(
        functools.partial(apart_backward_kernel, sz, steps),
        grid=(2 * steps,),
        out_shape=tuple(jax.ShapeDtypeStruct(shape, kind) for shape, kind in outs),
        in_specs=[apart_full(entry.shape) for entry in small] + specs,
        out_specs=tuple(apart_full(shape) for shape, kind in outs),
        scratch_shapes=[
            pltpu.VMEM((tokens, sz.width), F32),
            pltpu.VMEM((tokens, sz.width), F32),
        ],
        compiler_params=pltpu.CompilerParams(
            dimension_semantics=("arbitrary",), vmem_limit_bytes=48 * MIB
        ),
        name="token_backward",
    )(*small, *ff)


def apart_last_kernel(
    sz,
    back_ref,
    through_ref,
    gate_grad_ref,
    skip_ref,
    normed_ref,
    x_ref,
    gain_ref,
    w_in,
    w_gate,
    grad_middle_ref,
    input_grad,
    input_gain,
    grad_in,
):
    grad_in[...], input_gain[...] = apart_input_backward(
        sz,
        back_ref[...],
        through_ref[...],
        gate_grad_ref[...],
        skip_ref[...],
        normed_ref[...],
        x_ref[...].astype(F32),
        gain_ref[0:1, :],
        w_in,
        w_gate,
        grad_middle_ref[...],
        input_grad,
    )


def apart_last(sz, blocks, *args):
    tokens = args[5].shape[0]
    outs = apart_input_outs(sz, blocks) + (((tokens, sz.width), F32),)
    return pl.pallas_call(
        functools.partial(apart_last_kernel, sz),
        out_shape=tuple(jax.ShapeDtypeStruct(shape, kind) for shape, kind in outs),
        in_specs=[whole()] * len(args),
        out_specs=(whole(),) * len(outs),
        compiler_params=pltpu.CompilerParams(vmem_limit_bytes=32 * MIB),
        name="last_projection",
    )(*args)


def apart_ff_grads_kernel(normed_ref, grad_ref, up_ref, down_ref, out_ref, hidden, grad_gate, grad_up):
    tokens = normed_ref.shape[0]
    chunk = 256
    for start in range(0, tokens, chunk):
        rows = pl.ds(start, chunk)
        normed = normed_ref[rows, :]
        gate = nn(normed, up_ref[0])
        up = nn(normed, up_ref[1])
        through = nn(grad_ref[rows, :], down_ref[...])
        value, slope = gelu_parts(gate)
        hidden[rows, :] = (value * up).astype(BF16)
        grad_gate[rows, :] = (slope * up * through).astype(BF16)
        grad_up[rows, :] = (value * through).astype(BF16)
    out_ref[0] = tn(normed_ref[...], grad_gate[...]).astype(BF16)
    out_ref[1] = tn(normed_ref[...], grad_up[...]).astype(BF16)
    out_ref[2] = tn(grad_ref[...], hidden[...]).astype(BF16)


def apart_ff_grads(normed, grad, up, down):
    tokens, width = normed.shape
    units = down.shape[1]
    return pl.pallas_call(
        apart_ff_grads_kernel,
        out_shape=jax.ShapeDtypeStruct((3, width, units), BF16),
        in_specs=[whole()] * 4,
        out_specs=whole(),
        scratch_shapes=[pltpu.VMEM((tokens, units), BF16)] * 3,
        compiler_params=pltpu.CompilerParams(vmem_limit_bytes=48 * MIB),
        name="ff_weight_grads",
    )(normed, grad, up, down)


def apart_row_exchange_kernel(rows, parts, *refs):
    sources, targets, sems = refs[:parts], refs[parts : 2 * parts], refs[2 * parts]
    row = lax.axis_index("rows")
    col = lax.axis_index("hid")
    barrier = pltpu.get_barrier_semaphore()

    def greet(step, carry):
        peer = lax.rem(row + step, rows)
        pl.semaphore_signal(barrier, inc=1, device_id=(peer, col), device_id_type=MESH)
        return carry

    lax.fori_loop(1, rows, greet, 0)
    for part in range(parts):
        pltpu.make_async_copy(
            sources[part].at[row], targets[part].at[row], sems.at[part, 2]
        ).start()
    pl.semaphore_wait(barrier, rows - 1)

    def post(step, carry):
        peer = lax.rem(row + step, rows)
        for part in range(parts):
            pltpu.make_async_remote_copy(
                src_ref=sources[part].at[peer],
                dst_ref=targets[part].at[row],
                send_sem=sems.at[part, 0],
                recv_sem=sems.at[part, 1],
                device_id=(peer, col),
                device_id_type=MESH,
            ).start()
        return carry

    lax.fori_loop(1, rows, post, 0)
    for part in range(parts):
        pltpu.make_async_copy(
            sources[part].at[0], targets[part].at[0], sems.at[part, 2]
        ).wait()
        span = pl.ds(0, rows - 1)
        pltpu.make_async_remote_copy(
            src_ref=sources[part].at[span],
            dst_ref=targets[part].at[span],
            send_sem=sems.at[part, 0],
            recv_sem=sems.at[part, 1],
            device_id=(lax.rem(row + 1, rows), col),
            device_id_type=MESH,
        ).wait()


def apart_row_exchange(arrays, rows, cid):
    parts = len(arrays)
    return pl.pallas_call(
        functools.partial(apart_row_exchange_kernel, rows, parts),
        out_shape=tuple(jax.ShapeDtypeStruct(entry.shape, entry.dtype) for entry in arrays),
        in_specs=[pl.BlockSpec(memory_space=pl.ANY)] * parts,
        out_specs=(pl.BlockSpec(memory_space=pl.ANY),) * parts,
        scratch_shapes=[pltpu.SemaphoreType.DMA((parts, 3))],
        compiler_params=pltpu.CompilerParams(collective_id=cid, has_side_effects=True),
        name="row_exchange",
    )(*arrays)


def apart_swap(value):
    return lax.ppermute(value, "hid", [(0, 1), (1, 0)])


def apart_both_halves(own, axis):
    other = apart_swap(own)
    low = lax.axis_index("hid") == 0
    return jnp.concatenate([jnp.where(low, own, other), jnp.where(low, other, own)], axis=axis)


def apart_own_tokens(part):
    tokens = part.shape[0] // 2
    side = lax.axis_index("hid")
    keep = lax.dynamic_slice_in_dim(part, side * tokens, tokens, 0)
    other = apart_swap(lax.dynamic_slice_in_dim(part, (1 - side) * tokens, tokens, 0))
    low = side == 0
    return jnp.concatenate([jnp.where(low, keep, other), jnp.where(low, other, keep)], axis=1)


def apart_own_features(part):
    half = part.shape[1] // 2
    side = lax.axis_index("hid")
    keep = lax.dynamic_slice_in_dim(part, side * half, half, 1)
    other = apart_swap(lax.dynamic_slice_in_dim(part, (1 - side) * half, half, 1))
    low = side == 0
    return jnp.concatenate([jnp.where(low, keep, other), jnp.where(low, other, keep)], axis=0)


def apart_padded_mixer(sz, mixer):
    layers, kinds, blocks, size, _ = mixer.shape
    chan_first = jnp.concatenate([jnp.swapaxes(mixer[:, :2], 3, 4), mixer[:, 2:]], axis=1)
    grouped = chan_first.reshape(layers, kinds, blocks, size // sz.chans, sz.chans, size)
    grouped = jnp.pad(grouped, ((0, 0),) * 4 + ((0, sz.piece - sz.chans), (0, 0)))
    grouped = grouped.reshape(layers, kinds, blocks, -1, size)
    parts = [
        jnp.pad(grouped[:, :, block], ((0, 0),) * 3 + ((block * size, (blocks - 1 - block) * size),))
        for block in range(blocks)
    ]
    return jnp.concatenate(parts, axis=2)


def apart_padded_channels(sz, values):
    lead = values.shape[:-1]
    grouped = values.reshape(lead + (sz.rows, sz.chans))
    grouped = jnp.pad(grouped, ((0, 0),) * (len(lead) + 1) + ((0, sz.piece - sz.chans),))
    return grouped.reshape(lead + (sz.padded,))


def apart_envelopes(sz):
    row = lax.axis_index("rows")
    first_chan = lax.axis_index("hid") * sz.half + row * sz.chans
    channels = first_chan + jnp.arange(sz.piece, dtype=jnp.int32)
    fraction = (channels * 37 % sz.width).astype(F32) / (sz.width - 1)
    start_log = math.log(1.0 / 40.0)
    rate = jnp.exp(start_log + (math.log(1.5 / sz.length) - start_log) * fraction)
    steps = jnp.arange(sz.length, dtype=jnp.int32).astype(F32)
    decay = jnp.exp(-steps[None, :] * rate[:, None])
    shape = decay * lax.rsqrt(2.0 * jnp.sum(decay * decay, axis=1, keepdims=True))
    return jnp.concatenate([shape, shape * (steps > 0)[None, :]], axis=0)


def apart_plane_gather(value):
    size = lax.axis_size("rows")
    for bit in (1, 2):
        other = lax.ppermute(value, "rows", [(r, r ^ bit) for r in range(size)])
        value = jnp.concatenate([value, other], axis=0)
    return jnp.concatenate([value, apart_swap(value)], axis=0)


def apart_on_device(hidden_in, d_out, gains, mixer, skip, filters, gate_up, down):
    layers = gate_up.shape[0]
    rows = lax.axis_size("rows")
    hid = lax.axis_size("hid")
    width = gate_up.shape[2]
    hidden = gate_up.shape[3] * hid
    blocks = mixer.shape[2] * hid
    block_size = mixer.shape[3]
    sz = apart_Sizes(rows, hid, width, hidden, hidden_in.shape[0] * rows)
    row = lax.axis_index("rows")

    x = apart_own_tokens(hidden_in)
    gains_all = apart_both_halves(gains, 2)
    skip_all = apart_both_halves(apart_padded_channels(sz, skip), 1)[:, :, None]
    weights = apart_both_halves(apart_padded_mixer(sz, mixer)[:, :, None], 2)
    gate_up_b = apart_swap(gate_up)
    down_b = apart_swap(down)
    ff = (gate_up, down, gate_up_b, down_b)
    grad_out = apart_own_tokens(d_out)

    tables = dft_tables(sz.length)
    pos = jnp.asarray(position_table(sz.length).T, F32).astype(BF16)
    env = apart_envelopes(sz)
    taps = lax.dynamic_slice_in_dim(filters, row * sz.chans, sz.chans, 3)
    taps = jnp.pad(taps, ((0, 0),) * 3 + ((0, sz.piece - sz.chans),))
    taps = jnp.swapaxes(taps, 2, 3).reshape(layers, 2 * sz.piece, ORDER).astype(BF16)

    normed, inner, gate = apart_first(sz, x, gains_all[0], weights[0, 0], weights[0, 1])
    stored = []
    for layer in range(layers):
        conv, filt_spec, sig_spec = apart_conv_forward(sz, inner, taps[layer], pos, env, tables, 0)
        stored.append(dict(x=x, normed=normed, inner=inner, gate=gate, f=filt_spec, s=sig_spec))
        if layer < layers - 1:
            summed, mixed, middle, normed_two, x, normed, next_inner, next_gate = apart_forward(
                sz,
                layer,
                conv,
                inner,
                gate,
                skip_all[layer],
                x,
                gains_all[layer],
                gains_all[layer + 1],
                weights[layer, 2],
                weights[layer + 1, 0],
                weights[layer + 1, 1],
                ff,
            )
            stored[-1].update(summed=summed, mixed=mixed, middle=middle, normed_two=normed_two)
            inner, gate = next_inner, next_gate

    top = layers - 1
    hidden_out, normed_two, *rest = apart_turn(
        sz,
        top,
        blocks,
        conv,
        inner,
        gate,
        skip_all[top],
        x,
        gains_all[top],
        grad_out,
        weights[top, 2],
        ff,
    )
    stored[top].update(normed_two=normed_two)
    grad_ff = grad_out
    units = sz.hidden // hid // 4
    unit_start = lax.rem(row, 4) * units
    ff_parts, mixer_parts, gain_parts, skip_parts, taps_parts = [], [], [], [], []
    for layer in reversed(range(layers)):
        kept = stored[layer]
        grad_middle, out_grad, grad_gate, grad_summed, grad_conv, gain_two = rest
        ff_parts.insert(
            0,
            apart_ff_grads(
                apart_plane_gather(kept["normed_two"]),
                apart_plane_gather(grad_ff),
                lax.dynamic_slice_in_dim(gate_up[layer], unit_start, units, 2),
                lax.dynamic_slice_in_dim(down[layer], unit_start, units, 1),
            ),
        )
        back, taps_grad = apart_conv_backward(
            sz, grad_conv, kept["f"], kept["s"], taps[layer], pos, env, tables, 1
        )
        skip_parts.insert(0, jnp.sum(grad_summed * kept["inner"].astype(F32), axis=1))
        taps_parts.insert(0, taps_grad)
        common = (
            back,
            grad_summed,
            grad_gate,
            skip_all[layer],
            kept["normed"],
            kept["x"],
            gains_all[layer],
            weights[layer, 0],
            weights[layer, 1],
            grad_middle,
        )
        if layer > 0:
            low = stored[layer - 1]
            in_grad, gain_one, grad_ff, *rest = apart_backward(
                sz,
                layer - 1,
                blocks,
                *common,
                low["normed_two"],
                low["middle"],
                low["summed"],
                low["gate"],
                low["mixed"],
                gains_all[layer - 1],
                weights[layer - 1, 2],
                ff,
            )
        else:
            in_grad, gain_one, grad_in = apart_last(sz, blocks, *common)
        mixer_parts.insert(0, jnp.concatenate([in_grad, out_grad], axis=0))
        gain_parts.insert(0, jnp.concatenate([gain_one, gain_two], axis=0))

    piece_rows = width // rows
    padded_rows = round_up(piece_rows, 16)
    pieces = jnp.stack(ff_parts).reshape(layers, 3, rows, piece_rows, units)
    pieces = jnp.pad(pieces, ((0, 0),) * 3 + ((0, padded_rows - piece_rows), (0, 0)))
    pieces = jnp.moveaxis(pieces, 2, 0)
    (arrived,) = apart_row_exchange((pieces,), rows, 2)
    arrived = arrived.reshape(rows // 4, 4, layers, 3, padded_rows, units)[:, :, :, :, :piece_rows]
    summed_ff = jnp.sum(arrived.astype(F32), axis=0)
    summed_ff = jnp.moveaxis(summed_ff, 0, 3).reshape(layers, 3, piece_rows, 4 * units)

    mixers = jnp.stack(mixer_parts).reshape(layers, 3, blocks, -1, sz.piece, block_size)
    mixers = mixers[:, :, :, :, : sz.chans].reshape(layers, 3, blocks, block_size, block_size)
    small = jnp.concatenate(
        [jnp.stack(gain_parts).reshape(-1), jnp.stack(skip_parts).reshape(-1)]
    )
    mixers, small = lax.psum((mixers.astype(F32), small), ("rows", "hid"))
    side = lax.axis_index("hid")
    mixers = lax.dynamic_slice_in_dim(mixers, side * (blocks // hid), blocks // hid, 2)
    mixers = jnp.concatenate([jnp.swapaxes(mixers[:, :2], 3, 4), mixers[:, 2:]], axis=1)
    gain_size = layers * 2 * width
    gain_out = lax.dynamic_slice_in_dim(
        small[:gain_size].reshape(layers, 2, width), side * sz.half, sz.half, 2
    )
    skip_out = small[gain_size:].reshape(layers, hid, rows, sz.piece)[..., : sz.chans]
    skip_out = lax.dynamic_index_in_dim(skip_out, side, 1, False).reshape(layers, sz.half)
    taps_out = jnp.stack(taps_parts).reshape(layers, 2, sz.piece, ORDER)[:, :, : sz.chans]
    taps_out = lax.all_gather(taps_out, "rows", axis=2, tiled=True)
    return (
        apart_own_features(hidden_out),
        apart_own_features(grad_in),
        gain_out,
        mixers,
        skip_out,
        jnp.swapaxes(taps_out, 2, 3),
        summed_ff[:, :2],
        summed_ff[:, 2],
    )


def on_device(*arrays):
    sz = Sizes.of(*arrays)
    return together(sz, *arrays) if sz.fits() else apart_on_device(*arrays)


def solution(mesh):
    placed = (
        P("rows", "hid"),
        P("rows", "hid"),
        P(None, None, "hid"),
        P(None, None, "hid", None, None),
        P(None, "hid"),
        P(None, None, None, "hid"),
        P(None, None, None, "hid"),
        P(None, None, "hid"),
    )
    return jax.shard_map(
        on_device,
        mesh=mesh,
        in_specs=placed,
        out_specs=(
            P("rows", "hid"),
            P("rows", "hid"),
            P(None, None, "hid"),
            P(None, None, "hid", None, None),
            P(None, "hid"),
            P(None, None, None, "hid"),
            P(None, None, "rows", "hid"),
            P(None, "rows", "hid"),
        ),
        check_vma=False,
    )
```

```python
import functools
import math

import jax
import jax.numpy as jnp
import numpy as np
from jax import lax
from jax.experimental import pallas as pl
from jax.experimental.pallas import tpu as pltpu
from jax.sharding import PartitionSpec as P

ORDER = 128
SEQ_LEN = 8192
LANES = 128
NORM_EPS = 1e-05
DECAY = 0.02
MESH = pl.DeviceIdType.MESH
BF16 = jnp.bfloat16
F32 = jnp.float32
MIB = 2**20
GELU_C = math.sqrt(2.0 / math.pi)


def round_up(value, step):
    return -(-value // step) * step


def whole():
    return pl.BlockSpec(memory_space=pltpu.VMEM)


def nn(a, b):
    return lax.dot_general(a, b, (((1,), (0,)), ((), ())), preferred_element_type=F32)


def nt(a, b):
    return lax.dot_general(a, b, (((1,), (1,)), ((), ())), preferred_element_type=F32)


def tn(a, b):
    return lax.dot_general(a, b, (((0,), (0,)), ((), ())), preferred_element_type=F32)


def position_table(length):
    half_order = ORDER // 2
    index_list = np.arange(half_order)
    multiple = 1 + index_list * index_list * (length // 4) // (half_order * half_order)
    phase = (np.arange(length)[:, None] * multiple[None, :] % length) * (2.0 * math.pi / length)
    return np.concatenate([np.sin(phase), np.cos(phase)], axis=1)


def dft_tables(length):
    blocks = length // LANES
    size = 2 * length
    outer = 2 * blocks
    k = np.arange(outer)
    n = np.arange(blocks)
    m = np.arange(LANES)
    angle = 2.0 * math.pi * (np.outer(k, n) % outer) / outer
    outer_fwd = np.concatenate([np.cos(angle), -np.sin(angle)], axis=0)
    outer_inv = np.concatenate([np.cos(angle), -np.sin(angle)], axis=0).T / size
    angle = 2.0 * math.pi * (np.outer(m, m) % LANES) / LANES
    cos, sin = np.cos(angle), np.sin(angle)
    inner_fwd = np.block([[cos, -sin], [sin, cos]])
    inner_inv = np.block([[cos, sin], [-sin, cos]])
    angle = 2.0 * math.pi * np.outer(k, m) / size
    twist = np.concatenate([np.cos(angle), np.sin(angle)], axis=1)
    half = lambda table: jnp.asarray(table, F32).astype(BF16)
    return (half(outer_fwd), half(outer_inv), half(inner_fwd), half(inner_inv), jnp.asarray(twist, F32))


def normalize(values):
    mean = jnp.mean(values, axis=1, keepdims=True)
    square = jnp.mean(values * values, axis=1, keepdims=True)
    inv = lax.rsqrt(square - mean * mean + NORM_EPS)
    return (values - mean) * inv, inv


def norm_back(grad, normal, inv, gain):
    scaled = grad * gain
    mean = jnp.mean(scaled, axis=1, keepdims=True)
    cross = jnp.mean(scaled * normal, axis=1, keepdims=True)
    return inv * (scaled - mean - normal * cross), jnp.sum(grad * normal, axis=0, keepdims=True)


def gelu_parts(gate):
    square = gate * gate
    tanh = jnp.tanh(GELU_C * gate * (1.0 + 0.044715 * square))
    half = 0.5 * (1.0 + tanh)
    value = gate * half
    slope = half + 0.5 * gate * (1.0 - tanh * tanh) * (GELU_C * (1.0 + 3.0 * 0.044715 * square))
    return value, slope


class Sizes:
    def __init__(self, rows, hid, tokens, width, hidden, layers, blocks):
        self.rows, self.hid, self.width, self.layers = rows, hid, width, layers
        self.count = rows * hid
        self.own = tokens // self.count
        self.half = width // hid
        self.units = hidden // hid
        self.blocks = blocks
        self.size = width // blocks
        self.side_blocks = blocks // hid
        self.couple = 2 * width // self.count
        self.big = round_up(self.couple // 2, 16)
        self.small = self.couple - self.big
        self.length = min(SEQ_LEN, tokens)
        self.seqs = tokens // self.length
        self.steps = self.length // LANES
        self.outer = 2 * self.steps
        self.pairs = self.seqs * self.big
        self.group = 4
        self.peers = rows // self.group
        self.part = self.units // self.group
        self.depth = width // rows
        self.deep = round_up(self.depth, 16)
        self.deeps = tuple(
            round_up(-(-(matrices * self.size + 16) // rows), 16)
            for matrices in (3 * layers - 1, 1)
        )
        self.taps_rows = round_up(2 * self.big + 1, 16)


    @classmethod
    def of(cls, hidden_in, d_out, gains, mixer, skip, filters, gate_up, down):
        rows, hid = lax.axis_size("rows"), lax.axis_size("hid")
        layers, _, width, units = gate_up.shape
        tokens = hidden_in.shape[0] * rows
        return cls(rows, hid, tokens, width, units * hid, layers, mixer.shape[2] * hid)


    def fits(self):
        whole_tiles = self.small == 16 and self.big == 32 and self.rows % 8 == 0
        whole_tiles = whole_tiles and self.own == LANES and self.depth % 16 == 0
        whole_tiles = whole_tiles and self.peers == 4 and self.layers == 2 and self.seqs == 1
        whole_tiles = whole_tiles and all(self.size % deep == 0 for deep in self.deeps)
        total = 0
        for spec in layout(self)[1]:
            size = jnp.dtype(spec.dtype).itemsize
            *lead, rows, lanes = spec.shape
            total += math.prod(lead) * round_up(rows, 32 // size) * round_up(lanes, LANES) * size
        return whole_tiles and total <= 60 * MIB


class Links:
    def __init__(self, sz, sems, local_sems):
        self.sz, self.sems, self.local_sems = sz, sems, local_sems
        self.used = 0
        self.used_local = 0
        self.row = lax.axis_index("rows")
        self.col = lax.axis_index("hid")
        self.plane = lax.rem(self.row, sz.peers)
        self.line = self.row // sz.peers

    def pair(self):
        first = self.used
        self.used += 2
        return self.sems.at[first], self.sems.at[first + 1]

    def copy(self, source, target, pair, row, col):
        return pltpu.make_async_remote_copy(
            src_ref=source,
            dst_ref=target,
            send_sem=pair[0],
            recv_sem=pair[1],
            device_id=(row, col),
            device_id_type=MESH,
        )

    def sibling(self, source, target):
        copy = self.copy(source, target, self.pair(), self.row, self.sz.hid - 1 - self.col)
        copy.start()
        return copy

    def load(self, source, target):
        copy = pltpu.make_async_copy(source, target, self.local_sems.at[self.used_local])
        self.used_local += 1
        copy.start()
        return copy

    def groups(self, count, me, row_of, source_of, target):
        pair = self.pair()

        def post(step, carry):
            member = lax.rem(me + step, count)
            self.copy(source_of(member), target, pair, row_of(member), self.col).start()
            return carry

        lax.fori_loop(1, count, post, 0)
        return pair

    def in_plane(self, source_of, target):
        row_of = lambda member: self.line * self.sz.peers + member
        return self.groups(self.sz.peers, self.plane, row_of, source_of, target)

    def in_line(self, source_of, target):
        row_of = lambda member: member * self.sz.peers + self.plane
        return self.groups(self.sz.group, self.line, row_of, source_of, target)

    def in_rows(self, source_of, target):
        return self.groups(self.sz.rows, self.row, lambda member: member, source_of, target)

    def wait(self, pair, span):
        self.copy(span, span, pair, self.row, self.sz.hid - 1 - self.col).wait()


class Plane:
    def __init__(self, links):
        self.links = links
        self.me = links.plane
        along_x = self.me + 1 - 2 * lax.rem(self.me, 2)
        along_y = self.me + 2 - 4 * (self.me // 2)
        self.near = (along_x, along_y)
        self.far = (along_y, along_x)
        self.across = 3 - self.me

    def send(self, copies):
        links = self.links
        pair = links.pair()
        for source, target, member in copies:
            row = links.line * links.sz.peers + member
            links.copy(source, target, pair, row, links.col).start()
        return pair


class PlaneSum(Plane):
    def __init__(self, links, source, first, give, second):
        super().__init__(links)
        self.source, self.first, self.give, self.second = source, first, give, second

    def start(self):
        copies = []
        for half in range(2):
            for which, member in enumerate((self.near[half], self.across)):
                target = self.first.at[half, which]
                copies.append((self.source(member, half), target, self.near[half]))
        self.pair = self.send(copies)

    def middle(self):
        self.links.wait(self.pair, self.first)
        copies = []
        for half in range(2):
            theirs = self.source(self.far[half], half)[...].astype(F32)
            self.give[half] = (theirs + self.first[half, 1].astype(F32)).astype(BF16)
            mine = self.source(self.me, half)[...].astype(F32)
            self.first[half, 0] = (mine + self.first[half, 0].astype(F32)).astype(BF16)
            copies.append((self.give.at[half], self.second.at[half], self.far[half]))
        self.pair = self.send(copies)

    def end(self):
        self.links.wait(self.pair, self.second)

    def sums(self):
        for half in range(2):
            total = self.first[half, 0].astype(F32) + self.second[half].astype(F32)
            self.second[half] = total.astype(BF16)
        count = self.links.sz.group // 2
        return lambda member: self.second.at[member // count, lax.rem(member, count)]


class DirectSum(Plane):
    def __init__(self, links, source, parts):
        super().__init__(links)
        self.source, self.parts = source, parts

    def start(self):
        self.pair = self.links.in_plane(self.source, self.parts.at[self.me])

    def end(self):
        links = self.links
        links.wait(self.pair, self.parts.at[pl.ds(0, links.sz.peers - 1)])

    def sums(self):
        self.parts[self.me] = self.source(self.me)[...]
        total = self.parts[0].astype(F32)
        for member in range(1, self.links.sz.peers):
            total += self.parts[member].astype(F32)
        self.parts[0] = total.astype(BF16)
        return lambda member: self.parts.at[0, member]


class PlaneSpread(Plane):
    def __init__(self, links, place, span):
        super().__init__(links)
        self.place, self.span = place, span

    def start(self):
        copies = []
        for half in range(2):
            here = self.place(self.me, half)
            copies.append((here, here, self.near[half]))
        self.pair = self.send(copies)

    def middle(self):
        self.links.wait(self.pair, self.span(1))
        copies = []
        for half in range(2):
            for member in (self.me, self.near[half]):
                here = self.place(member, half)
                copies.append((here, here, self.far[half]))
        self.pair = self.send(copies)

    def end(self):
        self.links.wait(self.pair, self.span(2))


LOAD_BUFFERS = ("mine", "give", "got", "first", "second_give", "second", "line_in", "out")


class Payload:
    def __init__(self, sz, b, links, index, output):
        self.sz, self.links, self.output = sz, links, output
        self.direct = index == 1
        self.deep = sz.deeps[index]
        for name in LOAD_BUFFERS:
            setattr(self, name, getattr(b, "load_" + name)[index])
        half = lambda which: pl.ds(which * (sz.group // 2), sz.group // 2)
        self.plane = PlaneSum(
            links,
            lambda member, which: self.mine.at[member, half(which)],
            self.first,
            self.second_give,
            self.second,
        )
        if self.direct:
            self.plane = DirectSum(links, lambda member: self.mine.at[member], b.late_parts)
        self.spread = PlaneSpread(
            links,
            lambda member, which: self.got.at[member, half(which)],
            lambda count: self.got.at[pl.ds(0, count)],
        )
        self.half = half

    def matrix(self, place, values):
        sz = self.sz
        low = lax.axis_index("hid") == 0
        left = jnp.concatenate(values[: sz.side_blocks], axis=1)
        right = jnp.concatenate(values[sz.side_blocks :], axis=1)
        mine = jnp.where(low, left, right).astype(BF16)
        give = jnp.where(low, right, left).astype(BF16)
        count = sz.size // self.deep
        for part in range(count):
            index = place * count + part
            rows = slice(part * self.deep, (part + 1) * self.deep)
            self.mine[index // sz.group, index % sz.group] = mine[rows, :]
            self.give[index // sz.group, index % sz.group] = give[rows, :]

    def rows16(self, place, mine, give):
        index = place * (self.sz.size // self.deep)
        self.mine[index // self.sz.group, index % self.sz.group, 0:16] = mine.astype(BF16)
        self.give[index // self.sz.group, index % self.sz.group, 0:16] = give.astype(BF16)

    def to_partner(self):
        self.copy = self.links.sibling(self.give, self.got)

    def to_plane(self):
        done(self.copy)
        self.mine[...] = (self.mine[...].astype(F32) + self.got[...].astype(F32)).astype(BF16)
        self.plane.start()

    def middle(self):
        self.plane.middle()

    def to_line(self):
        self.plane.end()
        self.sums = self.plane.sums()
        links = self.links
        self.pair = links.in_line(self.sums, self.line_in.at[links.line])

    def back_line(self):
        links, sz = self.links, self.sz
        links.wait(self.pair, self.line_in.at[pl.ds(0, sz.group - 1)])
        self.line_in[links.line] = self.sums(links.line)[...]
        total = self.line_in[0].astype(F32)
        for member in range(1, sz.group):
            total += self.line_in[member].astype(F32)
        self.out[...] = total.astype(BF16)
        self.got[links.plane, links.line] = self.out[...]
        self.pair = links.in_line(lambda member: self.out, self.got.at[links.plane, links.line])

    def back_plane(self):
        links = self.links
        links.wait(self.pair, self.got.at[0, pl.ds(0, self.sz.group - 1)])
        if self.direct:
            place = self.got.at[links.plane]
            self.pair = links.in_plane(lambda member: place, place)
        else:
            self.spread.start()

    def finish(self):
        if self.direct:
            self.links.wait(self.pair, self.got.at[pl.ds(0, self.sz.peers - 1)])
        else:
            self.spread.end()
        return self.links.load(self.got, self.output)


def greet_all(sz):
    me = lax.axis_index("rows") * sz.hid + lax.axis_index("hid")
    barrier = pltpu.get_barrier_semaphore()

    def greet(step, carry):
        peer = lax.rem(me + step, sz.count)
        pl.semaphore_signal(
            barrier,
            inc=1,
            device_id=(peer // sz.hid, lax.rem(peer, sz.hid)),
            device_id_type=MESH,
        )
        return carry

    lax.fori_loop(1, sz.count, greet, 0)
    return barrier


class Exchange:
    def __init__(self, sz, links):
        self.sz, self.links = sz, links
        self.odd = lax.rem(links.row, 2)
        self.token = links.row * sz.hid + links.col

    def channels(self, row, col, part):
        sz = self.sz
        start = col * sz.half + (row // 2) * sz.couple + lax.rem(row, 2) * sz.big
        return pl.ds(pl.multiple_of(start + part * 16, 16), 16)

    def block(self, token):
        return pl.ds(pl.multiple_of(token * 16, 16), 16)

    def far_first(self):
        line = self.links.line
        odd = lax.rem(line, 2)
        across = 2 * (1 - line // 2)
        return across + odd, across + 1 - odd, line + 1 - 2 * odd, line

    def owners(self, part, body):
        if part == 0:
            body()
        else:
            pl.when(self.odd == 0)(body)

    def local(self):
        local = self.links.local_sems.at[self.links.used_local]
        self.links.used_local += 1
        return local

    def to_owners(self, source, target):
        return [self.part_to_owners(source, target, part) for part in range(2)]

    def part_to_owners(self, source, target, part):
        sz, links = self.sz, self.links
        pair, local = links.pair(), self.local()
        there = target.at[part, self.block(self.token)]

        def own():
            mine = source.at[self.channels(links.row, links.col, part)]
            pltpu.make_async_copy(mine, there, local).start()

        self.owners(part, own)
        apart = 1 + part
        devices = sz.peers * sz.hid // apart
        first = (links.plane // apart) * sz.hid + links.col

        for turn, line in enumerate(self.far_first()):

            def post(step, carry):
                index = lax.rem(first + step, devices)
                row, col = line * sz.peers + apart * (index // sz.hid), lax.rem(index, sz.hid)
                piece = source.at[self.channels(row, col, part)]
                links.copy(piece, there, pair, row, col).start()
                return carry

            if turn < sz.group - 1:
                lax.fori_loop(0, devices, post, 0)
            else:
                lax.fori_loop(1, devices, post, 0)
                if part == 1:

                    @pl.when(self.odd == 1)
                    def _():
                        post(0, 0)

        return pair, local

    def to_tokens(self, source, target, part):
        sz, links = self.sz, self.links
        pair, local = links.pair(), self.local()
        there = target.at[self.channels(links.row, links.col, part)]

        def send():
            mine = source.at[part, self.block(self.token)]
            pltpu.make_async_copy(mine, there, local).start()
            devices = sz.peers * sz.hid
            first = links.plane * sz.hid + links.col

            for turn, line in enumerate(self.far_first()):

                def post(step, carry):
                    index = lax.rem(first + step, devices)
                    row, col = line * sz.peers + index // sz.hid, lax.rem(index, sz.hid)
                    piece = source.at[part, self.block(row * sz.hid + col)]
                    links.copy(piece, there, pair, row, col).start()
                    return carry

                lax.fori_loop(0 if turn < sz.group - 1 else 1, devices, post, 0)

        self.owners(part, send)
        return pair, local

    def wait(self, tokens, part, flat, sent_to_owners):
        sz, links = self.sz, self.links
        pair, local = tokens
        rows = lambda count: flat.at[pl.ds(0, count * 16)]
        all_devices = sz.count - 1

        def owner_side():
            pltpu.make_async_copy(rows(1), rows(1), local).wait()
            copy = links.copy(rows(all_devices), rows(all_devices), pair, links.row, 1 - links.col)
            if sent_to_owners:
                copy.wait_recv()
            else:
                copy.wait_send()

        def token_side(count):
            copy = links.copy(rows(count), rows(count), pair, links.row, 1 - links.col)
            if sent_to_owners:
                copy.wait_send()
            else:
                copy.wait_recv()

        self.owners(part, owner_side)
        if part == 0:
            token_side(all_devices)
        else:
            pl.when(self.odd == 0)(lambda: token_side(sz.count // 2 - 1))
            pl.when(self.odd == 1)(lambda: token_side(sz.count // 2))

    def owners_wait(self, tokens, part, target):
        self.wait(tokens[part], part, target.at[0], True)

    def tokens_wait(self, tokens, source):
        for part in range(2):
            self.wait(tokens[part], part, source.at[0], False)


CHUNK = 8


def place(index, size):
    return pl.ds(pl.multiple_of(index * size, size), size)


def dft(sz, b, source, base, stride, target, first=0, chunks=4, unroll=2):
    steps, outer = sz.steps, sz.outer

    def chunk(index, carry):
        cos = b.twist[:, :LANES]
        sin = b.twist[:, LANES:]
        for line in range(CHUNK):
            start = base + (index - first) * CHUNK + line
            b.wide[:, line * LANES : (line + 1) * LANES] = source[
                pl.ds(start, steps, stride=stride), :
            ].astype(BF16)
        b.mid[...] = nn(b.outer_fwd[...], b.wide[...])
        for line in range(CHUNK):
            lanes = slice(line * LANES, (line + 1) * LANES)
            real = b.mid[0:outer, lanes]
            imag = b.mid[outer : 2 * outer, lanes]
            rows = slice(line * outer, (line + 1) * outer)
            b.turned[rows, 0:LANES] = (real * cos + imag * sin).astype(BF16)
            b.turned[rows, LANES:] = (imag * cos - real * sin).astype(BF16)
        target[place(index, CHUNK * outer), :] = nn(b.turned[...], b.inner_fwd[...])
        return carry

    lax.fori_loop(first, first + chunks, chunk, 0, unroll=unroll)


def inverse_dft(sz, b, target, base, stride, first=0, chunks=4, unroll=2):
    steps, outer = sz.steps, sz.outer

    def chunk(index, carry):
        cos = b.twist[:, :LANES]
        sin = b.twist[:, LANES:]
        part = nn(b.flat[place(index, CHUNK * outer), :], b.inner_inv[...])
        for line in range(CHUNK):
            rows = slice(line * outer, (line + 1) * outer)
            lanes = slice(line * LANES, (line + 1) * LANES)
            real = part[rows, :LANES]
            imag = part[rows, LANES:]
            b.mid_half[0:outer, lanes] = (real * cos - imag * sin).astype(BF16)
            b.mid_half[outer : 2 * outer, lanes] = (imag * cos + real * sin).astype(BF16)
        value = nn(b.outer_inv[...], b.mid_half[...])
        for line in range(CHUNK):
            start = base + (index - first) * CHUNK + line
            target[pl.ds(start, steps, stride=stride), :] = value[
                :, line * LANES : (line + 1) * LANES
            ]
        return carry

    lax.fori_loop(first, first + chunks, chunk, 0, unroll=unroll)


def first_channel(sz):
    row = lax.axis_index("rows")
    return (row // 2) * sz.couple + lax.rem(row, 2) * sz.big


def own_taps(sz, filters):
    start = first_channel(sz)
    chan = lax.broadcasted_iota(jnp.int32, (sz.big, sz.half), 0)
    lane = lax.broadcasted_iota(jnp.int32, (sz.big, sz.half), 1)
    pick = jnp.where(lane == start + chan, 1.0, 0.0).astype(BF16)
    parts = [nt(pick, filters[way].astype(BF16)) for way in range(2)]
    return jnp.concatenate(parts, axis=0).astype(BF16)


def own_envelope(sz, env):
    first_chan = lax.axis_index("hid") * sz.half + first_channel(sz)
    channel = first_chan + lax.broadcasted_iota(jnp.int32, (sz.big, LANES), 0)
    fraction = lax.rem(channel * 37, sz.width).astype(F32) / (sz.width - 1)
    start_log = math.log(1.0 / 40.0)
    rate = jnp.exp(start_log + (math.log(1.5 / sz.length) - start_log) * fraction)
    lane = lax.broadcasted_iota(jnp.int32, (sz.big, LANES), 1)

    def decays(step, power):
        decay = jnp.exp(-(lane + step * LANES).astype(F32) * rate)
        env[0 : sz.big, place(step, LANES)] = decay
        return power + decay * decay

    power = lax.fori_loop(0, sz.steps, decays, jnp.zeros((sz.big, LANES), F32), unroll=4)
    scale = lax.rsqrt(2.0 * jnp.sum(power, axis=1, keepdims=True))

    def scaled(step, carry):
        value = env[0 : sz.big, place(step, LANES)] * scale
        env[0 : sz.big, place(step, LANES)] = value
        env[sz.big :, place(step, LANES)] = jnp.where(lane + step * LANES > 0, value, 0.0)
        return carry

    lax.fori_loop(0, sz.steps, scaled, 0, unroll=4)


def filter_spectrum(sz, b, layer):
    piece, steps, outer = sz.big, sz.steps, sz.outer
    taps = own_taps(sz, b.filters[layer])
    count = 4

    def chunk(index, carry):
        lanes = place(index, count * LANES)
        kernels = nn(taps, b.pos[:, lanes]) * b.env[:, lanes]
        rows = pl.multiple_of(index * count * 2 * piece, 2 * piece)
        for step in range(count):
            b.tall[pl.ds(rows + step * 2 * piece, 2 * piece), :] = kernels[
                :, step * LANES : (step + 1) * LANES
            ]
        return carry

    lax.fori_loop(0, steps // count, chunk, 0, unroll=2)
    spec = b.filt_spec[layer]
    span = sz.big * outer
    for way in range(2):
        dft(sz, b, b.tall, way * piece, 2 * piece, b.spec, unroll=1)
        if way == 0:
            spec[...] = b.spec[0:span, :].astype(BF16)
        else:
            spec[:, :LANES] = (spec[:, :LANES].astype(F32) + b.spec[0:span, :LANES]).astype(BF16)
            spec[:, LANES:] = (spec[:, LANES:].astype(F32) - b.spec[0:span, LANES:]).astype(BF16)


def convolve(sz, b, layer, landed, part, back):
    count = 16 // CHUNK
    b.tall[0 : sz.count * 16, :] = landed[part].astype(F32)
    dft(sz, b, b.tall, 0, 16, b.spec, part * count, count, True)
    filt = b.filt_spec[layer]
    rows = slice(part * 16 * sz.outer, (part + 1) * 16 * sz.outer)
    re, im = b.spec[rows, :LANES], b.spec[rows, LANES:]
    fil_re, fil_im = filt[rows, :LANES].astype(F32), filt[rows, LANES:].astype(F32)
    if back:
        b.flat[rows, :LANES] = (re * fil_re + im * fil_im).astype(BF16)
        b.flat[rows, LANES:] = (im * fil_re - re * fil_im).astype(BF16)
    else:
        b.sig_spec[layer][rows, :LANES] = re.astype(BF16)
        b.sig_spec[layer][rows, LANES:] = im.astype(BF16)
        b.flat[rows, :LANES] = (re * fil_re - im * fil_im).astype(BF16)
        b.flat[rows, LANES:] = (re * fil_im + im * fil_re).astype(BF16)
    inverse_dft(sz, b, b.tall, 0, 16, part * count, count, True)
    b.staged[part] = b.tall[0 : sz.count * 16, :].astype(BF16)


def conv_forward(sz, b, layer, landed, part):
    convolve(sz, b, layer, landed, part, False)


def conv_backward(sz, b, layer, landed, part):
    convolve(sz, b, layer, landed, part, True)


def taps_gradient(sz, b, layer, landed, signal):
    span = sz.big * sz.outer
    total_re = jnp.zeros((span, LANES), F32)
    total_im = jnp.zeros((span, LANES), F32)
    for seq in range(sz.seqs):
        rows = slice(seq * span, (seq + 1) * span)
        re, im = b.spec[rows, :LANES], b.spec[rows, LANES:]
        sig = b.sig_spec[layer]
        sig_re, sig_im = sig[rows, :LANES].astype(F32), sig[rows, LANES:].astype(F32)
        total_re += re * sig_re + im * sig_im
        total_im += im * sig_re - re * sig_im
    piece = sz.big
    b.tall[...] = jnp.zeros_like(b.tall)
    for way in range(2):
        b.flat[0:span, :LANES] = total_re.astype(BF16)
        b.flat[0:span, LANES:] = (total_im if way == 0 else -total_im).astype(BF16)
        inverse_dft(sz, b, b.tall, way * piece, 2 * piece, unroll=True)
    taps = own_taps(sz, b.filters[layer])
    count = 4

    def chunk(index, total):
        lanes = place(index, count * LANES)
        rows = pl.multiple_of(index * count * 2 * piece, 2 * piece)
        raw = nn(taps, b.pos[:, lanes])
        grads = jnp.concatenate(
            [b.tall[pl.ds(rows + step * 2 * piece, 2 * piece), :] for step in range(count)],
            axis=1,
        )
        grads = grads * b.env[:, lanes] + (2.0 * DECAY) * raw
        return total + nt(grads.astype(BF16), b.pos[:, lanes])

    start = jnp.zeros((2 * piece, ORDER), F32)
    total = lax.fori_loop(0, sz.steps // count, chunk, start, unroll=2)

    columns = []
    for part in range(2):

        def product(block, products):
            rows = place(block, 16)
            here = landed[part, rows, :].astype(F32)
            return products + here * signal[part, rows, :].astype(F32)

        start = jnp.zeros((16, LANES), F32)
        products = lax.fori_loop(0, sz.count, product, start, unroll=4)
        columns.append(jnp.sum(products, axis=1, keepdims=True))
    column = jnp.concatenate(columns, axis=0)
    row = jnp.transpose(jnp.broadcast_to(column, (piece, LANES)))[0:8, :]
    b.taps_work[...] = jnp.zeros_like(b.taps_work)
    b.taps_work[0 : sz.big, :] = total[0 : sz.big, :]
    b.taps_work[sz.big : 2 * sz.big, :] = total[piece : piece + sz.big, :]
    b.taps_work[2 * sz.big : 2 * sz.big + 1, 0:piece] = row[0:1, :]


def block_of(sz, block):
    return slice(block * sz.size, (block + 1) * sz.size)


def project(sz, b, layer):
    for block in range(sz.blocks):
        rows = block_of(sz, block)
        part = b.normed[layer][:, rows]
        b.inner[layer][rows, :] = nt(b.mixer[layer, 0, block], part).astype(BF16)
        b.gate[layer][rows, :] = nt(b.mixer[layer, 1, block], part)


def mix(sz, b, layer, conv):
    summed, mixed, middle = b.summed[layer], b.mixed[layer], b.middle[layer]
    summed[...] = conv[...].astype(F32) + b.skip[layer][...] * b.inner[layer][...].astype(F32)
    mixed[...] = (b.gate[layer][...] * summed[...]).astype(BF16)
    for block in range(sz.blocks):
        rows = block_of(sz, block)
        middle[:, rows] = tn(mixed[rows, :], b.mixer[layer, 2, block])
    middle[...] = middle[...] + b.stream[layer][...]


def gain_gradient(sz, b, row, value, mine, give):
    low = lax.axis_index("hid") == 0
    left, right = value[:, : sz.half], value[:, sz.half :]
    mine[row : row + 1, :] = jnp.where(low, left, right)
    give[row : row + 1, :] = jnp.where(low, right, left)


def mixer_backward(sz, b, layer, grad_next, total):
    normal, inv = normalize(b.middle[layer][...])
    gain = b.gain[layer, 1:2, :]
    back, gain_grad = norm_back(total, normal, inv, gain)
    result = grad_next + back
    b.grad_middle[...] = result
    b.grad_o[...] = result.astype(BF16)
    for block in range(sz.blocks):
        rows = block_of(sz, block)
        grad_mixed = nt(b.mixer[layer, 2, block], b.grad_o[:, rows])
        b.gate_grad[rows, :] = (grad_mixed * b.summed[layer][rows, :]).astype(BF16)
        through = grad_mixed * b.gate[layer][rows, :]
        b.summed_grad[rows, :] = through
        b.conv_grad[rows, :] = through.astype(BF16)
    return gain_grad


def out_gradient(sz, b, layer):
    return [
        nn(b.mixed[layer][block_of(sz, block), :], b.grad_o[:, block_of(sz, block)])
        for block in range(sz.blocks)
    ]


def in_gradient(sz, b, layer, grads):
    return [
        jnp.transpose(
            nn(grads[block_of(sz, block), :], b.normed[layer][:, block_of(sz, block)])
        )
        for block in range(sz.blocks)
    ]


def input_backward(sz, b, layer, back):
    direct = b.skip[layer][...] * b.summed_grad[...]
    b.inner_grad[...] = (direct + back[...].astype(F32)).astype(BF16)
    for block in range(sz.blocks):
        rows = block_of(sz, block)
        b.grad_sum[0 : sz.own, rows] = tn(b.inner_grad[rows, :], b.mixer[layer, 0, block]) + tn(
            b.gate_grad[rows, :], b.mixer[layer, 1, block]
        )
    normal, inv = normalize(b.stream[layer][...])
    result, gain_grad = norm_back(
        b.grad_sum[0 : sz.own, :], normal, inv, b.gain[layer, 0:1, :]
    )
    return b.grad_middle[...] + result, gain_grad


def ff_forward(sz, b, layer):
    tile = 512
    rows = slice(0, 2 * sz.own)
    b.out_sum[...] = jnp.zeros_like(b.out_sum)

    def body(step, carry):
        lanes = pl.ds(pl.multiple_of(step * tile, tile), tile)
        normed = b.nbuf[layer][rows, :]
        gate = nn(normed, b.up[layer, 0, :, lanes])
        up = nn(normed, b.up[layer, 1, :, lanes])
        value, _ = gelu_parts(gate)
        b.out_sum[...] += nt((value * up).astype(BF16), b.down[layer, :, lanes])
        return carry

    lax.fori_loop(0, sz.units // tile, body, 0)


def ff_backward(sz, b, layer, with_out):
    tile = 512
    rows = slice(0, 2 * sz.own)
    b.grad_sum[...] = jnp.zeros_like(b.grad_sum)
    if with_out:
        b.out_sum[...] = jnp.zeros_like(b.out_sum)

    def body(step, carry):
        lanes = pl.ds(pl.multiple_of(step * tile, tile), tile)
        normed = b.nbuf[layer][rows, :]
        gate = nn(normed, b.up[layer, 0, :, lanes])
        up = nn(normed, b.up[layer, 1, :, lanes])
        through = nn(b.gbuf[layer][rows, :], b.down[layer, :, lanes])
        value, slope = gelu_parts(gate)
        if with_out:
            b.out_sum[...] += nt((value * up).astype(BF16), b.down[layer, :, lanes])
        gate_grad = (slope * up * through).astype(BF16)
        up_grad = (value * through).astype(BF16)
        b.grad_sum[...] += nt(gate_grad, b.up[layer, 0, :, lanes]) + nt(
            up_grad, b.up[layer, 1, :, lanes]
        )
        return carry

    lax.fori_loop(0, sz.units // tile, body, 0)


def ff_gradients(sz, b, layer, links, between=(None, None, None)):
    start = pl.multiple_of(links.line * sz.part, LANES)
    units = pl.ds(start, sz.part)
    chunk = 2 * sz.own

    def body(step, carry):
        rows = pl.ds(pl.multiple_of(step * chunk, chunk), chunk)
        normed = b.nbuf[layer][rows, :]
        gate = nn(normed, b.up[layer, 0, :, units])
        up = nn(normed, b.up[layer, 1, :, units])
        through = nn(b.gbuf[layer][rows, :], b.down[layer, :, units])
        value, slope = gelu_parts(gate)
        b.unit_grad[0, rows, :] = (slope * up * through).astype(BF16)
        b.unit_grad[1, rows, :] = (value * through).astype(BF16)
        b.unit_grad[2, rows, :] = (value * up).astype(BF16)
        return carry

    lax.fori_loop(0, sz.group, body, 0)
    split = sz.width // 2
    moving = []
    for kind in range(3):
        if between[kind] is not None:
            between[kind]()
        left = b.gbuf[layer] if kind == 2 else b.nbuf[layer]

        def part(index, carry):
            lanes = place(index, split)
            b.product[...] = tn(left[:, lanes], b.unit_grad[kind])
            count = split // sz.depth
            for each in range(count):
                line = index * (count // sz.peers) + each // sz.peers
                rows = slice(each * sz.depth, (each + 1) * sz.depth)
                b.pieces[kind, each % sz.peers, line, 0 : sz.depth, :] = b.product[rows, :].astype(
                    BF16
                )
            return carry

        lax.fori_loop(0, 2, part, 0)
        half = lambda which: pl.ds(which * (sz.group // 2), sz.group // 2)
        plane = PlaneSum(
            links,
            lambda member, which, kind=kind: b.pieces.at[kind, member, half(which)],
            b.plane_first[layer].at[kind],
            b.plane_give[layer].at[kind],
            b.plane_second[layer].at[kind],
        )
        plane.start()
        moving.append(plane)
    return moving


def done(copy):
    copy.wait()


class Named:
    pass


def layout(sz):
    layers, own, width = sz.layers, sz.own, sz.width
    wide = 2 * sz.big * sz.steps
    per_layer = dict(
        stream=((own, width), F32),
        normed=((own, width), BF16),
        inner=((width, own), BF16),
        gate=((width, own), F32),
        summed=((width, own), F32),
        mixed=((width, own), BF16),
        middle=((own, width), F32),
        nbuf=((2 * sz.group * own, width), BF16),
        gbuf=((2 * sz.group * own, width), BF16),
        skip=((width, LANES), F32),
        filt_spec=((sz.big * sz.outer, 2 * LANES), BF16),
        sig_spec=((sz.pairs * sz.outer, 2 * LANES), BF16),
        fore_in=((2, sz.count * 16, LANES), BF16),
        fore_out=((width, own), BF16),
        back_in=((2, sz.count * 16, LANES), BF16),
        back_out=((width, own), BF16),
        plane_first=((3, 2, 2, sz.group // 2, sz.deep, sz.part), BF16),
        plane_give=((3, 2, sz.group // 2, sz.deep, sz.part), BF16),
        plane_second=((3, 2, sz.group // 2, sz.deep, sz.part), BF16),
        grad_got=((own, width), BF16),
        out_got=((own, width), BF16),
    )
    single = dict(
        x=((own, width), BF16),
        gain=((layers, 2, width), F32),
        skip_rows=((layers, width), F32),
        mixer=((layers, 3, sz.blocks, sz.size, sz.size), BF16),
        filters=((layers, 2, ORDER, sz.half), F32),
        pos=((ORDER, sz.length), BF16),
        outer_fwd=((2 * sz.outer, sz.steps), BF16),
        outer_inv=((sz.steps, 2 * sz.outer), BF16),
        inner_fwd=((2 * LANES, 2 * LANES), BF16),
        inner_inv=((2 * LANES, 2 * LANES), BF16),
        twist=((sz.outer, 2 * LANES), F32),
        up=((layers, 2, width, sz.units), BF16),
        down=((layers, width, sz.units), BF16),
        env=((2 * sz.big, sz.length), F32),
        tall=((max(wide, sz.count * sz.big), LANES), F32),
        wide=((sz.steps, CHUNK * LANES), BF16),
        turned=((CHUNK * sz.outer, 2 * LANES), BF16),
        mid=((2 * sz.outer, CHUNK * LANES), F32),
        flat=((sz.pairs * sz.outer, 2 * LANES), BF16),
        mid_half=((2 * sz.outer, CHUNK * LANES), BF16),
        spec=((sz.pairs * sz.outer, 2 * LANES), F32),
        conv_grad=((width, own), BF16),
        staged=((2, sz.count * 16, LANES), BF16),
        grad_middle=((own, width), F32),
        grad_o=((own, width), BF16),
        gate_grad=((width, own), BF16),
        summed_grad=((width, own), F32),
        inner_grad=((width, own), BF16),
        out_sum=((2 * own, width), F32),
        grad_sum=((2 * own, width), F32),
        out_give=((own, width), BF16),
        sum_give=((own, width), BF16),
        unit_grad=((3, 2 * sz.group * own, sz.part), BF16),
        product=((width // 2, sz.part), F32),
        pieces=((3, sz.peers, sz.group, sz.deep, sz.part), BF16),
        taps_work=((sz.taps_rows, ORDER), F32),
        gain_mine=((16, sz.half), F32),
        gain_give=((16, sz.half), F32),
        late_parts=((sz.peers, sz.group, sz.deeps[1], sz.half), BF16),
        late_gain_mine=((16, sz.half), F32),
        late_gain_give=((16, sz.half), F32),
        out_keep=((2, own, sz.half), BF16),
        taps_line=((layers, sz.group, sz.taps_rows, ORDER), BF16),
    )
    names, specs = [], []
    for name, (shape, kind) in per_layer.items():
        for layer in range(layers):
            names.append((name, layer))
            specs.append(pltpu.VMEM(shape, kind))
    for index, deep in enumerate(sz.deeps):
        part = (sz.group // 2, deep, sz.half)
        whole_load = (sz.peers, sz.group, deep, sz.half)
        line = (sz.group, deep, sz.half)
        shapes = (whole_load,) * 3 + ((2, 2) + part, (2,) + part, (2,) + part, line, line[1:])
        for name, shape in zip(LOAD_BUFFERS, shapes):
            names.append(("load_" + name, index))
            specs.append(pltpu.VMEM(shape, BF16))
    for name, (shape, kind) in single.items():
        names.append((name, None))
        specs.append(pltpu.VMEM(shape, kind))
    return names, specs


TABLES = ("pos", "outer_fwd", "outer_inv", "inner_fwd", "inner_inv", "twist")
INPUTS = ("hidden_in", "d_out", "gains", "mixer", "skip", "filters", "gate_up", "down") + TABLES
OUTPUTS = ("hidden_out", "grad_in", "early", "late", "taps", "units")


def program_kernel(sz, *refs):
    names, _ = layout(sz)
    inputs = dict(zip(INPUTS, refs))
    outputs = dict(zip(OUTPUTS, refs[len(INPUTS) :]))
    scratch = refs[len(INPUTS) + len(OUTPUTS) :]
    b = Named()
    for (name, layer), ref in zip(names, scratch):
        if layer is None:
            setattr(b, name, ref)
        else:
            setattr(b, name, getattr(b, name, ()) + (ref,))
    links = Links(sz, scratch[len(names)], scratch[len(names) + 1])
    own = sz.own
    top = sz.layers - 1
    col = links.col
    low = col == 0
    mine_rows = pl.ds(pl.multiple_of(col * own, own), own)
    other_rows = pl.ds(pl.multiple_of((1 - col) * own, own), own)

    barrier = greet_all(sz)
    lanes = pl.ds(pl.multiple_of(col * sz.half, sz.half), sz.half)
    sides = pl.ds(col * sz.side_blocks, sz.side_blocks)
    slots = lambda first, count: pl.ds(first * own, count * own)
    near_slots, line_slots, far_slots = slots(0, 2), slots(2, 3), slots(5, 3)
    halves = {
        "x": (inputs["hidden_in"].at[mine_rows], b.x.at[:, lanes]),
        "gains": (inputs["gains"], b.gain.at[:, :, lanes]),
        "mixer": (inputs["mixer"].at[0, pl.ds(0, 2)], b.mixer.at[0, pl.ds(0, 2), sides]),
        "skip": (inputs["skip"], b.skip_rows.at[:, lanes]),
        "out_mixer": (inputs["mixer"].at[0, pl.ds(2, 1)], b.mixer.at[0, pl.ds(2, 1), sides]),
    }
    if sz.layers > 1:
        above = pl.ds(1, sz.layers - 1)
        halves["mixers"] = (inputs["mixer"].at[above], b.mixer.at[above, :, sides])
    loads = {name: links.load(*pair) for name, pair in halves.items()}
    for name in ("filters",) + TABLES:
        loads[name] = links.load(inputs[name], getattr(b, name))
    grads = b.gbuf[top]
    loads["g"] = links.load(inputs["d_out"].at[mine_rows], grads.at[slots(0, 1), lanes])
    loads["g_near"] = links.load(inputs["d_out"].at[other_rows], grads.at[slots(1, 1), lanes])
    b.gain_mine[...] = jnp.zeros_like(b.gain_mine)
    b.gain_give[...] = jnp.zeros_like(b.gain_give)
    b.late_gain_mine[...] = jnp.zeros_like(b.late_gain_mine)
    b.late_gain_give[...] = jnp.zeros_like(b.late_gain_give)
    pl.semaphore_wait(barrier, sz.count - 1)
    got = {}
    for name, (source, target) in halves.items():
        if name == "x":
            source = inputs["hidden_in"].at[other_rows]
        got[name] = links.sibling(source, target)
    got["g"] = links.sibling(inputs["d_out"].at[other_rows], grads.at[slots(0, 1), lanes])
    got["g_near"] = links.sibling(inputs["d_out"].at[mine_rows], grads.at[slots(1, 1), lanes])

    def both(*wanted):
        for name in wanted:
            done(loads[name])
            done(got[name])

    def turn_mixer(layer, kind):
        for block in range(sz.blocks):
            b.mixer[layer, kind, block] = jnp.transpose(b.mixer[layer, kind, block])

    def norm_to(source, target, layer, which):
        normal, _ = normalize(source)
        target[...] = (normal * b.gain[layer, which : which + 1, :]).astype(BF16)

    def slot_of(place, member):
        return 2 + (member if member < place else member - 1)

    class Gather:
        moves = (
            {0: [(0, 1)], 1: [(1, 0), (1, 2)], 2: [(2, 1), (2, 3)], 3: [(3, 2)]},
            {1: [(2, 0), (0, 2)], 2: [(3, 1), (1, 3)]},
            {1: [(3, 0)], 2: [(0, 3)]},
        )
        coming = ((1, 2, 2, 1), (1, 1, 1, 1), (1, 0, 0, 1))

        def __init__(self, buffer):
            self.buffer = buffer
            self.pairs = [None] * 3

        def near(self):
            return links.sibling(self.buffer.at[slots(0, 1)], self.buffer.at[slots(1, 1)])

        def views(self, place, whose, target):
            here = 0 if whose == place else slot_of(place, whose)
            there = slot_of(target, whose)
            return [(self.buffer.at[slots(here, 1)], self.buffer.at[slots(there, 1)])]

        def span(self, count):
            return self.buffer.at[slots(0, count)]

        def step(self, index):
            if index > 0:
                self.wait(index - 1)
            pair = links.pair()
            for place, moves in self.moves[index].items():

                @pl.when(links.line == place)
                def _():
                    for whose, target in moves:
                        for source, there in self.views(place, whose, target):
                            row = target * sz.peers + links.plane
                            links.copy(source, there, pair, row, col).start()

            self.pairs[index] = pair

        def wait(self, index):
            pair = self.pairs[index]
            if True:
                for place in range(sz.group):
                    came = self.coming[index][place]
                    sent = len(self.moves[index].get(place, ()))

                    @pl.when(links.line == place)
                    def _():
                        if came:
                            span = self.span(came)
                            links.copy(span, span, pair, links.row, 1 - col).wait_recv()
                        if sent:
                            span = self.span(sent)
                            links.copy(span, span, pair, links.row, 1 - col).wait_send()

        def rest(self):
            self.wait(2)
            self.copies = [links.sibling(self.buffer.at[line_slots], self.buffer.at[far_slots])]

        def finish(self):
            for copy in self.copies:
                done(copy)

    class ArgumentGather(Gather):
        def views(self, place, whose, target):
            there = slot_of(target, whose)
            pairs = []
            for rows, shift in ((mine_rows, 0), (other_rows, 3)):
                if whose == place:
                    source = inputs["d_out"].at[rows]
                else:
                    source = self.buffer.at[slots(slot_of(place, whose) + shift, 1), lanes]
                pairs.append((source, self.buffer.at[slots(there + shift, 1), lanes]))
            return pairs

        def span(self, count):
            return self.buffer.at[slots(0, 2 * count), lanes]

        def rest(self):
            self.wait(2)
            self.copies = [
                links.sibling(self.buffer.at[line_slots, lanes], self.buffer.at[far_slots, lanes]),
                links.sibling(self.buffer.at[far_slots, lanes], self.buffer.at[line_slots, lanes]),
            ]

    top_grads = ArgumentGather(grads)
    top_grads.step(0)
    both("x", "gains")
    b.stream[0][...] = b.x[...].astype(F32)
    norm_to(b.stream[0][...], b.normed[0], 0, 0)
    both("mixer")
    turn_mixer(0, 0)
    turn_mixer(0, 1)

    exchange = Exchange(sz, links)
    project(sz, b, 0)
    normed_parts = []
    for layer in range(sz.layers):
        moving = exchange.to_owners(b.inner[layer], b.fore_in[layer])
        if layer == 0:
            for each in range(sz.layers):
                loads["up", each] = links.load(inputs["gate_up"].at[each], b.up.at[each])
                loads["down", each] = links.load(inputs["down"].at[each], b.down.at[each])
            for name in ("filters", "pos", "outer_fwd", "inner_fwd", "twist"):
                done(loads[name])
            own_envelope(sz, b.env)
            filter_spectrum(sz, b, 0)
            for name in ("outer_inv", "inner_inv"):
                done(loads[name])
            both("skip", "g", "g_near")
            for each in range(sz.layers):
                row = b.skip_rows[each : each + 1, :]
                b.skip[each][...] = jnp.transpose(jnp.broadcast_to(row, (LANES, sz.width)))
        returning = []
        for part in range(2):
            exchange.owners_wait(moving, part, b.fore_in[layer])
            conv_forward(sz, b, layer, b.fore_in[layer], part)
            returning.append(exchange.to_tokens(b.staged, b.fore_out[layer], part))
        if layer == 0:
            top_grads.step(1)
        else:
            top_grads.rest()
        if layer == 0:
            both("out_mixer")
            if sz.layers > 1:
                both("mixers")
            for each in range(1, sz.layers):
                turn_mixer(each, 0)
                turn_mixer(each, 1)
        if layer < top:
            filter_spectrum(sz, b, layer + 1)
        done(loads["up", layer])
        done(loads["down", layer])
        if layer == 0:
            top_grads.step(2)
        exchange.tokens_wait(returning, b.staged)
        mix(sz, b, layer, b.fore_out[layer])
        norm_to(b.middle[layer][...], b.nbuf[layer].at[slots(0, 1)], layer, 1)
        normed_parts.append(Gather(b.nbuf[layer]))
        near = normed_parts[layer].near()
        if layer == top:
            normed_parts[layer].step(0)
        done(near)
        if layer < top:
            ff_forward(sz, b, layer)
            b.out_give[...] = b.out_sum[own:, :].astype(BF16)
            moving = links.sibling(b.out_give, b.out_got[layer])
            done(moving)
            value = b.middle[layer][...] + b.out_sum[0:own, :] + b.out_got[layer][...].astype(F32)
            b.stream[layer + 1][...] = value
            norm_to(value, b.normed[layer + 1], layer + 1, 0)
            project(sz, b, layer + 1)

    ff_backward(sz, b, top, True)
    b.sum_give[...] = b.grad_sum[own:, :].astype(BF16)
    moving = links.sibling(b.sum_give, b.grad_got[top])
    b.out_give[...] = b.out_sum[own:, :].astype(BF16)
    out_moving = links.sibling(b.out_give, b.out_got[top])
    normed_parts[top].step(1)
    done(moving)
    total = b.grad_sum[0:own, :] + b.grad_got[top][...].astype(F32)
    grad_next = b.gbuf[top][0:own, :].astype(F32)
    gain_grad = mixer_backward(sz, b, top, grad_next, total)
    moving = exchange.to_owners(b.conv_grad, b.back_in[top])
    gain_gradient(sz, b, 2 * top, gain_grad, b.gain_mine, b.gain_give)
    early = Payload(sz, b, links, 0, outputs["early"])
    late = Payload(sz, b, links, 1, outputs["late"])
    early.matrix(0, out_gradient(sz, b, top))
    done(out_moving)
    value = b.middle[top][...] + b.out_sum[0:own, :] + b.out_got[top][...].astype(F32)
    value = value.astype(BF16)
    left, right = value[:, : sz.half], value[:, sz.half :]
    b.out_keep[0] = jnp.where(low, left, right)
    b.out_keep[1] = jnp.where(low, right, left)
    place = outputs["hidden_out"].at[mine_rows]
    ending = [links.load(b.out_keep.at[0], place), links.sibling(b.out_keep.at[1], place)]
    top_grads.finish()
    normed_parts[top].step(2)

    plane_moving = {}
    taps_moving = {}
    units_moving = []

    def taps_to_line(layer):
        taps_gradient(sz, b, layer, b.back_in[layer], b.fore_in[layer])
        place = b.taps_line.at[layer, links.line]
        b.taps_line[layer, links.line] = b.taps_work[...].astype(BF16)
        taps_moving[layer] = links.in_line(lambda member: place, place)

    def taps_to_plane(layer):
        links.wait(taps_moving[layer], b.taps_line.at[layer, pl.ds(0, sz.group - 1)])
        place = outputs["taps"].at[layer, links.plane]
        ending.append(links.load(b.taps_line.at[layer], place))
        taps_moving[layer] = links.in_plane(lambda member: b.taps_line.at[layer], place)

    def units_middle(layer, kinds=(0, 1, 2)):
        for kind in kinds:
            plane_moving[layer][kind].middle()

    def units_end(layer, kinds=(0, 1, 2)):
        for kind in kinds:
            plane = plane_moving[layer][kind]
            plane.end()
            part = plane.sums()
            target = outputs["units"].at[layer, kind, links.line]
            ending.append(links.load(part(links.line), target))
            pair = links.in_line(part, target)
            units_moving.append((layer, kind, pair))

    def convolve_back(layer):
        returning = []
        for part in range(2):
            exchange.owners_wait(moving, part, b.back_in[layer])
            conv_backward(sz, b, layer, b.back_in[layer], part)
            returning.append(exchange.to_tokens(b.staged, b.back_out[layer], part))
        return returning

    moving = convolve_back(top)
    normed_parts[top].rest()
    normed_parts[0].step(0)
    normed_parts[top].finish()
    plane_moving[top] = ff_gradients(sz, b, top, links)
    exchange.tokens_wait(moving, b.staged)
    value, gain_grad = input_backward(sz, b, top, b.back_out[top])
    b.out_sum[0:own, :] = value
    b.gbuf[0][0:own, :] = value.astype(BF16)
    gather = Gather(b.gbuf[0])
    near = gather.near()
    gather.step(0)
    normed_parts[0].step(1)
    gain_gradient(sz, b, 2 * top - 1, gain_grad, b.gain_mine, b.gain_give)
    early.matrix(1, in_gradient(sz, b, top, b.inner_grad))
    early.matrix(2, in_gradient(sz, b, top, b.gate_grad))
    done(near)
    ff_backward(sz, b, 0, False)
    b.sum_give[...] = b.grad_sum[own:, :].astype(BF16)
    moving = links.sibling(b.sum_give, b.grad_got[0])
    gather.step(1)
    normed_parts[0].step(2)
    done(moving)
    total = b.grad_sum[0:own, :] + b.grad_got[0][...].astype(F32)
    gain_grad = mixer_backward(sz, b, 0, b.out_sum[0:own, :], total)

    moving = exchange.to_owners(b.conv_grad, b.back_in[0])
    units_middle(top)
    gain_gradient(sz, b, 0, gain_grad, b.gain_mine, b.gain_give)
    early.matrix(3, out_gradient(sz, b, 0))
    early.matrix(4, in_gradient(sz, b, 0, b.gate_grad))
    early.rows16(5, b.gain_mine[...], b.gain_give[...])
    early.to_partner()
    taps_to_line(top)
    gather.step(2)
    early.to_plane()
    moving = convolve_back(0)
    units_end(top)
    normed_parts[0].rest()
    gather.rest()
    taps_to_plane(top)
    normed_parts[0].finish()
    gather.finish()
    between = (early.middle, None, None)
    plane_moving[0] = ff_gradients(sz, b, 0, links, between)
    exchange.tokens_wait(moving, b.staged)
    value, gain_grad = input_backward(sz, b, 0, b.back_out[0])

    left, right = value[:, : sz.half], value[:, sz.half :]
    keep, give = b.out_sum.at[0:own, 0 : sz.half], b.out_sum.at[own:, 0 : sz.half]
    keep[...] = jnp.where(low, left, right)
    give[...] = jnp.where(low, right, left)
    late.matrix(0, in_gradient(sz, b, 0, b.inner_grad))
    gain_gradient(sz, b, 0, gain_grad, b.late_gain_mine, b.late_gain_give)
    late.rows16(1, b.late_gain_mine[...], b.late_gain_give[...])
    late.to_partner()
    place = outputs["grad_in"].at[mine_rows]
    ending += [links.load(keep, place), links.sibling(give, place)]

    early.to_line()
    late.to_plane()
    units_middle(0, (0,))
    early.back_line()
    taps_to_line(0)
    late.to_line()
    units_middle(0, (1,))
    early.back_plane()
    units_middle(0, (2,))
    late.back_line()
    units_end(0, (0,))
    early.spread.middle()
    late.back_plane()
    units_end(0, (1, 2))
    taps_to_plane(0)
    ending += [early.finish(), late.finish()]
    for layer, kind, pair in units_moving:
        links.wait(pair, outputs["units"].at[layer, kind, pl.ds(0, sz.group - 1)])
    for layer, pair in taps_moving.items():
        links.wait(pair, outputs["taps"].at[layer, pl.ds(0, sz.peers - 1)])
    for copy in ending:
        done(copy)


def results_kernel(sz, *refs):
    raw, outs, scratch = refs[:6], refs[6:14], refs[14:]
    targets, held = scratch[:6], scratch[6:14]
    hidden_out, grad_in, gain_out, mixer_out, skip_out, taps_out, pair_out, down_out = held
    early, late, taps, units = targets[2:]
    channels, sems = scratch[14:]
    targets = (hidden_out, grad_in) + targets[2:]
    copies = [
        pltpu.make_async_copy(source, target, sems.at[index])
        for index, (source, target) in enumerate(zip(raw, targets))
    ]
    for copy in reversed(copies):
        copy.start()
    leaving = []

    def leave(index):
        copy = pltpu.make_async_copy(held[index], outs[index], sems.at[7 + index])
        copy.start()
        leaving.append(copy)

    layers = sz.layers
    copies[5].wait()
    for kind in range(3):
        for layer in range(layers):
            for line in range(sz.group):
                lanes = slice(line * sz.part, (line + 1) * sz.part)
                value = units[layer, kind, line].astype(F32)
                if kind < 2:
                    pair_out[layer, kind, :, lanes] = value
                else:
                    down_out[layer, :, lanes] = value
    leave(6)
    leave(7)
    copies[4].wait()
    for layer in range(layers):
        for way in range(3):
            for row in range(sz.rows):
                part = taps[layer, row % sz.peers, row // sz.peers]
                begin = (row // 2) * sz.couple + (row % 2) * sz.big
                size = sz.small if row % 2 else sz.big
                if way < 2:
                    value = part[way * sz.big : way * sz.big + size, :].astype(F32)
                else:
                    line = part[2 * sz.big : 2 * sz.big + 16, :].astype(F32)[0:1, :]
                    value = jnp.transpose(jnp.broadcast_to(line, (LANES, ORDER)))[0:size, :]
                channels[begin : begin + size, :] = value
            turned = jnp.transpose(channels[...])
            if way < 2:
                taps_out[layer, way] = turned
            else:
                skip_out[layer : layer + 1, :] = turned[0:1, :]
    leave(4)
    leave(5)
    for copy in copies[2:4]:
        copy.wait()

    def matrix(payload, place, layer, kind):
        deep = payload.shape[2]
        count = sz.size // deep
        for part in range(count):
            index = place * count + part
            rows = payload[index // sz.group, index % sz.group].astype(F32)
            for block in range(sz.side_blocks):
                mixer_out[layer, kind, block, part * deep : (part + 1) * deep, :] = rows[
                    :, block_of(sz, block)
                ]

    for place, (layer, kind) in enumerate(((1, 2), (1, 0), (1, 1), (0, 2), (0, 1))):
        matrix(early, place, layer, kind)
    matrix(late, 0, 0, 0)

    def gain_rows(payload, place):
        index = place * (sz.size // payload.shape[2])
        return payload[index // sz.group, index % sz.group].astype(F32)

    gains = gain_rows(early, 5)
    gain_out[0, 0:1, :] = gain_rows(late, 1)[0:1, :]
    for row in range(1, 2 * layers):
        gain_out[row // 2, row % 2 : row % 2 + 1, :] = gains[row - 1 : row, :]
    leave(2)
    leave(3)
    for index in range(2):
        copies[index].wait()
        leave(index)
    for copy in leaving:
        copy.wait()


def results(sz, *arrays):
    layers = sz.layers
    outs = (
        ((2 * sz.own, sz.half), BF16),
        ((2 * sz.own, sz.half), F32),
        ((layers, 2, sz.half), F32),
        ((layers, 3, sz.side_blocks, sz.size, sz.size), F32),
        ((layers, sz.half), F32),
        ((layers, 2, ORDER, sz.half), F32),
        ((layers, 2, sz.depth, sz.units), F32),
        ((layers, sz.depth, sz.units), F32),
    )
    anywhere = pl.BlockSpec(memory_space=pl.ANY)
    return pl.pallas_call(
        functools.partial(results_kernel, sz),
        out_shape=tuple(jax.ShapeDtypeStruct(shape, kind) for shape, kind in outs),
        in_specs=[anywhere] * len(arrays),
        out_specs=(anywhere,) * len(outs),
        scratch_shapes=[pltpu.VMEM(entry.shape, entry.dtype) for entry in arrays]
        + [pltpu.VMEM(shape, kind) for shape, kind in outs]
        + [pltpu.VMEM((sz.half, ORDER), F32), pltpu.SemaphoreType.DMA((15,))],
        compiler_params=pltpu.CompilerParams(vmem_limit_bytes=62 * MIB),
        name="results",
    )(*arrays)


def program(sz, arrays):
    names, scratch = layout(sz)
    outs = (
        ((2 * sz.own, sz.half), BF16),
        ((2 * sz.own, sz.half), F32),
        ((sz.peers, sz.group, sz.deeps[0], sz.half), BF16),
        ((sz.peers, sz.group, sz.deeps[1], sz.half), BF16),
        ((sz.layers, sz.peers, sz.group, sz.taps_rows, ORDER), BF16),
        ((sz.layers, 3, sz.group, sz.deep, sz.part), BF16),
    )
    return pl.pallas_call(
        functools.partial(program_kernel, sz),
        out_shape=tuple(jax.ShapeDtypeStruct(shape, kind) for shape, kind in outs),
        in_specs=[pl.BlockSpec(memory_space=pl.ANY)] * len(arrays),
        out_specs=(pl.BlockSpec(memory_space=pl.ANY),) * len(outs),
        scratch_shapes=scratch
        + [pltpu.SemaphoreType.DMA((220,)), pltpu.SemaphoreType.DMA((80,))],
        compiler_params=pltpu.CompilerParams(
            collective_id=0, has_side_effects=True, vmem_limit_bytes=63 * MIB
        ),
        name="program",
    )(*arrays)


def together(sz, hidden_in, d_out, gains, mixer, skip, filters, gate_up, down):
    pos = jnp.asarray(position_table(sz.length).T, F32).astype(BF16)
    arrays = (hidden_in, d_out, gains, mixer, skip, filters, gate_up, down, pos)
    raw = program(sz, arrays + dft_tables(sz.length))

    return results(sz, *raw)


def apart_enter(count, hid):
    me = lax.axis_index("rows") * hid + lax.axis_index("hid")
    barrier = pltpu.get_barrier_semaphore()

    def greet(step, carry):
        peer = lax.rem(me + step, count)
        pl.semaphore_signal(
            barrier, inc=1, device_id=(peer // hid, lax.rem(peer, hid)), device_id_type=MESH
        )
        return carry

    lax.fori_loop(1, count, greet, 0)
    return barrier


def apart_exchange_start(source, target, sems, count, rows, hid, piece, by_owner):
    send, recv, local = sems
    row = lax.axis_index("rows")
    col = lax.axis_index("hid")
    token_id = row * hid + col
    owner_id = col * rows + row
    mine_there = token_id if by_owner else owner_id
    mine_here = owner_id if by_owner else token_id
    at = lambda index: pl.ds(pl.multiple_of(index * piece, piece), piece)
    pltpu.make_async_copy(source.at[at(mine_here)], target.at[at(mine_there)], local).start()

    def post(step, carry):
        peer = lax.rem(token_id + step, count)
        peer_row = peer // hid
        peer_col = lax.rem(peer, hid)
        there = (peer_col * rows + peer_row) if by_owner else peer
        pltpu.make_async_remote_copy(
            src_ref=source.at[at(there)],
            dst_ref=target.at[at(mine_there)],
            send_sem=send,
            recv_sem=recv,
            device_id=(peer_row, peer_col),
            device_id_type=MESH,
        ).start()
        return carry

    lax.fori_loop(1, count, post, 0)


def apart_exchange_wait(source, target, sems, count, rows, hid, piece):
    send, recv, local = sems
    row = lax.axis_index("rows")
    col = lax.axis_index("hid")
    pltpu.make_async_copy(
        source.at[pl.ds(0, piece)], target.at[pl.ds(0, piece)], local
    ).wait()
    span = pl.ds(0, (count - 1) * piece)
    pltpu.make_async_remote_copy(
        src_ref=source.at[span],
        dst_ref=target.at[span],
        send_sem=send,
        recv_sem=recv,
        device_id=(row, hid - 1 - col),
        device_id_type=MESH,
    ).wait()


class apart_Sizes:
    def __init__(self, rows, hid, width, hidden, tokens):
        self.rows, self.hid, self.width, self.hidden = rows, hid, width, hidden
        self.count = rows * hid
        self.chans = width // self.count
        self.piece = round_up(self.chans, 16)
        self.length = min(SEQ_LEN, tokens)
        self.seqs = tokens // self.length
        self.blocks = self.length // LANES
        self.outer = 2 * self.blocks
        self.pairs = self.seqs * self.chans
        self.half = width // hid
        self.padded = rows * self.piece
        self.channels = self.count * self.piece


def apart_spread_in(source, wide, lines, stride, blocks):
    for place, line in enumerate(lines):
        wide[:, place * LANES : (place + 1) * LANES] = source[
            pl.ds(line, blocks, stride=stride), :
        ].astype(wide.dtype)


def apart_dft(wide, spectrum, tables, mid, flat, lines, outer, offset=0):
    outer_fwd, inner_fwd, twist = tables
    mid[:, : lines * LANES] = nn(outer_fwd[...], wide[:, : lines * LANES])
    cos = twist[:, :LANES]
    sin = twist[:, LANES:]
    for line in range(lines):
        lanes = pl.ds(line * LANES, LANES)
        real = mid[0:outer, lanes]
        imag = mid[outer : 2 * outer, lanes]
        rows = pl.ds(line * outer, outer)
        flat[rows, 0:LANES] = (real * cos + imag * sin).astype(BF16)
        flat[rows, LANES:] = (imag * cos - real * sin).astype(BF16)
    spectrum[0 : lines * outer, :] = nn(flat[0 : lines * outer, :], inner_fwd[...])


def apart_inverse_dft(flat, tables, mid_half, lines, outer):
    outer_inv, inner_inv, twist = tables
    cos = twist[:, :LANES]
    sin = twist[:, LANES:]
    for line in range(lines):
        rows = pl.ds(line * outer, outer)
        lanes = pl.ds(line * LANES, LANES)
        part = nn(flat[rows, :], inner_inv[...])
        real = part[:, :LANES]
        imag = part[:, LANES:]
        mid_half[0:outer, lanes] = (real * cos - imag * sin).astype(BF16)
        mid_half[outer : 2 * outer, lanes] = (imag * cos + real * sin).astype(BF16)
    return nn(outer_inv[...], mid_half[:, : lines * LANES])


def apart_spread_out(value, target, lines, stride, blocks):
    for place, line in enumerate(lines):
        target[pl.ds(line, blocks, stride=stride), :] = value[
            :, place * LANES : (place + 1) * LANES
        ]


def apart_signal_lines(sz):
    return [seq * sz.blocks * sz.piece + chan for seq in range(sz.seqs) for chan in range(sz.chans)]


def apart_conv_forward_kernel(
    sz,
    inner_ref,
    taps_ref,
    pos_ref,
    env_ref,
    outer_fwd,
    outer_inv,
    inner_fwd,
    inner_inv,
    twist,
    conv_ref,
    filt_spec,
    sig_spec,
    landed,
    staged,
    tall,
    wide,
    mid,
    flat,
    mid_half,
    sems_in,
    sems_out,
):
    barrier = apart_enter(sz.count, sz.hid)
    pl.semaphore_wait(barrier, sz.count - 1)
    into = tuple(sems_in.at[i] for i in range(3))
    back = tuple(sems_out.at[i] for i in range(3))
    apart_exchange_start(inner_ref, landed, into, sz.count, sz.rows, sz.hid, sz.piece, True)

    piece, blocks, outer = sz.piece, sz.blocks, sz.outer
    step = 4
    for start in range(0, blocks, step):
        span = slice(start * LANES, (start + step) * LANES)
        raw = nn(taps_ref[...], pos_ref[:, span])
        kernels = raw * env_ref[:, span]
        for block in range(step):
            tall[pl.ds((start + block) * 2 * piece, 2 * piece), :] = kernels[
                :, block * LANES : (block + 1) * LANES
            ]
    lines = [way * piece + chan for way in range(2) for chan in range(sz.chans)]
    apart_spread_in(tall, wide, lines, 2 * piece, blocks)
    apart_dft(wide, sig_spec, (outer_fwd, inner_fwd, twist), mid, flat, len(lines), outer)
    span = sz.chans * outer
    filt_spec[:, :LANES] = sig_spec[0:span, :LANES] + sig_spec[span : 2 * span, :LANES]
    filt_spec[:, LANES:] = sig_spec[0:span, LANES:] - sig_spec[span : 2 * span, LANES:]

    apart_exchange_wait(inner_ref, landed, into, sz.count, sz.rows, sz.hid, piece)
    tall[0 : sz.channels, :] = landed[...].astype(F32)
    lines = apart_signal_lines(sz)
    apart_spread_in(tall, wide, lines, piece, blocks)
    apart_dft(wide, sig_spec, (outer_fwd, inner_fwd, twist), mid, flat, sz.pairs, outer)
    for seq in range(sz.seqs):
        rows = pl.ds(seq * span, span)
        sig_re, sig_im = sig_spec[rows, :LANES], sig_spec[rows, LANES:]
        fil_re, fil_im = filt_spec[:, :LANES], filt_spec[:, LANES:]
        flat[rows, :LANES] = (sig_re * fil_re - sig_im * fil_im).astype(BF16)
        flat[rows, LANES:] = (sig_re * fil_im + sig_im * fil_re).astype(BF16)
    result = apart_inverse_dft(flat, (outer_inv, inner_inv, twist), mid_half, sz.pairs, outer)
    apart_spread_out(result, tall, lines, piece, blocks)
    staged[...] = tall[0 : sz.channels, :].astype(BF16)
    apart_exchange_start(staged, conv_ref, back, sz.count, sz.rows, sz.hid, piece, False)
    apart_exchange_wait(staged, conv_ref, back, sz.count, sz.rows, sz.hid, piece)


def apart_conv_forward(sz, inner, taps, pos, env, tables, cid):
    outer_fwd, outer_inv, inner_fwd, inner_inv, twist = tables
    wide_lines = max(2 * sz.chans, sz.pairs)
    return pl.pallas_call(
        functools.partial(apart_conv_forward_kernel, sz),
        out_shape=(
            jax.ShapeDtypeStruct((sz.channels, LANES), BF16),
            jax.ShapeDtypeStruct((sz.chans * sz.outer, 2 * LANES), F32),
            jax.ShapeDtypeStruct((wide_lines * sz.outer, 2 * LANES), F32),
        ),
        in_specs=[whole()] * 9,
        out_specs=(whole(),) * 3,
        scratch_shapes=[
            pltpu.VMEM((sz.channels, LANES), BF16),
            pltpu.VMEM((sz.channels, LANES), BF16),
            pltpu.VMEM((max(2 * sz.piece * sz.blocks, sz.channels), LANES), F32),
            pltpu.VMEM((sz.blocks, wide_lines * LANES), BF16),
            pltpu.VMEM((2 * sz.outer, wide_lines * LANES), F32),
            pltpu.VMEM((wide_lines * sz.outer, 2 * LANES), BF16),
            pltpu.VMEM((2 * sz.outer, sz.pairs * LANES), BF16),
            pltpu.SemaphoreType.DMA((3,)),
            pltpu.SemaphoreType.DMA((3,)),
        ],
        compiler_params=pltpu.CompilerParams(
            collective_id=cid, has_side_effects=True, vmem_limit_bytes=48 * MIB
        ),
        name="conv_forward",
    )(inner, taps, pos, env, outer_fwd, outer_inv, inner_fwd, inner_inv, twist)


def apart_conv_backward_kernel(
    sz,
    grad_ref,
    filt_spec,
    sig_spec,
    taps_ref,
    pos_ref,
    env_ref,
    outer_fwd,
    outer_inv,
    inner_fwd,
    inner_inv,
    twist,
    back_ref,
    taps_grad,
    landed,
    staged,
    tall,
    wide,
    mid,
    flat,
    mid_half,
    grad_spec,
    sems_in,
    sems_out,
):
    barrier = apart_enter(sz.count, sz.hid)
    pl.semaphore_wait(barrier, sz.count - 1)
    into = tuple(sems_in.at[i] for i in range(3))
    back = tuple(sems_out.at[i] for i in range(3))
    piece, blocks, outer = sz.piece, sz.blocks, sz.outer
    apart_exchange_start(grad_ref, landed, into, sz.count, sz.rows, sz.hid, piece, True)
    apart_exchange_wait(grad_ref, landed, into, sz.count, sz.rows, sz.hid, piece)
    tall[0 : sz.channels, :] = landed[...].astype(F32)
    lines = apart_signal_lines(sz)
    apart_spread_in(tall, wide, lines, piece, blocks)
    apart_dft(wide, grad_spec, (outer_fwd, inner_fwd, twist), mid, flat, sz.pairs, outer)
    span = sz.chans * outer
    for seq in range(sz.seqs):
        rows = pl.ds(seq * span, span)
        re, im = grad_spec[rows, :LANES], grad_spec[rows, LANES:]
        fil_re, fil_im = filt_spec[:, :LANES], filt_spec[:, LANES:]
        flat[rows, :LANES] = (re * fil_re + im * fil_im).astype(BF16)
        flat[rows, LANES:] = (im * fil_re - re * fil_im).astype(BF16)
    inv_tables = (outer_inv, inner_inv, twist)
    result = apart_inverse_dft(flat, inv_tables, mid_half, sz.pairs, outer)
    apart_spread_out(result, tall, lines, piece, blocks)
    staged[...] = tall[0 : sz.channels, :].astype(BF16)
    apart_exchange_start(staged, back_ref, back, sz.count, sz.rows, sz.hid, piece, False)

    total_re = jnp.zeros((span, LANES), F32)
    total_im = jnp.zeros((span, LANES), F32)
    for seq in range(sz.seqs):
        rows = pl.ds(seq * span, span)
        re, im = grad_spec[rows, :LANES], grad_spec[rows, LANES:]
        sig_re, sig_im = sig_spec[rows, :LANES], sig_spec[rows, LANES:]
        total_re += re * sig_re + im * sig_im
        total_im += im * sig_re - re * sig_im
    flat[0:span, :LANES] = total_re.astype(BF16)
    flat[span : 2 * span, :LANES] = total_re.astype(BF16)
    flat[0:span, LANES:] = total_im.astype(BF16)
    flat[span : 2 * span, LANES:] = (-total_im).astype(BF16)
    result = apart_inverse_dft(flat, inv_tables, mid_half, 2 * sz.chans, outer)
    lines = [way * piece + chan for way in range(2) for chan in range(sz.chans)]
    if sz.chans < piece:
        tall[...] = jnp.zeros_like(tall)
    apart_spread_out(result, tall, lines, 2 * piece, blocks)
    total = jnp.zeros((2 * piece, ORDER), F32)
    step = 4
    for start in range(0, blocks, step):
        span = slice(start * LANES, (start + step) * LANES)
        raw = nn(taps_ref[...], pos_ref[:, span])
        grads = jnp.concatenate(
            [
                tall[pl.ds((start + block) * 2 * piece, 2 * piece), :]
                for block in range(step)
            ],
            axis=1,
        )
        grads = grads * env_ref[:, span] + (2.0 * DECAY) * raw
        total += nt(grads.astype(BF16), pos_ref[:, span])
    taps_grad[...] = total

    apart_exchange_wait(staged, back_ref, back, sz.count, sz.rows, sz.hid, piece)


def apart_conv_backward(sz, grad, filt_spec, sig_spec, taps, pos, env, tables, cid):
    outer_fwd, outer_inv, inner_fwd, inner_inv, twist = tables
    wide_lines = max(2 * sz.chans, sz.pairs)
    return pl.pallas_call(
        functools.partial(apart_conv_backward_kernel, sz),
        out_shape=(
            jax.ShapeDtypeStruct((sz.channels, LANES), BF16),
            jax.ShapeDtypeStruct((2 * sz.piece, ORDER), F32),
        ),
        in_specs=[whole()] * 11,
        out_specs=(whole(),) * 2,
        scratch_shapes=[
            pltpu.VMEM((sz.channels, LANES), BF16),
            pltpu.VMEM((sz.channels, LANES), BF16),
            pltpu.VMEM((max(2 * sz.piece * sz.blocks, sz.channels), LANES), F32),
            pltpu.VMEM((sz.blocks, wide_lines * LANES), BF16),
            pltpu.VMEM((2 * sz.outer, wide_lines * LANES), F32),
            pltpu.VMEM((wide_lines * sz.outer, 2 * LANES), BF16),
            pltpu.VMEM((2 * sz.outer, wide_lines * LANES), BF16),
            pltpu.VMEM((sz.pairs * sz.outer, 2 * LANES), F32),
            pltpu.SemaphoreType.DMA((3,)),
            pltpu.SemaphoreType.DMA((3,)),
        ],
        compiler_params=pltpu.CompilerParams(
            collective_id=cid, has_side_effects=True, vmem_limit_bytes=48 * MIB
        ),
        name="conv_backward",
    )(grad, filt_spec, sig_spec, taps, pos, env, outer_fwd, outer_inv, inner_fwd, inner_inv, twist)


def apart_project(sz, normed, w_in, w_gate, inner_ref, gate_ref):
    for side in range(sz.hid):
        rows = slice(side * sz.padded, (side + 1) * sz.padded)
        part = normed[:, side * sz.half : (side + 1) * sz.half]
        inner_ref[rows, :] = nt(w_in[side], part).astype(BF16)
        gate_ref[rows, :] = nt(w_gate[side], part)


def apart_first_kernel(sz, x_ref, gain_ref, w_in, w_gate, normed_ref, inner_ref, gate_ref):
    normal, _ = normalize(x_ref[...].astype(F32))
    normed = (normal * gain_ref[0:1, :]).astype(BF16)
    normed_ref[...] = normed
    apart_project(sz, normed, w_in, w_gate, inner_ref, gate_ref)


def apart_first(sz, x, gains, w_in, w_gate):
    tokens = x.shape[0]
    return pl.pallas_call(
        functools.partial(apart_first_kernel, sz),
        out_shape=(
            jax.ShapeDtypeStruct((tokens, sz.width), BF16),
            jax.ShapeDtypeStruct((sz.channels, tokens), BF16),
            jax.ShapeDtypeStruct((sz.channels, tokens), F32),
        ),
        in_specs=[whole()] * 4,
        out_specs=(whole(),) * 3,
        compiler_params=pltpu.CompilerParams(vmem_limit_bytes=32 * MIB),
        name="first_projection",
    )(x, gains, w_in, w_gate)


def apart_mix_out(sz, mixed, w_out):
    parts = []
    for side in range(sz.hid):
        rows = slice(side * sz.padded, (side + 1) * sz.padded)
        parts.append(tn(mixed[rows, :], w_out[side]))
    return jnp.concatenate(parts, axis=1)


def apart_ff_specs(sz, layer, tile):
    steps = sz.hidden // sz.hid // tile
    first_half = lambda i: jnp.minimum(i, steps - 1)
    second = lambda i: jnp.maximum(i - steps, 0)
    specs = []
    for place in (first_half, second):
        specs.append(
            pl.BlockSpec((1, 2, sz.width, tile), lambda i, place=place: (layer, 0, 0, place(i)))
        )
        specs.append(pl.BlockSpec((1, sz.width, tile), lambda i, place=place: (layer, 0, place(i))))
    return specs, steps


def apart_forward_kernel(
    sz,
    steps,
    conv_ref,
    inner_ref,
    gate_ref,
    skip_ref,
    x_ref,
    gain_ref,
    next_gain,
    w_out,
    w_in,
    w_gate,
    up_a,
    down_a,
    up_b,
    down_b,
    summed_ref,
    mixed_ref,
    middle_ref,
    normed_two,
    next_x,
    next_normed,
    next_inner,
    next_gate,
):
    index = pl.program_id(0)

    @pl.when(index == 0)
    def _():
        summed = conv_ref[...].astype(F32) + skip_ref[...] * inner_ref[...].astype(F32)
        summed_ref[...] = summed
        mixed_ref[...] = (gate_ref[...] * summed).astype(BF16)
        middle = x_ref[...].astype(F32) + apart_mix_out(sz, mixed_ref, w_out)
        middle_ref[...] = middle
        normal, _ = normalize(middle)
        normed_two[...] = (normal * gain_ref[1:2, :]).astype(BF16)
        next_x[...] = middle

    def accumulate(up_ref, down_ref):
        gate = nn(normed_two[...], up_ref[0, 0])
        up = nn(normed_two[...], up_ref[0, 1])
        value, _ = gelu_parts(gate)
        next_x[...] += nt((value * up).astype(BF16), down_ref[0])

    pl.when(index < steps)(lambda: accumulate(up_a, down_a))
    pl.when(index >= steps)(lambda: accumulate(up_b, down_b))

    @pl.when(index == 2 * steps - 1)
    def _():
        normal, _ = normalize(next_x[...])
        normed = (normal * next_gain[0:1, :]).astype(BF16)
        next_normed[...] = normed
        apart_project(sz, normed, w_in, w_gate, next_inner, next_gate)


def apart_full(shape):
    return pl.BlockSpec(shape, lambda i: (0,) * len(shape))


def apart_forward(sz, layer, conv, inner, gate, skip, x, gains, next_gains, w_out, w_in, w_gate, ff):
    tokens = x.shape[0]
    tile = 512
    specs, steps = apart_ff_specs(sz, layer, tile)
    small = (conv, inner, gate, skip, x, gains, next_gains, w_out, w_in, w_gate)
    outs = (
        ((sz.channels, tokens), F32),
        ((sz.channels, tokens), BF16),
        ((tokens, sz.width), F32),
        ((tokens, sz.width), BF16),
        ((tokens, sz.width), F32),
        ((tokens, sz.width), BF16),
        ((sz.channels, tokens), BF16),
        ((sz.channels, tokens), F32),
    )
    return pl.pallas_call(
        functools.partial(apart_forward_kernel, sz, steps),
        grid=(2 * steps,),
        out_shape=tuple(jax.ShapeDtypeStruct(shape, kind) for shape, kind in outs),
        in_specs=[apart_full(entry.shape) for entry in small] + specs,
        out_specs=tuple(apart_full(shape) for shape, kind in outs),
        compiler_params=pltpu.CompilerParams(
            dimension_semantics=("arbitrary",), vmem_limit_bytes=48 * MIB
        ),
        name="token_forward",
    )(*small, *ff)


def apart_block_grads(sz, tall, flat, target, slot):
    blocks_side = target.shape[1] // sz.hid
    size = sz.half // blocks_side
    rows = sz.padded // blocks_side
    for side in range(sz.hid):
        for block in range(blocks_side):
            begin = side * sz.padded + block * rows
            place = side * sz.half + block * size
            target[slot, side * blocks_side + block] = nn(
                tall[begin : begin + rows, :], flat[:, place : place + size]
            ).astype(target.dtype)


def apart_ff_backward_tile(normed, grad, up_ref, down_ref, total, out_total):
    gate = nn(normed, up_ref[0, 0])
    up = nn(normed, up_ref[0, 1])
    grad_hidden = nn(grad, down_ref[0])
    value, slope = gelu_parts(gate)
    if out_total is not None:
        out_total[...] += nt((value * up).astype(BF16), down_ref[0])
    grad_gate = (slope * up * grad_hidden).astype(BF16)
    grad_up = (value * grad_hidden).astype(BF16)
    total[...] += nt(grad_gate, up_ref[0, 0]) + nt(grad_up, up_ref[0, 1])


def apart_mixer_backward(
    sz, grad_next, middle, total, gain, mixed, summed, gate, w_out, outs
):
    grad_middle, mixer_grad, grad_gate, grad_summed, grad_conv, gain_grad = outs
    normal, inv = normalize(middle)
    back, gain_grad[...] = norm_back(total, normal, inv, gain)
    result = grad_next + back
    grad_middle[...] = result
    grad_o = result.astype(BF16)
    apart_block_grads(sz, mixed, grad_o, mixer_grad, 0)
    for side in range(sz.hid):
        rows = slice(side * sz.padded, (side + 1) * sz.padded)
        grad_mixed = nt(w_out[side], grad_o[:, side * sz.half : (side + 1) * sz.half])
        grad_gate[rows, :] = (grad_mixed * summed[rows, :]).astype(BF16)
        through = grad_mixed * gate[rows, :]
        grad_summed[rows, :] = through
        grad_conv[rows, :] = through.astype(BF16)


def apart_mixer_outs(sz, tokens, blocks):
    size = sz.width // blocks
    return (
        ((tokens, sz.width), F32),
        ((1, blocks, sz.channels // blocks, size), BF16),
        ((sz.channels, tokens), BF16),
        ((sz.channels, tokens), F32),
        ((sz.channels, tokens), BF16),
        ((1, sz.width), F32),
    )


def apart_turn_kernel(
    sz,
    steps,
    conv_ref,
    inner_ref,
    gate_ref,
    skip_ref,
    x_ref,
    gain_ref,
    grad_ref,
    w_out,
    up_a,
    down_a,
    up_b,
    down_b,
    hidden_out,
    normed_two,
    grad_middle,
    mixer_grad,
    grad_gate,
    grad_summed,
    grad_conv,
    gain_grad,
    summed,
    mixed,
    middle,
    out_total,
    total,
):
    index = pl.program_id(0)

    @pl.when(index == 0)
    def _():
        summed[...] = conv_ref[...].astype(F32) + skip_ref[...] * inner_ref[...].astype(F32)
        mixed[...] = (gate_ref[...] * summed[...]).astype(BF16)
        middle[...] = x_ref[...].astype(F32) + apart_mix_out(sz, mixed, w_out)
        normal, _ = normalize(middle[...])
        normed_two[...] = (normal * gain_ref[1:2, :]).astype(BF16)
        out_total[...] = middle[...]
        total[...] = jnp.zeros_like(total)

    def accumulate(up_ref, down_ref):
        apart_ff_backward_tile(normed_two[...], grad_ref[...], up_ref, down_ref, total, out_total)

    pl.when(index < steps)(lambda: accumulate(up_a, down_a))
    pl.when(index >= steps)(lambda: accumulate(up_b, down_b))

    @pl.when(index == 2 * steps - 1)
    def _():
        hidden_out[...] = out_total[...].astype(BF16)
        outs = (grad_middle, mixer_grad, grad_gate, grad_summed, grad_conv, gain_grad)
        apart_mixer_backward(
            sz,
            grad_ref[...].astype(F32),
            middle[...],
            total[...],
            gain_ref[1:2, :],
            mixed,
            summed,
            gate_ref,
            w_out,
            outs,
        )


def apart_turn(sz, layer, blocks, conv, inner, gate, skip, x, gains, grad, w_out, ff):
    tokens = x.shape[0]
    specs, steps = apart_ff_specs(sz, layer, 512)
    small = (conv, inner, gate, skip, x, gains, grad, w_out)
    outs = (((tokens, sz.width), BF16), ((tokens, sz.width), BF16)) + apart_mixer_outs(sz, tokens, blocks)
    return pl.pallas_call(
        functools.partial(apart_turn_kernel, sz, steps),
        grid=(2 * steps,),
        out_shape=tuple(jax.ShapeDtypeStruct(shape, kind) for shape, kind in outs),
        in_specs=[apart_full(entry.shape) for entry in small] + specs,
        out_specs=tuple(apart_full(shape) for shape, kind in outs),
        scratch_shapes=[
            pltpu.VMEM((sz.channels, tokens), F32),
            pltpu.VMEM((sz.channels, tokens), BF16),
            pltpu.VMEM((tokens, sz.width), F32),
            pltpu.VMEM((tokens, sz.width), F32),
            pltpu.VMEM((tokens, sz.width), F32),
        ],
        compiler_params=pltpu.CompilerParams(
            dimension_semantics=("arbitrary",), vmem_limit_bytes=48 * MIB
        ),
        name="token_turn",
    )(*small, *ff)


def apart_input_backward(
    sz, back, through, grad_gate, skip, normed, x, gain, w_in, w_gate, grad_middle, mixer_grad
):
    inner_grad = (skip * through + back.astype(F32)).astype(BF16)
    apart_block_grads(sz, inner_grad, normed, mixer_grad, 0)
    apart_block_grads(sz, grad_gate, normed, mixer_grad, 1)
    parts = []
    for side in range(sz.hid):
        rows = slice(side * sz.padded, (side + 1) * sz.padded)
        parts.append(tn(inner_grad[rows, :], w_in[side]) + tn(grad_gate[rows, :], w_gate[side]))
    normal, inv = normalize(x)
    result, gain_grad = norm_back(jnp.concatenate(parts, axis=1), normal, inv, gain)
    return grad_middle + result, gain_grad


def apart_backward_kernel(
    sz,
    steps,
    back_ref,
    through_ref,
    gate_grad_ref,
    skip_ref,
    normed_ref,
    x_ref,
    gain_ref,
    w_in,
    w_gate,
    grad_middle_ref,
    normed_two,
    middle_ref,
    summed_ref,
    gate_ref,
    mixed_ref,
    low_gain,
    w_out,
    up_a,
    down_a,
    up_b,
    down_b,
    input_grad,
    input_gain,
    grad_ff,
    grad_middle,
    mixer_grad,
    grad_gate,
    grad_summed,
    grad_conv,
    gain_grad,
    grad_next,
    total,
):
    index = pl.program_id(0)

    @pl.when(index == 0)
    def _():
        result, input_gain[...] = apart_input_backward(
            sz,
            back_ref[...],
            through_ref[...],
            gate_grad_ref[...],
            skip_ref[...],
            normed_ref[...],
            x_ref[...],
            gain_ref[0:1, :],
            w_in,
            w_gate,
            grad_middle_ref[...],
            input_grad,
        )
        grad_next[...] = result
        grad_ff[...] = result.astype(BF16)
        total[...] = jnp.zeros_like(total)

    def accumulate(up_ref, down_ref):
        apart_ff_backward_tile(normed_two[...], grad_ff[...], up_ref, down_ref, total, None)

    pl.when(index < steps)(lambda: accumulate(up_a, down_a))
    pl.when(index >= steps)(lambda: accumulate(up_b, down_b))

    @pl.when(index == 2 * steps - 1)
    def _():
        outs = (grad_middle, mixer_grad, grad_gate, grad_summed, grad_conv, gain_grad)
        apart_mixer_backward(
            sz,
            grad_next[...],
            middle_ref[...],
            total[...],
            low_gain[1:2, :],
            mixed_ref,
            summed_ref,
            gate_ref,
            w_out,
            outs,
        )


def apart_input_outs(sz, blocks):
    size = sz.width // blocks
    return (((2, blocks, sz.channels // blocks, size), BF16), ((1, sz.width), F32))


def apart_backward(
    sz,
    layer,
    blocks,
    back,
    through,
    gate_grad,
    skip,
    normed,
    x,
    gains,
    w_in,
    w_gate,
    grad_middle,
    normed_two,
    middle,
    summed,
    gate,
    mixed,
    low_gains,
    w_out,
    ff,
):
    tokens = x.shape[0]
    specs, steps = apart_ff_specs(sz, layer, 512)
    small = (
        back,
        through,
        gate_grad,
        skip,
        normed,
        x,
        gains,
        w_in,
        w_gate,
        grad_middle,
        normed_two,
        middle,
        summed,
        gate,
        mixed,
        low_gains,
        w_out,
    )
    outs = (
        apart_input_outs(sz, blocks) + (((tokens, sz.width), BF16),) + apart_mixer_outs(sz, tokens, blocks)
    )
    return pl.pallas_call(
        functools.partial(apart_backward_kernel, sz, steps),
        grid=(2 * steps,),
        out_shape=tuple(jax.ShapeDtypeStruct(shape, kind) for shape, kind in outs),
        in_specs=[apart_full(entry.shape) for entry in small] + specs,
        out_specs=tuple(apart_full(shape) for shape, kind in outs),
        scratch_shapes=[
            pltpu.VMEM((tokens, sz.width), F32),
            pltpu.VMEM((tokens, sz.width), F32),
        ],
        compiler_params=pltpu.CompilerParams(
            dimension_semantics=("arbitrary",), vmem_limit_bytes=48 * MIB
        ),
        name="token_backward",
    )(*small, *ff)


def apart_last_kernel(
    sz,
    back_ref,
    through_ref,
    gate_grad_ref,
    skip_ref,
    normed_ref,
    x_ref,
    gain_ref,
    w_in,
    w_gate,
    grad_middle_ref,
    input_grad,
    input_gain,
    grad_in,
):
    grad_in[...], input_gain[...] = apart_input_backward(
        sz,
        back_ref[...],
        through_ref[...],
        gate_grad_ref[...],
        skip_ref[...],
        normed_ref[...],
        x_ref[...].astype(F32),
        gain_ref[0:1, :],
        w_in,
        w_gate,
        grad_middle_ref[...],
        input_grad,
    )


def apart_last(sz, blocks, *args):
    tokens = args[5].shape[0]
    outs = apart_input_outs(sz, blocks) + (((tokens, sz.width), F32),)
    return pl.pallas_call(
        functools.partial(apart_last_kernel, sz),
        out_shape=tuple(jax.ShapeDtypeStruct(shape, kind) for shape, kind in outs),
        in_specs=[whole()] * len(args),
        out_specs=(whole(),) * len(outs),
        compiler_params=pltpu.CompilerParams(vmem_limit_bytes=32 * MIB),
        name="last_projection",
    )(*args)


def apart_ff_grads_kernel(normed_ref, grad_ref, up_ref, down_ref, out_ref, hidden, grad_gate, grad_up):
    tokens = normed_ref.shape[0]
    chunk = 256
    for start in range(0, tokens, chunk):
        rows = pl.ds(start, chunk)
        normed = normed_ref[rows, :]
        gate = nn(normed, up_ref[0])
        up = nn(normed, up_ref[1])
        through = nn(grad_ref[rows, :], down_ref[...])
        value, slope = gelu_parts(gate)
        hidden[rows, :] = (value * up).astype(BF16)
        grad_gate[rows, :] = (slope * up * through).astype(BF16)
        grad_up[rows, :] = (value * through).astype(BF16)
    out_ref[0] = tn(normed_ref[...], grad_gate[...]).astype(BF16)
    out_ref[1] = tn(normed_ref[...], grad_up[...]).astype(BF16)
    out_ref[2] = tn(grad_ref[...], hidden[...]).astype(BF16)


def apart_ff_grads(normed, grad, up, down):
    tokens, width = normed.shape
    units = down.shape[1]
    return pl.pallas_call(
        apart_ff_grads_kernel,
        out_shape=jax.ShapeDtypeStruct((3, width, units), BF16),
        in_specs=[whole()] * 4,
        out_specs=whole(),
        scratch_shapes=[pltpu.VMEM((tokens, units), BF16)] * 3,
        compiler_params=pltpu.CompilerParams(vmem_limit_bytes=48 * MIB),
        name="ff_weight_grads",
    )(normed, grad, up, down)


def apart_row_exchange_kernel(rows, parts, *refs):
    sources, targets, sems = refs[:parts], refs[parts : 2 * parts], refs[2 * parts]
    row = lax.axis_index("rows")
    col = lax.axis_index("hid")
    barrier = pltpu.get_barrier_semaphore()

    def greet(step, carry):
        peer = lax.rem(row + step, rows)
        pl.semaphore_signal(barrier, inc=1, device_id=(peer, col), device_id_type=MESH)
        return carry

    lax.fori_loop(1, rows, greet, 0)
    for part in range(parts):
        pltpu.make_async_copy(
            sources[part].at[row], targets[part].at[row], sems.at[part, 2]
        ).start()
    pl.semaphore_wait(barrier, rows - 1)

    def post(step, carry):
        peer = lax.rem(row + step, rows)
        for part in range(parts):
            pltpu.make_async_remote_copy(
                src_ref=sources[part].at[peer],
                dst_ref=targets[part].at[row],
                send_sem=sems.at[part, 0],
                recv_sem=sems.at[part, 1],
                device_id=(peer, col),
                device_id_type=MESH,
            ).start()
        return carry

    lax.fori_loop(1, rows, post, 0)
    for part in range(parts):
        pltpu.make_async_copy(
            sources[part].at[0], targets[part].at[0], sems.at[part, 2]
        ).wait()
        span = pl.ds(0, rows - 1)
        pltpu.make_async_remote_copy(
            src_ref=sources[part].at[span],
            dst_ref=targets[part].at[span],
            send_sem=sems.at[part, 0],
            recv_sem=sems.at[part, 1],
            device_id=(lax.rem(row + 1, rows), col),
            device_id_type=MESH,
        ).wait()


def apart_row_exchange(arrays, rows, cid):
    parts = len(arrays)
    return pl.pallas_call(
        functools.partial(apart_row_exchange_kernel, rows, parts),
        out_shape=tuple(jax.ShapeDtypeStruct(entry.shape, entry.dtype) for entry in arrays),
        in_specs=[pl.BlockSpec(memory_space=pl.ANY)] * parts,
        out_specs=(pl.BlockSpec(memory_space=pl.ANY),) * parts,
        scratch_shapes=[pltpu.SemaphoreType.DMA((parts, 3))],
        compiler_params=pltpu.CompilerParams(collective_id=cid, has_side_effects=True),
        name="row_exchange",
    )(*arrays)


def apart_swap(value):
    return lax.ppermute(value, "hid", [(0, 1), (1, 0)])


def apart_both_halves(own, axis):
    other = apart_swap(own)
    low = lax.axis_index("hid") == 0
    return jnp.concatenate([jnp.where(low, own, other), jnp.where(low, other, own)], axis=axis)


def apart_own_tokens(part):
    tokens = part.shape[0] // 2
    side = lax.axis_index("hid")
    keep = lax.dynamic_slice_in_dim(part, side * tokens, tokens, 0)
    other = apart_swap(lax.dynamic_slice_in_dim(part, (1 - side) * tokens, tokens, 0))
    low = side == 0
    return jnp.concatenate([jnp.where(low, keep, other), jnp.where(low, other, keep)], axis=1)


def apart_own_features(part):
    half = part.shape[1] // 2
    side = lax.axis_index("hid")
    keep = lax.dynamic_slice_in_dim(part, side * half, half, 1)
    other = apart_swap(lax.dynamic_slice_in_dim(part, (1 - side) * half, half, 1))
    low = side == 0
    return jnp.concatenate([jnp.where(low, keep, other), jnp.where(low, other, keep)], axis=0)


def apart_padded_mixer(sz, mixer):
    layers, kinds, blocks, size, _ = mixer.shape
    chan_first = jnp.concatenate([jnp.swapaxes(mixer[:, :2], 3, 4), mixer[:, 2:]], axis=1)
    grouped = chan_first.reshape(layers, kinds, blocks, size // sz.chans, sz.chans, size)
    grouped = jnp.pad(grouped, ((0, 0),) * 4 + ((0, sz.piece - sz.chans), (0, 0)))
    grouped = grouped.reshape(layers, kinds, blocks, -1, size)
    parts = [
        jnp.pad(grouped[:, :, block], ((0, 0),) * 3 + ((block * size, (blocks - 1 - block) * size),))
        for block in range(blocks)
    ]
    return jnp.concatenate(parts, axis=2)


def apart_padded_channels(sz, values):
    lead = values.shape[:-1]
    grouped = values.reshape(lead + (sz.rows, sz.chans))
    grouped = jnp.pad(grouped, ((0, 0),) * (len(lead) + 1) + ((0, sz.piece - sz.chans),))
    return grouped.reshape(lead + (sz.padded,))


def apart_envelopes(sz):
    row = lax.axis_index("rows")
    first_chan = lax.axis_index("hid") * sz.half + row * sz.chans
    channels = first_chan + jnp.arange(sz.piece, dtype=jnp.int32)
    fraction = (channels * 37 % sz.width).astype(F32) / (sz.width - 1)
    start_log = math.log(1.0 / 40.0)
    rate = jnp.exp(start_log + (math.log(1.5 / sz.length) - start_log) * fraction)
    steps = jnp.arange(sz.length, dtype=jnp.int32).astype(F32)
    decay = jnp.exp(-steps[None, :] * rate[:, None])
    shape = decay * lax.rsqrt(2.0 * jnp.sum(decay * decay, axis=1, keepdims=True))
    return jnp.concatenate([shape, shape * (steps > 0)[None, :]], axis=0)


def apart_plane_gather(value):
    size = lax.axis_size("rows")
    for bit in (1, 2):
        other = lax.ppermute(value, "rows", [(r, r ^ bit) for r in range(size)])
        value = jnp.concatenate([value, other], axis=0)
    return jnp.concatenate([value, apart_swap(value)], axis=0)


def apart_on_device(hidden_in, d_out, gains, mixer, skip, filters, gate_up, down):
    layers = gate_up.shape[0]
    rows = lax.axis_size("rows")
    hid = lax.axis_size("hid")
    width = gate_up.shape[2]
    hidden = gate_up.shape[3] * hid
    blocks = mixer.shape[2] * hid
    block_size = mixer.shape[3]
    sz = apart_Sizes(rows, hid, width, hidden, hidden_in.shape[0] * rows)
    row = lax.axis_index("rows")

    x = apart_own_tokens(hidden_in)
    gains_all = apart_both_halves(gains, 2)
    skip_all = apart_both_halves(apart_padded_channels(sz, skip), 1)[:, :, None]
    weights = apart_both_halves(apart_padded_mixer(sz, mixer)[:, :, None], 2)
    gate_up_b = apart_swap(gate_up)
    down_b = apart_swap(down)
    ff = (gate_up, down, gate_up_b, down_b)
    grad_out = apart_own_tokens(d_out)

    tables = dft_tables(sz.length)
    pos = jnp.asarray(position_table(sz.length).T, F32).astype(BF16)
    env = apart_envelopes(sz)
    taps = lax.dynamic_slice_in_dim(filters, row * sz.chans, sz.chans, 3)
    taps = jnp.pad(taps, ((0, 0),) * 3 + ((0, sz.piece - sz.chans),))
    taps = jnp.swapaxes(taps, 2, 3).reshape(layers, 2 * sz.piece, ORDER).astype(BF16)

    normed, inner, gate = apart_first(sz, x, gains_all[0], weights[0, 0], weights[0, 1])
    stored = []
    for layer in range(layers):
        conv, filt_spec, sig_spec = apart_conv_forward(sz, inner, taps[layer], pos, env, tables, 0)
        stored.append(dict(x=x, normed=normed, inner=inner, gate=gate, f=filt_spec, s=sig_spec))
        if layer < layers - 1:
            summed, mixed, middle, normed_two, x, normed, next_inner, next_gate = apart_forward(
                sz,
                layer,
                conv,
                inner,
                gate,
                skip_all[layer],
                x,
                gains_all[layer],
                gains_all[layer + 1],
                weights[layer, 2],
                weights[layer + 1, 0],
                weights[layer + 1, 1],
                ff,
            )
            stored[-1].update(summed=summed, mixed=mixed, middle=middle, normed_two=normed_two)
            inner, gate = next_inner, next_gate

    top = layers - 1
    hidden_out, normed_two, *rest = apart_turn(
        sz,
        top,
        blocks,
        conv,
        inner,
        gate,
        skip_all[top],
        x,
        gains_all[top],
        grad_out,
        weights[top, 2],
        ff,
    )
    stored[top].update(normed_two=normed_two)
    grad_ff = grad_out
    units = sz.hidden // hid // 4
    unit_start = lax.rem(row, 4) * units
    ff_parts, mixer_parts, gain_parts, skip_parts, taps_parts = [], [], [], [], []
    for layer in reversed(range(layers)):
        kept = stored[layer]
        grad_middle, out_grad, grad_gate, grad_summed, grad_conv, gain_two = rest
        ff_parts.insert(
            0,
            apart_ff_grads(
                apart_plane_gather(kept["normed_two"]),
                apart_plane_gather(grad_ff),
                lax.dynamic_slice_in_dim(gate_up[layer], unit_start, units, 2),
                lax.dynamic_slice_in_dim(down[layer], unit_start, units, 1),
            ),
        )
        back, taps_grad = apart_conv_backward(
            sz, grad_conv, kept["f"], kept["s"], taps[layer], pos, env, tables, 1
        )
        skip_parts.insert(0, jnp.sum(grad_summed * kept["inner"].astype(F32), axis=1))
        taps_parts.insert(0, taps_grad)
        common = (
            back,
            grad_summed,
            grad_gate,
            skip_all[layer],
            kept["normed"],
            kept["x"],
            gains_all[layer],
            weights[layer, 0],
            weights[layer, 1],
            grad_middle,
        )
        if layer > 0:
            low = stored[layer - 1]
            in_grad, gain_one, grad_ff, *rest = apart_backward(
                sz,
                layer - 1,
                blocks,
                *common,
                low["normed_two"],
                low["middle"],
                low["summed"],
                low["gate"],
                low["mixed"],
                gains_all[layer - 1],
                weights[layer - 1, 2],
                ff,
            )
        else:
            in_grad, gain_one, grad_in = apart_last(sz, blocks, *common)
        mixer_parts.insert(0, jnp.concatenate([in_grad, out_grad], axis=0))
        gain_parts.insert(0, jnp.concatenate([gain_one, gain_two], axis=0))

    piece_rows = width // rows
    padded_rows = round_up(piece_rows, 16)
    pieces = jnp.stack(ff_parts).reshape(layers, 3, rows, piece_rows, units)
    pieces = jnp.pad(pieces, ((0, 0),) * 3 + ((0, padded_rows - piece_rows), (0, 0)))
    pieces = jnp.moveaxis(pieces, 2, 0)
    (arrived,) = apart_row_exchange((pieces,), rows, 2)
    arrived = arrived.reshape(rows // 4, 4, layers, 3, padded_rows, units)[:, :, :, :, :piece_rows]
    summed_ff = jnp.sum(arrived.astype(F32), axis=0)
    summed_ff = jnp.moveaxis(summed_ff, 0, 3).reshape(layers, 3, piece_rows, 4 * units)

    mixers = jnp.stack(mixer_parts).reshape(layers, 3, blocks, -1, sz.piece, block_size)
    mixers = mixers[:, :, :, :, : sz.chans].reshape(layers, 3, blocks, block_size, block_size)
    small = jnp.concatenate(
        [jnp.stack(gain_parts).reshape(-1), jnp.stack(skip_parts).reshape(-1)]
    )
    mixers, small = lax.psum((mixers.astype(F32), small), ("rows", "hid"))
    side = lax.axis_index("hid")
    mixers = lax.dynamic_slice_in_dim(mixers, side * (blocks // hid), blocks // hid, 2)
    mixers = jnp.concatenate([jnp.swapaxes(mixers[:, :2], 3, 4), mixers[:, 2:]], axis=1)
    gain_size = layers * 2 * width
    gain_out = lax.dynamic_slice_in_dim(
        small[:gain_size].reshape(layers, 2, width), side * sz.half, sz.half, 2
    )
    skip_out = small[gain_size:].reshape(layers, hid, rows, sz.piece)[..., : sz.chans]
    skip_out = lax.dynamic_index_in_dim(skip_out, side, 1, False).reshape(layers, sz.half)
    taps_out = jnp.stack(taps_parts).reshape(layers, 2, sz.piece, ORDER)[:, :, : sz.chans]
    taps_out = lax.all_gather(taps_out, "rows", axis=2, tiled=True)
    return (
        apart_own_features(hidden_out),
        apart_own_features(grad_in),
        gain_out,
        mixers,
        skip_out,
        jnp.swapaxes(taps_out, 2, 3),
        summed_ff[:, :2],
        summed_ff[:, 2],
    )


def on_device(*arrays):
    sz = Sizes.of(*arrays)
    return together(sz, *arrays) if sz.fits() else apart_on_device(*arrays)


def solution(mesh):
    placed = (
        P("rows", "hid"),
        P("rows", "hid"),
        P(None, None, "hid"),
        P(None, None, "hid", None, None),
        P(None, "hid"),
        P(None, None, None, "hid"),
        P(None, None, None, "hid"),
        P(None, None, "hid"),
    )
    return jax.shard_map(
        on_device,
        mesh=mesh,
        in_specs=placed,
        out_specs=(
            P("rows", "hid"),
            P("rows", "hid"),
            P(None, None, "hid"),
            P(None, None, "hid", None, None),
            P(None, "hid"),
            P(None, None, None, "hid"),
            P(None, None, "rows", "hid"),
            P(None, "rows", "hid"),
        ),
        check_vma=False,
    )
```

```python
import functools
import math

import jax
import jax.numpy as jnp
import numpy as np
from jax import lax
from jax.experimental import pallas as pl
from jax.experimental.pallas import tpu as pltpu
from jax.sharding import PartitionSpec as P

ORDER = 128
SEQ_LEN = 8192
LANES = 128
NORM_EPS = 1e-05
DECAY = 0.02
MESH = pl.DeviceIdType.MESH
BF16 = jnp.bfloat16
F32 = jnp.float32
MIB = 2**20
GELU_C = math.sqrt(2.0 / math.pi)


def round_up(value, step):
    return -(-value // step) * step


def whole():
    return pl.BlockSpec(memory_space=pltpu.VMEM)


def nn(a, b):
    return lax.dot_general(a, b, (((1,), (0,)), ((), ())), preferred_element_type=F32)


def nt(a, b):
    return lax.dot_general(a, b, (((1,), (1,)), ((), ())), preferred_element_type=F32)


def tn(a, b):
    return lax.dot_general(a, b, (((0,), (0,)), ((), ())), preferred_element_type=F32)


def position_table(length):
    half_order = ORDER // 2
    index_list = np.arange(half_order)
    multiple = 1 + index_list * index_list * (length // 4) // (half_order * half_order)
    phase = (np.arange(length)[:, None] * multiple[None, :] % length) * (2.0 * math.pi / length)
    return np.concatenate([np.sin(phase), np.cos(phase)], axis=1)


def dft_tables(length):
    blocks = length // LANES
    size = 2 * length
    outer = 2 * blocks
    k = np.arange(outer)
    n = np.arange(blocks)
    m = np.arange(LANES)
    angle = 2.0 * math.pi * (np.outer(k, n) % outer) / outer
    outer_fwd = np.concatenate([np.cos(angle), -np.sin(angle)], axis=0)
    outer_inv = np.concatenate([np.cos(angle), -np.sin(angle)], axis=0).T / size
    angle = 2.0 * math.pi * (np.outer(m, m) % LANES) / LANES
    cos, sin = np.cos(angle), np.sin(angle)
    inner_fwd = np.block([[cos, -sin], [sin, cos]])
    inner_inv = np.block([[cos, sin], [-sin, cos]])
    angle = 2.0 * math.pi * np.outer(k, m) / size
    twist = np.concatenate([np.cos(angle), np.sin(angle)], axis=1)
    half = lambda table: jnp.asarray(table, F32).astype(BF16)
    return (half(outer_fwd), half(outer_inv), half(inner_fwd), half(inner_inv), jnp.asarray(twist, F32))


def normalize(values):
    mean = jnp.mean(values, axis=1, keepdims=True)
    square = jnp.mean(values * values, axis=1, keepdims=True)
    inv = lax.rsqrt(square - mean * mean + NORM_EPS)
    return (values - mean) * inv, inv


def norm_back(grad, normal, inv, gain):
    scaled = grad * gain
    mean = jnp.mean(scaled, axis=1, keepdims=True)
    cross = jnp.mean(scaled * normal, axis=1, keepdims=True)
    return inv * (scaled - mean - normal * cross), jnp.sum(grad * normal, axis=0, keepdims=True)


def gelu_parts(gate):
    square = gate * gate
    tanh = jnp.tanh(GELU_C * gate * (1.0 + 0.044715 * square))
    half = 0.5 * (1.0 + tanh)
    value = gate * half
    slope = half + 0.5 * gate * (1.0 - tanh * tanh) * (GELU_C * (1.0 + 3.0 * 0.044715 * square))
    return value, slope


class Sizes:
    def __init__(self, rows, hid, tokens, width, hidden, layers, blocks):
        self.rows, self.hid, self.width, self.layers = rows, hid, width, layers
        self.count = rows * hid
        self.own = tokens // self.count
        self.half = width // hid
        self.units = hidden // hid
        self.blocks = blocks
        self.size = width // blocks
        self.side_blocks = blocks // hid
        self.couple = 2 * width // self.count
        self.big = round_up(self.couple // 2, 16)
        self.small = self.couple - self.big
        self.length = min(SEQ_LEN, tokens)
        self.seqs = tokens // self.length
        self.steps = self.length // LANES
        self.outer = 2 * self.steps
        self.pairs = self.seqs * self.big
        self.group = 4
        self.peers = rows // self.group
        self.part = self.units // self.group
        self.depth = width // rows
        self.deep = round_up(self.depth, 16)
        self.deeps = tuple(
            round_up(-(-(matrices * self.size + 16) // rows), 16)
            for matrices in (3 * layers - 1, 1)
        )
        self.taps_rows = round_up(2 * self.big + 1, 16)


    @classmethod
    def of(cls, hidden_in, d_out, gains, mixer, skip, filters, gate_up, down):
        rows, hid = lax.axis_size("rows"), lax.axis_size("hid")
        layers, _, width, units = gate_up.shape
        tokens = hidden_in.shape[0] * rows
        return cls(rows, hid, tokens, width, units * hid, layers, mixer.shape[2] * hid)


    def fits(self):
        whole_tiles = self.small == 16 and self.big == 32 and self.rows % 8 == 0
        whole_tiles = whole_tiles and self.own == LANES and self.depth % 16 == 0
        whole_tiles = whole_tiles and self.peers == 4 and self.layers == 2 and self.seqs == 1
        whole_tiles = whole_tiles and all(self.size % deep == 0 for deep in self.deeps)
        total = 0
        for spec in layout(self)[1]:
            size = jnp.dtype(spec.dtype).itemsize
            *lead, rows, lanes = spec.shape
            total += math.prod(lead) * round_up(rows, 32 // size) * round_up(lanes, LANES) * size
        return whole_tiles and total <= 60 * MIB


class Links:
    def __init__(self, sz, sems, local_sems):
        self.sz, self.sems, self.local_sems = sz, sems, local_sems
        self.used = 0
        self.used_local = 0
        self.row = lax.axis_index("rows")
        self.col = lax.axis_index("hid")
        self.plane = lax.rem(self.row, sz.peers)
        self.line = self.row // sz.peers

    def pair(self):
        first = self.used
        self.used += 2
        return self.sems.at[first], self.sems.at[first + 1]

    def copy(self, source, target, pair, row, col):
        return pltpu.make_async_remote_copy(
            src_ref=source,
            dst_ref=target,
            send_sem=pair[0],
            recv_sem=pair[1],
            device_id=(row, col),
            device_id_type=MESH,
        )

    def sibling(self, source, target):
        copy = self.copy(source, target, self.pair(), self.row, self.sz.hid - 1 - self.col)
        copy.start()
        return copy

    def load(self, source, target):
        copy = pltpu.make_async_copy(source, target, self.local_sems.at[self.used_local])
        self.used_local += 1
        copy.start()
        return copy

    def groups(self, count, me, row_of, source_of, target):
        pair = self.pair()

        def post(step, carry):
            member = lax.rem(me + step, count)
            self.copy(source_of(member), target, pair, row_of(member), self.col).start()
            return carry

        lax.fori_loop(1, count, post, 0)
        return pair

    def in_plane(self, source_of, target):
        row_of = lambda member: self.line * self.sz.peers + member
        return self.groups(self.sz.peers, self.plane, row_of, source_of, target)

    def in_line(self, source_of, target):
        row_of = lambda member: member * self.sz.peers + self.plane
        return self.groups(self.sz.group, self.line, row_of, source_of, target)

    def in_rows(self, source_of, target):
        return self.groups(self.sz.rows, self.row, lambda member: member, source_of, target)

    def wait(self, pair, span):
        self.copy(span, span, pair, self.row, self.sz.hid - 1 - self.col).wait()


class Plane:
    def __init__(self, links):
        self.links = links
        self.me = links.plane
        along_x = self.me + 1 - 2 * lax.rem(self.me, 2)
        along_y = self.me + 2 - 4 * (self.me // 2)
        self.near = (along_x, along_y)
        self.far = (along_y, along_x)
        self.across = 3 - self.me

    def send(self, copies):
        links = self.links
        pair = links.pair()
        for source, target, member in copies:
            row = links.line * links.sz.peers + member
            links.copy(source, target, pair, row, links.col).start()
        return pair


class PlaneSum(Plane):
    def __init__(self, links, source, first, give, second):
        super().__init__(links)
        self.source, self.first, self.give, self.second = source, first, give, second

    def start(self):
        copies = []
        for half in range(2):
            for which, member in enumerate((self.near[half], self.across)):
                target = self.first.at[half, which]
                copies.append((self.source(member, half), target, self.near[half]))
        self.pair = self.send(copies)

    def middle(self):
        self.links.wait(self.pair, self.first)
        copies = []
        for half in range(2):
            theirs = self.source(self.far[half], half)[...].astype(F32)
            self.give[half] = (theirs + self.first[half, 1].astype(F32)).astype(BF16)
            mine = self.source(self.me, half)[...].astype(F32)
            self.first[half, 0] = (mine + self.first[half, 0].astype(F32)).astype(BF16)
            copies.append((self.give.at[half], self.second.at[half], self.far[half]))
        self.pair = self.send(copies)

    def end(self):
        self.links.wait(self.pair, self.second)

    def sums(self):
        for half in range(2):
            total = self.first[half, 0].astype(F32) + self.second[half].astype(F32)
            self.second[half] = total.astype(BF16)
        count = self.links.sz.group // 2
        return lambda member: self.second.at[member // count, lax.rem(member, count)]


class DirectSum(Plane):
    def __init__(self, links, source, parts):
        super().__init__(links)
        self.source, self.parts = source, parts

    def start(self):
        self.pair = self.links.in_plane(self.source, self.parts.at[self.me])

    def end(self):
        links = self.links
        links.wait(self.pair, self.parts.at[pl.ds(0, links.sz.peers - 1)])

    def sums(self):
        self.parts[self.me] = self.source(self.me)[...]
        total = self.parts[0].astype(F32)
        for member in range(1, self.links.sz.peers):
            total += self.parts[member].astype(F32)
        self.parts[0] = total.astype(BF16)
        return lambda member: self.parts.at[0, member]


class PlaneSpread(Plane):
    def __init__(self, links, place, span):
        super().__init__(links)
        self.place, self.span = place, span

    def start(self):
        copies = []
        for half in range(2):
            here = self.place(self.me, half)
            copies.append((here, here, self.near[half]))
        self.pair = self.send(copies)

    def middle(self):
        self.links.wait(self.pair, self.span(1))
        copies = []
        for half in range(2):
            for member in (self.me, self.near[half]):
                here = self.place(member, half)
                copies.append((here, here, self.far[half]))
        self.pair = self.send(copies)

    def end(self):
        self.links.wait(self.pair, self.span(2))


LOAD_BUFFERS = ("mine", "give", "got", "first", "second_give", "second", "line_in", "out")


class Payload:
    def __init__(self, sz, b, links, index, output):
        self.sz, self.links, self.output = sz, links, output
        self.direct = index == 1
        self.deep = sz.deeps[index]
        for name in LOAD_BUFFERS:
            setattr(self, name, getattr(b, "load_" + name)[index])
        half = lambda which: pl.ds(which * (sz.group // 2), sz.group // 2)
        self.plane = PlaneSum(
            links,
            lambda member, which: self.mine.at[member, half(which)],
            self.first,
            self.second_give,
            self.second,
        )
        if self.direct:
            self.plane = DirectSum(links, lambda member: self.mine.at[member], b.late_parts)
        self.spread = PlaneSpread(
            links,
            lambda member, which: self.got.at[member, half(which)],
            lambda count: self.got.at[pl.ds(0, count)],
        )
        self.half = half

    def matrix(self, place, values):
        sz = self.sz
        low = lax.axis_index("hid") == 0
        left = jnp.concatenate(values[: sz.side_blocks], axis=1)
        right = jnp.concatenate(values[sz.side_blocks :], axis=1)
        mine = jnp.where(low, left, right).astype(BF16)
        give = jnp.where(low, right, left).astype(BF16)
        count = sz.size // self.deep
        for part in range(count):
            index = place * count + part
            rows = slice(part * self.deep, (part + 1) * self.deep)
            self.mine[index // sz.group, index % sz.group] = mine[rows, :]
            self.give[index // sz.group, index % sz.group] = give[rows, :]

    def rows16(self, place, mine, give):
        index = place * (self.sz.size // self.deep)
        self.mine[index // self.sz.group, index % self.sz.group, 0:16] = mine.astype(BF16)
        self.give[index // self.sz.group, index % self.sz.group, 0:16] = give.astype(BF16)

    def to_partner(self):
        self.copy = self.links.sibling(self.give, self.got)

    def to_plane(self):
        done(self.copy)
        self.mine[...] = (self.mine[...].astype(F32) + self.got[...].astype(F32)).astype(BF16)
        self.plane.start()

    def middle(self):
        self.plane.middle()

    def to_line(self):
        self.plane.end()
        self.sums = self.plane.sums()
        links = self.links
        self.pair = links.in_line(self.sums, self.line_in.at[links.line])

    def back_line(self):
        links, sz = self.links, self.sz
        links.wait(self.pair, self.line_in.at[pl.ds(0, sz.group - 1)])
        self.line_in[links.line] = self.sums(links.line)[...]
        total = self.line_in[0].astype(F32)
        for member in range(1, sz.group):
            total += self.line_in[member].astype(F32)
        self.out[...] = total.astype(BF16)
        self.got[links.plane, links.line] = self.out[...]
        self.pair = links.in_line(lambda member: self.out, self.got.at[links.plane, links.line])

    def back_plane(self):
        links = self.links
        links.wait(self.pair, self.got.at[0, pl.ds(0, self.sz.group - 1)])
        if self.direct:
            place = self.got.at[links.plane]
            self.pair = links.in_plane(lambda member: place, place)
        else:
            self.spread.start()

    def finish(self):
        if self.direct:
            self.links.wait(self.pair, self.got.at[pl.ds(0, self.sz.peers - 1)])
        else:
            self.spread.end()
        return self.links.load(self.got, self.output)


def greet_all(sz):
    me = lax.axis_index("rows") * sz.hid + lax.axis_index("hid")
    barrier = pltpu.get_barrier_semaphore()

    def greet(step, carry):
        peer = lax.rem(me + step, sz.count)
        pl.semaphore_signal(
            barrier,
            inc=1,
            device_id=(peer // sz.hid, lax.rem(peer, sz.hid)),
            device_id_type=MESH,
        )
        return carry

    lax.fori_loop(1, sz.count, greet, 0)
    return barrier


class Exchange:
    def __init__(self, sz, links):
        self.sz, self.links = sz, links
        self.odd = lax.rem(links.row, 2)
        self.token = links.row * sz.hid + links.col

    def channels(self, row, col, part):
        sz = self.sz
        start = col * sz.half + (row // 2) * sz.couple + lax.rem(row, 2) * sz.big
        return pl.ds(pl.multiple_of(start + part * 16, 16), 16)

    def block(self, token):
        return pl.ds(pl.multiple_of(token * 16, 16), 16)

    def far_first(self):
        line = self.links.line
        odd = lax.rem(line, 2)
        across = 2 * (1 - line // 2)
        return across + odd, across + 1 - odd, line + 1 - 2 * odd, line

    def owners(self, part, body):
        if part == 0:
            body()
        else:
            pl.when(self.odd == 0)(body)

    def local(self):
        local = self.links.local_sems.at[self.links.used_local]
        self.links.used_local += 1
        return local

    def to_owners(self, source, target):
        return [self.part_to_owners(source, target, part) for part in range(2)]

    def part_to_owners(self, source, target, part):
        sz, links = self.sz, self.links
        pair, local = links.pair(), self.local()
        there = target.at[part, self.block(self.token)]

        def own():
            mine = source.at[self.channels(links.row, links.col, part)]
            pltpu.make_async_copy(mine, there, local).start()

        self.owners(part, own)
        apart = 1 + part
        devices = sz.peers * sz.hid // apart
        first = (links.plane // apart) * sz.hid + links.col

        for turn, line in enumerate(self.far_first()):

            def post(step, carry):
                index = lax.rem(first + step, devices)
                row, col = line * sz.peers + apart * (index // sz.hid), lax.rem(index, sz.hid)
                piece = source.at[self.channels(row, col, part)]
                links.copy(piece, there, pair, row, col).start()
                return carry

            if turn < sz.group - 1:
                lax.fori_loop(0, devices, post, 0)
            else:
                lax.fori_loop(1, devices, post, 0)
                if part == 1:

                    @pl.when(self.odd == 1)
                    def _():
                        post(0, 0)

        return pair, local

    def to_tokens(self, source, target, part):
        sz, links = self.sz, self.links
        pair, local = links.pair(), self.local()
        there = target.at[self.channels(links.row, links.col, part)]

        def send():
            mine = source.at[part, self.block(self.token)]
            pltpu.make_async_copy(mine, there, local).start()
            devices = sz.peers * sz.hid
            first = links.plane * sz.hid + links.col

            for turn, line in enumerate(self.far_first()):

                def post(step, carry):
                    index = lax.rem(first + step, devices)
                    row, col = line * sz.peers + index // sz.hid, lax.rem(index, sz.hid)
                    piece = source.at[part, self.block(row * sz.hid + col)]
                    links.copy(piece, there, pair, row, col).start()
                    return carry

                lax.fori_loop(0 if turn < sz.group - 1 else 1, devices, post, 0)

        self.owners(part, send)
        return pair, local

    def wait(self, tokens, part, flat, sent_to_owners):
        sz, links = self.sz, self.links
        pair, local = tokens
        rows = lambda count: flat.at[pl.ds(0, count * 16)]
        all_devices = sz.count - 1

        def owner_side():
            pltpu.make_async_copy(rows(1), rows(1), local).wait()
            copy = links.copy(rows(all_devices), rows(all_devices), pair, links.row, 1 - links.col)
            if sent_to_owners:
                copy.wait_recv()
            else:
                copy.wait_send()

        def token_side(count):
            copy = links.copy(rows(count), rows(count), pair, links.row, 1 - links.col)
            if sent_to_owners:
                copy.wait_send()
            else:
                copy.wait_recv()

        self.owners(part, owner_side)
        if part == 0:
            token_side(all_devices)
        else:
            pl.when(self.odd == 0)(lambda: token_side(sz.count // 2 - 1))
            pl.when(self.odd == 1)(lambda: token_side(sz.count // 2))

    def owners_wait(self, tokens, part, target):
        self.wait(tokens[part], part, target.at[0], True)

    def tokens_wait(self, tokens, source):
        for part in range(2):
            self.wait(tokens[part], part, source.at[0], False)


CHUNK = 8


def place(index, size):
    return pl.ds(pl.multiple_of(index * size, size), size)


def dft(sz, b, source, base, stride, target, first=0, chunks=4, unroll=2):
    steps, outer = sz.steps, sz.outer

    def chunk(index, carry):
        cos = b.twist[:, :LANES]
        sin = b.twist[:, LANES:]
        for line in range(CHUNK):
            start = base + (index - first) * CHUNK + line
            b.wide[:, line * LANES : (line + 1) * LANES] = source[
                pl.ds(start, steps, stride=stride), :
            ].astype(BF16)
        b.mid[...] = nn(b.outer_fwd[...], b.wide[...])
        for line in range(CHUNK):
            lanes = slice(line * LANES, (line + 1) * LANES)
            real = b.mid[0:outer, lanes]
            imag = b.mid[outer : 2 * outer, lanes]
            rows = slice(line * outer, (line + 1) * outer)
            b.turned[rows, 0:LANES] = (real * cos + imag * sin).astype(BF16)
            b.turned[rows, LANES:] = (imag * cos - real * sin).astype(BF16)
        target[place(index, CHUNK * outer), :] = nn(b.turned[...], b.inner_fwd[...])
        return carry

    lax.fori_loop(first, first + chunks, chunk, 0, unroll=unroll)


def inverse_dft(sz, b, target, base, stride, first=0, chunks=4, unroll=2):
    steps, outer = sz.steps, sz.outer

    def chunk(index, carry):
        cos = b.twist[:, :LANES]
        sin = b.twist[:, LANES:]
        part = nn(b.flat[place(index, CHUNK * outer), :], b.inner_inv[...])
        for line in range(CHUNK):
            rows = slice(line * outer, (line + 1) * outer)
            lanes = slice(line * LANES, (line + 1) * LANES)
            real = part[rows, :LANES]
            imag = part[rows, LANES:]
            b.mid_half[0:outer, lanes] = (real * cos - imag * sin).astype(BF16)
            b.mid_half[outer : 2 * outer, lanes] = (imag * cos + real * sin).astype(BF16)
        value = nn(b.outer_inv[...], b.mid_half[...])
        for line in range(CHUNK):
            start = base + (index - first) * CHUNK + line
            target[pl.ds(start, steps, stride=stride), :] = value[
                :, line * LANES : (line + 1) * LANES
            ]
        return carry

    lax.fori_loop(first, first + chunks, chunk, 0, unroll=unroll)


def first_channel(sz):
    row = lax.axis_index("rows")
    return (row // 2) * sz.couple + lax.rem(row, 2) * sz.big


def own_taps(sz, filters):
    start = first_channel(sz)
    chan = lax.broadcasted_iota(jnp.int32, (sz.big, sz.half), 0)
    lane = lax.broadcasted_iota(jnp.int32, (sz.big, sz.half), 1)
    pick = jnp.where(lane == start + chan, 1.0, 0.0).astype(BF16)
    parts = [nt(pick, filters[way].astype(BF16)) for way in range(2)]
    return jnp.concatenate(parts, axis=0).astype(BF16)


def own_envelope(sz, env):
    first_chan = lax.axis_index("hid") * sz.half + first_channel(sz)
    channel = first_chan + lax.broadcasted_iota(jnp.int32, (sz.big, LANES), 0)
    fraction = lax.rem(channel * 37, sz.width).astype(F32) / (sz.width - 1)
    start_log = math.log(1.0 / 40.0)
    rate = jnp.exp(start_log + (math.log(1.5 / sz.length) - start_log) * fraction)
    lane = lax.broadcasted_iota(jnp.int32, (sz.big, LANES), 1)

    def decays(step, power):
        decay = jnp.exp(-(lane + step * LANES).astype(F32) * rate)
        env[0 : sz.big, place(step, LANES)] = decay
        return power + decay * decay

    power = lax.fori_loop(0, sz.steps, decays, jnp.zeros((sz.big, LANES), F32), unroll=4)
    scale = lax.rsqrt(2.0 * jnp.sum(power, axis=1, keepdims=True))

    def scaled(step, carry):
        value = env[0 : sz.big, place(step, LANES)] * scale
        env[0 : sz.big, place(step, LANES)] = value
        env[sz.big :, place(step, LANES)] = jnp.where(lane + step * LANES > 0, value, 0.0)
        return carry

    lax.fori_loop(0, sz.steps, scaled, 0, unroll=4)


def filter_spectrum(sz, b, layer):
    piece, steps, outer = sz.big, sz.steps, sz.outer
    taps = own_taps(sz, b.filters[layer])
    count = 4

    def chunk(index, carry):
        lanes = place(index, count * LANES)
        kernels = nn(taps, b.pos[:, lanes]) * b.env[:, lanes]
        rows = pl.multiple_of(index * count * 2 * piece, 2 * piece)
        for step in range(count):
            b.tall[pl.ds(rows + step * 2 * piece, 2 * piece), :] = kernels[
                :, step * LANES : (step + 1) * LANES
            ]
        return carry

    lax.fori_loop(0, steps // count, chunk, 0, unroll=2)
    spec = b.filt_spec[layer]
    span = sz.big * outer
    for way in range(2):
        dft(sz, b, b.tall, way * piece, 2 * piece, b.spec, unroll=1)
        if way == 0:
            spec[...] = b.spec[0:span, :].astype(BF16)
        else:
            spec[:, :LANES] = (spec[:, :LANES].astype(F32) + b.spec[0:span, :LANES]).astype(BF16)
            spec[:, LANES:] = (spec[:, LANES:].astype(F32) - b.spec[0:span, LANES:]).astype(BF16)


def convolve(sz, b, layer, landed, part, back):
    count = 16 // CHUNK
    b.tall[0 : sz.count * 16, :] = landed[part].astype(F32)
    dft(sz, b, b.tall, 0, 16, b.spec, part * count, count, True)
    filt = b.filt_spec[layer]
    rows = slice(part * 16 * sz.outer, (part + 1) * 16 * sz.outer)
    re, im = b.spec[rows, :LANES], b.spec[rows, LANES:]
    fil_re, fil_im = filt[rows, :LANES].astype(F32), filt[rows, LANES:].astype(F32)
    if back:
        b.flat[rows, :LANES] = (re * fil_re + im * fil_im).astype(BF16)
        b.flat[rows, LANES:] = (im * fil_re - re * fil_im).astype(BF16)
    else:
        b.sig_spec[layer][rows, :LANES] = re.astype(BF16)
        b.sig_spec[layer][rows, LANES:] = im.astype(BF16)
        b.flat[rows, :LANES] = (re * fil_re - im * fil_im).astype(BF16)
        b.flat[rows, LANES:] = (re * fil_im + im * fil_re).astype(BF16)
    inverse_dft(sz, b, b.tall, 0, 16, part * count, count, True)
    b.staged[part] = b.tall[0 : sz.count * 16, :].astype(BF16)


def conv_forward(sz, b, layer, landed, part):
    convolve(sz, b, layer, landed, part, False)


def conv_backward(sz, b, layer, landed, part):
    convolve(sz, b, layer, landed, part, True)


def taps_gradient(sz, b, layer, landed, signal):
    span = sz.big * sz.outer
    total_re = jnp.zeros((span, LANES), F32)
    total_im = jnp.zeros((span, LANES), F32)
    for seq in range(sz.seqs):
        rows = slice(seq * span, (seq + 1) * span)
        re, im = b.spec[rows, :LANES], b.spec[rows, LANES:]
        sig = b.sig_spec[layer]
        sig_re, sig_im = sig[rows, :LANES].astype(F32), sig[rows, LANES:].astype(F32)
        total_re += re * sig_re + im * sig_im
        total_im += im * sig_re - re * sig_im
    piece = sz.big
    b.tall[...] = jnp.zeros_like(b.tall)
    for way in range(2):
        b.flat[0:span, :LANES] = total_re.astype(BF16)
        b.flat[0:span, LANES:] = (total_im if way == 0 else -total_im).astype(BF16)
        inverse_dft(sz, b, b.tall, way * piece, 2 * piece, unroll=True)
    taps = own_taps(sz, b.filters[layer])
    count = 4

    def chunk(index, total):
        lanes = place(index, count * LANES)
        rows = pl.multiple_of(index * count * 2 * piece, 2 * piece)
        raw = nn(taps, b.pos[:, lanes])
        grads = jnp.concatenate(
            [b.tall[pl.ds(rows + step * 2 * piece, 2 * piece), :] for step in range(count)],
            axis=1,
        )
        grads = grads * b.env[:, lanes] + (2.0 * DECAY) * raw
        return total + nt(grads.astype(BF16), b.pos[:, lanes])

    start = jnp.zeros((2 * piece, ORDER), F32)
    total = lax.fori_loop(0, sz.steps // count, chunk, start, unroll=2)

    columns = []
    for part in range(2):

        def product(block, products):
            rows = place(block, 16)
            here = landed[part, rows, :].astype(F32)
            return products + here * signal[part, rows, :].astype(F32)

        start = jnp.zeros((16, LANES), F32)
        products = lax.fori_loop(0, sz.count, product, start, unroll=4)
        columns.append(jnp.sum(products, axis=1, keepdims=True))
    column = jnp.concatenate(columns, axis=0)
    row = jnp.transpose(jnp.broadcast_to(column, (piece, LANES)))[0:8, :]
    b.taps_work[...] = jnp.zeros_like(b.taps_work)
    b.taps_work[0 : sz.big, :] = total[0 : sz.big, :]
    b.taps_work[sz.big : 2 * sz.big, :] = total[piece : piece + sz.big, :]
    b.taps_work[2 * sz.big : 2 * sz.big + 1, 0:piece] = row[0:1, :]


def block_of(sz, block):
    return slice(block * sz.size, (block + 1) * sz.size)


def project(sz, b, layer):
    for block in range(sz.blocks):
        rows = block_of(sz, block)
        part = b.normed[layer][:, rows]
        b.inner[layer][rows, :] = nt(b.mixer[layer, 0, block], part).astype(BF16)
        b.gate[layer][rows, :] = nt(b.mixer[layer, 1, block], part)


def mix(sz, b, layer, conv):
    summed, mixed, middle = b.summed[layer], b.mixed[layer], b.middle[layer]
    summed[...] = conv[...].astype(F32) + b.skip[layer][...] * b.inner[layer][...].astype(F32)
    mixed[...] = (b.gate[layer][...] * summed[...]).astype(BF16)
    for block in range(sz.blocks):
        rows = block_of(sz, block)
        middle[:, rows] = tn(mixed[rows, :], b.mixer[layer, 2, block])
    middle[...] = middle[...] + b.stream[layer][...]


def gain_gradient(sz, b, row, value, mine, give):
    low = lax.axis_index("hid") == 0
    left, right = value[:, : sz.half], value[:, sz.half :]
    mine[row : row + 1, :] = jnp.where(low, left, right)
    give[row : row + 1, :] = jnp.where(low, right, left)


def mixer_backward(sz, b, layer, grad_next, total):
    normal, inv = normalize(b.middle[layer][...])
    gain = b.gain[layer, 1:2, :]
    back, gain_grad = norm_back(total, normal, inv, gain)
    result = grad_next + back
    b.grad_middle[...] = result
    b.grad_o[...] = result.astype(BF16)
    for block in range(sz.blocks):
        rows = block_of(sz, block)
        grad_mixed = nt(b.mixer[layer, 2, block], b.grad_o[:, rows])
        b.gate_grad[rows, :] = (grad_mixed * b.summed[layer][rows, :]).astype(BF16)
        through = grad_mixed * b.gate[layer][rows, :]
        b.summed_grad[rows, :] = through
        b.conv_grad[rows, :] = through.astype(BF16)
    return gain_grad


def out_gradient(sz, b, layer):
    return [
        nn(b.mixed[layer][block_of(sz, block), :], b.grad_o[:, block_of(sz, block)])
        for block in range(sz.blocks)
    ]


def in_gradient(sz, b, layer, grads):
    return [
        jnp.transpose(
            nn(grads[block_of(sz, block), :], b.normed[layer][:, block_of(sz, block)])
        )
        for block in range(sz.blocks)
    ]


def input_backward(sz, b, layer, back):
    direct = b.skip[layer][...] * b.summed_grad[...]
    b.inner_grad[...] = (direct + back[...].astype(F32)).astype(BF16)
    for block in range(sz.blocks):
        rows = block_of(sz, block)
        b.grad_sum[0 : sz.own, rows] = tn(b.inner_grad[rows, :], b.mixer[layer, 0, block]) + tn(
            b.gate_grad[rows, :], b.mixer[layer, 1, block]
        )
    normal, inv = normalize(b.stream[layer][...])
    result, gain_grad = norm_back(
        b.grad_sum[0 : sz.own, :], normal, inv, b.gain[layer, 0:1, :]
    )
    return b.grad_middle[...] + result, gain_grad


def ff_forward(sz, b, layer):
    tile = 512
    rows = slice(0, 2 * sz.own)
    b.out_sum[...] = jnp.zeros_like(b.out_sum)

    def body(step, carry):
        lanes = pl.ds(pl.multiple_of(step * tile, tile), tile)
        normed = b.nbuf[layer][rows, :]
        gate = nn(normed, b.up[layer, 0, :, lanes])
        up = nn(normed, b.up[layer, 1, :, lanes])
        value, _ = gelu_parts(gate)
        b.out_sum[...] += nt((value * up).astype(BF16), b.down[layer, :, lanes])
        return carry

    lax.fori_loop(0, sz.units // tile, body, 0)


def ff_backward(sz, b, layer, with_out):
    tile = 512
    rows = slice(0, 2 * sz.own)
    b.grad_sum[...] = jnp.zeros_like(b.grad_sum)
    if with_out:
        b.out_sum[...] = jnp.zeros_like(b.out_sum)

    def body(step, carry):
        lanes = pl.ds(pl.multiple_of(step * tile, tile), tile)
        normed = b.nbuf[layer][rows, :]
        gate = nn(normed, b.up[layer, 0, :, lanes])
        up = nn(normed, b.up[layer, 1, :, lanes])
        through = nn(b.gbuf[layer][rows, :], b.down[layer, :, lanes])
        value, slope = gelu_parts(gate)
        if with_out:
            b.out_sum[...] += nt((value * up).astype(BF16), b.down[layer, :, lanes])
        gate_grad = (slope * up * through).astype(BF16)
        up_grad = (value * through).astype(BF16)
        b.grad_sum[...] += nt(gate_grad, b.up[layer, 0, :, lanes]) + nt(
            up_grad, b.up[layer, 1, :, lanes]
        )
        return carry

    lax.fori_loop(0, sz.units // tile, body, 0)


def ff_gradients(sz, b, layer, links, between=(None, None, None)):
    start = pl.multiple_of(links.line * sz.part, LANES)
    units = pl.ds(start, sz.part)
    chunk = 2 * sz.own

    def body(step, carry):
        rows = pl.ds(pl.multiple_of(step * chunk, chunk), chunk)
        normed = b.nbuf[layer][rows, :]
        gate = nn(normed, b.up[layer, 0, :, units])
        up = nn(normed, b.up[layer, 1, :, units])
        through = nn(b.gbuf[layer][rows, :], b.down[layer, :, units])
        value, slope = gelu_parts(gate)
        b.unit_grad[0, rows, :] = (slope * up * through).astype(BF16)
        b.unit_grad[1, rows, :] = (value * through).astype(BF16)
        b.unit_grad[2, rows, :] = (value * up).astype(BF16)
        return carry

    lax.fori_loop(0, sz.group, body, 0)
    split = sz.width // 2
    moving = []
    for kind in range(3):
        if between[kind] is not None:
            between[kind]()
        left = b.gbuf[layer] if kind == 2 else b.nbuf[layer]

        def part(index, carry):
            lanes = place(index, split)
            b.product[...] = tn(left[:, lanes], b.unit_grad[kind])
            count = split // sz.depth
            for each in range(count):
                line = index * (count // sz.peers) + each // sz.peers
                rows = slice(each * sz.depth, (each + 1) * sz.depth)
                b.pieces[kind, each % sz.peers, line, 0 : sz.depth, :] = b.product[rows, :].astype(
                    BF16
                )
            return carry

        lax.fori_loop(0, 2, part, 0)
        half = lambda which: pl.ds(which * (sz.group // 2), sz.group // 2)
        plane = PlaneSum(
            links,
            lambda member, which, kind=kind: b.pieces.at[kind, member, half(which)],
            b.plane_first[layer].at[kind],
            b.plane_give[layer].at[kind],
            b.plane_second[layer].at[kind],
        )
        plane.start()
        moving.append(plane)
    return moving


def done(copy):
    copy.wait()


class Named:
    pass


def layout(sz):
    layers, own, width = sz.layers, sz.own, sz.width
    wide = 2 * sz.big * sz.steps
    per_layer = dict(
        stream=((own, width), F32),
        normed=((own, width), BF16),
        inner=((width, own), BF16),
        gate=((width, own), F32),
        summed=((width, own), F32),
        mixed=((width, own), BF16),
        middle=((own, width), F32),
        nbuf=((2 * sz.group * own, width), BF16),
        gbuf=((2 * sz.group * own, width), BF16),
        skip=((width, LANES), F32),
        filt_spec=((sz.big * sz.outer, 2 * LANES), BF16),
        sig_spec=((sz.pairs * sz.outer, 2 * LANES), BF16),
        fore_in=((2, sz.count * 16, LANES), BF16),
        fore_out=((width, own), BF16),
        back_in=((2, sz.count * 16, LANES), BF16),
        back_out=((width, own), BF16),
        plane_first=((3, 2, 2, sz.group // 2, sz.deep, sz.part), BF16),
        plane_give=((3, 2, sz.group // 2, sz.deep, sz.part), BF16),
        plane_second=((3, 2, sz.group // 2, sz.deep, sz.part), BF16),
        grad_got=((own, width), BF16),
        out_got=((own, width), BF16),
    )
    single = dict(
        x=((own, width), BF16),
        gain=((layers, 2, width), F32),
        skip_rows=((layers, width), F32),
        mixer=((layers, 3, sz.blocks, sz.size, sz.size), BF16),
        filters=((layers, 2, ORDER, sz.half), F32),
        pos=((ORDER, sz.length), BF16),
        outer_fwd=((2 * sz.outer, sz.steps), BF16),
        outer_inv=((sz.steps, 2 * sz.outer), BF16),
        inner_fwd=((2 * LANES, 2 * LANES), BF16),
        inner_inv=((2 * LANES, 2 * LANES), BF16),
        twist=((sz.outer, 2 * LANES), F32),
        up=((layers, 2, width, sz.units), BF16),
        down=((layers, width, sz.units), BF16),
        env=((2 * sz.big, sz.length), F32),
        tall=((max(wide, sz.count * sz.big) + 2 * sz.big, LANES), F32),
        wide=((sz.steps, CHUNK * LANES), BF16),
        turned=((CHUNK * sz.outer, 2 * LANES), BF16),
        mid=((2 * sz.outer, CHUNK * LANES), F32),
        flat=((sz.pairs * sz.outer, 2 * LANES), BF16),
        mid_half=((2 * sz.outer, CHUNK * LANES), BF16),
        spec=((sz.pairs * sz.outer, 2 * LANES), F32),
        conv_grad=((width, own), BF16),
        staged=((2, sz.count * 16, LANES), BF16),
        grad_middle=((own, width), F32),
        grad_o=((own, width), BF16),
        gate_grad=((width, own), BF16),
        summed_grad=((width, own), F32),
        inner_grad=((width, own), BF16),
        out_sum=((2 * own, width), F32),
        grad_sum=((2 * own, width), F32),
        out_give=((own, width), BF16),
        sum_give=((own, width), BF16),
        unit_grad=((3, 2 * sz.group * own, sz.part), BF16),
        product=((width // 2, sz.part), F32),
        pieces=((3, sz.peers, sz.group, sz.deep, sz.part), BF16),
        taps_work=((sz.taps_rows, ORDER), F32),
        gain_mine=((16, sz.half), F32),
        gain_give=((16, sz.half), F32),
        late_parts=((sz.peers, sz.group, sz.deeps[1], sz.half), BF16),
        late_gain_mine=((16, sz.half), F32),
        late_gain_give=((16, sz.half), F32),
        out_keep=((2, own, sz.half), BF16),
        taps_line=((layers, sz.group, sz.taps_rows, ORDER), BF16),
    )
    names, specs = [], []
    for name, (shape, kind) in per_layer.items():
        for layer in range(layers):
            names.append((name, layer))
            specs.append(pltpu.VMEM(shape, kind))
    for index, deep in enumerate(sz.deeps):
        part = (sz.group // 2, deep, sz.half)
        whole_load = (sz.peers, sz.group, deep, sz.half)
        line = (sz.group, deep, sz.half)
        shapes = (whole_load,) * 3 + ((2, 2) + part, (2,) + part, (2,) + part, line, line[1:])
        for name, shape in zip(LOAD_BUFFERS, shapes):
            names.append(("load_" + name, index))
            specs.append(pltpu.VMEM(shape, BF16))
    for name, (shape, kind) in single.items():
        names.append((name, None))
        specs.append(pltpu.VMEM(shape, kind))
    return names, specs


TABLES = ("pos", "outer_fwd", "outer_inv", "inner_fwd", "inner_inv", "twist")
INPUTS = ("hidden_in", "d_out", "gains", "mixer", "skip", "filters", "gate_up", "down") + TABLES
OUTPUTS = ("hidden_out", "grad_in", "early", "late", "taps", "units")


def program_kernel(sz, *refs):
    names, _ = layout(sz)
    inputs = dict(zip(INPUTS, refs))
    outputs = dict(zip(OUTPUTS, refs[len(INPUTS) :]))
    scratch = refs[len(INPUTS) + len(OUTPUTS) :]
    b = Named()
    for (name, layer), ref in zip(names, scratch):
        if layer is None:
            setattr(b, name, ref)
        else:
            setattr(b, name, getattr(b, name, ()) + (ref,))
    links = Links(sz, scratch[len(names)], scratch[len(names) + 1])
    own = sz.own
    top = sz.layers - 1
    col = links.col
    low = col == 0
    mine_rows = pl.ds(pl.multiple_of(col * own, own), own)
    other_rows = pl.ds(pl.multiple_of((1 - col) * own, own), own)

    barrier = greet_all(sz)
    lanes = pl.ds(pl.multiple_of(col * sz.half, sz.half), sz.half)
    sides = pl.ds(col * sz.side_blocks, sz.side_blocks)
    slots = lambda first, count: pl.ds(first * own, count * own)
    near_slots, line_slots, far_slots = slots(0, 2), slots(2, 3), slots(5, 3)
    halves = {
        "x": (inputs["hidden_in"].at[mine_rows], b.x.at[:, lanes]),
        "gains": (inputs["gains"], b.gain.at[:, :, lanes]),
        "mixer": (inputs["mixer"].at[0, pl.ds(0, 2)], b.mixer.at[0, pl.ds(0, 2), sides]),
        "skip": (inputs["skip"], b.skip_rows.at[:, lanes]),
        "out_mixer": (inputs["mixer"].at[0, pl.ds(2, 1)], b.mixer.at[0, pl.ds(2, 1), sides]),
    }
    if sz.layers > 1:
        above = pl.ds(1, sz.layers - 1)
        halves["mixers"] = (inputs["mixer"].at[above], b.mixer.at[above, :, sides])
    loads = {name: links.load(*pair) for name, pair in halves.items()}
    for name in ("filters",) + TABLES:
        loads[name] = links.load(inputs[name], getattr(b, name))
    grads = b.gbuf[top]
    loads["g"] = links.load(inputs["d_out"].at[mine_rows], grads.at[slots(0, 1), lanes])
    loads["g_near"] = links.load(inputs["d_out"].at[other_rows], grads.at[slots(1, 1), lanes])
    b.gain_mine[...] = jnp.zeros_like(b.gain_mine)
    b.gain_give[...] = jnp.zeros_like(b.gain_give)
    b.late_gain_mine[...] = jnp.zeros_like(b.late_gain_mine)
    b.late_gain_give[...] = jnp.zeros_like(b.late_gain_give)
    pl.semaphore_wait(barrier, sz.count - 1)
    got = {}
    for name, (source, target) in halves.items():
        if name == "x":
            source = inputs["hidden_in"].at[other_rows]
        got[name] = links.sibling(source, target)
    got["g"] = links.sibling(inputs["d_out"].at[other_rows], grads.at[slots(0, 1), lanes])
    got["g_near"] = links.sibling(inputs["d_out"].at[mine_rows], grads.at[slots(1, 1), lanes])

    def both(*wanted):
        for name in wanted:
            done(loads[name])
            done(got[name])

    def turn_mixer(layer, kind):
        for block in range(sz.blocks):
            b.mixer[layer, kind, block] = jnp.transpose(b.mixer[layer, kind, block])

    def norm_to(source, target, layer, which):
        normal, _ = normalize(source)
        target[...] = (normal * b.gain[layer, which : which + 1, :]).astype(BF16)

    def slot_of(place, member):
        return 2 + (member if member < place else member - 1)

    class Gather:
        moves = (
            {0: [(0, 1)], 1: [(1, 0), (1, 2)], 2: [(2, 1), (2, 3)], 3: [(3, 2)]},
            {1: [(2, 0), (0, 2)], 2: [(3, 1), (1, 3)]},
            {1: [(3, 0)], 2: [(0, 3)]},
        )
        coming = ((1, 2, 2, 1), (1, 1, 1, 1), (1, 0, 0, 1))

        def __init__(self, buffer):
            self.buffer = buffer
            self.pairs = [None] * 3

        def near(self):
            return links.sibling(self.buffer.at[slots(0, 1)], self.buffer.at[slots(1, 1)])

        def views(self, place, whose, target):
            here = 0 if whose == place else slot_of(place, whose)
            there = slot_of(target, whose)
            return [(self.buffer.at[slots(here, 1)], self.buffer.at[slots(there, 1)])]

        def span(self, count):
            return self.buffer.at[slots(0, count)]

        def step(self, index):
            if index > 0:
                self.wait(index - 1)
            pair = links.pair()
            for place, moves in self.moves[index].items():

                @pl.when(links.line == place)
                def _():
                    for whose, target in moves:
                        for source, there in self.views(place, whose, target):
                            row = target * sz.peers + links.plane
                            links.copy(source, there, pair, row, col).start()

            self.pairs[index] = pair

        def wait(self, index):
            pair = self.pairs[index]
            if True:
                for place in range(sz.group):
                    came = self.coming[index][place]
                    sent = len(self.moves[index].get(place, ()))

                    @pl.when(links.line == place)
                    def _():
                        if came:
                            span = self.span(came)
                            links.copy(span, span, pair, links.row, 1 - col).wait_recv()
                        if sent:
                            span = self.span(sent)
                            links.copy(span, span, pair, links.row, 1 - col).wait_send()

        def rest(self):
            self.wait(2)
            self.copies = [links.sibling(self.buffer.at[line_slots], self.buffer.at[far_slots])]

        def finish(self):
            for copy in self.copies:
                done(copy)

    class ArgumentGather(Gather):
        def views(self, place, whose, target):
            there = slot_of(target, whose)
            pairs = []
            for rows, shift in ((mine_rows, 0), (other_rows, 3)):
                if whose == place:
                    source = inputs["d_out"].at[rows]
                else:
                    source = self.buffer.at[slots(slot_of(place, whose) + shift, 1), lanes]
                pairs.append((source, self.buffer.at[slots(there + shift, 1), lanes]))
            return pairs

        def span(self, count):
            return self.buffer.at[slots(0, 2 * count), lanes]

        def rest(self):
            self.wait(2)
            self.copies = [
                links.sibling(self.buffer.at[line_slots, lanes], self.buffer.at[far_slots, lanes]),
                links.sibling(self.buffer.at[far_slots, lanes], self.buffer.at[line_slots, lanes]),
            ]

    top_grads = ArgumentGather(grads)
    top_grads.step(0)
    both("x", "gains")
    b.stream[0][...] = b.x[...].astype(F32)
    norm_to(b.stream[0][...], b.normed[0], 0, 0)
    both("mixer")
    turn_mixer(0, 0)
    turn_mixer(0, 1)

    exchange = Exchange(sz, links)
    project(sz, b, 0)
    normed_parts = []
    for layer in range(sz.layers):
        moving = exchange.to_owners(b.inner[layer], b.fore_in[layer])
        if layer == 0:
            for each in range(sz.layers):
                loads["up", each] = links.load(inputs["gate_up"].at[each], b.up.at[each])
                loads["down", each] = links.load(inputs["down"].at[each], b.down.at[each])
            for name in ("filters", "pos", "outer_fwd", "inner_fwd", "twist"):
                done(loads[name])
            own_envelope(sz, b.env)
            filter_spectrum(sz, b, 0)
            for name in ("outer_inv", "inner_inv"):
                done(loads[name])
            both("skip", "g", "g_near")
            for each in range(sz.layers):
                row = b.skip_rows[each : each + 1, :]
                b.skip[each][...] = jnp.transpose(jnp.broadcast_to(row, (LANES, sz.width)))
        returning = []
        for part in range(2):
            exchange.owners_wait(moving, part, b.fore_in[layer])
            conv_forward(sz, b, layer, b.fore_in[layer], part)
            returning.append(exchange.to_tokens(b.staged, b.fore_out[layer], part))
        if layer == 0:
            top_grads.step(1)
        else:
            top_grads.rest()
        if layer == 0:
            both("out_mixer")
            if sz.layers > 1:
                both("mixers")
            for each in range(1, sz.layers):
                turn_mixer(each, 0)
                turn_mixer(each, 1)
        if layer < top:
            filter_spectrum(sz, b, layer + 1)
        done(loads["up", layer])
        done(loads["down", layer])
        if layer == 0:
            top_grads.step(2)
        exchange.tokens_wait(returning, b.staged)
        mix(sz, b, layer, b.fore_out[layer])
        norm_to(b.middle[layer][...], b.nbuf[layer].at[slots(0, 1)], layer, 1)
        normed_parts.append(Gather(b.nbuf[layer]))
        near = normed_parts[layer].near()
        if layer == top:
            normed_parts[layer].step(0)
        done(near)
        if layer < top:
            ff_forward(sz, b, layer)
            b.out_give[...] = b.out_sum[own:, :].astype(BF16)
            moving = links.sibling(b.out_give, b.out_got[layer])
            done(moving)
            value = b.middle[layer][...] + b.out_sum[0:own, :] + b.out_got[layer][...].astype(F32)
            b.stream[layer + 1][...] = value
            norm_to(value, b.normed[layer + 1], layer + 1, 0)
            project(sz, b, layer + 1)

    ff_backward(sz, b, top, True)
    b.sum_give[...] = b.grad_sum[own:, :].astype(BF16)
    moving = links.sibling(b.sum_give, b.grad_got[top])
    b.out_give[...] = b.out_sum[own:, :].astype(BF16)
    out_moving = links.sibling(b.out_give, b.out_got[top])
    normed_parts[top].step(1)
    done(moving)
    total = b.grad_sum[0:own, :] + b.grad_got[top][...].astype(F32)
    grad_next = b.gbuf[top][0:own, :].astype(F32)
    gain_grad = mixer_backward(sz, b, top, grad_next, total)
    moving = exchange.to_owners(b.conv_grad, b.back_in[top])
    gain_gradient(sz, b, 2 * top, gain_grad, b.gain_mine, b.gain_give)
    early = Payload(sz, b, links, 0, outputs["early"])
    late = Payload(sz, b, links, 1, outputs["late"])
    early.matrix(0, out_gradient(sz, b, top))
    done(out_moving)
    value = b.middle[top][...] + b.out_sum[0:own, :] + b.out_got[top][...].astype(F32)
    value = value.astype(BF16)
    left, right = value[:, : sz.half], value[:, sz.half :]
    b.out_keep[0] = jnp.where(low, left, right)
    b.out_keep[1] = jnp.where(low, right, left)
    place = outputs["hidden_out"].at[mine_rows]
    ending = [links.load(b.out_keep.at[0], place), links.sibling(b.out_keep.at[1], place)]
    top_grads.finish()
    normed_parts[top].step(2)

    plane_moving = {}
    taps_moving = {}
    units_moving = []

    def taps_to_line(layer):
        taps_gradient(sz, b, layer, b.back_in[layer], b.fore_in[layer])
        place = b.taps_line.at[layer, links.line]
        b.taps_line[layer, links.line] = b.taps_work[...].astype(BF16)
        taps_moving[layer] = links.in_line(lambda member: place, place)

    def taps_to_plane(layer):
        links.wait(taps_moving[layer], b.taps_line.at[layer, pl.ds(0, sz.group - 1)])
        place = outputs["taps"].at[layer, links.plane]
        ending.append(links.load(b.taps_line.at[layer], place))
        taps_moving[layer] = links.in_plane(lambda member: b.taps_line.at[layer], place)

    def units_middle(layer, kinds=(0, 1, 2)):
        for kind in kinds:
            plane_moving[layer][kind].middle()

    def units_end(layer, kinds=(0, 1, 2)):
        for kind in kinds:
            plane = plane_moving[layer][kind]
            plane.end()
            part = plane.sums()
            target = outputs["units"].at[layer, kind, links.line]
            ending.append(links.load(part(links.line), target))
            pair = links.in_line(part, target)
            units_moving.append((layer, kind, pair))

    def convolve_back(layer):
        returning = []
        for part in range(2):
            exchange.owners_wait(moving, part, b.back_in[layer])
            conv_backward(sz, b, layer, b.back_in[layer], part)
            returning.append(exchange.to_tokens(b.staged, b.back_out[layer], part))
        return returning

    moving = convolve_back(top)
    normed_parts[top].rest()
    normed_parts[0].step(0)
    normed_parts[top].finish()
    plane_moving[top] = ff_gradients(sz, b, top, links)
    exchange.tokens_wait(moving, b.staged)
    value, gain_grad = input_backward(sz, b, top, b.back_out[top])
    b.out_sum[0:own, :] = value
    b.gbuf[0][0:own, :] = value.astype(BF16)
    gather = Gather(b.gbuf[0])
    near = gather.near()
    gather.step(0)
    normed_parts[0].step(1)
    gain_gradient(sz, b, 2 * top - 1, gain_grad, b.gain_mine, b.gain_give)
    early.matrix(1, in_gradient(sz, b, top, b.inner_grad))
    early.matrix(2, in_gradient(sz, b, top, b.gate_grad))
    done(near)
    ff_backward(sz, b, 0, False)
    b.sum_give[...] = b.grad_sum[own:, :].astype(BF16)
    moving = links.sibling(b.sum_give, b.grad_got[0])
    gather.step(1)
    normed_parts[0].step(2)
    done(moving)
    total = b.grad_sum[0:own, :] + b.grad_got[0][...].astype(F32)
    gain_grad = mixer_backward(sz, b, 0, b.out_sum[0:own, :], total)

    moving = exchange.to_owners(b.conv_grad, b.back_in[0])
    units_middle(top)
    gain_gradient(sz, b, 0, gain_grad, b.gain_mine, b.gain_give)
    early.matrix(3, out_gradient(sz, b, 0))
    early.matrix(4, in_gradient(sz, b, 0, b.gate_grad))
    early.rows16(5, b.gain_mine[...], b.gain_give[...])
    early.to_partner()
    taps_to_line(top)
    gather.step(2)
    early.to_plane()
    moving = convolve_back(0)
    units_end(top)
    normed_parts[0].rest()
    gather.rest()
    taps_to_plane(top)
    normed_parts[0].finish()
    gather.finish()
    between = (early.middle, None, None)
    plane_moving[0] = ff_gradients(sz, b, 0, links, between)
    exchange.tokens_wait(moving, b.staged)
    value, gain_grad = input_backward(sz, b, 0, b.back_out[0])

    left, right = value[:, : sz.half], value[:, sz.half :]
    keep, give = b.out_sum.at[0:own, 0 : sz.half], b.out_sum.at[own:, 0 : sz.half]
    keep[...] = jnp.where(low, left, right)
    give[...] = jnp.where(low, right, left)
    late.matrix(0, in_gradient(sz, b, 0, b.inner_grad))
    gain_gradient(sz, b, 0, gain_grad, b.late_gain_mine, b.late_gain_give)
    late.rows16(1, b.late_gain_mine[...], b.late_gain_give[...])
    late.to_partner()
    place = outputs["grad_in"].at[mine_rows]
    ending += [links.load(keep, place), links.sibling(give, place)]

    early.to_line()
    late.to_plane()
    units_middle(0, (0,))
    early.back_line()
    taps_to_line(0)
    late.to_line()
    units_middle(0, (1,))
    early.back_plane()
    units_middle(0, (2,))
    late.back_line()
    units_end(0, (0,))
    early.spread.middle()
    late.back_plane()
    units_end(0, (1, 2))
    taps_to_plane(0)
    ending += [early.finish(), late.finish()]
    for layer, kind, pair in units_moving:
        links.wait(pair, outputs["units"].at[layer, kind, pl.ds(0, sz.group - 1)])
    for layer, pair in taps_moving.items():
        links.wait(pair, outputs["taps"].at[layer, pl.ds(0, sz.peers - 1)])
    for copy in ending:
        done(copy)


def results_kernel(sz, *refs):
    raw, outs, scratch = refs[:6], refs[6:14], refs[14:]
    targets, held = scratch[:6], scratch[6:14]
    hidden_out, grad_in, gain_out, mixer_out, skip_out, taps_out, pair_out, down_out = held
    early, late, taps, units = targets[2:]
    channels, sems = scratch[14:]
    targets = (hidden_out, grad_in) + targets[2:]
    copies = [
        pltpu.make_async_copy(source, target, sems.at[index])
        for index, (source, target) in enumerate(zip(raw, targets))
    ]
    for copy in reversed(copies):
        copy.start()
    leaving = []

    def leave(index):
        copy = pltpu.make_async_copy(held[index], outs[index], sems.at[7 + index])
        copy.start()
        leaving.append(copy)

    layers = sz.layers
    copies[5].wait()
    for kind in range(3):
        for layer in range(layers):
            for line in range(sz.group):
                lanes = slice(line * sz.part, (line + 1) * sz.part)
                value = units[layer, kind, line].astype(F32)
                if kind < 2:
                    pair_out[layer, kind, :, lanes] = value
                else:
                    down_out[layer, :, lanes] = value
    leave(6)
    leave(7)
    copies[4].wait()
    for layer in range(layers):
        for way in range(3):
            for row in range(sz.rows):
                part = taps[layer, row % sz.peers, row // sz.peers]
                begin = (row // 2) * sz.couple + (row % 2) * sz.big
                size = sz.small if row % 2 else sz.big
                if way < 2:
                    value = part[way * sz.big : way * sz.big + size, :].astype(F32)
                else:
                    line = part[2 * sz.big : 2 * sz.big + 16, :].astype(F32)[0:1, :]
                    value = jnp.transpose(jnp.broadcast_to(line, (LANES, ORDER)))[0:size, :]
                channels[begin : begin + size, :] = value
            turned = jnp.transpose(channels[...])
            if way < 2:
                taps_out[layer, way] = turned
            else:
                skip_out[layer : layer + 1, :] = turned[0:1, :]
    leave(4)
    leave(5)
    for copy in copies[2:4]:
        copy.wait()

    def matrix(payload, place, layer, kind):
        deep = payload.shape[2]
        count = sz.size // deep
        for part in range(count):
            index = place * count + part
            rows = payload[index // sz.group, index % sz.group].astype(F32)
            for block in range(sz.side_blocks):
                mixer_out[layer, kind, block, part * deep : (part + 1) * deep, :] = rows[
                    :, block_of(sz, block)
                ]

    for place, (layer, kind) in enumerate(((1, 2), (1, 0), (1, 1), (0, 2), (0, 1))):
        matrix(early, place, layer, kind)
    matrix(late, 0, 0, 0)

    def gain_rows(payload, place):
        index = place * (sz.size // payload.shape[2])
        return payload[index // sz.group, index % sz.group].astype(F32)

    gains = gain_rows(early, 5)
    gain_out[0, 0:1, :] = gain_rows(late, 1)[0:1, :]
    for row in range(1, 2 * layers):
        gain_out[row // 2, row % 2 : row % 2 + 1, :] = gains[row - 1 : row, :]
    leave(2)
    leave(3)
    for index in range(2):
        copies[index].wait()
        leave(index)
    for copy in leaving:
        copy.wait()


def results(sz, *arrays):
    layers = sz.layers
    outs = (
        ((2 * sz.own, sz.half), BF16),
        ((2 * sz.own, sz.half), F32),
        ((layers, 2, sz.half), F32),
        ((layers, 3, sz.side_blocks, sz.size, sz.size), F32),
        ((layers, sz.half), F32),
        ((layers, 2, ORDER, sz.half), F32),
        ((layers, 2, sz.depth, sz.units), F32),
        ((layers, sz.depth, sz.units), F32),
    )
    anywhere = pl.BlockSpec(memory_space=pl.ANY)
    return pl.pallas_call(
        functools.partial(results_kernel, sz),
        out_shape=tuple(jax.ShapeDtypeStruct(shape, kind) for shape, kind in outs),
        in_specs=[anywhere] * len(arrays),
        out_specs=(anywhere,) * len(outs),
        scratch_shapes=[pltpu.VMEM(entry.shape, entry.dtype) for entry in arrays]
        + [pltpu.VMEM(shape, kind) for shape, kind in outs]
        + [pltpu.VMEM((sz.half, ORDER), F32), pltpu.SemaphoreType.DMA((15,))],
        compiler_params=pltpu.CompilerParams(vmem_limit_bytes=62 * MIB),
        name="results",
    )(*arrays)


def program(sz, arrays):
    names, scratch = layout(sz)
    outs = (
        ((2 * sz.own, sz.half), BF16),
        ((2 * sz.own, sz.half), F32),
        ((sz.peers, sz.group, sz.deeps[0], sz.half), BF16),
        ((sz.peers, sz.group, sz.deeps[1], sz.half), BF16),
        ((sz.layers, sz.peers, sz.group, sz.taps_rows, ORDER), BF16),
        ((sz.layers, 3, sz.group, sz.deep, sz.part), BF16),
    )
    return pl.pallas_call(
        functools.partial(program_kernel, sz),
        out_shape=tuple(jax.ShapeDtypeStruct(shape, kind) for shape, kind in outs),
        in_specs=[pl.BlockSpec(memory_space=pl.ANY)] * len(arrays),
        out_specs=(pl.BlockSpec(memory_space=pl.ANY),) * len(outs),
        scratch_shapes=scratch
        + [pltpu.SemaphoreType.DMA((220,)), pltpu.SemaphoreType.DMA((80,))],
        compiler_params=pltpu.CompilerParams(
            collective_id=0, has_side_effects=True, vmem_limit_bytes=63 * MIB
        ),
        name="program",
    )(*arrays)


def together(sz, hidden_in, d_out, gains, mixer, skip, filters, gate_up, down):
    pos = jnp.asarray(position_table(sz.length).T, F32).astype(BF16)
    arrays = (hidden_in, d_out, gains, mixer, skip, filters, gate_up, down, pos)
    raw = program(sz, arrays + dft_tables(sz.length))

    return results(sz, *raw)


def apart_enter(count, hid):
    me = lax.axis_index("rows") * hid + lax.axis_index("hid")
    barrier = pltpu.get_barrier_semaphore()

    def greet(step, carry):
        peer = lax.rem(me + step, count)
        pl.semaphore_signal(
            barrier, inc=1, device_id=(peer // hid, lax.rem(peer, hid)), device_id_type=MESH
        )
        return carry

    lax.fori_loop(1, count, greet, 0)
    return barrier


def apart_exchange_start(source, target, sems, count, rows, hid, piece, by_owner):
    send, recv, local = sems
    row = lax.axis_index("rows")
    col = lax.axis_index("hid")
    token_id = row * hid + col
    owner_id = col * rows + row
    mine_there = token_id if by_owner else owner_id
    mine_here = owner_id if by_owner else token_id
    at = lambda index: pl.ds(pl.multiple_of(index * piece, piece), piece)
    pltpu.make_async_copy(source.at[at(mine_here)], target.at[at(mine_there)], local).start()

    def post(step, carry):
        peer = lax.rem(token_id + step, count)
        peer_row = peer // hid
        peer_col = lax.rem(peer, hid)
        there = (peer_col * rows + peer_row) if by_owner else peer
        pltpu.make_async_remote_copy(
            src_ref=source.at[at(there)],
            dst_ref=target.at[at(mine_there)],
            send_sem=send,
            recv_sem=recv,
            device_id=(peer_row, peer_col),
            device_id_type=MESH,
        ).start()
        return carry

    lax.fori_loop(1, count, post, 0)


def apart_exchange_wait(source, target, sems, count, rows, hid, piece):
    send, recv, local = sems
    row = lax.axis_index("rows")
    col = lax.axis_index("hid")
    pltpu.make_async_copy(
        source.at[pl.ds(0, piece)], target.at[pl.ds(0, piece)], local
    ).wait()
    span = pl.ds(0, (count - 1) * piece)
    pltpu.make_async_remote_copy(
        src_ref=source.at[span],
        dst_ref=target.at[span],
        send_sem=send,
        recv_sem=recv,
        device_id=(row, hid - 1 - col),
        device_id_type=MESH,
    ).wait()


class apart_Sizes:
    def __init__(self, rows, hid, width, hidden, tokens):
        self.rows, self.hid, self.width, self.hidden = rows, hid, width, hidden
        self.count = rows * hid
        self.chans = width // self.count
        self.piece = round_up(self.chans, 16)
        self.length = min(SEQ_LEN, tokens)
        self.seqs = tokens // self.length
        self.blocks = self.length // LANES
        self.outer = 2 * self.blocks
        self.pairs = self.seqs * self.chans
        self.half = width // hid
        self.padded = rows * self.piece
        self.channels = self.count * self.piece


def apart_spread_in(source, wide, lines, stride, blocks):
    for place, line in enumerate(lines):
        wide[:, place * LANES : (place + 1) * LANES] = source[
            pl.ds(line, blocks, stride=stride), :
        ].astype(wide.dtype)


def apart_dft(wide, spectrum, tables, mid, flat, lines, outer, offset=0):
    outer_fwd, inner_fwd, twist = tables
    mid[:, : lines * LANES] = nn(outer_fwd[...], wide[:, : lines * LANES])
    cos = twist[:, :LANES]
    sin = twist[:, LANES:]
    for line in range(lines):
        lanes = pl.ds(line * LANES, LANES)
        real = mid[0:outer, lanes]
        imag = mid[outer : 2 * outer, lanes]
        rows = pl.ds(line * outer, outer)
        flat[rows, 0:LANES] = (real * cos + imag * sin).astype(BF16)
        flat[rows, LANES:] = (imag * cos - real * sin).astype(BF16)
    spectrum[0 : lines * outer, :] = nn(flat[0 : lines * outer, :], inner_fwd[...])


def apart_inverse_dft(flat, tables, mid_half, lines, outer):
    outer_inv, inner_inv, twist = tables
    cos = twist[:, :LANES]
    sin = twist[:, LANES:]
    for line in range(lines):
        rows = pl.ds(line * outer, outer)
        lanes = pl.ds(line * LANES, LANES)
        part = nn(flat[rows, :], inner_inv[...])
        real = part[:, :LANES]
        imag = part[:, LANES:]
        mid_half[0:outer, lanes] = (real * cos - imag * sin).astype(BF16)
        mid_half[outer : 2 * outer, lanes] = (imag * cos + real * sin).astype(BF16)
    return nn(outer_inv[...], mid_half[:, : lines * LANES])


def apart_spread_out(value, target, lines, stride, blocks):
    for place, line in enumerate(lines):
        target[pl.ds(line, blocks, stride=stride), :] = value[
            :, place * LANES : (place + 1) * LANES
        ]


def apart_signal_lines(sz):
    return [seq * sz.blocks * sz.piece + chan for seq in range(sz.seqs) for chan in range(sz.chans)]


def apart_conv_forward_kernel(
    sz,
    inner_ref,
    taps_ref,
    pos_ref,
    env_ref,
    outer_fwd,
    outer_inv,
    inner_fwd,
    inner_inv,
    twist,
    conv_ref,
    filt_spec,
    sig_spec,
    landed,
    staged,
    tall,
    wide,
    mid,
    flat,
    mid_half,
    sems_in,
    sems_out,
):
    barrier = apart_enter(sz.count, sz.hid)
    pl.semaphore_wait(barrier, sz.count - 1)
    into = tuple(sems_in.at[i] for i in range(3))
    back = tuple(sems_out.at[i] for i in range(3))
    apart_exchange_start(inner_ref, landed, into, sz.count, sz.rows, sz.hid, sz.piece, True)

    piece, blocks, outer = sz.piece, sz.blocks, sz.outer
    step = 4
    for start in range(0, blocks, step):
        span = slice(start * LANES, (start + step) * LANES)
        raw = nn(taps_ref[...], pos_ref[:, span])
        kernels = raw * env_ref[:, span]
        for block in range(step):
            tall[pl.ds((start + block) * 2 * piece, 2 * piece), :] = kernels[
                :, block * LANES : (block + 1) * LANES
            ]
    lines = [way * piece + chan for way in range(2) for chan in range(sz.chans)]
    apart_spread_in(tall, wide, lines, 2 * piece, blocks)
    apart_dft(wide, sig_spec, (outer_fwd, inner_fwd, twist), mid, flat, len(lines), outer)
    span = sz.chans * outer
    filt_spec[:, :LANES] = sig_spec[0:span, :LANES] + sig_spec[span : 2 * span, :LANES]
    filt_spec[:, LANES:] = sig_spec[0:span, LANES:] - sig_spec[span : 2 * span, LANES:]

    apart_exchange_wait(inner_ref, landed, into, sz.count, sz.rows, sz.hid, piece)
    tall[0 : sz.channels, :] = landed[...].astype(F32)
    lines = apart_signal_lines(sz)
    apart_spread_in(tall, wide, lines, piece, blocks)
    apart_dft(wide, sig_spec, (outer_fwd, inner_fwd, twist), mid, flat, sz.pairs, outer)
    for seq in range(sz.seqs):
        rows = pl.ds(seq * span, span)
        sig_re, sig_im = sig_spec[rows, :LANES], sig_spec[rows, LANES:]
        fil_re, fil_im = filt_spec[:, :LANES], filt_spec[:, LANES:]
        flat[rows, :LANES] = (sig_re * fil_re - sig_im * fil_im).astype(BF16)
        flat[rows, LANES:] = (sig_re * fil_im + sig_im * fil_re).astype(BF16)
    result = apart_inverse_dft(flat, (outer_inv, inner_inv, twist), mid_half, sz.pairs, outer)
    apart_spread_out(result, tall, lines, piece, blocks)
    staged[...] = tall[0 : sz.channels, :].astype(BF16)
    apart_exchange_start(staged, conv_ref, back, sz.count, sz.rows, sz.hid, piece, False)
    apart_exchange_wait(staged, conv_ref, back, sz.count, sz.rows, sz.hid, piece)


def apart_conv_forward(sz, inner, taps, pos, env, tables, cid):
    outer_fwd, outer_inv, inner_fwd, inner_inv, twist = tables
    wide_lines = max(2 * sz.chans, sz.pairs)
    return pl.pallas_call(
        functools.partial(apart_conv_forward_kernel, sz),
        out_shape=(
            jax.ShapeDtypeStruct((sz.channels, LANES), BF16),
            jax.ShapeDtypeStruct((sz.chans * sz.outer, 2 * LANES), F32),
            jax.ShapeDtypeStruct((wide_lines * sz.outer, 2 * LANES), F32),
        ),
        in_specs=[whole()] * 9,
        out_specs=(whole(),) * 3,
        scratch_shapes=[
            pltpu.VMEM((sz.channels, LANES), BF16),
            pltpu.VMEM((sz.channels, LANES), BF16),
            pltpu.VMEM((max(2 * sz.piece * sz.blocks, sz.channels), LANES), F32),
            pltpu.VMEM((sz.blocks, wide_lines * LANES), BF16),
            pltpu.VMEM((2 * sz.outer, wide_lines * LANES), F32),
            pltpu.VMEM((wide_lines * sz.outer, 2 * LANES), BF16),
            pltpu.VMEM((2 * sz.outer, sz.pairs * LANES), BF16),
            pltpu.SemaphoreType.DMA((3,)),
            pltpu.SemaphoreType.DMA((3,)),
        ],
        compiler_params=pltpu.CompilerParams(
            collective_id=cid, has_side_effects=True, vmem_limit_bytes=48 * MIB
        ),
        name="conv_forward",
    )(inner, taps, pos, env, outer_fwd, outer_inv, inner_fwd, inner_inv, twist)


def apart_conv_backward_kernel(
    sz,
    grad_ref,
    filt_spec,
    sig_spec,
    taps_ref,
    pos_ref,
    env_ref,
    outer_fwd,
    outer_inv,
    inner_fwd,
    inner_inv,
    twist,
    back_ref,
    taps_grad,
    landed,
    staged,
    tall,
    wide,
    mid,
    flat,
    mid_half,
    grad_spec,
    sems_in,
    sems_out,
):
    barrier = apart_enter(sz.count, sz.hid)
    pl.semaphore_wait(barrier, sz.count - 1)
    into = tuple(sems_in.at[i] for i in range(3))
    back = tuple(sems_out.at[i] for i in range(3))
    piece, blocks, outer = sz.piece, sz.blocks, sz.outer
    apart_exchange_start(grad_ref, landed, into, sz.count, sz.rows, sz.hid, piece, True)
    apart_exchange_wait(grad_ref, landed, into, sz.count, sz.rows, sz.hid, piece)
    tall[0 : sz.channels, :] = landed[...].astype(F32)
    lines = apart_signal_lines(sz)
    apart_spread_in(tall, wide, lines, piece, blocks)
    apart_dft(wide, grad_spec, (outer_fwd, inner_fwd, twist), mid, flat, sz.pairs, outer)
    span = sz.chans * outer
    for seq in range(sz.seqs):
        rows = pl.ds(seq * span, span)
        re, im = grad_spec[rows, :LANES], grad_spec[rows, LANES:]
        fil_re, fil_im = filt_spec[:, :LANES], filt_spec[:, LANES:]
        flat[rows, :LANES] = (re * fil_re + im * fil_im).astype(BF16)
        flat[rows, LANES:] = (im * fil_re - re * fil_im).astype(BF16)
    inv_tables = (outer_inv, inner_inv, twist)
    result = apart_inverse_dft(flat, inv_tables, mid_half, sz.pairs, outer)
    apart_spread_out(result, tall, lines, piece, blocks)
    staged[...] = tall[0 : sz.channels, :].astype(BF16)
    apart_exchange_start(staged, back_ref, back, sz.count, sz.rows, sz.hid, piece, False)

    total_re = jnp.zeros((span, LANES), F32)
    total_im = jnp.zeros((span, LANES), F32)
    for seq in range(sz.seqs):
        rows = pl.ds(seq * span, span)
        re, im = grad_spec[rows, :LANES], grad_spec[rows, LANES:]
        sig_re, sig_im = sig_spec[rows, :LANES], sig_spec[rows, LANES:]
        total_re += re * sig_re + im * sig_im
        total_im += im * sig_re - re * sig_im
    flat[0:span, :LANES] = total_re.astype(BF16)
    flat[span : 2 * span, :LANES] = total_re.astype(BF16)
    flat[0:span, LANES:] = total_im.astype(BF16)
    flat[span : 2 * span, LANES:] = (-total_im).astype(BF16)
    result = apart_inverse_dft(flat, inv_tables, mid_half, 2 * sz.chans, outer)
    lines = [way * piece + chan for way in range(2) for chan in range(sz.chans)]
    if sz.chans < piece:
        tall[...] = jnp.zeros_like(tall)
    apart_spread_out(result, tall, lines, 2 * piece, blocks)
    total = jnp.zeros((2 * piece, ORDER), F32)
    step = 4
    for start in range(0, blocks, step):
        span = slice(start * LANES, (start + step) * LANES)
        raw = nn(taps_ref[...], pos_ref[:, span])
        grads = jnp.concatenate(
            [
                tall[pl.ds((start + block) * 2 * piece, 2 * piece), :]
                for block in range(step)
            ],
            axis=1,
        )
        grads = grads * env_ref[:, span] + (2.0 * DECAY) * raw
        total += nt(grads.astype(BF16), pos_ref[:, span])
    taps_grad[...] = total

    apart_exchange_wait(staged, back_ref, back, sz.count, sz.rows, sz.hid, piece)


def apart_conv_backward(sz, grad, filt_spec, sig_spec, taps, pos, env, tables, cid):
    outer_fwd, outer_inv, inner_fwd, inner_inv, twist = tables
    wide_lines = max(2 * sz.chans, sz.pairs)
    return pl.pallas_call(
        functools.partial(apart_conv_backward_kernel, sz),
        out_shape=(
            jax.ShapeDtypeStruct((sz.channels, LANES), BF16),
            jax.ShapeDtypeStruct((2 * sz.piece, ORDER), F32),
        ),
        in_specs=[whole()] * 11,
        out_specs=(whole(),) * 2,
        scratch_shapes=[
            pltpu.VMEM((sz.channels, LANES), BF16),
            pltpu.VMEM((sz.channels, LANES), BF16),
            pltpu.VMEM((max(2 * sz.piece * sz.blocks, sz.channels), LANES), F32),
            pltpu.VMEM((sz.blocks, wide_lines * LANES), BF16),
            pltpu.VMEM((2 * sz.outer, wide_lines * LANES), F32),
            pltpu.VMEM((wide_lines * sz.outer, 2 * LANES), BF16),
            pltpu.VMEM((2 * sz.outer, wide_lines * LANES), BF16),
            pltpu.VMEM((sz.pairs * sz.outer, 2 * LANES), F32),
            pltpu.SemaphoreType.DMA((3,)),
            pltpu.SemaphoreType.DMA((3,)),
        ],
        compiler_params=pltpu.CompilerParams(
            collective_id=cid, has_side_effects=True, vmem_limit_bytes=48 * MIB
        ),
        name="conv_backward",
    )(grad, filt_spec, sig_spec, taps, pos, env, outer_fwd, outer_inv, inner_fwd, inner_inv, twist)


def apart_project(sz, normed, w_in, w_gate, inner_ref, gate_ref):
    for side in range(sz.hid):
        rows = slice(side * sz.padded, (side + 1) * sz.padded)
        part = normed[:, side * sz.half : (side + 1) * sz.half]
        inner_ref[rows, :] = nt(w_in[side], part).astype(BF16)
        gate_ref[rows, :] = nt(w_gate[side], part)


def apart_first_kernel(sz, x_ref, gain_ref, w_in, w_gate, normed_ref, inner_ref, gate_ref):
    normal, _ = normalize(x_ref[...].astype(F32))
    normed = (normal * gain_ref[0:1, :]).astype(BF16)
    normed_ref[...] = normed
    apart_project(sz, normed, w_in, w_gate, inner_ref, gate_ref)


def apart_first(sz, x, gains, w_in, w_gate):
    tokens = x.shape[0]
    return pl.pallas_call(
        functools.partial(apart_first_kernel, sz),
        out_shape=(
            jax.ShapeDtypeStruct((tokens, sz.width), BF16),
            jax.ShapeDtypeStruct((sz.channels, tokens), BF16),
            jax.ShapeDtypeStruct((sz.channels, tokens), F32),
        ),
        in_specs=[whole()] * 4,
        out_specs=(whole(),) * 3,
        compiler_params=pltpu.CompilerParams(vmem_limit_bytes=32 * MIB),
        name="first_projection",
    )(x, gains, w_in, w_gate)


def apart_mix_out(sz, mixed, w_out):
    parts = []
    for side in range(sz.hid):
        rows = slice(side * sz.padded, (side + 1) * sz.padded)
        parts.append(tn(mixed[rows, :], w_out[side]))
    return jnp.concatenate(parts, axis=1)


def apart_ff_specs(sz, layer, tile):
    steps = sz.hidden // sz.hid // tile
    first_half = lambda i: jnp.minimum(i, steps - 1)
    second = lambda i: jnp.maximum(i - steps, 0)
    specs = []
    for place in (first_half, second):
        specs.append(
            pl.BlockSpec((1, 2, sz.width, tile), lambda i, place=place: (layer, 0, 0, place(i)))
        )
        specs.append(pl.BlockSpec((1, sz.width, tile), lambda i, place=place: (layer, 0, place(i))))
    return specs, steps


def apart_forward_kernel(
    sz,
    steps,
    conv_ref,
    inner_ref,
    gate_ref,
    skip_ref,
    x_ref,
    gain_ref,
    next_gain,
    w_out,
    w_in,
    w_gate,
    up_a,
    down_a,
    up_b,
    down_b,
    summed_ref,
    mixed_ref,
    middle_ref,
    normed_two,
    next_x,
    next_normed,
    next_inner,
    next_gate,
):
    index = pl.program_id(0)

    @pl.when(index == 0)
    def _():
        summed = conv_ref[...].astype(F32) + skip_ref[...] * inner_ref[...].astype(F32)
        summed_ref[...] = summed
        mixed_ref[...] = (gate_ref[...] * summed).astype(BF16)
        middle = x_ref[...].astype(F32) + apart_mix_out(sz, mixed_ref, w_out)
        middle_ref[...] = middle
        normal, _ = normalize(middle)
        normed_two[...] = (normal * gain_ref[1:2, :]).astype(BF16)
        next_x[...] = middle

    def accumulate(up_ref, down_ref):
        gate = nn(normed_two[...], up_ref[0, 0])
        up = nn(normed_two[...], up_ref[0, 1])
        value, _ = gelu_parts(gate)
        next_x[...] += nt((value * up).astype(BF16), down_ref[0])

    pl.when(index < steps)(lambda: accumulate(up_a, down_a))
    pl.when(index >= steps)(lambda: accumulate(up_b, down_b))

    @pl.when(index == 2 * steps - 1)
    def _():
        normal, _ = normalize(next_x[...])
        normed = (normal * next_gain[0:1, :]).astype(BF16)
        next_normed[...] = normed
        apart_project(sz, normed, w_in, w_gate, next_inner, next_gate)


def apart_full(shape):
    return pl.BlockSpec(shape, lambda i: (0,) * len(shape))


def apart_forward(sz, layer, conv, inner, gate, skip, x, gains, next_gains, w_out, w_in, w_gate, ff):
    tokens = x.shape[0]
    tile = 512
    specs, steps = apart_ff_specs(sz, layer, tile)
    small = (conv, inner, gate, skip, x, gains, next_gains, w_out, w_in, w_gate)
    outs = (
        ((sz.channels, tokens), F32),
        ((sz.channels, tokens), BF16),
        ((tokens, sz.width), F32),
        ((tokens, sz.width), BF16),
        ((tokens, sz.width), F32),
        ((tokens, sz.width), BF16),
        ((sz.channels, tokens), BF16),
        ((sz.channels, tokens), F32),
    )
    return pl.pallas_call(
        functools.partial(apart_forward_kernel, sz, steps),
        grid=(2 * steps,),
        out_shape=tuple(jax.ShapeDtypeStruct(shape, kind) for shape, kind in outs),
        in_specs=[apart_full(entry.shape) for entry in small] + specs,
        out_specs=tuple(apart_full(shape) for shape, kind in outs),
        compiler_params=pltpu.CompilerParams(
            dimension_semantics=("arbitrary",), vmem_limit_bytes=48 * MIB
        ),
        name="token_forward",
    )(*small, *ff)


def apart_block_grads(sz, tall, flat, target, slot):
    blocks_side = target.shape[1] // sz.hid
    size = sz.half // blocks_side
    rows = sz.padded // blocks_side
    for side in range(sz.hid):
        for block in range(blocks_side):
            begin = side * sz.padded + block * rows
            place = side * sz.half + block * size
            target[slot, side * blocks_side + block] = nn(
                tall[begin : begin + rows, :], flat[:, place : place + size]
            ).astype(target.dtype)


def apart_ff_backward_tile(normed, grad, up_ref, down_ref, total, out_total):
    gate = nn(normed, up_ref[0, 0])
    up = nn(normed, up_ref[0, 1])
    grad_hidden = nn(grad, down_ref[0])
    value, slope = gelu_parts(gate)
    if out_total is not None:
        out_total[...] += nt((value * up).astype(BF16), down_ref[0])
    grad_gate = (slope * up * grad_hidden).astype(BF16)
    grad_up = (value * grad_hidden).astype(BF16)
    total[...] += nt(grad_gate, up_ref[0, 0]) + nt(grad_up, up_ref[0, 1])


def apart_mixer_backward(
    sz, grad_next, middle, total, gain, mixed, summed, gate, w_out, outs
):
    grad_middle, mixer_grad, grad_gate, grad_summed, grad_conv, gain_grad = outs
    normal, inv = normalize(middle)
    back, gain_grad[...] = norm_back(total, normal, inv, gain)
    result = grad_next + back
    grad_middle[...] = result
    grad_o = result.astype(BF16)
    apart_block_grads(sz, mixed, grad_o, mixer_grad, 0)
    for side in range(sz.hid):
        rows = slice(side * sz.padded, (side + 1) * sz.padded)
        grad_mixed = nt(w_out[side], grad_o[:, side * sz.half : (side + 1) * sz.half])
        grad_gate[rows, :] = (grad_mixed * summed[rows, :]).astype(BF16)
        through = grad_mixed * gate[rows, :]
        grad_summed[rows, :] = through
        grad_conv[rows, :] = through.astype(BF16)


def apart_mixer_outs(sz, tokens, blocks):
    size = sz.width // blocks
    return (
        ((tokens, sz.width), F32),
        ((1, blocks, sz.channels // blocks, size), BF16),
        ((sz.channels, tokens), BF16),
        ((sz.channels, tokens), F32),
        ((sz.channels, tokens), BF16),
        ((1, sz.width), F32),
    )


def apart_turn_kernel(
    sz,
    steps,
    conv_ref,
    inner_ref,
    gate_ref,
    skip_ref,
    x_ref,
    gain_ref,
    grad_ref,
    w_out,
    up_a,
    down_a,
    up_b,
    down_b,
    hidden_out,
    normed_two,
    grad_middle,
    mixer_grad,
    grad_gate,
    grad_summed,
    grad_conv,
    gain_grad,
    summed,
    mixed,
    middle,
    out_total,
    total,
):
    index = pl.program_id(0)

    @pl.when(index == 0)
    def _():
        summed[...] = conv_ref[...].astype(F32) + skip_ref[...] * inner_ref[...].astype(F32)
        mixed[...] = (gate_ref[...] * summed[...]).astype(BF16)
        middle[...] = x_ref[...].astype(F32) + apart_mix_out(sz, mixed, w_out)
        normal, _ = normalize(middle[...])
        normed_two[...] = (normal * gain_ref[1:2, :]).astype(BF16)
        out_total[...] = middle[...]
        total[...] = jnp.zeros_like(total)

    def accumulate(up_ref, down_ref):
        apart_ff_backward_tile(normed_two[...], grad_ref[...], up_ref, down_ref, total, out_total)

    pl.when(index < steps)(lambda: accumulate(up_a, down_a))
    pl.when(index >= steps)(lambda: accumulate(up_b, down_b))

    @pl.when(index == 2 * steps - 1)
    def _():
        hidden_out[...] = out_total[...].astype(BF16)
        outs = (grad_middle, mixer_grad, grad_gate, grad_summed, grad_conv, gain_grad)
        apart_mixer_backward(
            sz,
            grad_ref[...].astype(F32),
            middle[...],
            total[...],
            gain_ref[1:2, :],
            mixed,
            summed,
            gate_ref,
            w_out,
            outs,
        )


def apart_turn(sz, layer, blocks, conv, inner, gate, skip, x, gains, grad, w_out, ff):
    tokens = x.shape[0]
    specs, steps = apart_ff_specs(sz, layer, 512)
    small = (conv, inner, gate, skip, x, gains, grad, w_out)
    outs = (((tokens, sz.width), BF16), ((tokens, sz.width), BF16)) + apart_mixer_outs(sz, tokens, blocks)
    return pl.pallas_call(
        functools.partial(apart_turn_kernel, sz, steps),
        grid=(2 * steps,),
        out_shape=tuple(jax.ShapeDtypeStruct(shape, kind) for shape, kind in outs),
        in_specs=[apart_full(entry.shape) for entry in small] + specs,
        out_specs=tuple(apart_full(shape) for shape, kind in outs),
        scratch_shapes=[
            pltpu.VMEM((sz.channels, tokens), F32),
            pltpu.VMEM((sz.channels, tokens), BF16),
            pltpu.VMEM((tokens, sz.width), F32),
            pltpu.VMEM((tokens, sz.width), F32),
            pltpu.VMEM((tokens, sz.width), F32),
        ],
        compiler_params=pltpu.CompilerParams(
            dimension_semantics=("arbitrary",), vmem_limit_bytes=48 * MIB
        ),
        name="token_turn",
    )(*small, *ff)


def apart_input_backward(
    sz, back, through, grad_gate, skip, normed, x, gain, w_in, w_gate, grad_middle, mixer_grad
):
    inner_grad = (skip * through + back.astype(F32)).astype(BF16)
    apart_block_grads(sz, inner_grad, normed, mixer_grad, 0)
    apart_block_grads(sz, grad_gate, normed, mixer_grad, 1)
    parts = []
    for side in range(sz.hid):
        rows = slice(side * sz.padded, (side + 1) * sz.padded)
        parts.append(tn(inner_grad[rows, :], w_in[side]) + tn(grad_gate[rows, :], w_gate[side]))
    normal, inv = normalize(x)
    result, gain_grad = norm_back(jnp.concatenate(parts, axis=1), normal, inv, gain)
    return grad_middle + result, gain_grad


def apart_backward_kernel(
    sz,
    steps,
    back_ref,
    through_ref,
    gate_grad_ref,
    skip_ref,
    normed_ref,
    x_ref,
    gain_ref,
    w_in,
    w_gate,
    grad_middle_ref,
    normed_two,
    middle_ref,
    summed_ref,
    gate_ref,
    mixed_ref,
    low_gain,
    w_out,
    up_a,
    down_a,
    up_b,
    down_b,
    input_grad,
    input_gain,
    grad_ff,
    grad_middle,
    mixer_grad,
    grad_gate,
    grad_summed,
    grad_conv,
    gain_grad,
    grad_next,
    total,
):
    index = pl.program_id(0)

    @pl.when(index == 0)
    def _():
        result, input_gain[...] = apart_input_backward(
            sz,
            back_ref[...],
            through_ref[...],
            gate_grad_ref[...],
            skip_ref[...],
            normed_ref[...],
            x_ref[...],
            gain_ref[0:1, :],
            w_in,
            w_gate,
            grad_middle_ref[...],
            input_grad,
        )
        grad_next[...] = result
        grad_ff[...] = result.astype(BF16)
        total[...] = jnp.zeros_like(total)

    def accumulate(up_ref, down_ref):
        apart_ff_backward_tile(normed_two[...], grad_ff[...], up_ref, down_ref, total, None)

    pl.when(index < steps)(lambda: accumulate(up_a, down_a))
    pl.when(index >= steps)(lambda: accumulate(up_b, down_b))

    @pl.when(index == 2 * steps - 1)
    def _():
        outs = (grad_middle, mixer_grad, grad_gate, grad_summed, grad_conv, gain_grad)
        apart_mixer_backward(
            sz,
            grad_next[...],
            middle_ref[...],
            total[...],
            low_gain[1:2, :],
            mixed_ref,
            summed_ref,
            gate_ref,
            w_out,
            outs,
        )


def apart_input_outs(sz, blocks):
    size = sz.width // blocks
    return (((2, blocks, sz.channels // blocks, size), BF16), ((1, sz.width), F32))


def apart_backward(
    sz,
    layer,
    blocks,
    back,
    through,
    gate_grad,
    skip,
    normed,
    x,
    gains,
    w_in,
    w_gate,
    grad_middle,
    normed_two,
    middle,
    summed,
    gate,
    mixed,
    low_gains,
    w_out,
    ff,
):
    tokens = x.shape[0]
    specs, steps = apart_ff_specs(sz, layer, 512)
    small = (
        back,
        through,
        gate_grad,
        skip,
        normed,
        x,
        gains,
        w_in,
        w_gate,
        grad_middle,
        normed_two,
        middle,
        summed,
        gate,
        mixed,
        low_gains,
        w_out,
    )
    outs = (
        apart_input_outs(sz, blocks) + (((tokens, sz.width), BF16),) + apart_mixer_outs(sz, tokens, blocks)
    )
    return pl.pallas_call(
        functools.partial(apart_backward_kernel, sz, steps),
        grid=(2 * steps,),
        out_shape=tuple(jax.ShapeDtypeStruct(shape, kind) for shape, kind in outs),
        in_specs=[apart_full(entry.shape) for entry in small] + specs,
        out_specs=tuple(apart_full(shape) for shape, kind in outs),
        scratch_shapes=[
            pltpu.VMEM((tokens, sz.width), F32),
            pltpu.VMEM((tokens, sz.width), F32),
        ],
        compiler_params=pltpu.CompilerParams(
            dimension_semantics=("arbitrary",), vmem_limit_bytes=48 * MIB
        ),
        name="token_backward",
    )(*small, *ff)


def apart_last_kernel(
    sz,
    back_ref,
    through_ref,
    gate_grad_ref,
    skip_ref,
    normed_ref,
    x_ref,
    gain_ref,
    w_in,
    w_gate,
    grad_middle_ref,
    input_grad,
    input_gain,
    grad_in,
):
    grad_in[...], input_gain[...] = apart_input_backward(
        sz,
        back_ref[...],
        through_ref[...],
        gate_grad_ref[...],
        skip_ref[...],
        normed_ref[...],
        x_ref[...].astype(F32),
        gain_ref[0:1, :],
        w_in,
        w_gate,
        grad_middle_ref[...],
        input_grad,
    )


def apart_last(sz, blocks, *args):
    tokens = args[5].shape[0]
    outs = apart_input_outs(sz, blocks) + (((tokens, sz.width), F32),)
    return pl.pallas_call(
        functools.partial(apart_last_kernel, sz),
        out_shape=tuple(jax.ShapeDtypeStruct(shape, kind) for shape, kind in outs),
        in_specs=[whole()] * len(args),
        out_specs=(whole(),) * len(outs),
        compiler_params=pltpu.CompilerParams(vmem_limit_bytes=32 * MIB),
        name="last_projection",
    )(*args)


def apart_ff_grads_kernel(normed_ref, grad_ref, up_ref, down_ref, out_ref, hidden, grad_gate, grad_up):
    tokens = normed_ref.shape[0]
    chunk = 256
    for start in range(0, tokens, chunk):
        rows = pl.ds(start, chunk)
        normed = normed_ref[rows, :]
        gate = nn(normed, up_ref[0])
        up = nn(normed, up_ref[1])
        through = nn(grad_ref[rows, :], down_ref[...])
        value, slope = gelu_parts(gate)
        hidden[rows, :] = (value * up).astype(BF16)
        grad_gate[rows, :] = (slope * up * through).astype(BF16)
        grad_up[rows, :] = (value * through).astype(BF16)
    out_ref[0] = tn(normed_ref[...], grad_gate[...]).astype(BF16)
    out_ref[1] = tn(normed_ref[...], grad_up[...]).astype(BF16)
    out_ref[2] = tn(grad_ref[...], hidden[...]).astype(BF16)


def apart_ff_grads(normed, grad, up, down):
    tokens, width = normed.shape
    units = down.shape[1]
    return pl.pallas_call(
        apart_ff_grads_kernel,
        out_shape=jax.ShapeDtypeStruct((3, width, units), BF16),
        in_specs=[whole()] * 4,
        out_specs=whole(),
        scratch_shapes=[pltpu.VMEM((tokens, units), BF16)] * 3,
        compiler_params=pltpu.CompilerParams(vmem_limit_bytes=48 * MIB),
        name="ff_weight_grads",
    )(normed, grad, up, down)


def apart_row_exchange_kernel(rows, parts, *refs):
    sources, targets, sems = refs[:parts], refs[parts : 2 * parts], refs[2 * parts]
    row = lax.axis_index("rows")
    col = lax.axis_index("hid")
    barrier = pltpu.get_barrier_semaphore()

    def greet(step, carry):
        peer = lax.rem(row + step, rows)
        pl.semaphore_signal(barrier, inc=1, device_id=(peer, col), device_id_type=MESH)
        return carry

    lax.fori_loop(1, rows, greet, 0)
    for part in range(parts):
        pltpu.make_async_copy(
            sources[part].at[row], targets[part].at[row], sems.at[part, 2]
        ).start()
    pl.semaphore_wait(barrier, rows - 1)

    def post(step, carry):
        peer = lax.rem(row + step, rows)
        for part in range(parts):
            pltpu.make_async_remote_copy(
                src_ref=sources[part].at[peer],
                dst_ref=targets[part].at[row],
                send_sem=sems.at[part, 0],
                recv_sem=sems.at[part, 1],
                device_id=(peer, col),
                device_id_type=MESH,
            ).start()
        return carry

    lax.fori_loop(1, rows, post, 0)
    for part in range(parts):
        pltpu.make_async_copy(
            sources[part].at[0], targets[part].at[0], sems.at[part, 2]
        ).wait()
        span = pl.ds(0, rows - 1)
        pltpu.make_async_remote_copy(
            src_ref=sources[part].at[span],
            dst_ref=targets[part].at[span],
            send_sem=sems.at[part, 0],
            recv_sem=sems.at[part, 1],
            device_id=(lax.rem(row + 1, rows), col),
            device_id_type=MESH,
        ).wait()


def apart_row_exchange(arrays, rows, cid):
    parts = len(arrays)
    return pl.pallas_call(
        functools.partial(apart_row_exchange_kernel, rows, parts),
        out_shape=tuple(jax.ShapeDtypeStruct(entry.shape, entry.dtype) for entry in arrays),
        in_specs=[pl.BlockSpec(memory_space=pl.ANY)] * parts,
        out_specs=(pl.BlockSpec(memory_space=pl.ANY),) * parts,
        scratch_shapes=[pltpu.SemaphoreType.DMA((parts, 3))],
        compiler_params=pltpu.CompilerParams(collective_id=cid, has_side_effects=True),
        name="row_exchange",
    )(*arrays)


def apart_swap(value):
    return lax.ppermute(value, "hid", [(0, 1), (1, 0)])


def apart_both_halves(own, axis):
    other = apart_swap(own)
    low = lax.axis_index("hid") == 0
    return jnp.concatenate([jnp.where(low, own, other), jnp.where(low, other, own)], axis=axis)


def apart_own_tokens(part):
    tokens = part.shape[0] // 2
    side = lax.axis_index("hid")
    keep = lax.dynamic_slice_in_dim(part, side * tokens, tokens, 0)
    other = apart_swap(lax.dynamic_slice_in_dim(part, (1 - side) * tokens, tokens, 0))
    low = side == 0
    return jnp.concatenate([jnp.where(low, keep, other), jnp.where(low, other, keep)], axis=1)


def apart_own_features(part):
    half = part.shape[1] // 2
    side = lax.axis_index("hid")
    keep = lax.dynamic_slice_in_dim(part, side * half, half, 1)
    other = apart_swap(lax.dynamic_slice_in_dim(part, (1 - side) * half, half, 1))
    low = side == 0
    return jnp.concatenate([jnp.where(low, keep, other), jnp.where(low, other, keep)], axis=0)


def apart_padded_mixer(sz, mixer):
    layers, kinds, blocks, size, _ = mixer.shape
    chan_first = jnp.concatenate([jnp.swapaxes(mixer[:, :2], 3, 4), mixer[:, 2:]], axis=1)
    grouped = chan_first.reshape(layers, kinds, blocks, size // sz.chans, sz.chans, size)
    grouped = jnp.pad(grouped, ((0, 0),) * 4 + ((0, sz.piece - sz.chans), (0, 0)))
    grouped = grouped.reshape(layers, kinds, blocks, -1, size)
    parts = [
        jnp.pad(grouped[:, :, block], ((0, 0),) * 3 + ((block * size, (blocks - 1 - block) * size),))
        for block in range(blocks)
    ]
    return jnp.concatenate(parts, axis=2)


def apart_padded_channels(sz, values):
    lead = values.shape[:-1]
    grouped = values.reshape(lead + (sz.rows, sz.chans))
    grouped = jnp.pad(grouped, ((0, 0),) * (len(lead) + 1) + ((0, sz.piece - sz.chans),))
    return grouped.reshape(lead + (sz.padded,))


def apart_envelopes(sz):
    row = lax.axis_index("rows")
    first_chan = lax.axis_index("hid") * sz.half + row * sz.chans
    channels = first_chan + jnp.arange(sz.piece, dtype=jnp.int32)
    fraction = (channels * 37 % sz.width).astype(F32) / (sz.width - 1)
    start_log = math.log(1.0 / 40.0)
    rate = jnp.exp(start_log + (math.log(1.5 / sz.length) - start_log) * fraction)
    steps = jnp.arange(sz.length, dtype=jnp.int32).astype(F32)
    decay = jnp.exp(-steps[None, :] * rate[:, None])
    shape = decay * lax.rsqrt(2.0 * jnp.sum(decay * decay, axis=1, keepdims=True))
    return jnp.concatenate([shape, shape * (steps > 0)[None, :]], axis=0)


def apart_plane_gather(value):
    size = lax.axis_size("rows")
    for bit in (1, 2):
        other = lax.ppermute(value, "rows", [(r, r ^ bit) for r in range(size)])
        value = jnp.concatenate([value, other], axis=0)
    return jnp.concatenate([value, apart_swap(value)], axis=0)


def apart_on_device(hidden_in, d_out, gains, mixer, skip, filters, gate_up, down):
    layers = gate_up.shape[0]
    rows = lax.axis_size("rows")
    hid = lax.axis_size("hid")
    width = gate_up.shape[2]
    hidden = gate_up.shape[3] * hid
    blocks = mixer.shape[2] * hid
    block_size = mixer.shape[3]
    sz = apart_Sizes(rows, hid, width, hidden, hidden_in.shape[0] * rows)
    row = lax.axis_index("rows")

    x = apart_own_tokens(hidden_in)
    gains_all = apart_both_halves(gains, 2)
    skip_all = apart_both_halves(apart_padded_channels(sz, skip), 1)[:, :, None]
    weights = apart_both_halves(apart_padded_mixer(sz, mixer)[:, :, None], 2)
    gate_up_b = apart_swap(gate_up)
    down_b = apart_swap(down)
    ff = (gate_up, down, gate_up_b, down_b)
    grad_out = apart_own_tokens(d_out)

    tables = dft_tables(sz.length)
    pos = jnp.asarray(position_table(sz.length).T, F32).astype(BF16)
    env = apart_envelopes(sz)
    taps = lax.dynamic_slice_in_dim(filters, row * sz.chans, sz.chans, 3)
    taps = jnp.pad(taps, ((0, 0),) * 3 + ((0, sz.piece - sz.chans),))
    taps = jnp.swapaxes(taps, 2, 3).reshape(layers, 2 * sz.piece, ORDER).astype(BF16)

    normed, inner, gate = apart_first(sz, x, gains_all[0], weights[0, 0], weights[0, 1])
    stored = []
    for layer in range(layers):
        conv, filt_spec, sig_spec = apart_conv_forward(sz, inner, taps[layer], pos, env, tables, 0)
        stored.append(dict(x=x, normed=normed, inner=inner, gate=gate, f=filt_spec, s=sig_spec))
        if layer < layers - 1:
            summed, mixed, middle, normed_two, x, normed, next_inner, next_gate = apart_forward(
                sz,
                layer,
                conv,
                inner,
                gate,
                skip_all[layer],
                x,
                gains_all[layer],
                gains_all[layer + 1],
                weights[layer, 2],
                weights[layer + 1, 0],
                weights[layer + 1, 1],
                ff,
            )
            stored[-1].update(summed=summed, mixed=mixed, middle=middle, normed_two=normed_two)
            inner, gate = next_inner, next_gate

    top = layers - 1
    hidden_out, normed_two, *rest = apart_turn(
        sz,
        top,
        blocks,
        conv,
        inner,
        gate,
        skip_all[top],
        x,
        gains_all[top],
        grad_out,
        weights[top, 2],
        ff,
    )
    stored[top].update(normed_two=normed_two)
    grad_ff = grad_out
    units = sz.hidden // hid // 4
    unit_start = lax.rem(row, 4) * units
    ff_parts, mixer_parts, gain_parts, skip_parts, taps_parts = [], [], [], [], []
    for layer in reversed(range(layers)):
        kept = stored[layer]
        grad_middle, out_grad, grad_gate, grad_summed, grad_conv, gain_two = rest
        ff_parts.insert(
            0,
            apart_ff_grads(
                apart_plane_gather(kept["normed_two"]),
                apart_plane_gather(grad_ff),
                lax.dynamic_slice_in_dim(gate_up[layer], unit_start, units, 2),
                lax.dynamic_slice_in_dim(down[layer], unit_start, units, 1),
            ),
        )
        back, taps_grad = apart_conv_backward(
            sz, grad_conv, kept["f"], kept["s"], taps[layer], pos, env, tables, 1
        )
        skip_parts.insert(0, jnp.sum(grad_summed * kept["inner"].astype(F32), axis=1))
        taps_parts.insert(0, taps_grad)
        common = (
            back,
            grad_summed,
            grad_gate,
            skip_all[layer],
            kept["normed"],
            kept["x"],
            gains_all[layer],
            weights[layer, 0],
            weights[layer, 1],
            grad_middle,
        )
        if layer > 0:
            low = stored[layer - 1]
            in_grad, gain_one, grad_ff, *rest = apart_backward(
                sz,
                layer - 1,
                blocks,
                *common,
                low["normed_two"],
                low["middle"],
                low["summed"],
                low["gate"],
                low["mixed"],
                gains_all[layer - 1],
                weights[layer - 1, 2],
                ff,
            )
        else:
            in_grad, gain_one, grad_in = apart_last(sz, blocks, *common)
        mixer_parts.insert(0, jnp.concatenate([in_grad, out_grad], axis=0))
        gain_parts.insert(0, jnp.concatenate([gain_one, gain_two], axis=0))

    piece_rows = width // rows
    padded_rows = round_up(piece_rows, 16)
    pieces = jnp.stack(ff_parts).reshape(layers, 3, rows, piece_rows, units)
    pieces = jnp.pad(pieces, ((0, 0),) * 3 + ((0, padded_rows - piece_rows), (0, 0)))
    pieces = jnp.moveaxis(pieces, 2, 0)
    (arrived,) = apart_row_exchange((pieces,), rows, 2)
    arrived = arrived.reshape(rows // 4, 4, layers, 3, padded_rows, units)[:, :, :, :, :piece_rows]
    summed_ff = jnp.sum(arrived.astype(F32), axis=0)
    summed_ff = jnp.moveaxis(summed_ff, 0, 3).reshape(layers, 3, piece_rows, 4 * units)

    mixers = jnp.stack(mixer_parts).reshape(layers, 3, blocks, -1, sz.piece, block_size)
    mixers = mixers[:, :, :, :, : sz.chans].reshape(layers, 3, blocks, block_size, block_size)
    small = jnp.concatenate(
        [jnp.stack(gain_parts).reshape(-1), jnp.stack(skip_parts).reshape(-1)]
    )
    mixers, small = lax.psum((mixers.astype(F32), small), ("rows", "hid"))
    side = lax.axis_index("hid")
    mixers = lax.dynamic_slice_in_dim(mixers, side * (blocks // hid), blocks // hid, 2)
    mixers = jnp.concatenate([jnp.swapaxes(mixers[:, :2], 3, 4), mixers[:, 2:]], axis=1)
    gain_size = layers * 2 * width
    gain_out = lax.dynamic_slice_in_dim(
        small[:gain_size].reshape(layers, 2, width), side * sz.half, sz.half, 2
    )
    skip_out = small[gain_size:].reshape(layers, hid, rows, sz.piece)[..., : sz.chans]
    skip_out = lax.dynamic_index_in_dim(skip_out, side, 1, False).reshape(layers, sz.half)
    taps_out = jnp.stack(taps_parts).reshape(layers, 2, sz.piece, ORDER)[:, :, : sz.chans]
    taps_out = lax.all_gather(taps_out, "rows", axis=2, tiled=True)
    return (
        apart_own_features(hidden_out),
        apart_own_features(grad_in),
        gain_out,
        mixers,
        skip_out,
        jnp.swapaxes(taps_out, 2, 3),
        summed_ff[:, :2],
        summed_ff[:, 2],
    )


def on_device(*arrays):
    sz = Sizes.of(*arrays)
    return together(sz, *arrays) if sz.fits() else apart_on_device(*arrays)


def solution(mesh):
    placed = (
        P("rows", "hid"),
        P("rows", "hid"),
        P(None, None, "hid"),
        P(None, None, "hid", None, None),
        P(None, "hid"),
        P(None, None, None, "hid"),
        P(None, None, None, "hid"),
        P(None, None, "hid"),
    )
    return jax.shard_map(
        on_device,
        mesh=mesh,
        in_specs=placed,
        out_specs=(
            P("rows", "hid"),
            P("rows", "hid"),
            P(None, None, "hid"),
            P(None, None, "hid", None, None),
            P(None, "hid"),
            P(None, None, None, "hid"),
            P(None, None, "rows", "hid"),
            P(None, "rows", "hid"),
        ),
        check_vma=False,
    )
```
